32 devices in a mesh: dp: 8 (over z, y), expert: 4 (over x, core).
Axes of the slice: x: 2, y: 2, z: 4, core: 2. Of those that a mesh axis runs over, the one named last changes fastest.
Arguments:
- patches: bfloat16 [32768, 768], P(('dp', 'expert')), may hold values from -6 to 6
- lengths: int32 [128, 3], P(('dp', 'expert')), may hold values from 1 to 196, 256 in all within a row
- slot_mask: int32 [128, 256], P(('dp', 'expert')), may hold values from 0 to 1
- expert_picks: int32 [32768, 2], P(('dp', 'expert')), may hold values from 0 to 7, all different within a row
- priority_rank: int32 [32, 1024], P(('dp', 'expert')), may hold values from 0 to 1023, each once within a row
- class_labels: int32 [18432, 384], P(('dp', 'expert')), may hold values 0 or 1
- dense_weights: float32 [5, 768, 768], P(None, ('dp', 'expert')), may hold values from -0.21875 to 0.21875
- dense_first: float32 [5, 768, 768], P(None, ('dp', 'expert')), may hold values from -9.1552734e-05 to 9.1552734e-05
- dense_second: float32 [5, 768, 768], P(None, ('dp', 'expert')), may hold values from 2.8257017e-12 to 1.1302807e-09
- dense_average: float32 [5, 768, 768], P(None, ('dp', 'expert')), may hold values from -0.21875 to 0.21875
- router_weights: float32 [768, 8], P(('dp', 'expert')), may hold values from -0.15625 to 0.15625
- router_first: float32 [768, 8], P(('dp', 'expert')), may hold values from -9.1552734e-05 to 9.1552734e-05
- router_second: float32 [768, 8], P(('dp', 'expert')), may hold values from 2.8257017e-12 to 1.1302807e-11
- router_average: float32 [768, 8], P(('dp', 'expert')), may hold values from -0.15625 to 0.15625
- norm_params: float32 [6, 768], P(None, ('dp', 'expert')), may hold values from -2 to 2
- norm_first: float32 [6, 768], P(None, ('dp', 'expert')), may hold values from -0.0012207031 to 0.0012207031
- norm_second: float32 [6, 768], P(None, ('dp', 'expert')), may hold values from 6.3578287e-10 to 2.5431315e-09
- norm_average: float32 [6, 768], P(None, ('dp', 'expert')), may hold values from 0.5 to 1.5
- expert_in: float32 [8, 3072, 768], P('expert', 'dp'), may hold values from -0.21875 to 0.21875
- in_first: float32 [8, 3072, 768], P('expert', 'dp'), may hold values from -9.1552734e-05 to 9.1552734e-05
- in_second: float32 [8, 3072, 768], P('expert', 'dp'), may hold values from 2.8257017e-12 to 1.1302807e-11
- in_average: float32 [8, 3072, 768], P('expert', 'dp'), may hold values from -0.21875 to 0.21875
- expert_out: float32 [8, 3072, 768], P('expert', 'dp'), may hold values from -0.875 to 0.875
- out_first: float32 [8, 3072, 768], P('expert', 'dp'), may hold values from -2.2888184e-05 to 2.2888184e-05
- out_second: float32 [8, 3072, 768], P('expert', 'dp'), may hold values from 1.7660636e-13 to 7.064254e-13
- out_average: float32 [8, 3072, 768], P('expert', 'dp'), may hold values from -0.875 to 0.875
- head_weights: float32 [18432, 768], P(('dp', 'expert')), may hold values from -1 to 1
- head_first: float32 [18432, 768], P(('dp', 'expert')), may hold values from -0.0004272461 to 0.0004272461
- head_second: float32 [18432, 768], P(('dp', 'expert')), may hold values from 1.4128508e-11 to 5.6514033e-11
- head_average: float32 [18432, 768], P(('dp', 'expert')), may hold values from -0.4375 to 0.4375
Outputs:
- loss_value: float32 [], replicated
- importance: float32 [8], replicated
- grad_norm: float32 [], replicated
- dense_new: float32 [5, 768, 768], P(None, ('dp', 'expert'))
- dense_first_new: float32 [5, 768, 768], P(None, ('dp', 'expert'))
- dense_second_new: float32 [5, 768, 768], P(None, ('dp', 'expert'))
- dense_average_new: float32 [5, 768, 768], P(None, ('dp', 'expert'))
- router_new: float32 [768, 8], P(('dp', 'expert'))
- router_first_new: float32 [768, 8], P(('dp', 'expert'))
- router_second_new: float32 [768, 8], P(('dp', 'expert'))
- router_average_new: float32 [768, 8], P(('dp', 'expert'))
- norm_new: float32 [6, 768], P(None, ('dp', 'expert'))
- norm_first_new: float32 [6, 768], P(None, ('dp', 'expert'))
- norm_second_new: float32 [6, 768], P(None, ('dp', 'expert'))
- norm_average_new: float32 [6, 768], P(None, ('dp', 'expert'))
- in_new: float32 [8, 3072, 768], P('expert', 'dp')
- in_first_new: float32 [8, 3072, 768], P('expert', 'dp')
- in_second_new: float32 [8, 3072, 768], P('expert', 'dp')
- in_average_new: float32 [8, 3072, 768], P('expert', 'dp')
- out_new: float32 [8, 3072, 768], P('expert', 'dp')
- out_first_new: float32 [8, 3072, 768], P('expert', 'dp')
- out_second_new: float32 [8, 3072, 768], P('expert', 'dp')
- out_average_new: float32 [8, 3072, 768], P('expert', 'dp')
- head_new: float32 [18432, 768], P(('dp', 'expert'))
- head_first_new: float32 [18432, 768], P(('dp', 'expert'))
- head_second_new: float32 [18432, 768], P(('dp', 'expert'))
- head_average_new: float32 [18432, 768], P(('dp', 'expert'))
The draws below stay inside these ranges and needn't reach their ends.
All inputs are finite; a program needn't handle non-finite values. No bound on the sum of `class_labels` on one device may be relied on, other than what follows from the above.
Results may differ from the reference program's by a relative error of at most 0.018.
The reference program's roundings to bfloat16 on the way count: a program that leaves them out, or rounds other values in their place, can miss the bound.
Values may be sent and summed in bfloat16 or wider, within the bound.
A program may use at most 320 MiB of HBM per device.

```python
import math
from functools import partial
import jax
import jax.numpy as jnp
import numpy as np
from jax import lax

D = 768
HEADS = 12
HD = 64
FF = 3072
P_SIZE = 768
CLASSES = 18432
SLOTS = 256
IMGS = 3
MOST = 196
ROWS_DEV = 4
TOP = 2
STEP_COUNT = 10
EXPERTS = 8
TOK_DEV = 1024
ROWS = 128
TOKENS = 32768
IMAGES = 384
CAP = 269
N_DP = 8
N_EXPERT = 4
DEVICES = 32


def draw_head_weights(key, part):
    key = jax.random.fold_in(key, 11)
    classes_pos = jnp.arange(CLASSES).astype(jnp.float32) / (CLASSES - 1)
    base = jnp.clip(jax.random.normal(key, (CLASSES, D), jnp.float32), -3.0, 3.0)
    rising = 1.0 + 2.0 * classes_pos
    return base * rising[:, None] / jnp.sqrt(jnp.float32(D))


def draw_norm_params(key, part):
    key = jax.random.fold_in(key, 12)
    gain_key, shift_key = jax.random.split(key)
    place = jnp.arange(D).astype(jnp.float32) / (D - 1)
    factor = jax.random.uniform(gain_key, (3, D), jnp.float32, 0.8, 1.2)
    shifts = jnp.clip(0.2 * jax.random.normal(shift_key, (3, D), jnp.float32), -0.6, 0.6)
    gain_rows = (0.5 + place[None, :]) * factor
    return jnp.concatenate([gain_rows, shifts], 0)


def draw_slot_mask(key, part):
    key = jax.random.fold_in(key, 13)
    row_ids = jnp.arange(ROWS, dtype=jnp.int32)
    device_ids = row_ids // ROWS_DEV
    dp_index = device_ids // N_EXPERT
    ex_index = device_ids % N_EXPERT
    limit = 250 + 350 * dp_index // max(N_DP - 1, 1) + 350 * ex_index // max(N_EXPERT - 1, 1)
    draws = jax.random.randint(key, (ROWS, SLOTS), 0, 1000)
    return (draws < limit[:, None]).astype(jnp.int32)


def draw_dense_second(key, part):
    key = jax.random.fold_in(key, 14)
    floor_rows = jnp.array([1.0, 100.0, 100.0, 1.0, 1.0], jnp.float32)[:, None, None] * (4e-05 / (D * CLASSES))
    unit = jax.random.uniform(key, (5, D, D), jnp.float32, 0.0, 1.0)
    return floor_rows * jnp.exp(1.3862944 * unit)


def set_ends(drawn, own_key, low, high):
    spot = [jax.random.randint(jax.random.fold_in(own_key, axis), (), 0, length) for axis, length in enumerate(drawn.shape)]
    main_axis = drawn.shape.index(max(drawn.shape))
    neighbour = spot[:main_axis] + [(spot[main_axis] + 1) % drawn.shape[main_axis]] + spot[main_axis + 1:]
    return drawn.at[tuple(spot)].set(low).at[tuple(neighbour)].set(high)


def steps_of(own_key, dims, cuts, least, top_value):
    loudness = 1.0
    for dim, parts in cuts:
        steps = jax.random.uniform(jax.random.fold_in(jax.random.fold_in(own_key, 6), dim), (parts,), jnp.float32, least / len(cuts), top_value / len(cuts))
        loudness = loudness * jnp.repeat(jnp.exp(steps), dims[dim] // parts).reshape((-1,) + (1,) * (len(dims) - 1 - dim))
    return loudness


def different_ones(rng, rows, amount, top, lift):
    order = jax.random.permutation(jax.random.fold_in(rng, 1), amount)
    favour = order
    for power in range(3):
        favour = favour * favour // amount
    favour = favour * lift // amount
    lots = jax.random.randint(jax.random.fold_in(rng, 2), (rows, amount), 0, 4096) + favour
    holders = jax.random.permutation(jax.random.fold_in(rng, 3), rows)[jnp.arange(amount) % rows]
    lots = jnp.where(jnp.arange(rows)[:, None] == holders[None, :], 1 << 14, lots)
    score = lots * amount + jnp.arange(amount)
    return lax.top_k(score.astype(jnp.int32), top)[1].astype(jnp.int32)


def length_profile(amount, total, reach, lean):
    weights = [(1 << 20) // math.isqrt(rank ** lean) + 1 for rank in range(2, amount + 1)]
    spare, counts = total - reach - (amount - 1), [1] * (amount - 1)
    while spare > 0:
        candidates = [i for i in range(amount - 1) if counts[i] < reach]
        pool, left = sum([weights[i] for i in candidates]), spare
        for i in candidates:
            addition = min(reach - counts[i], max(1, left * weights[i] // pool), spare)
            counts[i] = counts[i] + addition
            spare = spare - addition
    return np.array([reach] + counts)


def uneven(rng, count, total, most, slope):
    if count == 2:
        one = jax.random.randint(rng, (), max(1, total - most), min(most, total - 1) + 1)
        return jnp.stack([one, total - one])
    tallies = jnp.asarray(length_profile(count, total, most, slope), jnp.int32)
    couples = (count - 1) // 2
    donor, receiver = tallies[1:1 + 2 * couples:2], tallies[2:2 + 2 * couples:2]
    room = jnp.minimum(donor - 1, most - receiver)
    moved = jax.random.randint(jax.random.fold_in(rng, 1), (couples,), 0, 1 << 20) % (room + 1)
    tallies = tallies.at[1:1 + 2 * couples:2].set(donor - moved).at[2:2 + 2 * couples:2].set(receiver + moved)
    return tallies[jax.random.permutation(jax.random.fold_in(rng, 2), count)]


def bell_draw(key, shape, deviation, reach, pieces=(), kind=jnp.bfloat16):
    values = deviation * jax.random.normal(key, shape, jnp.float32)
    if pieces:
        values = values * steps_of(key, shape, pieces, -0.22, 0.18)
    return jnp.clip(values, -reach, reach).astype(kind)


def setup_inputs(seed: int = 0) -> dict:
    arg_keys = jax.random.split(jax.random.key(seed), 31)
    patches = bell_draw(arg_keys[0], (TOKENS, P_SIZE), 1.0, 6.0, ((0, 32),))
    lengths = jax.vmap(lambda own: uneven(own, IMGS, SLOTS, MOST, 1))(jax.random.split(arg_keys[1], ROWS)).reshape((ROWS, IMGS)).astype(jnp.int32)
    slot_mask = draw_slot_mask(jax.random.fold_in(arg_keys[30], 71), 0)
    expert_picks = different_ones(arg_keys[3], TOKENS, EXPERTS, TOP, 2048)
    priority_rank = jax.vmap(lambda own: jax.random.permutation(own, TOK_DEV))(jax.random.split(arg_keys[4], DEVICES)).reshape((DEVICES, TOK_DEV)).astype(jnp.int32)
    class_labels = set_ends((jax.random.randint(arg_keys[5], (CLASSES, IMAGES), 0, 32) < 1).astype(jnp.int32), jax.random.fold_in(arg_keys[5], 1), 0, 1)
    dense_weights = bell_draw(arg_keys[6], (5, D, D), D ** -0.5, 0.21875, ((1, 32),), jnp.float32)
    dense_first = bell_draw(arg_keys[7], (5, D, D), (0.022 * (D * CLASSES) ** -0.5), 9.1552734375e-05, ((1, 32),), jnp.float32)
    dense_second = draw_dense_second(jax.random.fold_in(arg_keys[30], 71), 0)
    dense_average = bell_draw(arg_keys[9], (5, D, D), D ** -0.5, 0.21875, ((1, 32),), jnp.float32)
    router_weights = bell_draw(arg_keys[10], (D, EXPERTS), (2 * D) ** -0.5, 0.15625, ((0, 32),), jnp.float32)
    router_first = bell_draw(arg_keys[11], (D, EXPERTS), (0.022 * (D * CLASSES) ** -0.5), 9.1552734375e-05, ((0, 32),), jnp.float32)
    router_second = jnp.clip(jnp.exp(math.log(1.1302806780799646e-11) - 1.3862944 * jax.random.uniform(arg_keys[12], (D, EXPERTS), jnp.float32) ** steps_of(arg_keys[12], (D, EXPERTS), ((0, 32),), -0.2, 0.2)), 2.8257016951999114e-12, 1.1302806780799646e-11)
    router_average = bell_draw(arg_keys[13], (D, EXPERTS), (2 * D) ** -0.5, 0.15625, ((0, 32),), jnp.float32)
    norm_params = draw_norm_params(jax.random.fold_in(arg_keys[30], 71), 0)
    norm_first = bell_draw(arg_keys[15], (6, D), (0.33 * (D * CLASSES) ** -0.5), 0.0012207031, ((1, 32),), jnp.float32)
    norm_second = jnp.clip(jnp.exp(math.log(2.543131483179195e-09) - 1.3862944 * jax.random.uniform(arg_keys[16], (6, D), jnp.float32) ** steps_of(arg_keys[16], (6, D), ((1, 32),), -0.2, 0.2)), 6.357828707947988e-10, 2.543131483179195e-09)
    norm_average = jnp.clip(0.5 + 1.0 * jax.random.uniform(arg_keys[17], (6, D), jnp.float32) ** steps_of(arg_keys[17], (6, D), ((1, 32),), -0.2, 0.2), 0.5, 1.5)
    expert_in = bell_draw(arg_keys[18], (EXPERTS, FF, D), D ** -0.5, 0.21875, ((0, 4), (1, 8)), jnp.float32)
    in_first = bell_draw(arg_keys[19], (EXPERTS, FF, D), (0.022 * (D * CLASSES) ** -0.5), 9.1552734375e-05, ((0, 4), (1, 8)), jnp.float32)
    in_second = jnp.clip(jnp.exp(math.log(1.1302806780799646e-11) - 1.3862944 * jax.random.uniform(arg_keys[20], (EXPERTS, FF, D), jnp.float32) ** steps_of(arg_keys[20], (EXPERTS, FF, D), ((0, 4), (1, 8)), -0.2, 0.2)), 2.8257016951999114e-12, 1.1302806780799646e-11)
    in_average = bell_draw(arg_keys[21], (EXPERTS, FF, D), D ** -0.5, 0.21875, ((0, 4), (1, 8)), jnp.float32)
    expert_out = bell_draw(arg_keys[22], (EXPERTS, FF, D), (FF // 64) ** -0.5, 0.875, ((0, 4), (1, 8)), jnp.float32)
    out_first = bell_draw(arg_keys[23], (EXPERTS, FF, D), (0.0055 * (D * CLASSES) ** -0.5), 2.288818359375e-05, ((0, 4), (1, 8)), jnp.float32)
    out_second = jnp.clip(jnp.exp(math.log(7.064254237999779e-13) - 1.3862944 * jax.random.uniform(arg_keys[24], (EXPERTS, FF, D), jnp.float32) ** steps_of(arg_keys[24], (EXPERTS, FF, D), ((0, 4), (1, 8)), -0.2, 0.2)), 1.7660635594999446e-13, 7.064254237999779e-13)
    out_average = bell_draw(arg_keys[25], (EXPERTS, FF, D), (FF // 64) ** -0.5, 0.875, ((0, 4), (1, 8)), jnp.float32)
    head_weights = draw_head_weights(jax.random.fold_in(arg_keys[30], 71), 0)
    head_first = bell_draw(arg_keys[27], (CLASSES, D), (0.11 * (D * CLASSES) ** -0.5), 0.0004272461, ((0, 32),), jnp.float32)
    head_second = jnp.clip(jnp.exp(math.log(5.651403303663649e-11) - 1.3862944 * jax.random.uniform(arg_keys[28], (CLASSES, D), jnp.float32) ** steps_of(arg_keys[28], (CLASSES, D), ((0, 32),), -0.2, 0.2)), 1.4128508259159123e-11, 5.651403303663649e-11)
    head_average = bell_draw(arg_keys[29], (CLASSES, D), (D // 4) ** -0.5, 0.4375, ((0, 32),), jnp.float32)
    return dict(patches=patches, lengths=lengths, slot_mask=slot_mask, expert_picks=expert_picks, priority_rank=priority_rank, class_labels=class_labels, dense_weights=dense_weights, dense_first=dense_first, dense_second=dense_second, dense_average=dense_average, router_weights=router_weights, router_first=router_first, router_second=router_second, router_average=router_average, norm_params=norm_params, norm_first=norm_first, norm_second=norm_second, norm_average=norm_average, expert_in=expert_in, in_first=in_first, in_second=in_second, in_average=in_average, expert_out=expert_out, out_first=out_first, out_second=out_second, out_average=out_average, head_weights=head_weights, head_first=head_first, head_second=head_second, head_average=head_average)


high_prec = lax.Precision.HIGHEST
eps_norm = 1e-06
aux_weight = 0.01
clip_limit = 1.0
base_rate = 0.05
norm_rate = 0.5
beta_first = 0.9
beta_second = 0.999
weight_decay = 0.1
polyak_decay = 0.7
adam_eps = 1e-08
mask_fill = -1e+30

@jax.custom_vjp
def low(v):
    return lax.optimization_barrier(v.astype(jnp.bfloat16)).astype(jnp.float32)

@jax.custom_vjp
def low_back(v):
    return v

def low_keep(v):
    return (low(v), None)

def low_pass(kept, grad):
    return (grad,)

def back_keep(v):
    return (v, None)

def back_low(kept, grad):
    return (low(grad),)
low.defvjp(low_keep, low_pass)
low_back.defvjp(back_keep, back_low)

def layer_norm(values, gain, shift):
    centre = values - lax.optimization_barrier(jnp.mean(values, -1, keepdims=True))
    spread = lax.optimization_barrier(jnp.mean(centre * centre, -1, keepdims=True))
    return centre * lax.rsqrt(spread + eps_norm) * gain + shift

def softmax_rows(logits):
    top_val = lax.optimization_barrier(jnp.max(logits, -1, keepdims=True))
    powers = jnp.exp(logits - top_val)
    return powers / lax.optimization_barrier(jnp.sum(powers, -1, keepdims=True))

def route(pick_ids, valid_flat, rank_ids, n_experts, capacity):
    columns = jnp.arange(n_experts, dtype=jnp.int32)
    first_hot = (pick_ids[:, 0:1] == columns[None, :]).astype(jnp.float32) * valid_flat[:, None]
    second_hot = (pick_ids[:, 1:2] == columns[None, :]).astype(jnp.float32) * valid_flat[:, None]
    before = (rank_ids[None, :] < rank_ids[:, None]).astype(jnp.float32)
    first_pos = lax.optimization_barrier(jnp.sum(first_hot * jnp.dot(before, first_hot, precision=high_prec), 1))
    second_pos = lax.optimization_barrier(jnp.sum(second_hot * (jnp.dot(before, second_hot, precision=high_prec) + lax.optimization_barrier(jnp.sum(first_hot, 0))[None, :]), 1))
    first_kept = valid_flat * (first_pos < capacity).astype(jnp.float32)
    second_kept = valid_flat * (second_pos < capacity).astype(jnp.float32)
    return (first_pos.astype(jnp.int32), second_pos.astype(jnp.int32), first_kept, second_kept)

def adam_update(weight, first_state, second_state, average_state, gradient, factor, step_rate):
    clipped = gradient * factor
    first_new = beta_first * first_state + (1.0 - beta_first) * clipped
    second_new = beta_second * second_state + (1.0 - beta_second) * clipped * clipped
    first_hat = first_new / (1.0 - beta_first ** STEP_COUNT)
    second_hat = second_new / (1.0 - beta_second ** STEP_COUNT)
    weight_new = weight - step_rate * (first_hat / (jnp.sqrt(second_hat) + adam_eps) + weight_decay * weight)
    average_new = polyak_decay * average_state + (1.0 - polyak_decay) * weight_new
    return (weight_new, first_new, second_new, average_new)

def slot_owner(safe_one, safe_two, kept_one, kept_two):
    token_ids = jnp.arange(TOK_DEV, dtype=jnp.int32)
    owner_ids = jnp.full((EXPERTS * CAP,), -1, jnp.int32)
    owner_ids = owner_ids.at[safe_one].max(jnp.where(kept_one > 0, token_ids, -1))
    owner_ids = owner_ids.at[safe_two].max(jnp.where(kept_two > 0, token_ids, -1))
    return owner_ids

def expert_block(block_args):
    rows_in, w_one, w_two = block_args
    hidden = low_back(jnp.dot(rows_in, w_one.T, precision=high_prec))
    activated = low(jax.nn.gelu(hidden))
    return low_back(low(jnp.dot(activated, w_two, precision=high_prec)))

def reference(patches, lengths, slot_mask, expert_picks, priority_rank, class_labels, dense_weights, dense_first, dense_second, dense_average, router_weights, router_first, router_second, router_average, norm_params, norm_first, norm_second, norm_average, expert_in, in_first, in_second, in_average, expert_out, out_first, out_second, out_average, head_weights, head_first, head_second, head_average):
    valid = slot_mask.astype(jnp.float32)
    positions = jnp.arange(SLOTS, dtype=jnp.int32)
    bounds = jnp.cumsum(lengths, 1)
    segment = lax.optimization_barrier(jnp.sum((positions[None, :, None] >= bounds[:, None, :]).astype(jnp.int32), -1))
    diagonal = positions[:, None] == positions[None, :]
    allowed = (segment[:, :, None] == segment[:, None, :]) & ((valid[:, None, :] > 0) | diagonal[None])
    member = (segment[:, None, :] == jnp.arange(IMGS, dtype=jnp.int32)[None, :, None]).astype(jnp.float32) * valid[:, None, :]
    pooling = member / jnp.maximum(lax.optimization_barrier(jnp.sum(member, -1, keepdims=True)), 1.0)
    valid_dev = valid.reshape(DEVICES, TOK_DEV)
    picks_dev = expert_picks.reshape(DEVICES, TOK_DEV, TOP)
    pos_one, pos_two, kept_one, kept_two = jax.vmap(partial(route, n_experts=EXPERTS, capacity=CAP))(picks_dev, valid_dev, priority_rank)
    safe_one = jnp.where(kept_one > 0, picks_dev[..., 0] * CAP + pos_one, 0)
    safe_two = jnp.where(kept_two > 0, picks_dev[..., 1] * CAP + pos_two, 0)
    owner_ids = jax.vmap(slot_owner)(safe_one, safe_two, kept_one, kept_two)
    slot_live = (owner_ids >= 0).astype(jnp.float32)
    owner_safe = jnp.maximum(owner_ids, 0)
    columns = jnp.arange(EXPERTS, dtype=jnp.int32)
    hot_one = (expert_picks[:, 0:1] == columns[None]).astype(jnp.float32)
    hot_two = (expert_picks[:, 1:2] == columns[None]).astype(jnp.float32)
    patch_vals = patches.astype(jnp.float32)
    label_vals = class_labels.astype(jnp.float32).T
    row_block = math.gcd(ROWS, 16)
    blocks = ROWS // row_block
    score_scale = HD ** (-0.5)
    allow_blocks = allowed.reshape(blocks, row_block, SLOTS, SLOTS)

    def attend_block(block_args):
        query_rows, key_rows, value_rows, allow_mask = block_args
        scores = low_back(jnp.einsum('rqhd,rkhd->rhqk', query_rows, key_rows, precision=high_prec) * score_scale)
        att_probs = softmax_rows(jnp.where(allow_mask[:, None], scores, mask_fill))
        return low_back(low(jnp.einsum('rhqk,rkhd->rqhd', low(att_probs), value_rows, precision=high_prec)))

    def forward(dense_vals, router_vals, norm_vals, w_in, w_out, head_vals):
        dense_b = low(dense_vals)
        router_b = low(router_vals)
        gain_rows = low(norm_vals)
        in_b = low(w_in)
        out_b = low(w_out)
        head_b = low(head_vals)
        x_zero = low_back(jnp.dot(patch_vals, dense_b[0], precision=high_prec))
        a_one = low(layer_norm(x_zero, gain_rows[0], gain_rows[3]))
        proj_qkv = low_back(low(jnp.einsum('td,kde->kte', a_one, dense_b[1:4], precision=high_prec)))
        grouped = proj_qkv.reshape(3, blocks, row_block, SLOTS, HEADS, HD)
        attended = lax.map(jax.checkpoint(attend_block), (grouped[0], grouped[1], grouped[2], allow_blocks))
        att_out = attended.reshape(TOKENS, D)
        x_one = x_zero + low_back(jnp.dot(att_out, dense_b[4], precision=high_prec))
        a_two = low(layer_norm(x_one, gain_rows[1], gain_rows[4]))
        router_probs = softmax_rows(low_back(jnp.dot(a_two, router_b, precision=high_prec)))
        importance = lax.optimization_barrier(jnp.sum(router_probs * valid.reshape(TOKENS, 1), 0))
        gate_one = lax.optimization_barrier(jnp.sum(router_probs * hot_one, 1)).reshape(DEVICES, TOK_DEV) * kept_one
        gate_two = lax.optimization_barrier(jnp.sum(router_probs * hot_two, 1)).reshape(DEVICES, TOK_DEV) * kept_two
        send_rows = jnp.take_along_axis(a_two.reshape(DEVICES, TOK_DEV, D), owner_safe[:, :, None], 1) * slot_live[:, :, None]
        send_rows = low_back(send_rows)
        by_expert = send_rows.reshape(DEVICES, EXPERTS, CAP, D).transpose(1, 0, 2, 3).reshape(EXPERTS, DEVICES * CAP, D)
        returned = lax.map(jax.checkpoint(expert_block), (by_expert, in_b, out_b))
        returned = returned.reshape(EXPERTS, DEVICES, CAP, D).transpose(1, 0, 2, 3).reshape(DEVICES, EXPERTS * CAP, D)
        mixed_rows = gate_one[:, :, None] * jnp.take_along_axis(returned, safe_one[:, :, None], 1)
        mixed_rows = mixed_rows + gate_two[:, :, None] * jnp.take_along_axis(returned, safe_two[:, :, None], 1)
        x_two = x_one + mixed_rows.reshape(TOKENS, D)
        pooled = jnp.einsum('ris,rsd->rid', pooling, x_two.reshape(ROWS, SLOTS, D), precision=high_prec).reshape(IMAGES, D)
        a_three = low(layer_norm(pooled, gain_rows[2], gain_rows[5]))
        logits = low_back(jnp.dot(a_three, head_b.T, precision=high_prec))
        label_loss = jnp.sum(jnp.logaddexp(logits, 0.0) - label_vals * logits) / IMAGES
        centre = jnp.mean(importance)
        spread = jnp.mean((importance - centre) ** 2)
        return (label_loss + aux_weight * spread / (centre * centre), importance)
    weights = (dense_weights, router_weights, norm_params, expert_in, expert_out, head_weights)
    loss_value, vjp_fn, importance = jax.vjp(forward, *weights, has_aux=True)
    gradients = vjp_fn(jnp.ones_like(loss_value))
    square_sum = jnp.sum(gradients[0] ** 2)
    for gradient in gradients[1:]:
        square_sum = square_sum + jnp.sum(gradient ** 2)
    grad_norm = jnp.sqrt(square_sum)
    factor = jnp.minimum(1.0, clip_limit / grad_norm)
    states = ((dense_first, dense_second, dense_average, base_rate), (router_first, router_second, router_average, base_rate), (norm_first, norm_second, norm_average, norm_rate), (in_first, in_second, in_average, base_rate), (out_first, out_second, out_average, base_rate), (head_first, head_second, head_average, base_rate))
    results = []
    for weight, gradient, state in zip(weights, gradients, states):
        results.extend(adam_update(weight, state[0], state[1], state[2], gradient, factor, state[3]))
    return (loss_value, importance, grad_norm, results[0], results[1], results[2], results[3], results[4], results[5], results[6], results[7], results[8], results[9], results[10], results[11], results[12], results[13], results[14], results[15], results[16], results[17], results[18], results[19], results[20], results[21], results[22], results[23])
```

```python
import functools

import jax
import jax.numpy as jnp
import numpy as np
from jax import lax
from jax.sharding import Mesh
from jax.sharding import PartitionSpec as P

HEADS = 12
TOP = 2
STEP_COUNT = 10
QUAD = 4

high_prec = lax.Precision.HIGHEST
eps_norm = 1e-06
aux_weight = 0.01
clip_limit = 1.0
base_rate = 0.05
norm_rate = 0.5
beta_first = 0.9
beta_second = 0.999
weight_decay = 0.1
polyak_decay = 0.7
adam_eps = 1e-08
mask_fill = -1e30

ALL = ("g", "r", "x", "c")
MEMBERS = ("x", "r")


def layer_norm(values, gain, shift):
    centre = values - jnp.mean(values, -1, keepdims=True)
    spread = jnp.mean(centre * centre, -1, keepdims=True)
    return centre * lax.rsqrt(spread + eps_norm) * gain + shift


def softmax_rows(logits):
    top_val = jnp.max(logits, -1, keepdims=True)
    powers = jnp.exp(logits - top_val)
    return powers / jnp.sum(powers, -1, keepdims=True)


def route(pick_ids, valid_flat, rank_ids, n_experts, capacity, padded):
    columns = jnp.arange(n_experts, dtype=jnp.int32)
    first_hot = (pick_ids[:, 0:1] == columns[None, :]).astype(jnp.float32) * valid_flat[:, None]
    second_hot = (pick_ids[:, 1:2] == columns[None, :]).astype(jnp.float32) * valid_flat[:, None]
    before = (rank_ids[None, :] < rank_ids[:, None]).astype(jnp.bfloat16)
    hot = jnp.concatenate([first_hot, second_hot], 1)
    ahead = jnp.dot(before, hot.astype(jnp.bfloat16), preferred_element_type=jnp.float32)
    first_pos = jnp.sum(first_hot * ahead[:, :n_experts], 1)
    second_pos = jnp.sum(second_hot * (ahead[:, n_experts:] + jnp.sum(first_hot, 0)[None, :]), 1)
    first_kept = valid_flat * (first_pos < capacity).astype(jnp.float32)
    second_kept = valid_flat * (second_pos < capacity).astype(jnp.float32)
    first_slot = jnp.where(
        first_kept > 0, pick_ids[:, 0] * padded + first_pos.astype(jnp.int32), -1
    )
    second_slot = jnp.where(
        second_kept > 0, pick_ids[:, 1] * padded + second_pos.astype(jnp.int32), -1
    )
    return (first_slot, second_slot, first_kept, second_kept)


def adam_update(weight, first_state, second_state, average_state, gradient, factor, step_rate):
    clipped = gradient * factor
    first_new = beta_first * first_state + (1.0 - beta_first) * clipped
    second_new = beta_second * second_state + (1.0 - beta_second) * clipped * clipped
    first_hat = first_new / (1.0 - beta_first**STEP_COUNT)
    second_hat = second_new / (1.0 - beta_second**STEP_COUNT)
    weight_new = weight - step_rate * (
        first_hat / (jnp.sqrt(second_hat) + adam_eps) + weight_decay * weight
    )
    average_new = polyak_decay * average_state + (1.0 - polyak_decay) * weight_new
    return (weight_new, first_new, second_new, average_new)


def split_heads(proj_qkv, allow_mask, n_heads):
    n_rows, n_slots_row = (allow_mask.shape[0], allow_mask.shape[1])
    head_dim = proj_qkv.shape[-1] // n_heads
    shaped = proj_qkv.reshape(3, n_rows, n_slots_row, n_heads, head_dim)
    scores = jnp.einsum(
        "rqhd,rkhd->rhqk", shaped[0], shaped[1], preferred_element_type=jnp.float32
    ) * head_dim ** (-0.5)
    return (shaped, jnp.where(allow_mask[:, None], scores, mask_fill), head_dim ** (-0.5))


def attention_forward(proj_qkv, allow_mask, n_heads):
    shaped, masked, unused_scale = split_heads(proj_qkv, allow_mask, n_heads)
    top_val = jnp.max(masked, -1, keepdims=True)
    powers = jnp.exp(masked - top_val)
    totals = jnp.sum(powers, -1, keepdims=True)
    att_probs = powers / totals
    output = jnp.einsum(
        "rhqk,rkhd->rqhd",
        att_probs.astype(jnp.bfloat16),
        shaped[2],
        preferred_element_type=jnp.float32,
    )
    return (
        output.astype(jnp.bfloat16).reshape(proj_qkv.shape[1], proj_qkv.shape[2]),
        top_val + jnp.log(totals),
    )


def attention_backward(proj_qkv, allow_mask, log_total, d_output, n_heads):
    shaped, masked, score_scale = split_heads(proj_qkv, allow_mask, n_heads)
    att_probs = jnp.exp(masked - log_total)
    grad_out = d_output.reshape(shaped.shape[1:])
    d_probs = jnp.einsum("rqhd,rkhd->rhqk", grad_out, shaped[2], preferred_element_type=jnp.float32)
    d_values = jnp.einsum(
        "rhqk,rqhd->rkhd",
        att_probs.astype(jnp.bfloat16),
        grad_out,
        preferred_element_type=jnp.float32,
    )
    d_scores = (att_probs * (d_probs - jnp.sum(att_probs * d_probs, -1, keepdims=True))).astype(
        jnp.bfloat16
    )
    d_query = (
        jnp.einsum("rhqk,rkhd->rqhd", d_scores, shaped[1], preferred_element_type=jnp.float32)
        * score_scale
    )
    d_keys = (
        jnp.einsum("rhqk,rqhd->rkhd", d_scores, shaped[0], preferred_element_type=jnp.float32)
        * score_scale
    )
    stacked = jnp.stack([d_query, d_keys, d_values]).astype(jnp.bfloat16)
    return stacked.reshape(proj_qkv.shape)


def shard_moves(n_blocks):
    span = 2 * n_blocks
    moves = []
    for step in range(span):
        pairs = []
        for place in range(QUAD * n_blocks):
            for core in range(2):
                target = (place + step) % span
                src = place * 2 + core
                dst = (target // 2 * QUAD + 2 * core + target % 2) * 2 + place // span
                pairs.append((src, dst))
        moves.append(pairs)
    return moves


def swap_cores(value):
    return lax.ppermute(value, "c", [(0, 1), (1, 0)])


def fetch_experts(expert_in, expert_out, n_blocks):
    place = lax.axis_index("g") * QUAD + lax.axis_index("r")
    odd = lax.rem(place, 2) == 1
    both = jnp.stack([expert_in, expert_out], 1).astype(jnp.bfloat16)
    ordered = [jnp.where(odd, both[1], both[0]), jnp.where(odd, both[0], both[1])]
    return [
        lax.ppermute(ordered[step % 2], ("g", "r", "c"), pairs)
        for step, pairs in enumerate(shard_moves(n_blocks))
    ]


def return_experts(parts, n_blocks):
    place = lax.axis_index("g") * QUAD + lax.axis_index("r")
    odd = lax.rem(place, 2) == 1
    sums = [None, None]
    for step, pairs in enumerate(shard_moves(n_blocks)):
        back = lax.ppermute(parts[step], ("g", "r", "c"), [(dst, src) for src, dst in pairs])
        back = back.astype(jnp.float32)
        sums[step % 2] = back if sums[step % 2] is None else sums[step % 2] + back
    zero, one = jnp.where(odd, sums[1], sums[0]), jnp.where(odd, sums[0], sums[1])
    return jnp.stack([zero[0], one[0]]), jnp.stack([zero[1], one[1]])


def to_members(value):
    return lax.all_to_all(value, MEMBERS, split_axis=0, concat_axis=0, tiled=True)


def body(
    patches,
    lengths,
    slot_mask,
    expert_picks,
    priority_rank,
    class_labels,
    dense_weights,
    dense_first,
    dense_second,
    dense_average,
    router_weights,
    router_first,
    router_second,
    router_average,
    norm_params,
    norm_first,
    norm_second,
    norm_average,
    expert_in,
    in_first,
    in_second,
    in_average,
    expert_out,
    out_first,
    out_second,
    out_average,
    head_weights,
    head_first,
    head_second,
    head_average,
):
    n_blocks = lax.axis_size("g")
    layer_b, router_b, norm_b = (
        lax.all_gather(dense_weights.astype(jnp.bfloat16), ALL, axis=1, tiled=True),
        lax.all_gather(router_weights.astype(jnp.bfloat16), ALL, axis=0, tiled=True),
        lax.all_gather(norm_params.astype(jnp.bfloat16), ALL, axis=1, tiled=True),
    )
    own_chunks = fetch_experts(expert_in, expert_out, n_blocks)
    own_half = jnp.stack(own_chunks, 1)
    other_half = swap_cores(own_half)
    w_one = jnp.concatenate([own_half[0], other_half[0]], 0)
    w_two = jnp.concatenate([own_half[1], other_half[1]], 0)
    gain_rows = norm_b.astype(jnp.float32)
    rows_here, n_slots_row = slot_mask.shape
    tokens = rows_here * n_slots_row
    model_width = layer_b.shape[2]
    n_experts = router_weights.shape[1]
    n_images = lengths.shape[0] * lengths.shape[1]
    capacity = (21 * tokens * TOP + 20 * n_experts - 1) // (20 * n_experts)
    padded = (capacity + 15) // 16 * 16
    n_slots = n_experts * padded
    w_one = w_one.reshape(-1, model_width)
    w_two = w_two.reshape(-1, model_width)
    valid = slot_mask.astype(jnp.float32)
    positions = jnp.arange(n_slots_row, dtype=jnp.int32)
    bounds = jnp.cumsum(lengths, 1)
    segment = jnp.sum((positions[None, :, None] >= bounds[:, None, :]).astype(jnp.int32), -1)
    diagonal = positions[:, None] == positions[None, :]
    allowed = (segment[:, :, None] == segment[:, None, :]) & (
        (valid[:, None, :] > 0) | diagonal[None]
    )
    member = (
        segment[:, None, :] == jnp.arange(lengths.shape[1], dtype=jnp.int32)[None, :, None]
    ).astype(jnp.float32) * valid[:, None, :]
    pooling = member / jnp.maximum(jnp.sum(member, -1, keepdims=True), 1.0)
    valid_flat = valid.reshape(tokens)
    pool_flat = jnp.sum(pooling, 1).reshape(tokens)
    image_flat = (segment + jnp.arange(rows_here)[:, None] * lengths.shape[1]).reshape(tokens)
    slot_one, slot_two, kept_one, kept_two = route(
        expert_picks, valid_flat, priority_rank[0], n_experts, capacity, padded
    )
    x_zero = jnp.dot(patches, layer_b[0], preferred_element_type=jnp.float32)
    a_one = layer_norm(x_zero, gain_rows[0], gain_rows[3]).astype(jnp.bfloat16)
    proj_qkv = jnp.einsum(
        "td,kde->kte", a_one, layer_b[1:4], preferred_element_type=jnp.float32
    ).astype(jnp.bfloat16)
    att_out, log_total = attention_forward(proj_qkv, allowed, HEADS)
    x_one = x_zero + jnp.dot(att_out, layer_b[4], preferred_element_type=jnp.float32)
    a_two = layer_norm(x_one, gain_rows[1], gain_rows[4]).astype(jnp.bfloat16)
    router_probs = softmax_rows(jnp.dot(a_two, router_b, preferred_element_type=jnp.float32))
    importance = lax.psum(jnp.sum(router_probs * valid_flat[:, None], 0), ALL)
    pick_one = expert_picks[:, 0]
    pick_two = expert_picks[:, 1]
    columns = jnp.arange(n_experts, dtype=jnp.int32)
    hot_one = (pick_one[:, None] == columns[None]).astype(jnp.float32)
    hot_two = (pick_two[:, None] == columns[None]).astype(jnp.float32)
    gate_one = jnp.sum(router_probs * hot_one, 1) * kept_one
    gate_two = jnp.sum(router_probs * hot_two, 1) * kept_two
    slot_ids = jnp.arange(n_slots, dtype=jnp.int32)
    match_one = slot_one[None, :] == slot_ids[:, None]
    match_two = slot_two[None, :] == slot_ids[:, None]
    match = (match_one | match_two).astype(jnp.bfloat16)
    send_rows = (
        jnp.dot(match, a_two, preferred_element_type=jnp.float32)
        .astype(jnp.bfloat16)
        .reshape(n_experts, padded, model_width)
    )
    held = jnp.where(match_one | match_two, 1.0, 0.0)
    slot_gate = jnp.sum(
        jnp.where(match_one, gate_one[None], 0.0) + jnp.where(match_two, gate_two[None], 0.0), 1
    )
    slot_pool = jnp.sum(held * pool_flat[None], 1)
    slot_image = jnp.sum(held * image_flat.astype(jnp.float32)[None], 1)
    details = jnp.stack([slot_gate, slot_pool, slot_image]).reshape(3, n_experts, padded)
    arrived = to_members(send_rows)
    details = to_members(details.transpose(1, 0, 2))
    got_gate, got_pool, got_image = details[:, 0], details[:, 1], details[:, 2]
    image_hot = (
        got_image[:, :, None] == jnp.arange(n_images).astype(jnp.float32)[None, None]
    ).astype(jnp.float32) * got_pool[:, :, None]
    rows_all = arrived.reshape(n_slots, model_width)
    hidden = jnp.dot(rows_all, w_one.T, preferred_element_type=jnp.float32)
    activated = jax.nn.gelu(hidden).astype(jnp.bfloat16)
    result = jnp.dot(activated, w_two, preferred_element_type=jnp.float32).astype(jnp.bfloat16)
    result = result.reshape(n_experts, padded, model_width).astype(jnp.float32)
    part_pooled = jnp.einsum(
        "dsi,dsw->diw", image_hot * got_gate[:, :, None], result, precision=high_prec
    )
    pooled = jnp.einsum(
        "ris,rsd->rid",
        pooling,
        x_one.reshape(rows_here, n_slots_row, model_width),
        precision=high_prec,
    ).reshape(-1, model_width)
    pooled = pooled + jnp.sum(to_members(part_pooled), 0)
    gathered = lax.all_gather(
        layer_norm(pooled, gain_rows[2], gain_rows[5]).astype(jnp.bfloat16),
        ALL,
        axis=0,
        tiled=True,
    )
    head_b = head_weights.astype(jnp.bfloat16)
    logits = jnp.dot(head_b, gathered.T, preferred_element_type=jnp.float32)
    labels = class_labels.astype(jnp.float32)
    n_images_all = gathered.shape[0]
    local_loss = jnp.sum(jnp.logaddexp(logits, 0.0) - labels * logits) / n_images_all
    centre = jnp.mean(importance)
    spread = jnp.mean((importance - centre) ** 2)
    d_imp = aux_weight * (
        2.0 * (importance - centre) / (n_experts * centre * centre)
        - 2.0 * spread / (n_experts * centre * centre * centre)
    )
    d_logits = ((jax.nn.sigmoid(logits) - labels) / n_images_all).astype(jnp.bfloat16)
    g_head = jnp.dot(d_logits, gathered, preferred_element_type=jnp.float32)
    d_rows = lax.psum_scatter(
        jnp.dot(d_logits.T, head_b, preferred_element_type=jnp.float32),
        ALL,
        scatter_dimension=0,
        tiled=True,
    )
    unused_out, norm_back = jax.vjp(layer_norm, pooled, gain_rows[2], gain_rows[5])
    d_pooled, g_gain_three, g_shift_three = norm_back(d_rows)
    d_two = jnp.einsum(
        "ris,rid->rsd", pooling, d_pooled.reshape(rows_here, -1, model_width), precision=high_prec
    ).reshape(tokens, model_width)
    d_pooled_all = lax.all_gather(d_pooled, MEMBERS, axis=0)
    d_two_slots = jnp.einsum("dsi,diw->dsw", image_hot, d_pooled_all, precision=high_prec)
    slot_d_gate = jnp.sum(d_two_slots * result, -1)
    d_all = (d_two_slots * got_gate[:, :, None]).astype(jnp.bfloat16).reshape(n_slots, model_width)
    d_act = jnp.dot(d_all, w_two.T, preferred_element_type=jnp.float32)
    d_hidden = jax.vjp(jax.nn.gelu, hidden)[1](d_act)[0].astype(jnp.bfloat16)
    d_inputs = jnp.dot(d_hidden, w_one, preferred_element_type=jnp.float32).astype(jnp.bfloat16)
    d_back = to_members(d_inputs.reshape(n_experts, padded, model_width))
    d_back = d_back.reshape(n_slots, model_width)
    back_gate = to_members(slot_d_gate).reshape(n_slots)
    g_two = jnp.dot(activated.T, d_all, preferred_element_type=jnp.float32)
    g_one = jnp.dot(d_hidden.T, rows_all, preferred_element_type=jnp.float32)
    half = g_one.shape[0] // 2
    grads = jnp.stack([g_one, g_two], 0).astype(jnp.bfloat16)
    summed = grads[:, :half].astype(jnp.float32) + swap_cores(grads[:, half:]).astype(jnp.float32)
    summed = summed.astype(jnp.bfloat16).reshape(2, 2 * n_blocks, -1, model_width)
    g_one, g_two = return_experts([summed[:, i] for i in range(2 * n_blocks)], n_blocks)
    d_gate_one = kept_one * jnp.take(back_gate, jnp.maximum(slot_one, 0), axis=0)
    d_gate_two = kept_two * jnp.take(back_gate, jnp.maximum(slot_two, 0), axis=0)
    d_a_two = lax.dot_general(
        match, d_back, (((0,), (0,)), ((), ())), preferred_element_type=jnp.float32
    )
    d_probs = (
        hot_one * d_gate_one[:, None]
        + hot_two * d_gate_two[:, None]
        + valid_flat[:, None] * d_imp[None, :]
    )
    d_router = (
        router_probs * (d_probs - jnp.sum(router_probs * d_probs, 1, keepdims=True))
    ).astype(jnp.bfloat16)
    g_router = jnp.dot(a_two.T, d_router, preferred_element_type=jnp.float32)
    d_a_two = d_a_two + jnp.dot(d_router, router_b.T, preferred_element_type=jnp.float32)
    unused_out, norm_back = jax.vjp(layer_norm, x_one, gain_rows[1], gain_rows[4])
    d_x_one, g_gain_two, g_shift_two = norm_back(d_a_two)
    d_x_one = d_x_one + d_two
    d_att_b = d_x_one.astype(jnp.bfloat16)
    g_out_proj = jnp.dot(att_out.T, d_att_b, preferred_element_type=jnp.float32)
    d_att_out = jnp.dot(d_att_b, layer_b[4].T, preferred_element_type=jnp.float32).astype(
        jnp.bfloat16
    )
    d_qkv = attention_backward(proj_qkv, allowed, log_total, d_att_out, HEADS)
    g_qkv = jnp.einsum("td,kte->kde", a_one, d_qkv, preferred_element_type=jnp.float32)
    d_a_one = jnp.einsum("kte,kde->td", d_qkv, layer_b[1:4], preferred_element_type=jnp.float32)
    unused_out, norm_back = jax.vjp(layer_norm, x_zero, gain_rows[0], gain_rows[3])
    d_x_zero, g_gain_one, g_shift_one = norm_back(d_a_one)
    d_x_zero = (d_x_zero + d_x_one).astype(jnp.bfloat16)
    g_embed = jnp.dot(patches.T, d_x_zero, preferred_element_type=jnp.float32)
    g_layers = jnp.concatenate([g_embed[None], g_qkv, g_out_proj[None]], 0)
    g_norms = jnp.stack(
        [g_gain_one, g_gain_two, g_gain_three, g_shift_one, g_shift_two, g_shift_three]
    )
    g_layers, g_router, g_norms = (
        lax.psum_scatter(
            g_layers.astype(jnp.bfloat16), ALL, scatter_dimension=1, tiled=True
        ).astype(jnp.float32),
        lax.psum_scatter(g_router, ALL, scatter_dimension=0, tiled=True),
        lax.psum_scatter(g_norms, ALL, scatter_dimension=1, tiled=True),
    )
    squares = (
        jnp.sum(g_layers * g_layers) + jnp.sum(g_router * g_router) + jnp.sum(g_norms * g_norms)
    )
    squares = squares + jnp.sum(g_one * g_one) + jnp.sum(g_two * g_two) + jnp.sum(g_head * g_head)
    loss_sum, square_sum = lax.psum((local_loss, squares), ALL)
    grad_norm = jnp.sqrt(square_sum)
    factor = jnp.minimum(1.0, clip_limit / grad_norm)
    loss_value = loss_sum + aux_weight * spread / (centre * centre)
    dense_out = adam_update(
        dense_weights, dense_first, dense_second, dense_average, g_layers, factor, base_rate
    )
    router_out = adam_update(
        router_weights, router_first, router_second, router_average, g_router, factor, base_rate
    )
    norm_out = adam_update(
        norm_params, norm_first, norm_second, norm_average, g_norms, factor, norm_rate
    )
    in_out = adam_update(expert_in, in_first, in_second, in_average, g_one, factor, base_rate)
    out_out = adam_update(expert_out, out_first, out_second, out_average, g_two, factor, base_rate)
    head_out = adam_update(
        head_weights, head_first, head_second, head_average, g_head, factor, base_rate
    )
    return (
        loss_value,
        importance,
        grad_norm,
        *dense_out,
        *router_out,
        *norm_out,
        *in_out,
        *out_out,
        *head_out,
    )


def solution(mesh):
    n_dp, n_expert = mesh.shape["dp"], mesh.shape["expert"]
    shaped = mesh.devices.reshape(n_dp // QUAD, QUAD, n_expert // 2, 2)
    fine = Mesh(shaped, ALL)
    rows = P(ALL, None)
    dense = P(None, ALL, None)
    norms = P(None, ALL)
    experts = P(("x", "c"), ("g", "r"), None)
    placed = (rows,) * 6 + (dense,) * 4 + (rows,) * 4 + (norms,) * 4 + (experts,) * 8 + (rows,) * 4
    results = (
        (P(),) * 3 + (dense,) * 4 + (rows,) * 4 + (norms,) * 4 + (experts,) * 8 + (rows,) * 4
    )
    return jax.shard_map(body, mesh=fine, in_specs=placed, out_specs=results, check_vma=False)
```

```python
import functools
import math

import jax
import jax.numpy as jnp
from jax import lax
from jax.experimental import pallas as pl
from jax.experimental.pallas import tpu as pltpu
from jax.sharding import Mesh
from jax.sharding import PartitionSpec as P

HEADS = 12
TOP = 2
STEP_COUNT = 10
QUAD = 4

high_prec = lax.Precision.HIGHEST
eps_norm = 1e-06
aux_weight = 0.01
clip_limit = 1.0
base_rate = 0.05
norm_rate = 0.5
beta_first = 0.9
beta_second = 0.999
weight_decay = 0.1
polyak_decay = 0.7
adam_eps = 1e-08
mask_fill = -1e30

ALL = ("g", "r", "x", "c")
MEMBERS = ("x", "r")


def layer_norm(values, gain, shift):
    centre = values - jnp.mean(values, -1, keepdims=True)
    spread = jnp.mean(centre * centre, -1, keepdims=True)
    return centre * lax.rsqrt(spread + eps_norm) * gain + shift


def softmax_rows(logits):
    top_val = jnp.max(logits, -1, keepdims=True)
    powers = jnp.exp(logits - top_val)
    return powers / jnp.sum(powers, -1, keepdims=True)


def route(pick_ids, valid_flat, rank_ids, n_experts, capacity, padded):
    columns = jnp.arange(n_experts, dtype=jnp.int32)
    first_hot = (pick_ids[:, 0:1] == columns[None, :]).astype(jnp.float32) * valid_flat[:, None]
    second_hot = (pick_ids[:, 1:2] == columns[None, :]).astype(jnp.float32) * valid_flat[:, None]
    before = (rank_ids[None, :] < rank_ids[:, None]).astype(jnp.bfloat16)
    hot = jnp.concatenate([first_hot, second_hot], 1)
    ahead = jnp.dot(before, hot.astype(jnp.bfloat16), preferred_element_type=jnp.float32)
    first_pos = jnp.sum(first_hot * ahead[:, :n_experts], 1)
    second_pos = jnp.sum(second_hot * (ahead[:, n_experts:] + jnp.sum(first_hot, 0)[None, :]), 1)
    first_kept = valid_flat * (first_pos < capacity).astype(jnp.float32)
    second_kept = valid_flat * (second_pos < capacity).astype(jnp.float32)
    first_slot = jnp.where(
        first_kept > 0, pick_ids[:, 0] * padded + first_pos.astype(jnp.int32), -1
    )
    second_slot = jnp.where(
        second_kept > 0, pick_ids[:, 1] * padded + second_pos.astype(jnp.int32), -1
    )
    return (first_slot, second_slot, first_kept, second_kept)


def adam_update(weight, first_state, second_state, average_state, gradient, factor, step_rate):
    clipped = gradient * factor
    first_new = beta_first * first_state + (1.0 - beta_first) * clipped
    second_new = beta_second * second_state + (1.0 - beta_second) * clipped * clipped
    first_hat = first_new / (1.0 - beta_first**STEP_COUNT)
    second_hat = second_new / (1.0 - beta_second**STEP_COUNT)
    weight_new = weight - step_rate * (
        first_hat / (jnp.sqrt(second_hat) + adam_eps) + weight_decay * weight
    )
    average_new = polyak_decay * average_state + (1.0 - polyak_decay) * weight_new
    return (weight_new, first_new, second_new, average_new)


def split_heads(proj_qkv, allow_mask, n_heads):
    n_rows, n_slots_row = (allow_mask.shape[0], allow_mask.shape[1])
    head_dim = proj_qkv.shape[-1] // n_heads
    shaped = proj_qkv.reshape(3, n_rows, n_slots_row, n_heads, head_dim)
    scores = jnp.einsum(
        "rqhd,rkhd->rhqk", shaped[0], shaped[1], preferred_element_type=jnp.float32
    ) * head_dim ** (-0.5)
    return (shaped, jnp.where(allow_mask[:, None], scores, mask_fill), head_dim ** (-0.5))


def attention_forward(proj_qkv, allow_mask, n_heads):
    shaped, masked, unused_scale = split_heads(proj_qkv, allow_mask, n_heads)
    top_val = jnp.max(masked, -1, keepdims=True)
    powers = jnp.exp(masked - top_val)
    totals = jnp.sum(powers, -1, keepdims=True)
    att_probs = powers / totals
    output = jnp.einsum(
        "rhqk,rkhd->rqhd",
        att_probs.astype(jnp.bfloat16),
        shaped[2],
        preferred_element_type=jnp.float32,
    )
    return (
        output.astype(jnp.bfloat16).reshape(proj_qkv.shape[1], proj_qkv.shape[2]),
        top_val + jnp.log(totals),
    )


def attention_backward(proj_qkv, allow_mask, log_total, d_output, n_heads):
    shaped, masked, score_scale = split_heads(proj_qkv, allow_mask, n_heads)
    att_probs = jnp.exp(masked - log_total)
    grad_out = d_output.reshape(shaped.shape[1:])
    d_probs = jnp.einsum("rqhd,rkhd->rhqk", grad_out, shaped[2], preferred_element_type=jnp.float32)
    d_values = jnp.einsum(
        "rhqk,rqhd->rkhd",
        att_probs.astype(jnp.bfloat16),
        grad_out,
        preferred_element_type=jnp.float32,
    )
    d_scores = (att_probs * (d_probs - jnp.sum(att_probs * d_probs, -1, keepdims=True))).astype(
        jnp.bfloat16
    )
    d_query = (
        jnp.einsum("rhqk,rkhd->rqhd", d_scores, shaped[1], preferred_element_type=jnp.float32)
        * score_scale
    )
    d_keys = (
        jnp.einsum("rhqk,rqhd->rkhd", d_scores, shaped[0], preferred_element_type=jnp.float32)
        * score_scale
    )
    stacked = jnp.stack([d_query, d_keys, d_values]).astype(jnp.bfloat16)
    return stacked.reshape(proj_qkv.shape)


MESH_ID = pl.DeviceIdType.MESH
VMEM = pltpu.VMEM
ANY = pl.ANY
MIB = 1 << 20


def whole(space=None):
    return pl.BlockSpec(memory_space=space or VMEM)


def round_up(value, step):
    return (value + step - 1) // step * step


class Place:
    def __init__(self, sizes):
        self.G, self.X = sizes["g"], sizes["x"]
        self.Z, self.Y = QUAD, sizes["g"]
        self.chips = self.Z * self.Y * self.X
        spot = lax.axis_index("g") * QUAD + lax.axis_index("r")
        self.z, self.y = lax.div(spot, self.Y), lax.rem(spot, self.Y)
        self.x, self.c = lax.axis_index("x"), lax.axis_index("c")
        self.g, self.r = lax.axis_index("g"), lax.axis_index("r")
        self.chip = spot * self.X + self.x
        self.member = self.x * QUAD + self.r

    def at(self, z=None, y=None, x=None, c=None):
        spot = (self.z if z is None else z) * self.Y + (self.y if y is None else y)
        return {
            "g": lax.div(spot, QUAD),
            "r": lax.rem(spot, QUAD),
            "x": self.x if x is None else x,
            "c": self.c if c is None else c,
        }

    def of_chip(self, chip):
        spot = lax.div(chip, self.X)
        return {
            "g": lax.div(spot, QUAD),
            "r": lax.rem(spot, QUAD),
            "x": lax.rem(chip, self.X),
            "c": self.c,
        }

    def of_member(self, member):
        return {
            "g": self.g,
            "r": lax.rem(member, QUAD),
            "x": lax.div(member, QUAD),
            "c": self.c,
        }

    def sibling(self):
        return self.at(c=1 - self.c)


def greet(peers):
    barrier = pltpu.get_barrier_semaphore()
    for peer in peers:
        pl.semaphore_signal(barrier, inc=1, device_id=peer, device_id_type=MESH_ID)
    pl.semaphore_wait(barrier, len(peers))


def send(src, dst, send_sem, recv_sem, peer):
    return pltpu.make_async_remote_copy(
        src_ref=src,
        dst_ref=dst,
        send_sem=send_sem,
        recv_sem=recv_sem,
        device_id=peer,
        device_id_type=MESH_ID,
    )


def others(me, count):
    return [lax.rem(me + step, count) for step in range(1, count)]


def grid_peers(at):
    peers = [at.at(z=z) for z in others(at.z, at.Z)]
    peers += [at.at(y=y) for y in others(at.y, at.Y)]
    peers += [at.at(x=x) for x in others(at.x, at.X)]
    return peers + [at.sibling()]


def gather_kernel(sizes, rows, mats, dense_ref, tail_ref, w_ref, gain_ref, router_ref, land, *sems):
    at = Place(sizes)
    Z, Y, X = at.Z, at.Y, at.X
    depth = land.shape[4]
    cut = depth // 2 // 16 * 16
    first, second = pl.ds(0, cut), pl.ds(cut, depth - cut)
    z_out, z_in, ya_out, ya_in, xb_out, xb_in, xa_out, xa_in, yb_out, yb_in, c_out, c_in = sems
    block = jnp.concatenate([dense_ref[...].reshape(mats * rows, -1), tail_ref[...]], 0)
    if block.shape[0] < depth:
        block = jnp.pad(block, ((0, depth - block.shape[0]), (0, 0)))
    mine = land.at[at.c, at.z, at.x, at.y]
    mine[...] = block.astype(jnp.bfloat16)
    greet(grid_peers(at))
    started = []

    def begin(copy):
        copy.start()
        started.append(copy)

    order = [at.z] + [lax.rem(at.z + k, Z) for k in (1, 3, 2)]
    for z in order[1:]:
        begin(send(mine, mine, z_out.at[z], z_in.at[at.z], at.at(z=z)))

    def one(z):
        part = land.at[at.c, z, at.x, at.y]
        for y in others(at.y, Y):
            begin(send(part.at[first], part.at[first], ya_out.at[z, y], ya_in.at[z, at.y], at.at(y=y)))
        for x in others(at.x, X):
            begin(send(part.at[second], part.at[second], xb_out.at[z, x], xb_in.at[z, at.x], at.at(x=x)))

    def two(z):
        for y in others(at.y, Y):
            part = land.at[at.c, z, at.x, y, first]
            send(part, part, ya_out.at[z, y], ya_in.at[z, y], at.at(y=y)).wait_recv()
        line = land.at[at.c, z, at.x, :, first]
        for x in others(at.x, X):
            begin(send(line, line, xa_out.at[z, x], xa_in.at[z, at.x], at.at(x=x)))
        for x in others(at.x, X):
            part = land.at[at.c, z, x, at.y, second]
            send(part, part, xb_out.at[z, x], xb_in.at[z, x], at.at(x=x)).wait_recv()
        line = land.at[at.c, z, :, at.y, second]
        for y in others(at.y, Y):
            begin(send(line, line, yb_out.at[z, y], yb_in.at[z, at.y], at.at(y=y)))

    def three(z):
        for x in others(at.x, X):
            line = land.at[at.c, z, x, :, first]
            send(line, line, xa_out.at[z, x], xa_in.at[z, x], at.at(x=x)).wait_recv()
        for y in others(at.y, Y):
            line = land.at[at.c, z, :, y, second]
            send(line, line, yb_out.at[z, y], yb_in.at[z, y], at.at(y=y)).wait_recv()
        plane = land.at[at.c, z]
        begin(send(plane, plane, c_out.at[z], c_in.at[z], at.sibling()))

    for step in range(Z + 2):
        if step < Z:
            if step > 0:
                z = order[step]
                part = land.at[at.c, z, at.x, at.y]
                send(part, part, z_out.at[z], z_in.at[z], at.at(z=z)).wait_recv()
            one(order[step])
        if 0 <= step - 1 < Z:
            two(order[step - 1])
        if 0 <= step - 2 < Z:
            three(order[step - 2])
    for z in order:
        plane = land.at[1 - at.c, z]
        send(plane, plane, c_out.at[z], c_in.at[z], at.sibling()).wait_recv()
    for copy in started:
        copy.wait_send()
    chips = [(z, y, x) for z in range(Z) for y in range(Y) for x in range(X)]
    cores = [(c, z, x, y) for z, y, x in chips for c in range(2)]
    group = 16 // math.gcd(16, rows)
    for start in range(0, len(cores), group):
        for mat in range(mats):
            w_ref[mat, start * rows : (start + group) * rows] = jnp.concatenate(
                [land[spot][mat * rows : (mat + 1) * rows] for spot in cores[start : start + group]], 0
            )
    base, count = mats * rows, tail_ref.shape[0]
    tails = [land[spot][base : base + count].astype(jnp.float32) for spot in cores]
    gain_ref[...] = jnp.concatenate([tail[:8, :rows] for tail in tails], 1)
    router_ref[...] = jnp.concatenate([tail[:, 128 : 128 + rows] for tail in tails], 1)


def gather_weights(sizes, dense, tail):
    mats, rows, width = dense.shape
    count = tail.shape[0]
    depth = round_up(mats * rows + count, 16)
    Z, Y, X = QUAD, sizes["g"], sizes["x"]
    dma = pltpu.SemaphoreType.DMA
    by_y, by_x = dma((Z, Y)), dma((Z, X))
    return pl.pallas_call(
        functools.partial(gather_kernel, sizes, rows, mats),
        out_shape=(
            jax.ShapeDtypeStruct((mats, width, width), jnp.bfloat16),
            jax.ShapeDtypeStruct((8, width), jnp.float32),
            jax.ShapeDtypeStruct((count, width), jnp.float32),
        ),
        in_specs=[whole()] * 2,
        out_specs=(whole(),) * 3,
        scratch_shapes=[VMEM((2, Z, X, Y, depth, width), jnp.bfloat16), dma((Z,)), dma((Z,))]
        + [by_y, by_y, by_x, by_x, by_x, by_x, by_y, by_y, dma((Z,)), dma((Z,))],
        compiler_params=pltpu.CompilerParams(
            collective_id=1, has_side_effects=True, vmem_limit_bytes=48 * MIB
        ),
        name="gather_weights",
    )(dense, tail)


def scatter_kernel(sizes, g_ref, out_ref, hold, sib, got_xa, got_yb, got_ya, got_xb, got_z, *sems):
    at = Place(sizes)
    Z, Y, X = at.Z, at.Y, at.X
    depth = g_ref.shape[4]
    cut = depth // 2 // 16 * 16
    first, second = pl.ds(0, cut), pl.ds(cut, depth - cut)
    c_out, c_in, xa_out, xa_in, yb_out, yb_in, ya_out, ya_in, xb_out, xb_in, z_out, z_in = sems
    greet(grid_peers(at))
    started = []

    def begin(copy):
        copy.start()
        started.append(copy)

    wide = lambda value: value.astype(jnp.float32)
    order = [lax.rem(at.z + k, Z) for k in (2, 1, 3)] + [at.z]
    for z in order:
        begin(send(g_ref.at[1 - at.c, z], sib.at[z], c_out.at[z], c_in.at[z], at.sibling()))

    def one(z):
        send(sib.at[z], sib.at[z], c_out.at[z], c_in.at[z], at.sibling()).wait_recv()
        hold[z] = (wide(g_ref[at.c, z]) + wide(sib[z])).astype(jnp.bfloat16)
        for x in others(at.x, X):
            begin(send(hold.at[z, x, :, first], got_xa.at[z, at.x], xa_out.at[z, x], xa_in.at[z, at.x], at.at(x=x)))
        for y in others(at.y, Y):
            begin(send(hold.at[z, :, y, second], got_yb.at[z, at.y], yb_out.at[z, y], yb_in.at[z, at.y], at.at(y=y)))

    def two(z):
        total = wide(hold[z, at.x, :, first])
        for x in others(at.x, X):
            send(got_xa.at[z, x], got_xa.at[z, x], xa_out.at[z, x], xa_in.at[z, x], at.at(x=x)).wait_recv()
            total = total + wide(got_xa[z, x])
        hold[z, at.x, :, first] = total.astype(jnp.bfloat16)
        for y in others(at.y, Y):
            begin(send(hold.at[z, at.x, y, first], got_ya.at[z, at.y], ya_out.at[z, y], ya_in.at[z, at.y], at.at(y=y)))
        total = wide(hold[z, :, at.y, second])
        for y in others(at.y, Y):
            send(got_yb.at[z, y], got_yb.at[z, y], yb_out.at[z, y], yb_in.at[z, y], at.at(y=y)).wait_recv()
            total = total + wide(got_yb[z, y])
        hold[z, :, at.y, second] = total.astype(jnp.bfloat16)
        for x in others(at.x, X):
            begin(send(hold.at[z, x, at.y, second], got_xb.at[z, at.x], xb_out.at[z, x], xb_in.at[z, at.x], at.at(x=x)))

    def three(z, last):
        total = wide(hold[z, at.x, at.y, first])
        for y in others(at.y, Y):
            send(got_ya.at[z, y], got_ya.at[z, y], ya_out.at[z, y], ya_in.at[z, y], at.at(y=y)).wait_recv()
            total = total + wide(got_ya[z, y])
        rest = wide(hold[z, at.x, at.y, second])
        for x in others(at.x, X):
            send(got_xb.at[z, x], got_xb.at[z, x], xb_out.at[z, x], xb_in.at[z, x], at.at(x=x)).wait_recv()
            rest = rest + wide(got_xb[z, x])
        if last:
            out_ref[first] = total
            out_ref[second] = rest
            return
        mine = hold.at[z, at.x, at.y]
        mine[first] = total.astype(jnp.bfloat16)
        mine[second] = rest.astype(jnp.bfloat16)
        begin(send(mine, got_z.at[at.z], z_out.at[z], z_in.at[at.z], at.at(z=z)))

    for step in range(Z + 2):
        if step < Z:
            one(order[step])
        if 0 <= step - 1 < Z:
            two(order[step - 1])
        if 0 <= step - 2 < Z:
            three(order[step - 2], step - 2 == Z - 1)
    for z in order[:-1]:
        send(got_z.at[z], got_z.at[z], z_out.at[z], z_in.at[z], at.at(z=z)).wait_recv()
        out_ref[...] += wide(got_z[z])
    for copy in started:
        copy.wait_send()


def scatter_dense(sizes, blocks):
    unused, Z, X, Y, depth, width = blocks.shape
    dma = pltpu.SemaphoreType.DMA
    by_y, by_x, by_z = dma((Z, Y)), dma((Z, X)), dma((Z,))
    cut = depth // 2 // 16 * 16
    half = jnp.bfloat16
    return pl.pallas_call(
        functools.partial(scatter_kernel, sizes),
        out_shape=jax.ShapeDtypeStruct((depth, width), jnp.float32),
        in_specs=[whole()],
        out_specs=whole(),
        scratch_shapes=[
            VMEM((Z, X, Y, depth, width), half),
            VMEM((Z, X, Y, depth, width), half),
            VMEM((Z, X, Y, cut, width), half),
            VMEM((Z, Y, X, depth - cut, width), half),
            VMEM((Z, Y, cut, width), half),
            VMEM((Z, X, depth - cut, width), half),
            VMEM((Z, depth, width), half),
        ]
        + [by_z, by_z, by_x, by_x, by_y, by_y, by_y, by_y, by_x, by_x, by_z, by_z],
        compiler_params=pltpu.CompilerParams(
            collective_id=2, has_side_effects=True, vmem_limit_bytes=48 * MIB
        ),
        name="scatter_dense",
    )(blocks)


def sums_kernel(sizes, in_ref, out_ref, land, out_sem, in_sem):
    at = Place(sizes)
    count = 2 * at.chips
    me = at.chip * 2 + at.c
    ids = others(me, count)

    def peer(device):
        spot = at.of_chip(lax.div(device, 2))
        spot["c"] = lax.rem(device, 2)
        return spot

    greet([peer(device) for device in ids])
    land[me] = in_ref[...]
    copies = [send(in_ref, land.at[me], out_sem.at[d], in_sem.at[me], peer(d)) for d in ids]
    for copy in copies:
        copy.start()
    for d in ids:
        send(land.at[d], land.at[d], out_sem.at[d], in_sem.at[d], peer(d)).wait_recv()
    out_ref[...] = jnp.sum(land[...], 0)
    for copy in copies:
        copy.wait_send()


def share_sums(sizes, values):
    count = sizes["g"] * QUAD * sizes["x"] * 2
    dma = pltpu.SemaphoreType.DMA
    return pl.pallas_call(
        functools.partial(sums_kernel, sizes),
        out_shape=jax.ShapeDtypeStruct(values.shape, jnp.float32),
        in_specs=[whole()],
        out_specs=whole(),
        scratch_shapes=[VMEM((count, *values.shape), jnp.float32), dma((count,)), dma((count,))],
        compiler_params=pltpu.CompilerParams(collective_id=3, has_side_effects=True),
        name="share_sums",
    )(values)


IMAGE_PAD = 16


def split_three(value):
    high = value.astype(jnp.bfloat16)
    rest = value - high.astype(jnp.float32)
    middle = rest.astype(jnp.bfloat16)
    return high, middle, (rest - middle.astype(jnp.float32)).astype(jnp.bfloat16)


def dot_f32(left, right, dims):
    return lax.dot_general(left, right, (dims, ((), ())), preferred_element_type=jnp.float32)


NN = ((1,), (0,))
NT = ((1,), (1,))
TN = ((0,), (0,))


def norm_parts(values):
    centre = values - jnp.mean(values, -1, keepdims=True)
    spread = jnp.mean(centre * centre, -1, keepdims=True)
    scale = lax.rsqrt(spread + eps_norm)
    return centre * scale, scale


def norm_back(d_out, scaled, scale, gain):
    pulled = d_out * gain
    return scale * (
        pulled
        - jnp.mean(pulled, -1, keepdims=True)
        - scaled * jnp.mean(pulled * scaled, -1, keepdims=True)
    )


def head_kernel(
    sizes, images, part_ref, own_ref, imp_ref, gain_ref, head_ref, label_ref,
    g_head_ref, d_pool_ref, own_d_ref, g_norm_ref, sums_ref, total_imp_ref,
    in_part, rows, d_rows, d_sib, d_sum, d_in, head_b, labels, d_logits, *sems
):
    at = Place(sizes)
    chips, members = at.chips, QUAD * at.X
    devices = 2 * chips
    p_out, p_in, r_out, r_in, s_out, s_in, d_out, d_in_sem, b_out, b_in = sems
    width = own_ref.shape[1]
    same_core = others(at.chip, chips)
    greet([at.of_chip(chip) for chip in same_core] + [at.sibling()])
    started = []

    def begin(copy):
        copy.start()
        started.append(copy)

    team = others(at.member, members)
    for member in team:
        begin(send(part_ref.at[member], in_part.at[at.member], p_out.at[member], p_in.at[at.member], at.of_member(member)))
    in_part[at.member] = part_ref[at.member]
    head_b[...] = head_ref[...].astype(jnp.bfloat16)
    wide = devices * IMAGE_PAD
    spot = lax.broadcasted_iota(jnp.int32, (label_ref.shape[1], wide), 1)
    given = lax.broadcasted_iota(jnp.int32, (label_ref.shape[1], wide), 0)
    image = lax.rem(spot, IMAGE_PAD)
    device = lax.rem(lax.div(spot, IMAGE_PAD), chips) * 2 + lax.div(spot, IMAGE_PAD * chips)
    chosen = ((device * images + image == given) & (image < images)).astype(jnp.bfloat16)
    labels[...] = dot_f32(label_ref[...].astype(jnp.float32).astype(jnp.bfloat16), chosen, NN).astype(jnp.bfloat16)
    for member in team:
        send(in_part.at[member], in_part.at[member], p_out.at[member], p_in.at[member], at.of_member(member)).wait_recv()
    pooled = own_ref[...] + jnp.sum(in_part[...], 0)
    scaled, scale = norm_parts(pooled)
    gain, shift = gain_ref[2:3], gain_ref[5:6]
    a_three = scaled * gain + shift
    row = lax.broadcasted_iota(jnp.int32, (IMAGE_PAD, width), 0)
    block = jnp.where(row < images, a_three, 0.0)
    pieces = split_three(imp_ref[...])
    for index, piece in enumerate(pieces):
        block = jnp.where(row == images + index, piece.astype(jnp.float32), block)
    rows[at.c, at.chip] = block.astype(jnp.bfloat16)
    mine = rows.at[at.c, at.chip]
    for chip in same_core:
        begin(send(mine, mine, r_out.at[chip], r_in.at[at.chip], at.of_chip(chip)))
    for chip in same_core:
        part = rows.at[at.c, chip]
        send(part, part, r_out.at[chip], r_in.at[chip], at.of_chip(chip)).wait_recv()
    begin(send(rows.at[at.c], rows.at[at.c], s_out.at[0], s_in.at[0], at.sibling()))
    send(rows.at[1 - at.c], rows.at[1 - at.c], s_out.at[0], s_in.at[0], at.sibling()).wait_recv()
    gathered = rows[...].reshape(wide, width)
    in_block = lax.rem(lax.broadcasted_iota(jnp.int32, (wide, width), 0), IMAGE_PAD)
    total = jnp.sum(jnp.where(in_block >= images, gathered.astype(jnp.float32), 0.0), 0, keepdims=True)
    total_imp_ref[...] = jnp.broadcast_to(total, total_imp_ref.shape)
    gathered = jnp.where(in_block < images, gathered.astype(jnp.float32), 0.0).astype(jnp.bfloat16)
    logits = dot_f32(head_b[...], gathered, NT)
    image = lax.rem(lax.broadcasted_iota(jnp.int32, logits.shape, 1), IMAGE_PAD)
    count = devices * images
    target = labels[...].astype(jnp.float32)
    power = jnp.exp(-jnp.abs(logits))
    loss = jnp.maximum(logits, 0.0) + jnp.log1p(power) - target * logits
    loss = jnp.sum(jnp.where(image < images, loss, 0.0), 1, keepdims=True)
    loss = jnp.sum(loss, 0, keepdims=True) / count
    sums_ref[...] = jnp.broadcast_to(loss, sums_ref.shape)
    chance = jnp.where(logits >= 0.0, 1.0, power) / (1.0 + power)
    d_logits[...] = jnp.where(image < images, (chance - target) / count, 0.0).astype(jnp.bfloat16)
    partial = dot_f32(d_logits[...], head_b[...], TN)
    d_rows[...] = partial.reshape(d_rows.shape).astype(jnp.bfloat16)
    begin(send(d_rows.at[1 - at.c], d_sib, s_out.at[1], s_in.at[1], at.sibling()))
    g_head_ref[...] = dot_f32(d_logits[...], gathered, NN)
    send(d_sib, d_sib, s_out.at[1], s_in.at[1], at.sibling()).wait_recv()
    d_sum[...] = (d_rows[at.c].astype(jnp.float32) + d_sib[...].astype(jnp.float32)).astype(jnp.bfloat16)
    for chip in same_core:
        begin(send(d_sum.at[chip], d_in.at[at.chip], d_out.at[chip], d_in_sem.at[at.chip], at.of_chip(chip)))
    d_in[at.chip] = d_sum[at.chip]
    for chip in same_core:
        send(d_in.at[chip], d_in.at[chip], d_out.at[chip], d_in_sem.at[chip], at.of_chip(chip)).wait_recv()
    d_norm = jnp.sum(d_in[...].astype(jnp.float32), 0)
    d_norm = jnp.where(row < images, d_norm, 0.0)
    d_pooled = norm_back(d_norm, scaled, scale, gain)
    d_pooled = jnp.where(row < images, d_pooled, 0.0)
    d_gain = jnp.sum(d_norm * scaled, 0, keepdims=True)
    d_shift = jnp.sum(d_norm, 0, keepdims=True)
    line = lax.broadcasted_iota(jnp.int32, g_norm_ref.shape, 0)
    g_norm_ref[...] = jnp.where(line == 2, d_gain, jnp.where(line == 5, d_shift, 0.0))
    own_d_ref[...] = d_pooled
    d_pool_ref[at.member] = d_pooled
    mine = d_pool_ref.at[at.member]
    for member in team:
        begin(send(own_d_ref, mine, b_out.at[member], b_in.at[at.member], at.of_member(member)))
    for member in team:
        part = d_pool_ref.at[member]
        send(part, part, b_out.at[member], b_in.at[member], at.of_member(member)).wait_recv()
    for copy in started:
        copy.wait_send()


def head_step(sizes, images, part, own, imp, gains, head, label):
    members = QUAD * sizes["x"]
    chips = members * sizes["g"]
    classes, width = head.shape
    wide = 2 * chips * IMAGE_PAD
    dma = pltpu.SemaphoreType.DMA
    by_member, by_chip = dma((members,)), dma((chips,))
    f32, half = jnp.float32, jnp.bfloat16
    blocks = (chips, IMAGE_PAD, width)
    return pl.pallas_call(
        functools.partial(head_kernel, sizes, images),
        out_shape=(
            jax.ShapeDtypeStruct((classes, width), f32),
            jax.ShapeDtypeStruct((members, IMAGE_PAD, width), f32),
            jax.ShapeDtypeStruct((IMAGE_PAD, width), f32),
            jax.ShapeDtypeStruct((8, width), f32),
            jax.ShapeDtypeStruct((8, 128), f32),
            jax.ShapeDtypeStruct((8, width), f32),
        ),
        in_specs=[whole()] * 6,
        out_specs=(whole(),) * 6,
        scratch_shapes=[
            VMEM((members, IMAGE_PAD, width), f32),
            VMEM((2, *blocks), half),
            VMEM((2, *blocks), half),
            VMEM(blocks, half),
            VMEM(blocks, half),
            VMEM(blocks, half),
            VMEM((classes, width), half),
            VMEM((classes, wide), half),
            VMEM((classes, wide), half),
        ]
        + [by_member, by_member, by_chip, by_chip, dma((2,)), dma((2,)), by_chip, by_chip]
        + [by_member, by_member],
        compiler_params=pltpu.CompilerParams(
            collective_id=4, has_side_effects=True, vmem_limit_bytes=56 * MIB
        ),
        name="head_step",
    )(part, own, imp, gains, head, label)


def shard_moves(n_blocks):
    span = 2 * n_blocks
    moves = []
    for step in range(span):
        pairs = []
        for place in range(QUAD * n_blocks):
            for core in range(2):
                target = (place + step) % span
                src = place * 2 + core
                dst = (target // 2 * QUAD + 2 * core + target % 2) * 2 + place // span
                pairs.append((src, dst))
        moves.append(pairs)
    return moves


def swap_cores(value):
    return lax.ppermute(value, "c", [(0, 1), (1, 0)])


def fetch_experts(expert_in, expert_out, n_blocks):
    place = lax.axis_index("g") * QUAD + lax.axis_index("r")
    odd = lax.rem(place, 2) == 1
    both = jnp.stack([expert_in, expert_out], 1).astype(jnp.bfloat16)
    ordered = [jnp.where(odd, both[1], both[0]), jnp.where(odd, both[0], both[1])]
    return [
        lax.ppermute(ordered[step % 2], ("g", "r", "c"), pairs)
        for step, pairs in enumerate(shard_moves(n_blocks))
    ]


def return_experts(parts, n_blocks):
    place = lax.axis_index("g") * QUAD + lax.axis_index("r")
    odd = lax.rem(place, 2) == 1
    sums = [None, None]
    for step, pairs in enumerate(shard_moves(n_blocks)):
        back = lax.ppermute(parts[step], ("g", "r", "c"), [(dst, src) for src, dst in pairs])
        back = back.astype(jnp.float32)
        sums[step % 2] = back if sums[step % 2] is None else sums[step % 2] + back
    zero, one = jnp.where(odd, sums[1], sums[0]), jnp.where(odd, sums[0], sums[1])
    return jnp.stack([zero[0], one[0]]), jnp.stack([zero[1], one[1]])


def to_members(value):
    return lax.all_to_all(value, MEMBERS, split_axis=0, concat_axis=0, tiled=True)


def body(
    patches,
    lengths,
    slot_mask,
    expert_picks,
    priority_rank,
    class_labels,
    dense_weights,
    dense_first,
    dense_second,
    dense_average,
    router_weights,
    router_first,
    router_second,
    router_average,
    norm_params,
    norm_first,
    norm_second,
    norm_average,
    expert_in,
    in_first,
    in_second,
    in_average,
    expert_out,
    out_first,
    out_second,
    out_average,
    head_weights,
    head_first,
    head_second,
    head_average,
):
    n_blocks = lax.axis_size("g")
    sizes = {name: lax.axis_size(name) for name in ALL}
    rows_own, n_experts = router_weights.shape
    n_tail = max(8, n_experts)
    tail = jnp.zeros((n_tail, dense_weights.shape[2]), jnp.float32)
    tail = tail.at[:6, :rows_own].set(norm_params)
    tail = tail.at[:n_experts, 128 : 128 + rows_own].set(router_weights.T)
    layer_b, gain_rows, router_t = gather_weights(sizes, dense_weights, tail)
    router_b = router_t[:n_experts].T.astype(jnp.bfloat16)
    expert_in_now, expert_out_now, layer_b = lax.optimization_barrier((expert_in, expert_out, layer_b))
    own_chunks = fetch_experts(expert_in_now, expert_out_now, n_blocks)
    own_half = jnp.stack(own_chunks, 1)
    other_half = swap_cores(own_half)
    w_one = jnp.concatenate([own_half[0], other_half[0]], 0)
    w_two = jnp.concatenate([own_half[1], other_half[1]], 0)
    rows_here, n_slots_row = slot_mask.shape
    tokens = rows_here * n_slots_row
    model_width = layer_b.shape[2]
    n_images = lengths.shape[0] * lengths.shape[1]
    capacity = (21 * tokens * TOP + 20 * n_experts - 1) // (20 * n_experts)
    padded = (capacity + 15) // 16 * 16
    n_slots = n_experts * padded
    w_one = w_one.reshape(-1, model_width)
    w_two = w_two.reshape(-1, model_width)
    valid = slot_mask.astype(jnp.float32)
    positions = jnp.arange(n_slots_row, dtype=jnp.int32)
    bounds = jnp.cumsum(lengths, 1)
    segment = jnp.sum((positions[None, :, None] >= bounds[:, None, :]).astype(jnp.int32), -1)
    diagonal = positions[:, None] == positions[None, :]
    allowed = (segment[:, :, None] == segment[:, None, :]) & (
        (valid[:, None, :] > 0) | diagonal[None]
    )
    member = (
        segment[:, None, :] == jnp.arange(lengths.shape[1], dtype=jnp.int32)[None, :, None]
    ).astype(jnp.float32) * valid[:, None, :]
    pooling = member / jnp.maximum(jnp.sum(member, -1, keepdims=True), 1.0)
    valid_flat = valid.reshape(tokens)
    pool_flat = jnp.sum(pooling, 1).reshape(tokens)
    image_flat = (segment + jnp.arange(rows_here)[:, None] * lengths.shape[1]).reshape(tokens)
    slot_one, slot_two, kept_one, kept_two = route(
        expert_picks, valid_flat, priority_rank[0], n_experts, capacity, padded
    )
    x_zero = jnp.dot(patches, layer_b[0], preferred_element_type=jnp.float32)
    a_one = layer_norm(x_zero, gain_rows[0], gain_rows[3]).astype(jnp.bfloat16)
    proj_qkv = jnp.einsum(
        "td,kde->kte", a_one, layer_b[1:4], preferred_element_type=jnp.float32
    ).astype(jnp.bfloat16)
    att_out, log_total = attention_forward(proj_qkv, allowed, HEADS)
    x_one = x_zero + jnp.dot(att_out, layer_b[4], preferred_element_type=jnp.float32)
    a_two = layer_norm(x_one, gain_rows[1], gain_rows[4]).astype(jnp.bfloat16)
    router_probs = softmax_rows(jnp.dot(a_two, router_b, preferred_element_type=jnp.float32))
    part_importance = jnp.sum(router_probs * valid_flat[:, None], 0)
    pick_one = expert_picks[:, 0]
    pick_two = expert_picks[:, 1]
    columns = jnp.arange(n_experts, dtype=jnp.int32)
    hot_one = (pick_one[:, None] == columns[None]).astype(jnp.float32)
    hot_two = (pick_two[:, None] == columns[None]).astype(jnp.float32)
    gate_one = jnp.sum(router_probs * hot_one, 1) * kept_one
    gate_two = jnp.sum(router_probs * hot_two, 1) * kept_two
    slot_ids = jnp.arange(n_slots, dtype=jnp.int32)
    match_one = slot_one[None, :] == slot_ids[:, None]
    match_two = slot_two[None, :] == slot_ids[:, None]
    match = (match_one | match_two).astype(jnp.bfloat16)
    send_rows = (
        jnp.dot(match, a_two, preferred_element_type=jnp.float32)
        .astype(jnp.bfloat16)
        .reshape(n_experts, padded, model_width)
    )
    held = jnp.where(match_one | match_two, 1.0, 0.0)
    slot_gate = jnp.sum(
        jnp.where(match_one, gate_one[None], 0.0) + jnp.where(match_two, gate_two[None], 0.0), 1
    )
    slot_pool = jnp.sum(held * pool_flat[None], 1)
    slot_image = jnp.sum(held * image_flat.astype(jnp.float32)[None], 1)
    details = jnp.stack([slot_gate, slot_pool, slot_image]).reshape(3, n_experts, padded)
    arrived = to_members(send_rows)
    details = to_members(details.transpose(1, 0, 2))
    got_gate, got_pool, got_image = details[:, 0], details[:, 1], details[:, 2]
    image_hot = (
        got_image[:, :, None] == jnp.arange(n_images).astype(jnp.float32)[None, None]
    ).astype(jnp.float32) * got_pool[:, :, None]
    rows_all = arrived.reshape(n_slots, model_width)
    hidden = jnp.dot(rows_all, w_one.T, preferred_element_type=jnp.float32)
    activated = jax.nn.gelu(hidden).astype(jnp.bfloat16)
    result = jnp.dot(activated, w_two, preferred_element_type=jnp.float32).astype(jnp.bfloat16)
    result = result.reshape(n_experts, padded, model_width).astype(jnp.float32)
    part_pooled = jnp.einsum(
        "dsi,dsw->diw", image_hot * got_gate[:, :, None], result, precision=high_prec
    )
    pooled = jnp.einsum(
        "ris,rsd->rid",
        pooling,
        x_one.reshape(rows_here, n_slots_row, model_width),
        precision=high_prec,
    ).reshape(-1, model_width)
    pad_rows = ((0, IMAGE_PAD - n_images), (0, 0))
    g_head, d_pooled_all, d_pooled, g_norm_three, local_loss, importance = head_step(
        sizes,
        n_images,
        jnp.pad(part_pooled, ((0, 0), *pad_rows)),
        jnp.pad(pooled, pad_rows),
        jnp.pad(part_importance, (0, model_width - n_experts))[None],
        gain_rows,
        head_weights,
        class_labels,
    )
    importance = importance[0, :n_experts]
    local_loss = local_loss[0, 0]
    d_pooled_all = d_pooled_all[:, :n_images]
    d_pooled = d_pooled[:n_images]
    centre = jnp.mean(importance)
    spread = jnp.mean((importance - centre) ** 2)
    d_imp = aux_weight * (
        2.0 * (importance - centre) / (n_experts * centre * centre)
        - 2.0 * spread / (n_experts * centre * centre * centre)
    )
    d_two = jnp.einsum(
        "ris,rid->rsd", pooling, d_pooled.reshape(rows_here, -1, model_width), precision=high_prec
    ).reshape(tokens, model_width)
    d_two_slots = jnp.einsum("dsi,diw->dsw", image_hot, d_pooled_all, precision=high_prec)
    slot_d_gate = jnp.sum(d_two_slots * result, -1)
    d_all = (d_two_slots * got_gate[:, :, None]).astype(jnp.bfloat16).reshape(n_slots, model_width)
    d_act = jnp.dot(d_all, w_two.T, preferred_element_type=jnp.float32)
    d_hidden = jax.vjp(jax.nn.gelu, hidden)[1](d_act)[0].astype(jnp.bfloat16)
    d_inputs = jnp.dot(d_hidden, w_one, preferred_element_type=jnp.float32).astype(jnp.bfloat16)
    d_back = to_members(d_inputs.reshape(n_experts, padded, model_width))
    d_back = d_back.reshape(n_slots, model_width)
    back_gate = to_members(slot_d_gate).reshape(n_slots)
    g_two = jnp.dot(activated.T, d_all, preferred_element_type=jnp.float32)
    g_one = jnp.dot(d_hidden.T, rows_all, preferred_element_type=jnp.float32)
    half = g_one.shape[0] // 2
    grads = jnp.stack([g_one, g_two], 0).astype(jnp.bfloat16)
    summed = grads[:, :half].astype(jnp.float32) + swap_cores(grads[:, half:]).astype(jnp.float32)
    summed = summed.astype(jnp.bfloat16).reshape(2, 2 * n_blocks, -1, model_width)
    g_one, g_two = return_experts([summed[:, i] for i in range(2 * n_blocks)], n_blocks)
    d_gate_one = kept_one * jnp.take(back_gate, jnp.maximum(slot_one, 0), axis=0)
    d_gate_two = kept_two * jnp.take(back_gate, jnp.maximum(slot_two, 0), axis=0)
    d_a_two = lax.dot_general(
        match, d_back, (((0,), (0,)), ((), ())), preferred_element_type=jnp.float32
    )
    d_probs = (
        hot_one * d_gate_one[:, None]
        + hot_two * d_gate_two[:, None]
        + valid_flat[:, None] * d_imp[None, :]
    )
    d_router = (
        router_probs * (d_probs - jnp.sum(router_probs * d_probs, 1, keepdims=True))
    ).astype(jnp.bfloat16)
    g_router = jnp.dot(a_two.T, d_router, preferred_element_type=jnp.float32)
    d_a_two = d_a_two + jnp.dot(d_router, router_b.T, preferred_element_type=jnp.float32)
    unused_out, norm_back = jax.vjp(layer_norm, x_one, gain_rows[1], gain_rows[4])
    d_x_one, g_gain_two, g_shift_two = norm_back(d_a_two)
    d_x_one = d_x_one + d_two
    d_att_b = d_x_one.astype(jnp.bfloat16)
    g_out_proj = jnp.dot(att_out.T, d_att_b, preferred_element_type=jnp.float32)
    d_att_out = jnp.dot(d_att_b, layer_b[4].T, preferred_element_type=jnp.float32).astype(
        jnp.bfloat16
    )
    d_qkv = attention_backward(proj_qkv, allowed, log_total, d_att_out, HEADS)
    g_qkv = jnp.einsum("td,kte->kde", a_one, d_qkv, preferred_element_type=jnp.float32)
    d_a_one = jnp.einsum("kte,kde->td", d_qkv, layer_b[1:4], preferred_element_type=jnp.float32)
    unused_out, norm_back = jax.vjp(layer_norm, x_zero, gain_rows[0], gain_rows[3])
    d_x_zero, g_gain_one, g_shift_one = norm_back(d_a_one)
    d_x_zero = (d_x_zero + d_x_one).astype(jnp.bfloat16)
    g_embed = jnp.dot(patches.T, d_x_zero, preferred_element_type=jnp.float32)
    g_layers = jnp.concatenate([g_embed[None], g_qkv, g_out_proj[None]], 0)
    zero = jnp.zeros_like(g_gain_one)
    g_norms = g_norm_three[:6] + jnp.stack(
        [g_gain_one, g_gain_two, zero, g_shift_one, g_shift_two, zero]
    )
    def spread_rows(value):
        value = value.reshape(value.shape[0], QUAD, n_blocks, sizes["x"], 2, rows_own, -1)
        return value.transpose(4, 1, 3, 2, 0, 5, 6)

    blocks = spread_rows(g_layers.astype(jnp.bfloat16))
    blocks = blocks.reshape(*blocks.shape[:4], -1, model_width)
    small = jnp.concatenate([g_norms, g_router.T], 0).astype(jnp.bfloat16)
    small = spread_rows(small[..., None])[..., 0]
    n_dense, n_small = blocks.shape[4], small.shape[4]
    depth = round_up(n_dense + n_small, 16)
    small = jnp.pad(small, ((0, 0),) * 4 + ((0, depth - n_dense - n_small), (0, model_width - rows_own)))
    reduced = scatter_dense(sizes, jnp.concatenate([blocks, small], 4))
    g_layers = reduced[:n_dense].reshape(-1, rows_own, model_width)
    g_norms = reduced[n_dense : n_dense + 6, :rows_own]
    g_router = reduced[n_dense + 6 : n_dense + n_small, :rows_own].T
    squares = (
        jnp.sum(g_layers * g_layers) + jnp.sum(g_router * g_router) + jnp.sum(g_norms * g_norms)
    )
    squares = squares + jnp.sum(g_one * g_one) + jnp.sum(g_two * g_two) + jnp.sum(g_head * g_head)
    line = lax.broadcasted_iota(jnp.int32, (8, 128), 0)
    all_sums = share_sums(sizes, jnp.where(line == 0, local_loss, squares))
    loss_sum, square_sum = all_sums[0, 0], all_sums[1, 0]
    grad_norm = jnp.sqrt(square_sum)
    factor = jnp.minimum(1.0, clip_limit / grad_norm)
    loss_value = loss_sum + aux_weight * spread / (centre * centre)
    dense_out = adam_update(
        dense_weights, dense_first, dense_second, dense_average, g_layers, factor, base_rate
    )
    router_out = adam_update(
        router_weights, router_first, router_second, router_average, g_router, factor, base_rate
    )
    norm_out = adam_update(
        norm_params, norm_first, norm_second, norm_average, g_norms, factor, norm_rate
    )
    in_out = adam_update(expert_in, in_first, in_second, in_average, g_one, factor, base_rate)
    out_out = adam_update(expert_out, out_first, out_second, out_average, g_two, factor, base_rate)
    head_out = adam_update(
        head_weights, head_first, head_second, head_average, g_head, factor, base_rate
    )
    return (
        loss_value,
        importance,
        grad_norm,
        *dense_out,
        *router_out,
        *norm_out,
        *in_out,
        *out_out,
        *head_out,
    )


def solution(mesh):
    n_dp, n_expert = mesh.shape["dp"], mesh.shape["expert"]
    shaped = mesh.devices.reshape(n_dp // QUAD, QUAD, n_expert // 2, 2)
    fine = Mesh(shaped, ALL)
    rows = P(ALL, None)
    dense = P(None, ALL, None)
    norms = P(None, ALL)
    experts = P(("x", "c"), ("g", "r"), None)
    placed = (rows,) * 6 + (dense,) * 4 + (rows,) * 4 + (norms,) * 4 + (experts,) * 8 + (rows,) * 4
    results = (
        (P(),) * 3 + (dense,) * 4 + (rows,) * 4 + (norms,) * 4 + (experts,) * 8 + (rows,) * 4
    )
    return jax.shard_map(body, mesh=fine, in_specs=placed, out_specs=results, check_vma=False)
```

```python
import functools
import math

import jax
import jax.numpy as jnp
from jax import lax
from jax.experimental import pallas as pl
from jax.experimental.pallas import tpu as pltpu
from jax.sharding import Mesh
from jax.sharding import PartitionSpec as P

HEADS = 12
TOP = 2
STEP_COUNT = 10
QUAD = 4

high_prec = lax.Precision.HIGHEST
eps_norm = 1e-06
aux_weight = 0.01
clip_limit = 1.0
base_rate = 0.05
norm_rate = 0.5
beta_first = 0.9
beta_second = 0.999
weight_decay = 0.1
polyak_decay = 0.7
adam_eps = 1e-08
mask_fill = -1e30

ALL = ("g", "r", "x", "c")
MEMBERS = ("x", "r")


def layer_norm(values, gain, shift):
    centre = values - jnp.mean(values, -1, keepdims=True)
    spread = jnp.mean(centre * centre, -1, keepdims=True)
    return centre * lax.rsqrt(spread + eps_norm) * gain + shift


def adam_update(weight, first_state, second_state, average_state, gradient, factor, step_rate):
    clipped = gradient * factor
    first_new = beta_first * first_state + (1.0 - beta_first) * clipped
    second_new = beta_second * second_state + (1.0 - beta_second) * clipped * clipped
    first_hat = first_new / (1.0 - beta_first**STEP_COUNT)
    second_hat = second_new / (1.0 - beta_second**STEP_COUNT)
    weight_new = weight - step_rate * (
        first_hat / (jnp.sqrt(second_hat) + adam_eps) + weight_decay * weight
    )
    average_new = polyak_decay * average_state + (1.0 - polyak_decay) * weight_new
    return (weight_new, first_new, second_new, average_new)


def split_heads(proj_qkv, allow_mask, n_heads):
    n_rows, n_slots_row = (allow_mask.shape[0], allow_mask.shape[1])
    head_dim = proj_qkv.shape[-1] // n_heads
    shaped = proj_qkv.reshape(3, n_rows, n_slots_row, n_heads, head_dim)
    scores = jnp.einsum(
        "rqhd,rkhd->rhqk", shaped[0], shaped[1], preferred_element_type=jnp.float32
    ) * head_dim ** (-0.5)
    return (shaped, jnp.where(allow_mask[:, None], scores, mask_fill), head_dim ** (-0.5))


def attention_backward(proj_qkv, allow_mask, log_total, d_output, n_heads):
    shaped, masked, score_scale = split_heads(proj_qkv, allow_mask, n_heads)
    att_probs = jnp.exp(masked - log_total)
    grad_out = d_output.reshape(shaped.shape[1:])
    d_probs = jnp.einsum("rqhd,rkhd->rhqk", grad_out, shaped[2], preferred_element_type=jnp.float32)
    d_values = jnp.einsum(
        "rhqk,rqhd->rkhd",
        att_probs.astype(jnp.bfloat16),
        grad_out,
        preferred_element_type=jnp.float32,
    )
    d_scores = (att_probs * (d_probs - jnp.sum(att_probs * d_probs, -1, keepdims=True))).astype(
        jnp.bfloat16
    )
    d_query = (
        jnp.einsum("rhqk,rkhd->rqhd", d_scores, shaped[1], preferred_element_type=jnp.float32)
        * score_scale
    )
    d_keys = (
        jnp.einsum("rhqk,rqhd->rkhd", d_scores, shaped[0], preferred_element_type=jnp.float32)
        * score_scale
    )
    stacked = jnp.stack([d_query, d_keys, d_values]).astype(jnp.bfloat16)
    return stacked.reshape(proj_qkv.shape)


MESH_ID = pl.DeviceIdType.MESH
VMEM = pltpu.VMEM
ANY = pl.ANY
MIB = 1 << 20


def whole(space=None):
    return pl.BlockSpec(memory_space=space or VMEM)


def round_up(value, step):
    return (value + step - 1) // step * step


class Place:
    def __init__(self, sizes):
        self.G, self.X = sizes["g"], sizes["x"]
        self.Z, self.Y = QUAD, sizes["g"]
        self.chips = self.Z * self.Y * self.X
        spot = lax.axis_index("g") * QUAD + lax.axis_index("r")
        self.z, self.y = lax.div(spot, self.Y), lax.rem(spot, self.Y)
        self.x, self.c = lax.axis_index("x"), lax.axis_index("c")
        self.g, self.r = lax.axis_index("g"), lax.axis_index("r")
        self.chip = spot * self.X + self.x
        self.member = self.x * QUAD + self.r

    def at(self, z=None, y=None, x=None, c=None):
        spot = (self.z if z is None else z) * self.Y + (self.y if y is None else y)
        return {
            "g": lax.div(spot, QUAD),
            "r": lax.rem(spot, QUAD),
            "x": self.x if x is None else x,
            "c": self.c if c is None else c,
        }

    def of_chip(self, chip):
        spot = lax.div(chip, self.X)
        return {
            "g": lax.div(spot, QUAD),
            "r": lax.rem(spot, QUAD),
            "x": lax.rem(chip, self.X),
            "c": self.c,
        }

    def of_member(self, member):
        return {
            "g": self.g,
            "r": lax.rem(member, QUAD),
            "x": lax.div(member, QUAD),
            "c": self.c,
        }

    def sibling(self):
        return self.at(c=1 - self.c)


def greet(peers):
    barrier = pltpu.get_barrier_semaphore()
    for peer in peers:
        pl.semaphore_signal(barrier, inc=1, device_id=peer, device_id_type=MESH_ID)
    pl.semaphore_wait(barrier, len(peers))


def send(src, dst, send_sem, recv_sem, peer):
    return pltpu.make_async_remote_copy(
        src_ref=src,
        dst_ref=dst,
        send_sem=send_sem,
        recv_sem=recv_sem,
        device_id=peer,
        device_id_type=MESH_ID,
    )


def others(me, count):
    return [lax.rem(me + step, count) for step in range(1, count)]


def grid_peers(at):
    peers = [at.at(z=z) for z in others(at.z, at.Z)]
    peers += [at.at(y=y) for y in others(at.y, at.Y)]
    peers += [at.at(x=x) for x in others(at.x, at.X)]
    return peers + [at.sibling()]


def gather_kernel(
    sizes, rows, mats, routing, dense_ref, tail_ref, pick_ref, rank_ref, mask_ref, length_ref,
    w_ref, gain_ref, router_ref, col_ref, land, *sems
):
    at = Place(sizes)
    Z, Y, X = at.Z, at.Y, at.X
    depth = land.shape[4]
    cut = depth // 2 // 16 * 16
    first, second = pl.ds(0, cut), pl.ds(cut, depth - cut)
    z_out, z_in, ya_out, ya_in, xb_out, xb_in, xa_out, xa_in, yb_out, yb_in, c_out, c_in = sems
    block = jnp.concatenate([dense_ref[...].reshape(mats * rows, -1), tail_ref[...]], 0)
    if block.shape[0] < depth:
        block = jnp.pad(block, ((0, depth - block.shape[0]), (0, 0)))
    mine = land.at[at.c, at.z, at.x, at.y]
    mine[...] = block.astype(jnp.bfloat16)
    greet(grid_peers(at))
    started = []

    def begin(copy):
        copy.start()
        started.append(copy)

    order = [at.z] + [lax.rem(at.z + k, Z) for k in (1, 3, 2)]
    for z in order[1:]:
        begin(send(mine, mine, z_out.at[z], z_in.at[at.z], at.at(z=z)))

    def one(z):
        part = land.at[at.c, z, at.x, at.y]
        for y in others(at.y, Y):
            begin(send(part.at[first], part.at[first], ya_out.at[z, y], ya_in.at[z, at.y], at.at(y=y)))
        for x in others(at.x, X):
            begin(send(part.at[second], part.at[second], xb_out.at[z, x], xb_in.at[z, at.x], at.at(x=x)))

    def two(z):
        for y in others(at.y, Y):
            part = land.at[at.c, z, at.x, y, first]
            send(part, part, ya_out.at[z, y], ya_in.at[z, y], at.at(y=y)).wait_recv()
        line = land.at[at.c, z, at.x, :, first]
        for x in others(at.x, X):
            begin(send(line, line, xa_out.at[z, x], xa_in.at[z, at.x], at.at(x=x)))
        for x in others(at.x, X):
            part = land.at[at.c, z, x, at.y, second]
            send(part, part, xb_out.at[z, x], xb_in.at[z, x], at.at(x=x)).wait_recv()
        line = land.at[at.c, z, :, at.y, second]
        for y in others(at.y, Y):
            begin(send(line, line, yb_out.at[z, y], yb_in.at[z, at.y], at.at(y=y)))

    def three(z):
        for x in others(at.x, X):
            line = land.at[at.c, z, x, :, first]
            send(line, line, xa_out.at[z, x], xa_in.at[z, x], at.at(x=x)).wait_recv()
        for y in others(at.y, Y):
            line = land.at[at.c, z, :, y, second]
            send(line, line, yb_out.at[z, y], yb_in.at[z, y], at.at(y=y)).wait_recv()
        plane = land.at[at.c, z]
        begin(send(plane, plane, c_out.at[z], c_in.at[z], at.sibling()))

    for step in range(Z + 2):
        if step < Z:
            if step > 0:
                z = order[step]
                part = land.at[at.c, z, at.x, at.y]
                send(part, part, z_out.at[z], z_in.at[z], at.at(z=z)).wait_recv()
            one(order[step])
        if step == 0:
            col_ref[...] = route_math(*routing, pick_ref, rank_ref, mask_ref, length_ref)
        if 0 <= step - 1 < Z:
            two(order[step - 1])
        if 0 <= step - 2 < Z:
            three(order[step - 2])
    for z in order:
        plane = land.at[1 - at.c, z]
        send(plane, plane, c_out.at[z], c_in.at[z], at.sibling()).wait_recv()
    for copy in started:
        copy.wait_send()
    chips = [(z, y, x) for z in range(Z) for y in range(Y) for x in range(X)]
    cores = [(c, z, x, y) for z, y, x in chips for c in range(2)]
    group = 16 // math.gcd(16, rows)
    for start in range(0, len(cores), group):
        for mat in range(mats):
            w_ref[mat, start * rows : (start + group) * rows] = jnp.concatenate(
                [land[spot][mat * rows : (mat + 1) * rows] for spot in cores[start : start + group]], 0
            )
    base, count = mats * rows, tail_ref.shape[0]
    tails = [land[spot][base : base + count].astype(jnp.float32) for spot in cores]
    gain_ref[...] = jnp.concatenate([tail[:8, :rows] for tail in tails], 1)
    router_ref[...] = jnp.concatenate([tail[:, 128 : 128 + rows] for tail in tails], 1)


def gather_weights(sizes, routing, dense, tail, picks, ranks, slot_mask, lengths):
    mats, rows, width = dense.shape
    count = tail.shape[0]
    depth = round_up(mats * rows + count, 16)
    Z, Y, X = QUAD, sizes["g"], sizes["x"]
    dma = pltpu.SemaphoreType.DMA
    by_y, by_x = dma((Z, Y)), dma((Z, X))
    return pl.pallas_call(
        functools.partial(gather_kernel, sizes, rows, mats, routing),
        out_shape=(
            jax.ShapeDtypeStruct((mats, width, width), jnp.bfloat16),
            jax.ShapeDtypeStruct((8, width), jnp.float32),
            jax.ShapeDtypeStruct((count, width), jnp.float32),
            jax.ShapeDtypeStruct((picks.shape[0], 128), jnp.float32),
        ),
        in_specs=[whole()] * 6,
        out_specs=(whole(),) * 4,
        scratch_shapes=[VMEM((2, Z, X, Y, depth, width), jnp.bfloat16), dma((Z,)), dma((Z,))]
        + [by_y, by_y, by_x, by_x, by_x, by_x, by_y, by_y, dma((Z,)), dma((Z,))],
        compiler_params=pltpu.CompilerParams(
            collective_id=1, has_side_effects=True, vmem_limit_bytes=48 * MIB
        ),
        name="gather_weights",
    )(dense, tail, picks, ranks, slot_mask, lengths)


def scatter_kernel(sizes, g_ref, out_ref, hold, sib, got_xa, got_yb, got_ya, got_xb, got_z, *sems):
    at = Place(sizes)
    Z, Y, X = at.Z, at.Y, at.X
    depth = g_ref.shape[4]
    cut = depth // 2 // 16 * 16
    first, second = pl.ds(0, cut), pl.ds(cut, depth - cut)
    c_out, c_in, xa_out, xa_in, yb_out, yb_in, ya_out, ya_in, xb_out, xb_in, z_out, z_in = sems
    greet(grid_peers(at))
    started = []

    def begin(copy):
        copy.start()
        started.append(copy)

    wide = lambda value: value.astype(jnp.float32)
    order = [lax.rem(at.z + k, Z) for k in (2, 1, 3)] + [at.z]
    for z in order:
        begin(send(g_ref.at[1 - at.c, z], sib.at[z], c_out.at[z], c_in.at[z], at.sibling()))

    def one(z):
        send(sib.at[z], sib.at[z], c_out.at[z], c_in.at[z], at.sibling()).wait_recv()
        hold[z] = (wide(g_ref[at.c, z]) + wide(sib[z])).astype(jnp.bfloat16)
        for x in others(at.x, X):
            begin(send(hold.at[z, x, :, first], got_xa.at[z, at.x], xa_out.at[z, x], xa_in.at[z, at.x], at.at(x=x)))
        for y in others(at.y, Y):
            begin(send(hold.at[z, :, y, second], got_yb.at[z, at.y], yb_out.at[z, y], yb_in.at[z, at.y], at.at(y=y)))

    def two(z):
        total = wide(hold[z, at.x, :, first])
        for x in others(at.x, X):
            send(got_xa.at[z, x], got_xa.at[z, x], xa_out.at[z, x], xa_in.at[z, x], at.at(x=x)).wait_recv()
            total = total + wide(got_xa[z, x])
        hold[z, at.x, :, first] = total.astype(jnp.bfloat16)
        for y in others(at.y, Y):
            begin(send(hold.at[z, at.x, y, first], got_ya.at[z, at.y], ya_out.at[z, y], ya_in.at[z, at.y], at.at(y=y)))
        total = wide(hold[z, :, at.y, second])
        for y in others(at.y, Y):
            send(got_yb.at[z, y], got_yb.at[z, y], yb_out.at[z, y], yb_in.at[z, y], at.at(y=y)).wait_recv()
            total = total + wide(got_yb[z, y])
        hold[z, :, at.y, second] = total.astype(jnp.bfloat16)
        for x in others(at.x, X):
            begin(send(hold.at[z, x, at.y, second], got_xb.at[z, at.x], xb_out.at[z, x], xb_in.at[z, at.x], at.at(x=x)))

    def three(z, last):
        total = wide(hold[z, at.x, at.y, first])
        for y in others(at.y, Y):
            send(got_ya.at[z, y], got_ya.at[z, y], ya_out.at[z, y], ya_in.at[z, y], at.at(y=y)).wait_recv()
            total = total + wide(got_ya[z, y])
        rest = wide(hold[z, at.x, at.y, second])
        for x in others(at.x, X):
            send(got_xb.at[z, x], got_xb.at[z, x], xb_out.at[z, x], xb_in.at[z, x], at.at(x=x)).wait_recv()
            rest = rest + wide(got_xb[z, x])
        if last:
            out_ref[first] = total
            out_ref[second] = rest
            return
        mine = hold.at[z, at.x, at.y]
        mine[first] = total.astype(jnp.bfloat16)
        mine[second] = rest.astype(jnp.bfloat16)
        begin(send(mine, got_z.at[at.z], z_out.at[z], z_in.at[at.z], at.at(z=z)))

    for step in range(Z + 2):
        if step < Z:
            one(order[step])
        if 0 <= step - 1 < Z:
            two(order[step - 1])
        if 0 <= step - 2 < Z:
            three(order[step - 2], step - 2 == Z - 1)
    for z in order[:-1]:
        send(got_z.at[z], got_z.at[z], z_out.at[z], z_in.at[z], at.at(z=z)).wait_recv()
        out_ref[...] += wide(got_z[z])
    for copy in started:
        copy.wait_send()


def scatter_dense(sizes, blocks):
    unused, Z, X, Y, depth, width = blocks.shape
    dma = pltpu.SemaphoreType.DMA
    by_y, by_x, by_z = dma((Z, Y)), dma((Z, X)), dma((Z,))
    cut = depth // 2 // 16 * 16
    half = jnp.bfloat16
    return pl.pallas_call(
        functools.partial(scatter_kernel, sizes),
        out_shape=jax.ShapeDtypeStruct((depth, width), jnp.float32),
        in_specs=[whole()],
        out_specs=whole(),
        scratch_shapes=[
            VMEM((Z, X, Y, depth, width), half),
            VMEM((Z, X, Y, depth, width), half),
            VMEM((Z, X, Y, cut, width), half),
            VMEM((Z, Y, X, depth - cut, width), half),
            VMEM((Z, Y, cut, width), half),
            VMEM((Z, X, depth - cut, width), half),
            VMEM((Z, depth, width), half),
        ]
        + [by_z, by_z, by_x, by_x, by_y, by_y, by_y, by_y, by_x, by_x, by_z, by_z],
        compiler_params=pltpu.CompilerParams(
            collective_id=2, has_side_effects=True, vmem_limit_bytes=48 * MIB
        ),
        name="scatter_dense",
    )(blocks)


def sums_kernel(sizes, in_ref, out_ref, land, out_sem, in_sem):
    at = Place(sizes)
    count = 2 * at.chips
    me = at.chip * 2 + at.c
    ids = others(me, count)

    def peer(device):
        spot = at.of_chip(lax.div(device, 2))
        spot["c"] = lax.rem(device, 2)
        return spot

    greet([peer(device) for device in ids])
    land[me] = in_ref[...]
    copies = [send(in_ref, land.at[me], out_sem.at[d], in_sem.at[me], peer(d)) for d in ids]
    for copy in copies:
        copy.start()
    for d in ids:
        send(land.at[d], land.at[d], out_sem.at[d], in_sem.at[d], peer(d)).wait_recv()
    out_ref[...] = jnp.sum(land[...], 0)
    for copy in copies:
        copy.wait_send()


def share_sums(sizes, values):
    count = sizes["g"] * QUAD * sizes["x"] * 2
    dma = pltpu.SemaphoreType.DMA
    return pl.pallas_call(
        functools.partial(sums_kernel, sizes),
        out_shape=jax.ShapeDtypeStruct(values.shape, jnp.float32),
        in_specs=[whole()],
        out_specs=whole(),
        scratch_shapes=[VMEM((count, *values.shape), jnp.float32), dma((count,)), dma((count,))],
        compiler_params=pltpu.CompilerParams(collective_id=3, has_side_effects=True),
        name="share_sums",
    )(values)


IMAGE_PAD = 16


def split_three(value):
    high = value.astype(jnp.bfloat16)
    rest = value - high.astype(jnp.float32)
    middle = rest.astype(jnp.bfloat16)
    return high, middle, (rest - middle.astype(jnp.float32)).astype(jnp.bfloat16)


def dot_f32(left, right, dims):
    return lax.dot_general(left, right, (dims, ((), ())), preferred_element_type=jnp.float32)


NN = ((1,), (0,))
NT = ((1,), (1,))
TN = ((0,), (0,))


def norm_parts(values):
    centre = values - jnp.mean(values, -1, keepdims=True)
    spread = jnp.mean(centre * centre, -1, keepdims=True)
    scale = lax.rsqrt(spread + eps_norm)
    return centre * scale, scale


def norm_back(d_out, scaled, scale, gain):
    pulled = d_out * gain
    return scale * (
        pulled
        - jnp.mean(pulled, -1, keepdims=True)
        - scaled * jnp.mean(pulled * scaled, -1, keepdims=True)
    )


def head_kernel(
    sizes, images, part_ref, own_ref, imp_ref, gain_ref, head_ref, label_ref,
    g_head_ref, d_pool_ref, own_d_ref, g_norm_ref, sums_ref, total_imp_ref,
    in_part, rows, d_rows, d_sib, d_sum, d_in, head_b, labels, d_logits, *sems
):
    at = Place(sizes)
    chips, members = at.chips, QUAD * at.X
    devices = 2 * chips
    p_out, p_in, r_out, r_in, s_out, s_in, d_out, d_in_sem, b_out, b_in = sems
    width = own_ref.shape[1]
    same_core = others(at.chip, chips)
    greet([at.of_chip(chip) for chip in same_core] + [at.sibling()])
    started = []

    def begin(copy):
        copy.start()
        started.append(copy)

    team = others(at.member, members)
    for member in team:
        begin(send(part_ref.at[member], in_part.at[at.member], p_out.at[member], p_in.at[at.member], at.of_member(member)))
    in_part[at.member] = part_ref[at.member]
    head_b[...] = head_ref[...].astype(jnp.bfloat16)
    wide = devices * IMAGE_PAD
    spot = lax.broadcasted_iota(jnp.int32, (label_ref.shape[1], wide), 1)
    given = lax.broadcasted_iota(jnp.int32, (label_ref.shape[1], wide), 0)
    image = lax.rem(spot, IMAGE_PAD)
    device = lax.rem(lax.div(spot, IMAGE_PAD), chips) * 2 + lax.div(spot, IMAGE_PAD * chips)
    chosen = ((device * images + image == given) & (image < images)).astype(jnp.bfloat16)
    labels[...] = dot_f32(label_ref[...].astype(jnp.float32).astype(jnp.bfloat16), chosen, NN).astype(jnp.bfloat16)
    for member in team:
        send(in_part.at[member], in_part.at[member], p_out.at[member], p_in.at[member], at.of_member(member)).wait_recv()
    pooled = own_ref[...] + jnp.sum(in_part[...], 0)
    scaled, scale = norm_parts(pooled)
    gain, shift = gain_ref[2:3], gain_ref[5:6]
    a_three = scaled * gain + shift
    row = lax.broadcasted_iota(jnp.int32, (IMAGE_PAD, width), 0)
    block = jnp.where(row < images, a_three, 0.0)
    pieces = split_three(imp_ref[0:1])
    for index, piece in enumerate(pieces):
        block = jnp.where(row == images + index, piece.astype(jnp.float32), block)
    rows[at.c, at.chip] = block.astype(jnp.bfloat16)
    mine = rows.at[at.c, at.chip]
    for chip in same_core:
        begin(send(mine, mine, r_out.at[chip], r_in.at[at.chip], at.of_chip(chip)))
    for chip in same_core:
        part = rows.at[at.c, chip]
        send(part, part, r_out.at[chip], r_in.at[chip], at.of_chip(chip)).wait_recv()
    begin(send(rows.at[at.c], rows.at[at.c], s_out.at[0], s_in.at[0], at.sibling()))
    send(rows.at[1 - at.c], rows.at[1 - at.c], s_out.at[0], s_in.at[0], at.sibling()).wait_recv()
    gathered = rows[...].reshape(wide, width)
    in_block = lax.rem(lax.broadcasted_iota(jnp.int32, (wide, width), 0), IMAGE_PAD)
    total = jnp.sum(jnp.where(in_block >= images, gathered.astype(jnp.float32), 0.0), 0, keepdims=True)
    total_imp_ref[...] = jnp.broadcast_to(total, total_imp_ref.shape)
    gathered = jnp.where(in_block < images, gathered.astype(jnp.float32), 0.0).astype(jnp.bfloat16)
    logits = dot_f32(head_b[...], gathered, NT)
    image = lax.rem(lax.broadcasted_iota(jnp.int32, logits.shape, 1), IMAGE_PAD)
    count = devices * images
    target = labels[...].astype(jnp.float32)
    power = jnp.exp(-jnp.abs(logits))
    loss = jnp.maximum(logits, 0.0) + jnp.log1p(power) - target * logits
    loss = jnp.sum(jnp.where(image < images, loss, 0.0), 1, keepdims=True)
    loss = jnp.sum(loss, 0, keepdims=True) / count
    sums_ref[...] = jnp.broadcast_to(loss, sums_ref.shape)
    chance = jnp.where(logits >= 0.0, 1.0, power) / (1.0 + power)
    d_logits[...] = jnp.where(image < images, (chance - target) / count, 0.0).astype(jnp.bfloat16)
    partial = dot_f32(d_logits[...], head_b[...], TN)
    d_rows[...] = partial.reshape(d_rows.shape).astype(jnp.bfloat16)
    begin(send(d_rows.at[1 - at.c], d_sib, s_out.at[1], s_in.at[1], at.sibling()))
    g_head_ref[...] = dot_f32(d_logits[...], gathered, NN)
    send(d_sib, d_sib, s_out.at[1], s_in.at[1], at.sibling()).wait_recv()
    d_sum[...] = (d_rows[at.c].astype(jnp.float32) + d_sib[...].astype(jnp.float32)).astype(jnp.bfloat16)
    for chip in same_core:
        begin(send(d_sum.at[chip], d_in.at[at.chip], d_out.at[chip], d_in_sem.at[at.chip], at.of_chip(chip)))
    d_in[at.chip] = d_sum[at.chip]
    for chip in same_core:
        send(d_in.at[chip], d_in.at[chip], d_out.at[chip], d_in_sem.at[chip], at.of_chip(chip)).wait_recv()
    d_norm = jnp.sum(d_in[...].astype(jnp.float32), 0)
    d_norm = jnp.where(row < images, d_norm, 0.0)
    d_pooled = norm_back(d_norm, scaled, scale, gain)
    d_pooled = jnp.where(row < images, d_pooled, 0.0)
    d_gain = jnp.sum(d_norm * scaled, 0, keepdims=True)
    d_shift = jnp.sum(d_norm, 0, keepdims=True)
    line = lax.broadcasted_iota(jnp.int32, g_norm_ref.shape, 0)
    g_norm_ref[...] = jnp.where(line == 2, d_gain, jnp.where(line == 5, d_shift, 0.0))
    own_d_ref[...] = d_pooled
    d_pool_ref[at.member] = d_pooled
    mine = d_pool_ref.at[at.member]
    for member in team:
        begin(send(own_d_ref, mine, b_out.at[member], b_in.at[at.member], at.of_member(member)))
    for member in team:
        part = d_pool_ref.at[member]
        send(part, part, b_out.at[member], b_in.at[member], at.of_member(member)).wait_recv()
    for copy in started:
        copy.wait_send()


def head_step(sizes, images, part, own, imp, gains, head, label):
    members = QUAD * sizes["x"]
    chips = members * sizes["g"]
    classes, width = head.shape
    wide = 2 * chips * IMAGE_PAD
    dma = pltpu.SemaphoreType.DMA
    by_member, by_chip = dma((members,)), dma((chips,))
    f32, half = jnp.float32, jnp.bfloat16
    blocks = (chips, IMAGE_PAD, width)
    return pl.pallas_call(
        functools.partial(head_kernel, sizes, images),
        out_shape=(
            jax.ShapeDtypeStruct((classes, width), f32),
            jax.ShapeDtypeStruct((members, IMAGE_PAD, width), f32),
            jax.ShapeDtypeStruct((IMAGE_PAD, width), f32),
            jax.ShapeDtypeStruct((8, width), f32),
            jax.ShapeDtypeStruct((8, 128), f32),
            jax.ShapeDtypeStruct((8, width), f32),
        ),
        in_specs=[whole()] * 6,
        out_specs=(whole(),) * 6,
        scratch_shapes=[
            VMEM((members, IMAGE_PAD, width), f32),
            VMEM((2, *blocks), half),
            VMEM((2, *blocks), half),
            VMEM(blocks, half),
            VMEM(blocks, half),
            VMEM(blocks, half),
            VMEM((classes, width), half),
            VMEM((classes, wide), half),
            VMEM((classes, wide), half),
        ]
        + [by_member, by_member, by_chip, by_chip, dma((2,)), dma((2,)), by_chip, by_chip]
        + [by_member, by_member],
        compiler_params=pltpu.CompilerParams(
            collective_id=4, has_side_effects=True, vmem_limit_bytes=56 * MIB
        ),
        name="head_step",
    )(part, own, imp, gains, head, label)


def route_math(per_image, n_experts, capacity, padded, pick_ref, rank_ref, mask_ref, length_ref):
    rows_here, span = mask_ref.shape
    tokens = rows_here * span
    valid = mask_ref[...].astype(jnp.float32)
    lengths = length_ref[...]
    position = lax.broadcasted_iota(jnp.int32, (rows_here, span), 1)
    segment = jnp.zeros((rows_here, span), jnp.int32)
    bound = jnp.zeros((rows_here, 1), jnp.int32)
    for image in range(per_image):
        bound = bound + lengths[:, image : image + 1]
        segment = segment + jnp.where(position >= bound, 1, 0)
    pool = jnp.zeros_like(valid)
    for image in range(per_image):
        member = jnp.where(segment == image, valid, 0.0)
        pool = pool + member / jnp.maximum(jnp.sum(member, 1, keepdims=True), 1.0)
    line = lax.broadcasted_iota(jnp.int32, (rows_here, span), 0)
    image = (segment + per_image * line).astype(jnp.float32)

    def flat(value):
        return jnp.concatenate([value[i : i + 1] for i in range(rows_here)], 1)

    rank_row = rank_ref[...].astype(jnp.float32)
    table = jnp.concatenate([flat(valid), flat(pool), flat(image), rank_row], 0)
    table = jnp.concatenate([table, jnp.zeros((124, tokens), jnp.float32)], 0).T
    valid_col, pool_col, image_col, rank_col = (table[:, i : i + 1] for i in range(4))
    picks = pick_ref[...]
    pick_one, pick_two = picks[:, 0:1], picks[:, 1:2]
    lane = lax.broadcasted_iota(jnp.int32, (tokens, 128), 1)
    in_first, in_second = lane < n_experts, (lane >= n_experts) & (lane < 2 * n_experts)
    hot = jnp.where(in_first & (pick_one == lane), valid_col, 0.0)
    hot = hot + jnp.where(in_second & (pick_two == lane - n_experts), valid_col, 0.0)
    shifted = jnp.where(in_second & (pick_one == lane - n_experts), valid_col, 0.0)
    before = jnp.where(rank_row < rank_col, 1.0, 0.0).astype(jnp.bfloat16)
    ahead = dot_f32(before, hot.astype(jnp.bfloat16), NN) + jnp.sum(shifted, 0, keepdims=True)
    counted = hot * ahead
    pos_one = jnp.sum(jnp.where(in_first, counted, 0.0), 1, keepdims=True)
    pos_two = jnp.sum(jnp.where(in_second, counted, 0.0), 1, keepdims=True)

    def place(pick, pos):
        kept = (valid_col > 0.0) & (pos < capacity)
        return jnp.where(kept, pick.astype(jnp.float32) * padded + pos, -1.0)

    columns = (
        place(pick_one, pos_one),
        place(pick_two, pos_two),
        valid_col,
        pool_col,
        image_col,
        pick_one.astype(jnp.float32),
        pick_two.astype(jnp.float32),
    )
    result = jnp.zeros((tokens, 128), jnp.float32)
    for index, column in enumerate(columns):
        result = jnp.where(lane == index, column, result)
    return result


def lane_mask(shape, left):
    lane = lax.broadcasted_iota(jnp.int32, shape, 1)
    return lane < 64 if left else lane >= 64


def allowed_slots(lengths, row, images, valid_row, span):
    query = lax.broadcasted_iota(jnp.int32, (span, span), 0)
    key = lax.broadcasted_iota(jnp.int32, (span, span), 1)
    bound = 0
    query_seg, key_seg = jnp.zeros((span, span), jnp.int32), jnp.zeros((span, span), jnp.int32)
    for image in range(images):
        bound = bound + lengths[row, image]
        query_seg = query_seg + jnp.where(query >= bound, 1, 0)
        key_seg = key_seg + jnp.where(key >= bound, 1, 0)
    return (query_seg == key_seg) & ((valid_row > 0) | (query == key))


def dense_forward_kernel(
    n_experts, images, length_ref, mask_ref, patch_ref, w_ref, gain_ref, router_ref, col_ref,
    x_zero_ref, a_one_ref, qkv_ref, att_ref, x_one_ref, a_two_ref, prob_ref, lse_ref, pool_ref, imp_ref
):
    row = pl.program_id(0)
    span, width = patch_ref.shape
    x_zero = dot_f32(patch_ref[...], w_ref[0], NN)
    x_zero_ref[...] = x_zero
    a_one = (norm_parts(x_zero)[0] * gain_ref[0:1] + gain_ref[3:4]).astype(jnp.bfloat16)
    a_one_ref[...] = a_one
    for part in range(3):
        qkv_ref[:, part * width : (part + 1) * width] = dot_f32(a_one, w_ref[1 + part], NN).astype(
            jnp.bfloat16
        )
    open_to = allowed_slots(length_ref, row, images, mask_ref[0], span)
    lane = lax.broadcasted_iota(jnp.int32, (span, 128), 1)
    logs = jnp.zeros((span, 128), jnp.float32)
    for pair in range(width // 128):
        query, key, value = (
            qkv_ref[:, part * width + pair * 128 : part * width + (pair + 1) * 128]
            for part in range(3)
        )
        outs = []
        for side in range(2):
            held = jnp.where((lane < 64) == (side == 0), query, jnp.zeros_like(query))
            scores = jnp.where(open_to, dot_f32(held, key, NT) * 64**-0.5, mask_fill)
            top = jnp.max(scores, 1, keepdims=True)
            powers = jnp.exp(scores - top)
            total = jnp.sum(powers, 1, keepdims=True)
            probs = (powers * (1.0 / total)).astype(jnp.bfloat16)
            outs.append(dot_f32(probs, value, NN))
            logs = jnp.where(lane == 2 * pair + side, top + jnp.log(total), logs)
        att_ref[:, pair * 128 : (pair + 1) * 128] = jnp.where(lane < 64, outs[0], outs[1]).astype(
            jnp.bfloat16
        )
    lse_ref[...] = logs
    x_one = x_zero + dot_f32(att_ref[...], w_ref[4], NN)
    x_one_ref[...] = x_one
    a_two = (norm_parts(x_one)[0] * gain_ref[1:2] + gain_ref[4:5]).astype(jnp.bfloat16)
    a_two_ref[...] = a_two
    routers = router_ref[...].astype(jnp.bfloat16)
    if routers.shape[0] < 128:
        routers = jnp.concatenate(
            [routers, jnp.zeros((128 - routers.shape[0], width), jnp.bfloat16)], 0
        )
    logits = jnp.where(lane < n_experts, dot_f32(a_two, routers, NT), mask_fill)
    powers = jnp.exp(logits - jnp.max(logits, 1, keepdims=True))
    probs = powers / jnp.sum(powers, 1, keepdims=True)
    prob_ref[...] = probs

    @pl.when(row == 0)
    def _():
        pool_ref[...] = jnp.zeros_like(pool_ref)
        imp_ref[...] = jnp.zeros_like(imp_ref)

    valid, pool, image = col_ref[:, 2:3], col_ref[:, 3:4], col_ref[:, 4:5]
    imp_ref[0:1, 0:128] += jnp.sum(probs * valid, 0, keepdims=True)
    line = lax.broadcasted_iota(jnp.int32, pool_ref.shape, 0)
    for index in range(images):
        number = row * images + index
        weight = jnp.where(image == number.astype(jnp.float32), pool, 0.0)
        pooled = jnp.sum(x_one * weight, 0, keepdims=True)
        pool_ref[...] = jnp.where(line == number, pooled, pool_ref[...])


def dense_forward(n_experts, lengths, slot_mask, patches, weights, gains, routers, columns):
    rows_here, span = slot_mask.shape
    tokens, width = patches.shape
    f32, half = jnp.float32, jnp.bfloat16

    def block(wide):
        return pl.BlockSpec((span, wide), lambda i: (i, 0))

    def out(wide, kind):
        return jax.ShapeDtypeStruct((tokens, wide), kind)

    def fixed(shape):
        return pl.BlockSpec(shape, lambda i: (0, 0))

    return pl.pallas_call(
        functools.partial(dense_forward_kernel, n_experts, lengths.shape[1]),
        grid=(rows_here,),
        out_shape=(
            out(width, f32), out(width, half), out(3 * width, half), out(width, half),
            out(width, f32), out(width, half), out(128, f32), out(128, f32),
            jax.ShapeDtypeStruct((IMAGE_PAD, width), f32), jax.ShapeDtypeStruct((8, width), f32),
        ),
        in_specs=[
            whole(pltpu.SMEM), pl.BlockSpec((1, 1, span), lambda i: (i, 0, 0)), block(width),
            whole(), whole(), whole(), block(128),
        ],
        out_specs=(
            block(width), block(width), block(3 * width), block(width), block(width), block(width),
            block(128), block(128), fixed((IMAGE_PAD, width)), fixed((8, width)),
        ),
        compiler_params=pltpu.CompilerParams(vmem_limit_bytes=48 * MIB),
        name="dense_forward",
    )(lengths, slot_mask[:, None, :], patches, weights, gains, routers, columns)


def dispatch_kernel(
    sizes, n_experts, padded, a_two_ref, prob_ref, col_ref, rows_ref, detail_ref,
    send_rows, send_detail, places, own_sem, r_out, r_in, m_out, m_in
):
    at = Place(sizes)
    tokens = a_two_ref.shape[0]
    team = others(at.member, n_experts)
    greet([at.of_member(member) for member in team])
    columns = col_ref[...]
    places[...] = columns.T[:8]
    lane = lax.broadcasted_iota(jnp.int32, (tokens, 128), 1)
    kind, expert = lax.div(lane, n_experts), lax.rem(lane, n_experts).astype(jnp.float32)
    slot_lane = lax.broadcasted_iota(jnp.int32, (tokens, send_detail.shape[2]), 1).astype(jnp.float32)
    pool, image = columns[:, 3:4], columns[:, 4:5]
    details = None
    for choice in range(2):
        slot, pick = columns[:, choice : choice + 1], columns[:, 5 + choice : 6 + choice]
        hot = (expert == pick) & (slot >= 0.0)
        gate = jnp.sum(jnp.where(hot & (kind == 0), prob_ref[...], 0.0), 1, keepdims=True)
        values = jnp.zeros((tokens, 128), jnp.float32)
        pieces = [*split_three(gate), *split_three(pool), image]
        for index, piece in enumerate(pieces):
            values = jnp.where(kind == index, piece.astype(jnp.float32), values)
        values = jnp.where(hot, values, 0.0).astype(jnp.bfloat16)
        spot = jnp.where(slot >= 0.0, slot - pick * padded, -1.0)
        chosen = jnp.where(spot == slot_lane, 1.0, 0.0).astype(jnp.bfloat16)
        found = dot_f32(values, chosen, TN)
        details = found if details is None else details + found
    n = n_experts
    gates = details[0:n] + details[n : 2 * n] + details[2 * n : 3 * n]
    pools = details[3 * n : 4 * n] + details[4 * n : 5 * n] + details[5 * n : 6 * n]
    images = details[6 * n : 7 * n]
    for index in range(n):
        for spot, value in enumerate((gates, pools, images)):
            send_detail[index, spot : spot + 1] = value[index : index + 1]
        send_detail[index, 3:8] = jnp.zeros((5, send_detail.shape[2]), jnp.float32)

    def rows_of(member):
        slots = lax.broadcasted_iota(jnp.int32, (padded, tokens), 0) + member * padded
        slots = slots.astype(jnp.float32)
        match = (slots == places[0:1]) | (slots == places[1:2])
        match = jnp.where(match, 1.0, 0.0).astype(jnp.bfloat16)
        send_rows[member] = dot_f32(match, a_two_ref[...], NN).astype(jnp.bfloat16)

    def row_copy(member, source):
        return send(
            send_rows.at[member], rows_ref.at[source], r_out.at[member], r_in.at[source], at.of_member(member)
        )

    def detail_copy(member, source):
        return send(
            send_detail.at[member], detail_ref.at[source], m_out.at[member], m_in.at[source], at.of_member(member)
        )

    def step(index, carry):
        member = lax.rem(at.member + index, n_experts)
        rows_of(member)
        row_copy(member, at.member).start()
        detail_copy(member, at.member).start()
        return carry

    lax.fori_loop(1, n_experts, step, 0)
    rows_of(at.member)
    keep_rows = pltpu.make_async_copy(send_rows.at[at.member], rows_ref.at[at.member], own_sem.at[0])
    keep_detail = pltpu.make_async_copy(send_detail.at[at.member], detail_ref.at[at.member], own_sem.at[1])
    keep_rows.start()
    keep_detail.start()
    for member in team:
        row_copy(member, member).wait_recv()
        detail_copy(member, member).wait_recv()
    for member in team:
        row_copy(member, at.member).wait_send()
        detail_copy(member, at.member).wait_send()
    keep_rows.wait()
    keep_detail.wait()


def dispatch(sizes, n_experts, padded, a_two, probs, columns):
    tokens, width = a_two.shape
    lanes = round_up(padded, 128)
    dma = pltpu.SemaphoreType.DMA
    each = dma((n_experts,))
    return pl.pallas_call(
        functools.partial(dispatch_kernel, sizes, n_experts, padded),
        out_shape=(
            jax.ShapeDtypeStruct((n_experts, padded, width), jnp.bfloat16),
            jax.ShapeDtypeStruct((n_experts, 8, lanes), jnp.float32),
        ),
        in_specs=[whole()] * 3,
        out_specs=(whole(ANY), whole(ANY)),
        scratch_shapes=[
            VMEM((n_experts, padded, width), jnp.bfloat16),
            VMEM((n_experts, 8, lanes), jnp.float32),
            VMEM((8, tokens), jnp.float32),
            dma((2,)), each, each, each, each,
        ],
        compiler_params=pltpu.CompilerParams(
            collective_id=5, has_side_effects=True, vmem_limit_bytes=48 * MIB
        ),
        name="dispatch",
    )(a_two, probs, columns)


def image_hot(detail, padded):
    image = detail[2:3, :padded]
    line = lax.broadcasted_iota(jnp.int32, (IMAGE_PAD, padded), 0).astype(jnp.float32)
    return line == image


def expert_forward_kernel(
    padded, rows_ref, detail_ref, own_ref, other_ref, act_ref, slope_ref, y_ref, part_ref
):
    many, unused, width = rows_ref.shape
    rows = rows_ref[...].reshape(many * padded, width)
    half = own_ref.shape[1]
    step = 384
    total = None
    for index, ref in enumerate((own_ref, other_ref)):
        for start in range(0, half, step):
            hidden = dot_f32(rows, ref[0, start : start + step], NT)
            square = hidden * hidden
            curve = jnp.tanh(0.7978845608 * hidden * (1.0 + 0.044715 * square))
            upper = 0.5 * (1.0 + curve)
            act = (hidden * upper).astype(jnp.bfloat16)
            slope = upper + 0.5 * hidden * (1.0 - curve * curve) * (
                0.7978845608 + 3.0 * 0.7978845608 * 0.044715 * square
            )
            spot = index * half + start
            act_ref[:, spot : spot + step] = act
            slope_ref[:, spot : spot + step] = slope.astype(jnp.bfloat16)
            found = dot_f32(act, ref[1, start : start + step], NN)
            total = found if total is None else total + found
    result = total.astype(jnp.bfloat16)
    y_ref[...] = result.reshape(many, padded, width)
    for source in range(many):
        detail = detail_ref[source]
        weight = detail[0:1, :padded] * detail[1:2, :padded]
        weights = jnp.where(image_hot(detail, padded), weight, 0.0)
        pieces = jnp.concatenate(split_three(weights), 0)
        sums = dot_f32(pieces, result[source * padded : (source + 1) * padded], NN)
        part_ref[source] = (
            sums[:IMAGE_PAD] + sums[IMAGE_PAD : 2 * IMAGE_PAD] + sums[2 * IMAGE_PAD :]
        )


def expert_forward(rows, details, own_half, other_half):
    sources, padded, width = rows.shape
    hidden = 2 * own_half.shape[1]
    many = max(1, 576 // padded)
    lanes = details.shape[2]
    half = jnp.bfloat16

    def by_source(*shape):
        return pl.BlockSpec((many, *shape), lambda i: (i, 0, 0))

    flat = pl.BlockSpec((many * padded, hidden), lambda i: (i, 0))
    return pl.pallas_call(
        functools.partial(expert_forward_kernel, padded),
        grid=(sources // many,),
        out_shape=(
            jax.ShapeDtypeStruct((sources * padded, hidden), half),
            jax.ShapeDtypeStruct((sources * padded, hidden), half),
            jax.ShapeDtypeStruct((sources, padded, width), half),
            jax.ShapeDtypeStruct((sources, IMAGE_PAD, width), jnp.float32),
        ),
        in_specs=[by_source(padded, width), by_source(8, lanes), whole(), whole()],
        out_specs=(flat, flat, by_source(padded, width), by_source(IMAGE_PAD, width)),
        compiler_params=pltpu.CompilerParams(vmem_limit_bytes=56 * MIB),
        name="expert_forward",
    )(rows, details, own_half, other_half)


def shard_moves(n_blocks):
    span = 2 * n_blocks
    moves = []
    for step in range(span):
        pairs = []
        for place in range(QUAD * n_blocks):
            for core in range(2):
                target = (place + step) % span
                src = place * 2 + core
                dst = (target // 2 * QUAD + 2 * core + target % 2) * 2 + place // span
                pairs.append((src, dst))
        moves.append(pairs)
    return moves


def swap_cores(value):
    return lax.ppermute(value, "c", [(0, 1), (1, 0)])


def fetch_experts(expert_in, expert_out, n_blocks):
    place = lax.axis_index("g") * QUAD + lax.axis_index("r")
    odd = lax.rem(place, 2) == 1
    both = jnp.stack([expert_in, expert_out], 1).astype(jnp.bfloat16)
    ordered = [jnp.where(odd, both[1], both[0]), jnp.where(odd, both[0], both[1])]
    return [
        lax.ppermute(ordered[step % 2], ("g", "r", "c"), pairs)
        for step, pairs in enumerate(shard_moves(n_blocks))
    ]


def return_experts(parts, n_blocks):
    place = lax.axis_index("g") * QUAD + lax.axis_index("r")
    odd = lax.rem(place, 2) == 1
    sums = [None, None]
    for step, pairs in enumerate(shard_moves(n_blocks)):
        back = lax.ppermute(parts[step], ("g", "r", "c"), [(dst, src) for src, dst in pairs])
        back = back.astype(jnp.float32)
        sums[step % 2] = back if sums[step % 2] is None else sums[step % 2] + back
    zero, one = jnp.where(odd, sums[1], sums[0]), jnp.where(odd, sums[0], sums[1])
    return jnp.stack([zero[0], one[0]]), jnp.stack([zero[1], one[1]])


def to_members(value):
    return lax.all_to_all(value, MEMBERS, split_axis=0, concat_axis=0, tiled=True)


def body(
    patches,
    lengths,
    slot_mask,
    expert_picks,
    priority_rank,
    class_labels,
    dense_weights,
    dense_first,
    dense_second,
    dense_average,
    router_weights,
    router_first,
    router_second,
    router_average,
    norm_params,
    norm_first,
    norm_second,
    norm_average,
    expert_in,
    in_first,
    in_second,
    in_average,
    expert_out,
    out_first,
    out_second,
    out_average,
    head_weights,
    head_first,
    head_second,
    head_average,
):
    n_blocks = lax.axis_size("g")
    sizes = {name: lax.axis_size(name) for name in ALL}
    rows_own, n_experts = router_weights.shape
    n_tail = max(8, n_experts)
    tail = jnp.zeros((n_tail, dense_weights.shape[2]), jnp.float32)
    tail = tail.at[:6, :rows_own].set(norm_params)
    tail = tail.at[:n_experts, 128 : 128 + rows_own].set(router_weights.T)
    rows_here, n_slots_row = slot_mask.shape
    tokens, model_width = patches.shape
    n_images = lengths.shape[0] * lengths.shape[1]
    capacity = (21 * tokens * TOP + 20 * n_experts - 1) // (20 * n_experts)
    padded = round_up(capacity, 16)
    n_slots = n_experts * padded
    layer_b, gain_rows, router_t, columns = gather_weights(
        sizes,
        (lengths.shape[1], n_experts, capacity, padded),
        dense_weights,
        tail,
        expert_picks,
        priority_rank,
        slot_mask,
        lengths,
    )
    router_b = router_t[:n_experts].T.astype(jnp.bfloat16)
    expert_in_now, expert_out_now, layer_b = lax.optimization_barrier((expert_in, expert_out, layer_b))
    own_chunks = fetch_experts(expert_in_now, expert_out_now, n_blocks)
    own_half = jnp.concatenate(own_chunks, 1)
    other_half = swap_cores(own_half)
    w_one = jnp.concatenate([own_half[0], other_half[0]], 0)
    w_two = jnp.concatenate([own_half[1], other_half[1]], 0)
    x_zero, a_one, qkv, att_out, x_one, a_two, router_probs, logs, pooled, part_importance = (
        dense_forward(
            n_experts, lengths, slot_mask, patches, layer_b, gain_rows, router_t, columns
        )
    )
    arrived, details = dispatch(sizes, n_experts, padded, a_two, router_probs, columns)
    activated, slope, result, part_pooled = expert_forward(arrived, details, own_half, other_half)

    valid = slot_mask.astype(jnp.float32)
    positions = jnp.arange(n_slots_row, dtype=jnp.int32)
    bounds = jnp.cumsum(lengths, 1)
    segment = jnp.sum((positions[None, :, None] >= bounds[:, None, :]).astype(jnp.int32), -1)
    diagonal = positions[:, None] == positions[None, :]
    allowed = (segment[:, :, None] == segment[:, None, :]) & (
        (valid[:, None, :] > 0) | diagonal[None]
    )
    member = (
        segment[:, None, :] == jnp.arange(lengths.shape[1], dtype=jnp.int32)[None, :, None]
    ).astype(jnp.float32) * valid[:, None, :]
    pooling = member / jnp.maximum(jnp.sum(member, -1, keepdims=True), 1.0)
    valid_flat = valid.reshape(tokens)
    slot_one, slot_two = columns[:, 0].astype(jnp.int32), columns[:, 1].astype(jnp.int32)
    kept_one = (slot_one >= 0).astype(jnp.float32)
    kept_two = (slot_two >= 0).astype(jnp.float32)
    router_probs = router_probs[:, :n_experts]
    proj_qkv = qkv.reshape(tokens, 3, model_width).transpose(1, 0, 2)
    log_total = logs[:, :HEADS].reshape(rows_here, n_slots_row, HEADS).transpose(0, 2, 1)[..., None]
    pick_one = expert_picks[:, 0]
    pick_two = expert_picks[:, 1]
    ids = jnp.arange(n_experts, dtype=jnp.int32)
    hot_one = (pick_one[:, None] == ids[None]).astype(jnp.float32)
    hot_two = (pick_two[:, None] == ids[None]).astype(jnp.float32)
    slot_ids = jnp.arange(n_slots, dtype=jnp.int32)
    match = (
        (slot_one[None, :] == slot_ids[:, None]) | (slot_two[None, :] == slot_ids[:, None])
    ).astype(jnp.bfloat16)
    got_gate, got_pool, got_image = (details[:, i, :padded] for i in range(3))
    image_hots = (
        got_image[:, :, None] == jnp.arange(n_images).astype(jnp.float32)[None, None]
    ).astype(jnp.float32) * got_pool[:, :, None]
    rows_all = arrived.reshape(n_slots, model_width)
    result = result.astype(jnp.float32)
    g_head, d_pooled_all, d_pooled, g_norm_three, local_loss, importance = head_step(
        sizes,
        n_images,
        part_pooled,
        pooled,
        part_importance,
        gain_rows,
        head_weights,
        class_labels,
    )
    importance = importance[0, :n_experts]
    local_loss = local_loss[0, 0]
    d_pooled_all = d_pooled_all[:, :n_images]
    d_pooled = d_pooled[:n_images]
    centre = jnp.mean(importance)
    spread = jnp.mean((importance - centre) ** 2)
    d_imp = aux_weight * (
        2.0 * (importance - centre) / (n_experts * centre * centre)
        - 2.0 * spread / (n_experts * centre * centre * centre)
    )
    d_two = jnp.einsum(
        "ris,rid->rsd", pooling, d_pooled.reshape(rows_here, -1, model_width), precision=high_prec
    ).reshape(tokens, model_width)
    d_two_slots = jnp.einsum("dsi,diw->dsw", image_hots, d_pooled_all, precision=high_prec)
    slot_d_gate = jnp.sum(d_two_slots * result, -1)
    d_all = (d_two_slots * got_gate[:, :, None]).astype(jnp.bfloat16).reshape(n_slots, model_width)
    d_act = jnp.dot(d_all, w_two.T, preferred_element_type=jnp.float32)
    d_hidden = (d_act * slope.astype(jnp.float32)).astype(jnp.bfloat16)
    d_inputs = jnp.dot(d_hidden, w_one, preferred_element_type=jnp.float32).astype(jnp.bfloat16)
    d_back = to_members(d_inputs.reshape(n_experts, padded, model_width))
    d_back = d_back.reshape(n_slots, model_width)
    back_gate = to_members(slot_d_gate).reshape(n_slots)
    g_two = jnp.dot(activated.T, d_all, preferred_element_type=jnp.float32)
    g_one = jnp.dot(d_hidden.T, rows_all, preferred_element_type=jnp.float32)
    half = g_one.shape[0] // 2
    grads = jnp.stack([g_one, g_two], 0).astype(jnp.bfloat16)
    summed = grads[:, :half].astype(jnp.float32) + swap_cores(grads[:, half:]).astype(jnp.float32)
    summed = summed.astype(jnp.bfloat16).reshape(2, 2 * n_blocks, -1, model_width)
    g_one, g_two = return_experts([summed[:, i] for i in range(2 * n_blocks)], n_blocks)
    d_gate_one = kept_one * jnp.take(back_gate, jnp.maximum(slot_one, 0), axis=0)
    d_gate_two = kept_two * jnp.take(back_gate, jnp.maximum(slot_two, 0), axis=0)
    d_a_two = lax.dot_general(
        match, d_back, (((0,), (0,)), ((), ())), preferred_element_type=jnp.float32
    )
    d_probs = (
        hot_one * d_gate_one[:, None]
        + hot_two * d_gate_two[:, None]
        + valid_flat[:, None] * d_imp[None, :]
    )
    d_router = (
        router_probs * (d_probs - jnp.sum(router_probs * d_probs, 1, keepdims=True))
    ).astype(jnp.bfloat16)
    g_router = jnp.dot(a_two.T, d_router, preferred_element_type=jnp.float32)
    d_a_two = d_a_two + jnp.dot(d_router, router_b.T, preferred_element_type=jnp.float32)
    unused_out, norm_back = jax.vjp(layer_norm, x_one, gain_rows[1], gain_rows[4])
    d_x_one, g_gain_two, g_shift_two = norm_back(d_a_two)
    d_x_one = d_x_one + d_two
    d_att_b = d_x_one.astype(jnp.bfloat16)
    g_out_proj = jnp.dot(att_out.T, d_att_b, preferred_element_type=jnp.float32)
    d_att_out = jnp.dot(d_att_b, layer_b[4].T, preferred_element_type=jnp.float32).astype(
        jnp.bfloat16
    )
    d_qkv = attention_backward(proj_qkv, allowed, log_total, d_att_out, HEADS)
    g_qkv = jnp.einsum("td,kte->kde", a_one, d_qkv, preferred_element_type=jnp.float32)
    d_a_one = jnp.einsum("kte,kde->td", d_qkv, layer_b[1:4], preferred_element_type=jnp.float32)
    unused_out, norm_back = jax.vjp(layer_norm, x_zero, gain_rows[0], gain_rows[3])
    d_x_zero, g_gain_one, g_shift_one = norm_back(d_a_one)
    d_x_zero = (d_x_zero + d_x_one).astype(jnp.bfloat16)
    g_embed = jnp.dot(patches.T, d_x_zero, preferred_element_type=jnp.float32)
    g_layers = jnp.concatenate([g_embed[None], g_qkv, g_out_proj[None]], 0)
    zero = jnp.zeros_like(g_gain_one)
    g_norms = g_norm_three[:6] + jnp.stack(
        [g_gain_one, g_gain_two, zero, g_shift_one, g_shift_two, zero]
    )
    def spread_rows(value):
        value = value.reshape(value.shape[0], QUAD, n_blocks, sizes["x"], 2, rows_own, -1)
        return value.transpose(4, 1, 3, 2, 0, 5, 6)

    blocks = spread_rows(g_layers.astype(jnp.bfloat16))
    blocks = blocks.reshape(*blocks.shape[:4], -1, model_width)
    small = jnp.concatenate([g_norms, g_router.T], 0).astype(jnp.bfloat16)
    small = spread_rows(small[..., None])[..., 0]
    n_dense, n_small = blocks.shape[4], small.shape[4]
    depth = round_up(n_dense + n_small, 16)
    small = jnp.pad(small, ((0, 0),) * 4 + ((0, depth - n_dense - n_small), (0, model_width - rows_own)))
    reduced = scatter_dense(sizes, jnp.concatenate([blocks, small], 4))
    g_layers = reduced[:n_dense].reshape(-1, rows_own, model_width)
    g_norms = reduced[n_dense : n_dense + 6, :rows_own]
    g_router = reduced[n_dense + 6 : n_dense + n_small, :rows_own].T
    squares = (
        jnp.sum(g_layers * g_layers) + jnp.sum(g_router * g_router) + jnp.sum(g_norms * g_norms)
    )
    squares = squares + jnp.sum(g_one * g_one) + jnp.sum(g_two * g_two) + jnp.sum(g_head * g_head)
    line = lax.broadcasted_iota(jnp.int32, (8, 128), 0)
    all_sums = share_sums(sizes, jnp.where(line == 0, local_loss, squares))
    loss_sum, square_sum = all_sums[0, 0], all_sums[1, 0]
    grad_norm = jnp.sqrt(square_sum)
    factor = jnp.minimum(1.0, clip_limit / grad_norm)
    loss_value = loss_sum + aux_weight * spread / (centre * centre)
    dense_out = adam_update(
        dense_weights, dense_first, dense_second, dense_average, g_layers, factor, base_rate
    )
    router_out = adam_update(
        router_weights, router_first, router_second, router_average, g_router, factor, base_rate
    )
    norm_out = adam_update(
        norm_params, norm_first, norm_second, norm_average, g_norms, factor, norm_rate
    )
    in_out = adam_update(expert_in, in_first, in_second, in_average, g_one, factor, base_rate)
    out_out = adam_update(expert_out, out_first, out_second, out_average, g_two, factor, base_rate)
    head_out = adam_update(
        head_weights, head_first, head_second, head_average, g_head, factor, base_rate
    )
    return (
        loss_value,
        importance,
        grad_norm,
        *dense_out,
        *router_out,
        *norm_out,
        *in_out,
        *out_out,
        *head_out,
    )


def solution(mesh):
    n_dp, n_expert = mesh.shape["dp"], mesh.shape["expert"]
    shaped = mesh.devices.reshape(n_dp // QUAD, QUAD, n_expert // 2, 2)
    fine = Mesh(shaped, ALL)
    rows = P(ALL, None)
    dense = P(None, ALL, None)
    norms = P(None, ALL)
    experts = P(("x", "c"), ("g", "r"), None)
    placed = (rows,) * 6 + (dense,) * 4 + (rows,) * 4 + (norms,) * 4 + (experts,) * 8 + (rows,) * 4
    results = (
        (P(),) * 3 + (dense,) * 4 + (rows,) * 4 + (norms,) * 4 + (experts,) * 8 + (rows,) * 4
    )
    return jax.shard_map(body, mesh=fine, in_specs=placed, out_specs=results, check_vma=False)
```

```python
import functools
import math

import jax
import jax.numpy as jnp
from jax import lax
from jax.experimental import pallas as pl
from jax.experimental.pallas import tpu as pltpu
from jax.sharding import Mesh
from jax.sharding import PartitionSpec as P

HEADS = 12
TOP = 2
STEP_COUNT = 10
QUAD = 4

high_prec = lax.Precision.HIGHEST
eps_norm = 1e-06
aux_weight = 0.01
clip_limit = 1.0
base_rate = 0.05
norm_rate = 0.5
beta_first = 0.9
beta_second = 0.999
weight_decay = 0.1
polyak_decay = 0.7
adam_eps = 1e-08
mask_fill = -1e30

ALL = ("g", "r", "x", "c")
MEMBERS = ("x", "r")


def adam_update(weight, first_state, second_state, average_state, gradient, factor, step_rate):
    clipped = gradient * factor
    first_new = beta_first * first_state + (1.0 - beta_first) * clipped
    second_new = beta_second * second_state + (1.0 - beta_second) * clipped * clipped
    first_hat = first_new / (1.0 - beta_first**STEP_COUNT)
    second_hat = second_new / (1.0 - beta_second**STEP_COUNT)
    weight_new = weight - step_rate * (
        first_hat / (jnp.sqrt(second_hat) + adam_eps) + weight_decay * weight
    )
    average_new = polyak_decay * average_state + (1.0 - polyak_decay) * weight_new
    return (weight_new, first_new, second_new, average_new)


MESH_ID = pl.DeviceIdType.MESH
VMEM = pltpu.VMEM
ANY = pl.ANY
MIB = 1 << 20


def cost(microseconds):
    return pl.CostEstimate(flops=int(microseconds * 1.15e9), bytes_accessed=0, transcendentals=0)


def whole(space=None):
    return pl.BlockSpec(memory_space=space or VMEM)


def round_up(value, step):
    return (value + step - 1) // step * step


class Place:
    def __init__(self, sizes):
        self.G, self.X = sizes["g"], sizes["x"]
        self.Z, self.Y = QUAD, sizes["g"]
        self.chips = self.Z * self.Y * self.X
        spot = lax.axis_index("g") * QUAD + lax.axis_index("r")
        self.z, self.y = lax.div(spot, self.Y), lax.rem(spot, self.Y)
        self.x, self.c = lax.axis_index("x"), lax.axis_index("c")
        self.g, self.r = lax.axis_index("g"), lax.axis_index("r")
        self.chip = spot * self.X + self.x
        self.member = self.x * QUAD + self.r

    def at(self, z=None, y=None, x=None, c=None):
        spot = (self.z if z is None else z) * self.Y + (self.y if y is None else y)
        return {
            "g": lax.div(spot, QUAD),
            "r": lax.rem(spot, QUAD),
            "x": self.x if x is None else x,
            "c": self.c if c is None else c,
        }

    def of_chip(self, chip):
        spot = lax.div(chip, self.X)
        return {
            "g": lax.div(spot, QUAD),
            "r": lax.rem(spot, QUAD),
            "x": lax.rem(chip, self.X),
            "c": self.c,
        }

    def of_member(self, member):
        return {
            "g": self.g,
            "r": lax.rem(member, QUAD),
            "x": lax.div(member, QUAD),
            "c": self.c,
        }

    def sibling(self):
        return self.at(c=1 - self.c)


def greet(peers):
    barrier = pltpu.get_barrier_semaphore()
    for peer in peers:
        pl.semaphore_signal(barrier, inc=1, device_id=peer, device_id_type=MESH_ID)
    pl.semaphore_wait(barrier, len(peers))


def send(src, dst, send_sem, recv_sem, peer):
    return pltpu.make_async_remote_copy(
        src_ref=src,
        dst_ref=dst,
        send_sem=send_sem,
        recv_sem=recv_sem,
        device_id=peer,
        device_id_type=MESH_ID,
    )


def others(me, count):
    return [lax.rem(me + step, count) for step in range(1, count)]


def grid_peers(at):
    peers = [at.at(z=z) for z in others(at.z, at.Z)]
    peers += [at.at(y=y) for y in others(at.y, at.Y)]
    peers += [at.at(x=x) for x in others(at.x, at.X)]
    return peers + [at.sibling()]


def gather_kernel(
    sizes, rows, mats, routing, dense_ref, tail_ref, pick_ref, rank_ref, mask_ref, length_ref,
    w_ref, gain_ref, router_ref, col_ref, land, *sems
):
    at = Place(sizes)
    Z, Y, X = at.Z, at.Y, at.X
    depth = land.shape[4]
    cut = depth // 2 // 16 * 16
    first, second = pl.ds(0, cut), pl.ds(cut, depth - cut)
    z_out, z_in, ya_out, ya_in, xb_out, xb_in, xa_out, xa_in, yb_out, yb_in, c_out, c_in = sems
    block = jnp.concatenate([dense_ref[...].reshape(mats * rows, -1), tail_ref[...]], 0)
    if block.shape[0] < depth:
        block = jnp.pad(block, ((0, depth - block.shape[0]), (0, 0)))
    mine = land.at[at.c, at.z, at.x, at.y]
    mine[...] = block.astype(jnp.bfloat16)
    greet(grid_peers(at))
    started = []

    def begin(copy):
        copy.start()
        started.append(copy)

    order = [at.z] + [lax.rem(at.z + k, Z) for k in (1, 3, 2)]
    for z in order[1:]:
        begin(send(mine, mine, z_out.at[z], z_in.at[at.z], at.at(z=z)))

    def one(z):
        part = land.at[at.c, z, at.x, at.y]
        for y in others(at.y, Y):
            begin(send(part.at[first], part.at[first], ya_out.at[z, y], ya_in.at[z, at.y], at.at(y=y)))
        for x in others(at.x, X):
            begin(send(part.at[second], part.at[second], xb_out.at[z, x], xb_in.at[z, at.x], at.at(x=x)))

    def two(z):
        for y in others(at.y, Y):
            part = land.at[at.c, z, at.x, y, first]
            send(part, part, ya_out.at[z, y], ya_in.at[z, y], at.at(y=y)).wait_recv()
        line = land.at[at.c, z, at.x, :, first]
        for x in others(at.x, X):
            begin(send(line, line, xa_out.at[z, x], xa_in.at[z, at.x], at.at(x=x)))
        for x in others(at.x, X):
            part = land.at[at.c, z, x, at.y, second]
            send(part, part, xb_out.at[z, x], xb_in.at[z, x], at.at(x=x)).wait_recv()
        line = land.at[at.c, z, :, at.y, second]
        for y in others(at.y, Y):
            begin(send(line, line, yb_out.at[z, y], yb_in.at[z, at.y], at.at(y=y)))

    def three(z):
        for x in others(at.x, X):
            line = land.at[at.c, z, x, :, first]
            send(line, line, xa_out.at[z, x], xa_in.at[z, x], at.at(x=x)).wait_recv()
        for y in others(at.y, Y):
            line = land.at[at.c, z, :, y, second]
            send(line, line, yb_out.at[z, y], yb_in.at[z, y], at.at(y=y)).wait_recv()
        plane = land.at[at.c, z]
        begin(send(plane, plane, c_out.at[z], c_in.at[z], at.sibling()))

    for step in range(Z + 2):
        if step < Z:
            if step > 0:
                z = order[step]
                part = land.at[at.c, z, at.x, at.y]
                send(part, part, z_out.at[z], z_in.at[z], at.at(z=z)).wait_recv()
            one(order[step])
        if step == 0:
            col_ref[...] = route_math(*routing, pick_ref, rank_ref, mask_ref, length_ref)
        if 0 <= step - 1 < Z:
            two(order[step - 1])
        if 0 <= step - 2 < Z:
            three(order[step - 2])
    for z in order:
        plane = land.at[1 - at.c, z]
        send(plane, plane, c_out.at[z], c_in.at[z], at.sibling()).wait_recv()
    for copy in started:
        copy.wait_send()
    chips = [(z, y, x) for z in range(Z) for y in range(Y) for x in range(X)]
    cores = [(c, z, x, y) for z, y, x in chips for c in range(2)]
    group = 16 // math.gcd(16, rows)
    for start in range(0, len(cores), group):
        for mat in range(mats):
            w_ref[mat, start * rows : (start + group) * rows] = jnp.concatenate(
                [land[spot][mat * rows : (mat + 1) * rows] for spot in cores[start : start + group]], 0
            )
    base, count = mats * rows, tail_ref.shape[0]
    tails = [land[spot][base : base + count].astype(jnp.float32) for spot in cores]
    gain_ref[...] = jnp.concatenate([tail[:8, :rows] for tail in tails], 1)
    router_ref[...] = jnp.concatenate([tail[:, 128 : 128 + rows] for tail in tails], 1)


def gather_weights(sizes, routing, dense, tail, picks, ranks, slot_mask, lengths):
    mats, rows, width = dense.shape
    count = tail.shape[0]
    depth = round_up(mats * rows + count, 16)
    Z, Y, X = QUAD, sizes["g"], sizes["x"]
    dma = pltpu.SemaphoreType.DMA
    by_y, by_x = dma((Z, Y)), dma((Z, X))
    return pl.pallas_call(
        functools.partial(gather_kernel, sizes, rows, mats, routing),
        out_shape=(
            jax.ShapeDtypeStruct((mats, width, width), jnp.bfloat16),
            jax.ShapeDtypeStruct((8, width), jnp.float32),
            jax.ShapeDtypeStruct((count, width), jnp.float32),
            jax.ShapeDtypeStruct((picks.shape[0], 128), jnp.float32),
        ),
        in_specs=[whole()] * 6,
        out_specs=(whole(),) * 4,
        scratch_shapes=[VMEM((2, Z, X, Y, depth, width), jnp.bfloat16), dma((Z,)), dma((Z,))]
        + [by_y, by_y, by_x, by_x, by_x, by_x, by_y, by_y, dma((Z,)), dma((Z,))],
        compiler_params=pltpu.CompilerParams(
            collective_id=1, has_side_effects=True, vmem_limit_bytes=48 * MIB
        ),
        cost_estimate=cost(44),
        name="gather_weights",
    )(dense, tail, picks, ranks, slot_mask, lengths)


def scatter_kernel(sizes, g_ref, out_ref, hold, sib, got_xa, got_yb, got_ya, got_xb, got_z, *sems):
    at = Place(sizes)
    Z, Y, X = at.Z, at.Y, at.X
    depth = g_ref.shape[4]
    cut = depth // 2 // 16 * 16
    first, second = pl.ds(0, cut), pl.ds(cut, depth - cut)
    c_out, c_in, xa_out, xa_in, yb_out, yb_in, ya_out, ya_in, xb_out, xb_in, z_out, z_in = sems
    greet(grid_peers(at))
    started = []

    def begin(copy):
        copy.start()
        started.append(copy)

    wide = lambda value: value.astype(jnp.float32)
    order = [lax.rem(at.z + k, Z) for k in (2, 1, 3)] + [at.z]
    for z in order:
        begin(send(g_ref.at[1 - at.c, z], sib.at[z], c_out.at[z], c_in.at[z], at.sibling()))

    def one(z):
        send(sib.at[z], sib.at[z], c_out.at[z], c_in.at[z], at.sibling()).wait_recv()
        hold[z] = (wide(g_ref[at.c, z]) + wide(sib[z])).astype(jnp.bfloat16)
        for x in others(at.x, X):
            begin(send(hold.at[z, x, :, first], got_xa.at[z, at.x], xa_out.at[z, x], xa_in.at[z, at.x], at.at(x=x)))
        for y in others(at.y, Y):
            begin(send(hold.at[z, :, y, second], got_yb.at[z, at.y], yb_out.at[z, y], yb_in.at[z, at.y], at.at(y=y)))

    def two(z):
        total = wide(hold[z, at.x, :, first])
        for x in others(at.x, X):
            send(got_xa.at[z, x], got_xa.at[z, x], xa_out.at[z, x], xa_in.at[z, x], at.at(x=x)).wait_recv()
            total = total + wide(got_xa[z, x])
        hold[z, at.x, :, first] = total.astype(jnp.bfloat16)
        for y in others(at.y, Y):
            begin(send(hold.at[z, at.x, y, first], got_ya.at[z, at.y], ya_out.at[z, y], ya_in.at[z, at.y], at.at(y=y)))
        total = wide(hold[z, :, at.y, second])
        for y in others(at.y, Y):
            send(got_yb.at[z, y], got_yb.at[z, y], yb_out.at[z, y], yb_in.at[z, y], at.at(y=y)).wait_recv()
            total = total + wide(got_yb[z, y])
        hold[z, :, at.y, second] = total.astype(jnp.bfloat16)
        for x in others(at.x, X):
            begin(send(hold.at[z, x, at.y, second], got_xb.at[z, at.x], xb_out.at[z, x], xb_in.at[z, at.x], at.at(x=x)))

    def three(z, last):
        total = wide(hold[z, at.x, at.y, first])
        for y in others(at.y, Y):
            send(got_ya.at[z, y], got_ya.at[z, y], ya_out.at[z, y], ya_in.at[z, y], at.at(y=y)).wait_recv()
            total = total + wide(got_ya[z, y])
        rest = wide(hold[z, at.x, at.y, second])
        for x in others(at.x, X):
            send(got_xb.at[z, x], got_xb.at[z, x], xb_out.at[z, x], xb_in.at[z, x], at.at(x=x)).wait_recv()
            rest = rest + wide(got_xb[z, x])
        if last:
            out_ref[first] = total
            out_ref[second] = rest
            return
        mine = hold.at[z, at.x, at.y]
        mine[first] = total.astype(jnp.bfloat16)
        mine[second] = rest.astype(jnp.bfloat16)
        begin(send(mine, got_z.at[at.z], z_out.at[z], z_in.at[at.z], at.at(z=z)))

    for step in range(Z + 2):
        if step < Z:
            one(order[step])
        if 0 <= step - 1 < Z:
            two(order[step - 1])
        if 0 <= step - 2 < Z:
            three(order[step - 2], step - 2 == Z - 1)
    for z in order[:-1]:
        send(got_z.at[z], got_z.at[z], z_out.at[z], z_in.at[z], at.at(z=z)).wait_recv()
        out_ref[...] += wide(got_z[z])
    for copy in started:
        copy.wait_send()


def scatter_dense(sizes, blocks):
    unused, Z, X, Y, depth, width = blocks.shape
    dma = pltpu.SemaphoreType.DMA
    by_y, by_x, by_z = dma((Z, Y)), dma((Z, X)), dma((Z,))
    cut = depth // 2 // 16 * 16
    half = jnp.bfloat16
    return pl.pallas_call(
        functools.partial(scatter_kernel, sizes),
        out_shape=jax.ShapeDtypeStruct((depth, width), jnp.float32),
        in_specs=[whole()],
        out_specs=whole(),
        scratch_shapes=[
            VMEM((Z, X, Y, depth, width), half),
            VMEM((Z, X, Y, depth, width), half),
            VMEM((Z, X, Y, cut, width), half),
            VMEM((Z, Y, X, depth - cut, width), half),
            VMEM((Z, Y, cut, width), half),
            VMEM((Z, X, depth - cut, width), half),
            VMEM((Z, depth, width), half),
        ]
        + [by_z, by_z, by_x, by_x, by_y, by_y, by_y, by_y, by_x, by_x, by_z, by_z],
        compiler_params=pltpu.CompilerParams(
            collective_id=2, has_side_effects=True, vmem_limit_bytes=48 * MIB
        ),
        cost_estimate=cost(45),
        name="scatter_dense",
    )(blocks)


def sums_kernel(sizes, in_ref, out_ref, land, out_sem, in_sem):
    at = Place(sizes)
    count = 2 * at.chips
    me = at.chip * 2 + at.c
    ids = others(me, count)

    def peer(device):
        spot = at.of_chip(lax.div(device, 2))
        spot["c"] = lax.rem(device, 2)
        return spot

    greet([peer(device) for device in ids])
    land[me] = in_ref[...]
    copies = [send(in_ref, land.at[me], out_sem.at[d], in_sem.at[me], peer(d)) for d in ids]
    for copy in copies:
        copy.start()
    for d in ids:
        send(land.at[d], land.at[d], out_sem.at[d], in_sem.at[d], peer(d)).wait_recv()
    out_ref[...] = jnp.sum(land[...], 0)
    for copy in copies:
        copy.wait_send()


def share_sums(sizes, values):
    count = sizes["g"] * QUAD * sizes["x"] * 2
    dma = pltpu.SemaphoreType.DMA
    return pl.pallas_call(
        functools.partial(sums_kernel, sizes),
        out_shape=jax.ShapeDtypeStruct(values.shape, jnp.float32),
        in_specs=[whole()],
        out_specs=whole(),
        scratch_shapes=[VMEM((count, *values.shape), jnp.float32), dma((count,)), dma((count,))],
        compiler_params=pltpu.CompilerParams(collective_id=3, has_side_effects=True),
        cost_estimate=cost(10),
        name="share_sums",
    )(values)


IMAGE_PAD = 16


def split_three(value):
    high = value.astype(jnp.bfloat16)
    rest = value - high.astype(jnp.float32)
    middle = rest.astype(jnp.bfloat16)
    return high, middle, (rest - middle.astype(jnp.float32)).astype(jnp.bfloat16)


def dot_f32(left, right, dims):
    return lax.dot_general(left, right, (dims, ((), ())), preferred_element_type=jnp.float32)


NN = ((1,), (0,))
NT = ((1,), (1,))
TN = ((0,), (0,))


def norm_parts(values):
    centre = values - jnp.mean(values, -1, keepdims=True)
    spread = jnp.mean(centre * centre, -1, keepdims=True)
    scale = lax.rsqrt(spread + eps_norm)
    return centre * scale, scale


def norm_back(d_out, scaled, scale, gain):
    pulled = d_out * gain
    return scale * (
        pulled
        - jnp.mean(pulled, -1, keepdims=True)
        - scaled * jnp.mean(pulled * scaled, -1, keepdims=True)
    )


def head_kernel(
    sizes, images, part_ref, own_ref, imp_ref, gain_ref, head_ref, label_ref,
    g_head_ref, d_pool_ref, own_d_ref, g_norm_ref, sums_ref, total_imp_ref,
    in_part, rows, d_rows, d_sib, d_sum, d_in, head_b, labels, d_logits, *sems
):
    at = Place(sizes)
    chips, members = at.chips, QUAD * at.X
    devices = 2 * chips
    p_out, p_in, r_out, r_in, s_out, s_in, d_out, d_in_sem, b_out, b_in = sems
    width = own_ref.shape[1]
    same_core = others(at.chip, chips)
    greet([at.of_chip(chip) for chip in same_core] + [at.sibling()])
    started = []

    def begin(copy):
        copy.start()
        started.append(copy)

    team = others(at.member, members)
    for member in team:
        begin(send(part_ref.at[member], in_part.at[at.member], p_out.at[member], p_in.at[at.member], at.of_member(member)))
    in_part[at.member] = part_ref[at.member]
    head_b[...] = head_ref[...].astype(jnp.bfloat16)
    wide = devices * IMAGE_PAD
    spot = lax.broadcasted_iota(jnp.int32, (label_ref.shape[1], wide), 1)
    given = lax.broadcasted_iota(jnp.int32, (label_ref.shape[1], wide), 0)
    image = lax.rem(spot, IMAGE_PAD)
    device = lax.rem(lax.div(spot, IMAGE_PAD), chips) * 2 + lax.div(spot, IMAGE_PAD * chips)
    chosen = ((device * images + image == given) & (image < images)).astype(jnp.bfloat16)
    labels[...] = dot_f32(label_ref[...].astype(jnp.float32).astype(jnp.bfloat16), chosen, NN).astype(jnp.bfloat16)
    for member in team:
        send(in_part.at[member], in_part.at[member], p_out.at[member], p_in.at[member], at.of_member(member)).wait_recv()
    pooled = own_ref[...] + jnp.sum(in_part[...], 0)
    scaled, scale = norm_parts(pooled)
    gain, shift = gain_ref[2:3], gain_ref[5:6]
    a_three = scaled * gain + shift
    row = lax.broadcasted_iota(jnp.int32, (IMAGE_PAD, width), 0)
    block = jnp.where(row < images, a_three, 0.0)
    pieces = split_three(imp_ref[0:1])
    for index, piece in enumerate(pieces):
        block = jnp.where(row == images + index, piece.astype(jnp.float32), block)
    rows[at.c, at.chip] = block.astype(jnp.bfloat16)
    mine = rows.at[at.c, at.chip]
    for chip in same_core:
        begin(send(mine, mine, r_out.at[chip], r_in.at[at.chip], at.of_chip(chip)))
    for chip in same_core:
        part = rows.at[at.c, chip]
        send(part, part, r_out.at[chip], r_in.at[chip], at.of_chip(chip)).wait_recv()
    begin(send(rows.at[at.c], rows.at[at.c], s_out.at[0], s_in.at[0], at.sibling()))
    send(rows.at[1 - at.c], rows.at[1 - at.c], s_out.at[0], s_in.at[0], at.sibling()).wait_recv()
    gathered = rows[...].reshape(wide, width)
    in_block = lax.rem(lax.broadcasted_iota(jnp.int32, (wide, width), 0), IMAGE_PAD)
    total = jnp.sum(jnp.where(in_block >= images, gathered.astype(jnp.float32), 0.0), 0, keepdims=True)
    total_imp_ref[...] = jnp.broadcast_to(total, total_imp_ref.shape)
    gathered = jnp.where(in_block < images, gathered.astype(jnp.float32), 0.0).astype(jnp.bfloat16)
    logits = dot_f32(head_b[...], gathered, NT)
    image = lax.rem(lax.broadcasted_iota(jnp.int32, logits.shape, 1), IMAGE_PAD)
    count = devices * images
    target = labels[...].astype(jnp.float32)
    power = jnp.exp(-jnp.abs(logits))
    loss = jnp.maximum(logits, 0.0) + jnp.log1p(power) - target * logits
    loss = jnp.sum(jnp.where(image < images, loss, 0.0), 1, keepdims=True)
    loss = jnp.sum(loss, 0, keepdims=True) / count
    sums_ref[...] = jnp.broadcast_to(loss, sums_ref.shape)
    chance = jnp.where(logits >= 0.0, 1.0, power) / (1.0 + power)
    d_logits[...] = jnp.where(image < images, (chance - target) / count, 0.0).astype(jnp.bfloat16)
    partial = dot_f32(d_logits[...], head_b[...], TN)
    d_rows[...] = partial.reshape(d_rows.shape).astype(jnp.bfloat16)
    begin(send(d_rows.at[1 - at.c], d_sib, s_out.at[1], s_in.at[1], at.sibling()))
    g_head_ref[...] = dot_f32(d_logits[...], gathered, NN)
    send(d_sib, d_sib, s_out.at[1], s_in.at[1], at.sibling()).wait_recv()
    d_sum[...] = (d_rows[at.c].astype(jnp.float32) + d_sib[...].astype(jnp.float32)).astype(jnp.bfloat16)
    for chip in same_core:
        begin(send(d_sum.at[chip], d_in.at[at.chip], d_out.at[chip], d_in_sem.at[at.chip], at.of_chip(chip)))
    d_in[at.chip] = d_sum[at.chip]
    for chip in same_core:
        send(d_in.at[chip], d_in.at[chip], d_out.at[chip], d_in_sem.at[chip], at.of_chip(chip)).wait_recv()
    d_norm = jnp.sum(d_in[...].astype(jnp.float32), 0)
    d_norm = jnp.where(row < images, d_norm, 0.0)
    d_pooled = norm_back(d_norm, scaled, scale, gain)
    d_pooled = jnp.where(row < images, d_pooled, 0.0)
    d_gain = jnp.sum(d_norm * scaled, 0, keepdims=True)
    d_shift = jnp.sum(d_norm, 0, keepdims=True)
    line = lax.broadcasted_iota(jnp.int32, g_norm_ref.shape, 0)
    g_norm_ref[...] = jnp.where(line == 2, d_gain, jnp.where(line == 5, d_shift, 0.0))
    own_d_ref[...] = d_pooled
    d_pool_ref[at.member] = d_pooled
    mine = d_pool_ref.at[at.member]
    for member in team:
        begin(send(own_d_ref, mine, b_out.at[member], b_in.at[at.member], at.of_member(member)))
    for member in team:
        part = d_pool_ref.at[member]
        send(part, part, b_out.at[member], b_in.at[member], at.of_member(member)).wait_recv()
    for copy in started:
        copy.wait_send()


def head_step(sizes, images, part, own, imp, gains, head, label):
    members = QUAD * sizes["x"]
    chips = members * sizes["g"]
    classes, width = head.shape
    wide = 2 * chips * IMAGE_PAD
    dma = pltpu.SemaphoreType.DMA
    by_member, by_chip = dma((members,)), dma((chips,))
    f32, half = jnp.float32, jnp.bfloat16
    blocks = (chips, IMAGE_PAD, width)
    return pl.pallas_call(
        functools.partial(head_kernel, sizes, images),
        out_shape=(
            jax.ShapeDtypeStruct((classes, width), f32),
            jax.ShapeDtypeStruct((members, IMAGE_PAD, width), f32),
            jax.ShapeDtypeStruct((IMAGE_PAD, width), f32),
            jax.ShapeDtypeStruct((8, width), f32),
            jax.ShapeDtypeStruct((8, 128), f32),
            jax.ShapeDtypeStruct((8, width), f32),
        ),
        in_specs=[whole()] * 6,
        out_specs=(whole(),) * 6,
        scratch_shapes=[
            VMEM((members, IMAGE_PAD, width), f32),
            VMEM((2, *blocks), half),
            VMEM((2, *blocks), half),
            VMEM(blocks, half),
            VMEM(blocks, half),
            VMEM(blocks, half),
            VMEM((classes, width), half),
            VMEM((classes, wide), half),
            VMEM((classes, wide), half),
        ]
        + [by_member, by_member, by_chip, by_chip, dma((2,)), dma((2,)), by_chip, by_chip]
        + [by_member, by_member],
        compiler_params=pltpu.CompilerParams(
            collective_id=4, has_side_effects=True, vmem_limit_bytes=56 * MIB
        ),
        cost_estimate=cost(42),
        name="head_step",
    )(part, own, imp, gains, head, label)


def route_math(per_image, n_experts, capacity, padded, pick_ref, rank_ref, mask_ref, length_ref):
    rows_here, span = mask_ref.shape
    tokens = rows_here * span
    valid = mask_ref[...].astype(jnp.float32)
    lengths = length_ref[...]
    position = lax.broadcasted_iota(jnp.int32, (rows_here, span), 1)
    segment = jnp.zeros((rows_here, span), jnp.int32)
    bound = jnp.zeros((rows_here, 1), jnp.int32)
    for image in range(per_image):
        bound = bound + lengths[:, image : image + 1]
        segment = segment + jnp.where(position >= bound, 1, 0)
    pool = jnp.zeros_like(valid)
    for image in range(per_image):
        member = jnp.where(segment == image, valid, 0.0)
        pool = pool + member / jnp.maximum(jnp.sum(member, 1, keepdims=True), 1.0)
    line = lax.broadcasted_iota(jnp.int32, (rows_here, span), 0)
    image = (segment + per_image * line).astype(jnp.float32)

    def flat(value):
        return jnp.concatenate([value[i : i + 1] for i in range(rows_here)], 1)

    rank_row = rank_ref[...].astype(jnp.float32)
    table = jnp.concatenate([flat(valid), flat(pool), flat(image), rank_row], 0)
    table = jnp.concatenate([table, jnp.zeros((124, tokens), jnp.float32)], 0).T
    valid_col, pool_col, image_col, rank_col = (table[:, i : i + 1] for i in range(4))
    picks = pick_ref[...]
    pick_one, pick_two = picks[:, 0:1], picks[:, 1:2]
    lane = lax.broadcasted_iota(jnp.int32, (tokens, 128), 1)
    in_first, in_second = lane < n_experts, (lane >= n_experts) & (lane < 2 * n_experts)
    hot = jnp.where(in_first & (pick_one == lane), valid_col, 0.0)
    hot = hot + jnp.where(in_second & (pick_two == lane - n_experts), valid_col, 0.0)
    shifted = jnp.where(in_second & (pick_one == lane - n_experts), valid_col, 0.0)
    before = jnp.where(rank_row < rank_col, 1.0, 0.0).astype(jnp.bfloat16)
    ahead = dot_f32(before, hot.astype(jnp.bfloat16), NN) + jnp.sum(shifted, 0, keepdims=True)
    counted = hot * ahead
    pos_one = jnp.sum(jnp.where(in_first, counted, 0.0), 1, keepdims=True)
    pos_two = jnp.sum(jnp.where(in_second, counted, 0.0), 1, keepdims=True)

    def place(pick, pos):
        kept = (valid_col > 0.0) & (pos < capacity)
        return jnp.where(kept, pick.astype(jnp.float32) * padded + pos, -1.0)

    columns = (
        place(pick_one, pos_one),
        place(pick_two, pos_two),
        valid_col,
        pool_col,
        image_col,
        pick_one.astype(jnp.float32),
        pick_two.astype(jnp.float32),
    )
    result = jnp.zeros((tokens, 128), jnp.float32)
    for index, column in enumerate(columns):
        result = jnp.where(lane == index, column, result)
    return result


def lane_mask(shape, left):
    lane = lax.broadcasted_iota(jnp.int32, shape, 1)
    return lane < 64 if left else lane >= 64


def allowed_slots(lengths, row, images, valid_row, span):
    query = lax.broadcasted_iota(jnp.int32, (span, span), 0)
    key = lax.broadcasted_iota(jnp.int32, (span, span), 1)
    bound = 0
    query_seg, key_seg = jnp.zeros((span, span), jnp.int32), jnp.zeros((span, span), jnp.int32)
    for image in range(images):
        bound = bound + lengths[row, image]
        query_seg = query_seg + jnp.where(query >= bound, 1, 0)
        key_seg = key_seg + jnp.where(key >= bound, 1, 0)
    return (query_seg == key_seg) & ((valid_row > 0) | (query == key))


def dense_forward_kernel(
    n_experts, images, length_ref, mask_ref, patch_ref, w_ref, gain_ref, router_ref, col_ref,
    x_zero_ref, a_one_ref, qkv_ref, att_ref, x_one_ref, a_two_ref, prob_ref, lse_ref, pool_ref, imp_ref
):
    row = pl.program_id(0)
    span, width = patch_ref.shape
    x_zero = dot_f32(patch_ref[...], w_ref[0], NN)
    x_zero_ref[...] = x_zero
    a_one = (norm_parts(x_zero)[0] * gain_ref[0:1] + gain_ref[3:4]).astype(jnp.bfloat16)
    a_one_ref[...] = a_one
    for part in range(3):
        qkv_ref[:, part * width : (part + 1) * width] = dot_f32(a_one, w_ref[1 + part], NN).astype(
            jnp.bfloat16
        )
    open_to = allowed_slots(length_ref, row, images, mask_ref[0], span)
    lane = lax.broadcasted_iota(jnp.int32, (span, 128), 1)
    logs = jnp.zeros((span, 128), jnp.float32)
    for pair in range(width // 128):
        query, key, value = (
            qkv_ref[:, part * width + pair * 128 : part * width + (pair + 1) * 128]
            for part in range(3)
        )
        outs = []
        for side in range(2):
            held = jnp.where((lane < 64) == (side == 0), query, jnp.zeros_like(query))
            scores = jnp.where(open_to, dot_f32(held, key, NT) * 64**-0.5, mask_fill)
            top = jnp.max(scores, 1, keepdims=True)
            powers = jnp.exp(scores - top)
            total = jnp.sum(powers, 1, keepdims=True)
            probs = (powers * (1.0 / total)).astype(jnp.bfloat16)
            outs.append(dot_f32(probs, value, NN))
            logs = jnp.where(lane == 2 * pair + side, top + jnp.log(total), logs)
        att_ref[:, pair * 128 : (pair + 1) * 128] = jnp.where(lane < 64, outs[0], outs[1]).astype(
            jnp.bfloat16
        )
    lse_ref[...] = logs
    x_one = x_zero + dot_f32(att_ref[...], w_ref[4], NN)
    x_one_ref[...] = x_one
    a_two = (norm_parts(x_one)[0] * gain_ref[1:2] + gain_ref[4:5]).astype(jnp.bfloat16)
    a_two_ref[...] = a_two
    routers = router_ref[...].astype(jnp.bfloat16)
    if routers.shape[0] < 128:
        routers = jnp.concatenate(
            [routers, jnp.zeros((128 - routers.shape[0], width), jnp.bfloat16)], 0
        )
    logits = jnp.where(lane < n_experts, dot_f32(a_two, routers, NT), mask_fill)
    powers = jnp.exp(logits - jnp.max(logits, 1, keepdims=True))
    probs = powers / jnp.sum(powers, 1, keepdims=True)
    prob_ref[...] = probs

    @pl.when(row == 0)
    def _():
        pool_ref[...] = jnp.zeros_like(pool_ref)
        imp_ref[...] = jnp.zeros_like(imp_ref)

    valid, pool, image = col_ref[:, 2:3], col_ref[:, 3:4], col_ref[:, 4:5]
    imp_ref[0:1, 0:128] += jnp.sum(probs * valid, 0, keepdims=True)
    line = lax.broadcasted_iota(jnp.int32, pool_ref.shape, 0)
    for index in range(images):
        number = row * images + index
        weight = jnp.where(image == number.astype(jnp.float32), pool, 0.0)
        pooled = jnp.sum(x_one * weight, 0, keepdims=True)
        pool_ref[...] = jnp.where(line == number, pooled, pool_ref[...])


def dense_forward(n_experts, lengths, slot_mask, patches, weights, gains, routers, columns):
    rows_here, span = slot_mask.shape
    tokens, width = patches.shape
    f32, half = jnp.float32, jnp.bfloat16

    def block(wide):
        return pl.BlockSpec((span, wide), lambda i: (i, 0))

    def out(wide, kind):
        return jax.ShapeDtypeStruct((tokens, wide), kind)

    def fixed(shape):
        return pl.BlockSpec(shape, lambda i: (0, 0))

    return pl.pallas_call(
        functools.partial(dense_forward_kernel, n_experts, lengths.shape[1]),
        grid=(rows_here,),
        out_shape=(
            out(width, f32), out(width, half), out(3 * width, half), out(width, half),
            out(width, f32), out(width, half), out(128, f32), out(128, f32),
            jax.ShapeDtypeStruct((IMAGE_PAD, width), f32), jax.ShapeDtypeStruct((8, width), f32),
        ),
        in_specs=[
            whole(pltpu.SMEM), pl.BlockSpec((1, 1, span), lambda i: (i, 0, 0)), block(width),
            whole(), whole(), whole(), block(128),
        ],
        out_specs=(
            block(width), block(width), block(3 * width), block(width), block(width), block(width),
            block(128), block(128), fixed((IMAGE_PAD, width)), fixed((8, width)),
        ),
        compiler_params=pltpu.CompilerParams(vmem_limit_bytes=48 * MIB),
        cost_estimate=cost(25),
        name="dense_forward",
    )(lengths, slot_mask[:, None, :], patches, weights, gains, routers, columns)


def dispatch_kernel(
    sizes, n_experts, padded, a_two_ref, prob_ref, col_ref, rows_ref, detail_ref,
    send_rows, send_detail, places, own_sem, r_out, r_in, m_out, m_in
):
    at = Place(sizes)
    tokens = a_two_ref.shape[0]
    team = others(at.member, n_experts)
    greet([at.of_member(member) for member in team])
    columns = col_ref[...]
    places[...] = columns.T[:8]
    lane = lax.broadcasted_iota(jnp.int32, (tokens, 128), 1)
    kind, expert = lax.div(lane, n_experts), lax.rem(lane, n_experts).astype(jnp.float32)
    slot_lane = lax.broadcasted_iota(jnp.int32, (tokens, send_detail.shape[2]), 1).astype(jnp.float32)
    pool, image = columns[:, 3:4], columns[:, 4:5]
    details = None
    for choice in range(2):
        slot, pick = columns[:, choice : choice + 1], columns[:, 5 + choice : 6 + choice]
        hot = (expert == pick) & (slot >= 0.0)
        gate = jnp.sum(jnp.where(hot & (kind == 0), prob_ref[...], 0.0), 1, keepdims=True)
        values = jnp.zeros((tokens, 128), jnp.float32)
        pieces = [*split_three(gate), *split_three(pool), image]
        for index, piece in enumerate(pieces):
            values = jnp.where(kind == index, piece.astype(jnp.float32), values)
        values = jnp.where(hot, values, 0.0).astype(jnp.bfloat16)
        spot = jnp.where(slot >= 0.0, slot - pick * padded, -1.0)
        chosen = jnp.where(spot == slot_lane, 1.0, 0.0).astype(jnp.bfloat16)
        found = dot_f32(values, chosen, TN)
        details = found if details is None else details + found
    n = n_experts
    gates = details[0:n] + details[n : 2 * n] + details[2 * n : 3 * n]
    pools = details[3 * n : 4 * n] + details[4 * n : 5 * n] + details[5 * n : 6 * n]
    images = details[6 * n : 7 * n]
    for index in range(n):
        for spot, value in enumerate((gates, pools, images)):
            send_detail[index, spot : spot + 1] = value[index : index + 1]
        send_detail[index, 3:8] = jnp.zeros((5, send_detail.shape[2]), jnp.float32)

    def rows_of(member):
        slots = lax.broadcasted_iota(jnp.int32, (padded, tokens), 0) + member * padded
        slots = slots.astype(jnp.float32)
        match = (slots == places[0:1]) | (slots == places[1:2])
        match = jnp.where(match, 1.0, 0.0).astype(jnp.bfloat16)
        send_rows[member] = dot_f32(match, a_two_ref[...], NN).astype(jnp.bfloat16)

    def row_copy(member, source):
        return send(
            send_rows.at[member], rows_ref.at[source], r_out.at[member], r_in.at[source], at.of_member(member)
        )

    def detail_copy(member, source):
        return send(
            send_detail.at[member], detail_ref.at[source], m_out.at[member], m_in.at[source], at.of_member(member)
        )

    def step(index, carry):
        member = lax.rem(at.member + index, n_experts)
        rows_of(member)
        row_copy(member, at.member).start()
        detail_copy(member, at.member).start()
        return carry

    lax.fori_loop(1, n_experts, step, 0)
    rows_of(at.member)
    keep_rows = pltpu.make_async_copy(send_rows.at[at.member], rows_ref.at[at.member], own_sem.at[0])
    keep_detail = pltpu.make_async_copy(send_detail.at[at.member], detail_ref.at[at.member], own_sem.at[1])
    keep_rows.start()
    keep_detail.start()
    for member in team:
        row_copy(member, member).wait_recv()
        detail_copy(member, member).wait_recv()
    for member in team:
        row_copy(member, at.member).wait_send()
        detail_copy(member, at.member).wait_send()
    keep_rows.wait()
    keep_detail.wait()


def dispatch(sizes, n_experts, padded, a_two, probs, columns):
    tokens, width = a_two.shape
    lanes = round_up(padded, 128)
    dma = pltpu.SemaphoreType.DMA
    each = dma((n_experts,))
    return pl.pallas_call(
        functools.partial(dispatch_kernel, sizes, n_experts, padded),
        out_shape=(
            jax.ShapeDtypeStruct((n_experts, padded, width), jnp.bfloat16),
            jax.ShapeDtypeStruct((n_experts, 8, lanes), jnp.float32),
        ),
        in_specs=[whole()] * 3,
        out_specs=(whole(ANY), whole(ANY)),
        scratch_shapes=[
            VMEM((n_experts, padded, width), jnp.bfloat16),
            VMEM((n_experts, 8, lanes), jnp.float32),
            VMEM((8, tokens), jnp.float32),
            dma((2,)), each, each, each, each,
        ],
        compiler_params=pltpu.CompilerParams(
            collective_id=5, has_side_effects=True, vmem_limit_bytes=48 * MIB
        ),
        cost_estimate=cost(50),
        name="dispatch",
    )(a_two, probs, columns)


def image_hot(detail, padded):
    image = detail[2:3, :padded]
    line = lax.broadcasted_iota(jnp.int32, (IMAGE_PAD, padded), 0).astype(jnp.float32)
    return line == image


def expert_forward_kernel(
    padded, rows_ref, detail_ref, own_ref, other_ref, act_ref, slope_ref, y_ref, part_ref
):
    many, unused, width = rows_ref.shape
    rows = rows_ref[...].reshape(many * padded, width)
    chunks, unused, part = act_ref.shape
    half = chunks // 2
    total = None
    for index in range(chunks):
        ref, start = (own_ref, index * part) if index < half else (other_ref, (index - half) * part)
        hidden = dot_f32(rows, ref[0, start : start + part], NT)
        square = hidden * hidden
        curve = jnp.tanh(hidden * (0.7978845608 + 0.7978845608 * 0.044715 * square))
        upper = 0.5 + 0.5 * curve
        gelu = hidden * upper
        act = gelu.astype(jnp.bfloat16)
        slope = upper + gelu * (1.0 - upper) * (
            2.0 * 0.7978845608 + 6.0 * 0.7978845608 * 0.044715 * square
        )
        act_ref[index] = act
        slope_ref[index] = slope.astype(jnp.bfloat16)
        found = dot_f32(act, ref[1, start : start + part], NN)
        total = found if total is None else total + found
    result = total.astype(jnp.bfloat16)
    y_ref[...] = result.reshape(many, padded, width)
    for source in range(many):
        detail = detail_ref[source]
        weight = detail[0:1, :padded] * detail[1:2, :padded]
        weights = jnp.where(image_hot(detail, padded), weight, 0.0)
        pieces = jnp.concatenate(split_three(weights), 0)
        sums = dot_f32(pieces, result[source * padded : (source + 1) * padded], NN)
        part_ref[source] = (
            sums[:IMAGE_PAD] + sums[IMAGE_PAD : 2 * IMAGE_PAD] + sums[2 * IMAGE_PAD :]
        )


def expert_forward(rows, details, own_half, other_half, chunks):
    sources, padded, width = rows.shape
    part = 2 * own_half.shape[1] // chunks
    many = max(1, 576 // padded)
    lanes = details.shape[2]
    half = jnp.bfloat16

    def by_source(*shape):
        return pl.BlockSpec((many, *shape), lambda i: (i, 0, 0))

    flat = pl.BlockSpec((chunks, many * padded, part), lambda i: (0, i, 0))
    return pl.pallas_call(
        functools.partial(expert_forward_kernel, padded),
        grid=(sources // many,),
        out_shape=(
            jax.ShapeDtypeStruct((chunks, sources * padded, part), half),
            jax.ShapeDtypeStruct((chunks, sources * padded, part), half),
            jax.ShapeDtypeStruct((sources, padded, width), half),
            jax.ShapeDtypeStruct((sources, IMAGE_PAD, width), jnp.float32),
        ),
        in_specs=[by_source(padded, width), by_source(8, lanes), whole(), whole()],
        out_specs=(flat, flat, by_source(padded, width), by_source(IMAGE_PAD, width)),
        compiler_params=pltpu.CompilerParams(vmem_limit_bytes=56 * MIB),
        cost_estimate=cost(40),
        name="expert_forward",
    )(rows, details, own_half, other_half)


def expert_backward_kernel(
    sizes, padded, rows_ref, detail_ref, pool_ref, y_ref, slope_ref, act_ref, own_ref, other_ref, *refs
):
    at = Place(sizes)
    sources, unused, width = rows_ref.shape
    chunks, unused, part = slope_ref.shape
    half = chunks // 2
    back_ref, gate_ref, *outs = refs[: 2 + half]
    d_hidden, d_rows, send_rows, send_gate, send_grad, got_grad = refs[2 + half : 8 + half]
    own_sem, r_out, r_in, m_out, m_in, g_out, g_in, g_keep = refs[8 + half :]
    many = y_ref.shape[0]
    rounds = sources // many
    step = pl.program_id(0)
    team = others(at.member, sources)

    def row_copy(member, source):
        return send(
            send_rows.at[member], back_ref.at[source], r_out.at[member], r_in.at[source], at.of_member(member)
        )

    def gate_copy(member, source):
        return send(
            send_gate.at[member], gate_ref.at[source], m_out.at[member], m_in.at[source], at.of_member(member)
        )

    def keep_copies():
        return (
            pltpu.make_async_copy(send_rows.at[at.member], back_ref.at[at.member], own_sem.at[0]),
            pltpu.make_async_copy(send_gate.at[at.member], gate_ref.at[at.member], own_sem.at[1]),
        )

    def grad_copy(index):
        return send(
            send_grad.at[index], got_grad.at[index], g_out.at[index], g_in.at[index], at.sibling()
        )

    def out_copy(index):
        return pltpu.make_async_copy(got_grad.at[index], outs[index], g_keep.at[index])

    @pl.when(step == 0)
    def _():
        greet([at.of_member(member) for member in team] + [at.sibling()])

    @pl.when(step < rounds)
    def _():
        block = lax.rem(lax.div(at.member, many) + 1 + step, rounds)
        d_out = []
        for index in range(many):
            source = block * many + index
            detail = detail_ref[source]
            hot = image_hot(detail, padded)
            hots = jnp.where(hot, 1.0, 0.0).astype(jnp.bfloat16)
            pools = jnp.concatenate(split_three(pool_ref[source]), 0)
            wide = dot_f32(jnp.concatenate([hots] * 3, 0), pools, TN)
            lanes = detail.shape[1]
            upright = jnp.concatenate([detail, jnp.zeros((120, lanes), jnp.float32)], 0).T
            gate, pool = upright[:padded, 0:1], upright[:padded, 1:2]
            d_out.append((gate * (pool * wide)).astype(jnp.bfloat16))
            along = dot_f32(pools, y_ref[index], NT)
            along = along[:IMAGE_PAD] + along[IMAGE_PAD : 2 * IMAGE_PAD] + along[2 * IMAGE_PAD :]
            d_gate = jnp.sum(jnp.where(hot, along, 0.0), 0, keepdims=True) * detail[1:2, :padded]
            send_gate[source] = jnp.zeros(detail.shape, jnp.float32)
            send_gate[source, 0:1, :padded] = d_gate
        d_out = jnp.concatenate(d_out, 0)
        count = many * padded
        span = pl.ds(pl.multiple_of(block * count, 16), count)
        d_rows[span] = d_out
        total = None
        for index in range(chunks):
            ref, start = (own_ref, index * part) if index < half else (other_ref, (index - half) * part)
            d_act = dot_f32(d_out, ref[1, start : start + part], NT)
            d_hid = (d_act * slope_ref[index].astype(jnp.float32)).astype(jnp.bfloat16)
            d_hidden[index, span] = d_hid
            found = dot_f32(d_hid, ref[0, start : start + part], NN)
            total = found if total is None else total + found
        total = total.astype(jnp.bfloat16)
        for index in range(many):
            source = block * many + index
            send_rows[source] = total[index * padded : (index + 1) * padded]

            @pl.when(source != at.member)
            def _():
                row_copy(source, at.member).start()
                gate_copy(source, at.member).start()

            @pl.when(source == at.member)
            def _():
                for copy in keep_copies():
                    copy.start()

    @pl.when(step >= rounds)
    def _():
        index = step - rounds
        chunk = lax.rem(index + half, chunks)
        rows = rows_ref[...].reshape(sources * padded, width)
        g_one = dot_f32(d_hidden[chunk], rows, TN)
        g_two = dot_f32(act_ref[0], d_rows[...], TN)

        @pl.when(index < half)
        def _():
            send_grad[index, 0] = g_one.astype(jnp.bfloat16)
            send_grad[index, 1] = g_two.astype(jnp.bfloat16)
            grad_copy(index).start()

        @pl.when(index >= half)
        def _():
            spot = index - half
            grad_copy(spot).wait_recv()
            got_grad[spot, 0] = (got_grad[spot, 0].astype(jnp.float32) + g_one).astype(jnp.bfloat16)
            got_grad[spot, 1] = (got_grad[spot, 1].astype(jnp.float32) + g_two).astype(jnp.bfloat16)

        for spot in range(half):

            @pl.when(index == spot + half)
            def _():
                out_copy(spot).start()

    @pl.when(step == rounds + chunks - 1)
    def _():
        for member in team:
            row_copy(member, member).wait_recv()
            gate_copy(member, member).wait_recv()
        for member in team:
            row_copy(member, at.member).wait_send()
            gate_copy(member, at.member).wait_send()
        for copy in keep_copies():
            copy.wait()
        for spot in range(half):
            grad_copy(spot).wait_send()
            out_copy(spot).wait()


def expert_backward(sizes, rows, details, pools, results, slopes, acts, own_half, other_half):
    sources, padded, width = rows.shape
    chunks, count, part = acts.shape
    many = max(1, 576 // padded)
    rounds, half = sources // many, chunks // 2
    lanes = details.shape[2]
    kind = jnp.bfloat16
    dma = pltpu.SemaphoreType.DMA
    each, parts = dma((sources,)), dma((half,))

    def block_of(step):
        member = lax.axis_index("x") * QUAD + lax.axis_index("r")
        return lax.rem(lax.div(member, many) + 1 + jnp.minimum(step, rounds - 1), rounds)

    def chunk_of(step):
        return lax.rem(jnp.maximum(step - rounds, 0) + half, chunks)

    return pl.pallas_call(
        functools.partial(expert_backward_kernel, sizes, padded),
        grid=(rounds + chunks,),
        out_shape=(
            jax.ShapeDtypeStruct((sources, padded, width), kind),
            jax.ShapeDtypeStruct((sources, 8, lanes), jnp.float32),
        )
        + (jax.ShapeDtypeStruct((2, part, width), kind),) * half,
        in_specs=[
            whole(), whole(), whole(),
            pl.BlockSpec((many, padded, width), lambda i: (block_of(i), 0, 0)),
            pl.BlockSpec((chunks, many * padded, part), lambda i: (0, block_of(i), 0)),
            pl.BlockSpec((1, count, part), lambda i: (chunk_of(i), 0, 0)),
            whole(), whole(),
        ],
        out_specs=(whole(ANY),) * (2 + half),
        scratch_shapes=[
            VMEM((chunks, count, part), kind),
            VMEM((count, width), kind),
            VMEM((sources, padded, width), kind),
            VMEM((sources, 8, lanes), jnp.float32),
            VMEM((half, 2, part, width), kind),
            VMEM((half, 2, part, width), kind),
            dma((2,)), each, each, each, each, parts, parts, parts,
        ],
        compiler_params=pltpu.CompilerParams(
            collective_id=6, has_side_effects=True, vmem_limit_bytes=62 * MIB
        ),
        cost_estimate=cost(65),
        name="expert_backward",
    )(rows, details, pools, results, slopes, acts, own_half, other_half)


def dense_backward_kernel(
    sizes, n_experts, images, padded, length_ref, mask_ref, patch_ref, x_zero_ref, a_one_ref, qkv_ref, att_ref,
    x_one_ref, a_two_ref, prob_ref, lse_ref, col_ref, w_ref, gain_ref, router_ref, back_ref, gate_ref,
    pool_ref, imp_ref, third_ref, out_ref, grads, g_router, g_norm, d_qkv
):
    row = pl.program_id(0)
    span, width = patch_ref.shape
    mats, rows = grads.shape[0], width // (8 * sizes["g"] * sizes["x"])

    @pl.when(row == 0)
    def _():
        grads[...] = jnp.zeros_like(grads)
        g_router[...] = jnp.zeros_like(g_router)
        g_norm[...] = third_ref[...]

    columns = col_ref[...]
    slot_one, slot_two = columns[:, 0:1], columns[:, 1:2]
    count = n_experts * padded
    slot = lax.broadcasted_iota(jnp.int32, (span, count), 1).astype(jnp.float32)
    match = jnp.where((slot == slot_one) | (slot == slot_two), 1.0, 0.0).astype(jnp.bfloat16)
    d_a_two = dot_f32(match, back_ref[...].reshape(count, width), NN)
    lanes = gate_ref.shape[2]
    spot = lax.broadcasted_iota(jnp.int32, (span, lanes), 1)
    inside = spot < padded
    spot = spot.astype(jnp.float32)
    found_one, found_two = jnp.zeros((span, lanes), jnp.float32), jnp.zeros((span, lanes), jnp.float32)
    for expert in range(n_experts):
        line = jnp.broadcast_to(gate_ref[expert, 0:1], (span, lanes))
        found_one = jnp.where(inside & (spot == slot_one - expert * padded), line, found_one)
        found_two = jnp.where(inside & (spot == slot_two - expert * padded), line, found_two)
    d_gate_one = jnp.sum(found_one, 1, keepdims=True)
    d_gate_two = jnp.sum(found_two, 1, keepdims=True)
    lane = lax.broadcasted_iota(jnp.int32, (span, 128), 1)
    number = lane.astype(jnp.float32)
    valid, pool, image = columns[:, 2:3], columns[:, 3:4], columns[:, 4:5]
    head = lax.broadcasted_iota(jnp.int32, (1, 128), 1) < n_experts
    importance = imp_ref[0:1, 0:128]
    centre = jnp.sum(jnp.where(head, importance, 0.0), 1, keepdims=True) / n_experts
    away = jnp.where(head, importance - centre, 0.0)
    spread = jnp.sum(away * away, 1, keepdims=True) / n_experts
    d_imp = aux_weight * (
        2.0 * away / (n_experts * centre * centre)
        - 2.0 * spread / (n_experts * centre * centre * centre)
    )
    d_probs = valid * d_imp
    d_probs = d_probs + jnp.where(number == columns[:, 5:6], d_gate_one, 0.0)
    d_probs = d_probs + jnp.where(number == columns[:, 6:7], d_gate_two, 0.0)
    probs = prob_ref[...]
    d_router = (probs * (d_probs - jnp.sum(probs * d_probs, 1, keepdims=True))).astype(jnp.bfloat16)
    g_router[...] += dot_f32(d_router, a_two_ref[...], TN)
    routers = router_ref[...].astype(jnp.bfloat16)
    if routers.shape[0] < 128:
        routers = jnp.concatenate(
            [routers, jnp.zeros((128 - routers.shape[0], width), jnp.bfloat16)], 0
        )
    d_a_two = d_a_two + dot_f32(d_router, routers, NN)
    scaled, scale = norm_parts(x_one_ref[...])
    g_norm[1:2] += jnp.sum(d_a_two * scaled, 0, keepdims=True)
    g_norm[4:5] += jnp.sum(d_a_two, 0, keepdims=True)
    d_x_one = norm_back(d_a_two, scaled, scale, gain_ref[1:2])
    for index in range(images):
        place = row * images + index
        weight = jnp.where(image == place.astype(jnp.float32), pool, 0.0)
        d_x_one = d_x_one + weight * pool_ref[pl.ds(place, 1)]
    d_att = d_x_one.astype(jnp.bfloat16)
    grads[4] += dot_f32(att_ref[...], d_att, TN)
    d_out = dot_f32(d_att, w_ref[4], NT).astype(jnp.bfloat16)
    open_to = allowed_slots(length_ref, row, images, mask_ref[0], span)
    logs = lse_ref[...]
    for pair in range(width // 128):
        query, key, value = (
            qkv_ref[:, part * width + pair * 128 : part * width + (pair + 1) * 128]
            for part in range(3)
        )
        d_pair = d_out[:, pair * 128 : (pair + 1) * 128]
        found = []
        for side in range(2):
            left = (lane < 64) == (side == 0)
            held = jnp.where(left, query, jnp.zeros_like(query))
            scores = jnp.where(open_to, dot_f32(held, key, NT) * 64**-0.5, mask_fill)
            total = logs[:, 2 * pair + side : 2 * pair + side + 1]
            chance = jnp.exp(scores - total)
            d_held = jnp.where(left, d_pair, jnp.zeros_like(d_pair))
            d_chance = dot_f32(d_held, value, NT)
            d_value = dot_f32(chance.astype(jnp.bfloat16), d_pair, TN)
            d_scores = chance * (d_chance - jnp.sum(chance * d_chance, 1, keepdims=True))
            d_scores = d_scores.astype(jnp.bfloat16)
            d_query = dot_f32(d_scores, key, NN) * 64**-0.5
            d_key = dot_f32(d_scores, query, TN) * 64**-0.5
            found.append((d_query, d_key, d_value))
        for part in range(3):
            d_qkv[:, part * width + pair * 128 : part * width + (pair + 1) * 128] = jnp.where(
                lane < 64, found[0][part], found[1][part]
            ).astype(jnp.bfloat16)
    d_a_one = None
    for part in range(3):
        piece = d_qkv[:, part * width : (part + 1) * width]
        grads[1 + part] += dot_f32(a_one_ref[...], piece, TN)
        found = dot_f32(piece, w_ref[1 + part], NT)
        d_a_one = found if d_a_one is None else d_a_one + found
    scaled, scale = norm_parts(x_zero_ref[...])
    g_norm[0:1] += jnp.sum(d_a_one * scaled, 0, keepdims=True)
    g_norm[3:4] += jnp.sum(d_a_one, 0, keepdims=True)
    d_x_zero = norm_back(d_a_one, scaled, scale, gain_ref[0:1]) + d_x_one
    grads[0] += dot_f32(patch_ref[...], d_x_zero.astype(jnp.bfloat16), TN)

    @pl.when(row == pl.num_programs(0) - 1)
    def _():
        Z, Y, X = QUAD, sizes["g"], sizes["x"]
        tall = max(8, n_experts)
        norms = g_norm[...]
        if tall > 8:
            norms = jnp.concatenate([norms, jnp.zeros((tall - 8, width), jnp.float32)], 0)
        router_grads = g_router[:tall]
        depth = out_ref.shape[4]
        device = 0
        for z in range(Z):
            for y in range(Y):
                for x in range(X):
                    for c in range(2):
                        spot = slice(device * rows, (device + 1) * rows)
                        blank = jnp.zeros((tall, 128 - rows), jnp.float32)
                        tail = [norms[:, spot], blank, router_grads[:, spot], blank]
                        tail.append(jnp.zeros((tall, width - 256), jnp.float32))
                        pieces = [grads[mat, spot] for mat in range(mats)]
                        pieces.append(jnp.concatenate(tail, 1))
                        left = depth - mats * rows - tall
                        if left:
                            pieces.append(jnp.zeros((left, width), jnp.float32))
                        out_ref[c, z, x, y] = jnp.concatenate(pieces, 0).astype(jnp.bfloat16)
                        device += 1


def dense_backward(
    sizes, n_experts, padded, rows_own, lengths, slot_mask, patches, kept, columns, weights, gains, routers, back,
    gates, pooled, importance, third
):
    rows_here, span = slot_mask.shape
    tokens, width = patches.shape
    mats = weights.shape[0]
    depth = round_up(mats * rows_own + max(8, n_experts), 16)
    x_zero, a_one, qkv, att, x_one, a_two, probs, logs = kept

    def block(wide):
        return pl.BlockSpec((span, wide), lambda i: (i, 0))

    return pl.pallas_call(
        functools.partial(dense_backward_kernel, sizes, n_experts, lengths.shape[1], padded),
        grid=(rows_here,),
        out_shape=jax.ShapeDtypeStruct(
            (2, QUAD, sizes["x"], sizes["g"], depth, width), jnp.bfloat16
        ),
        in_specs=[
            whole(pltpu.SMEM), pl.BlockSpec((1, 1, span), lambda i: (i, 0, 0)), block(width),
            block(width), block(width), block(3 * width), block(width), block(width), block(width),
            block(128), block(128), block(128),
        ]
        + [whole()] * 8,
        out_specs=whole(),
        scratch_shapes=[
            VMEM((mats, width, width), jnp.float32),
            VMEM((128, width), jnp.float32),
            VMEM((8, width), jnp.float32),
            VMEM((span, 3 * width), jnp.bfloat16),
        ],
        compiler_params=pltpu.CompilerParams(vmem_limit_bytes=60 * MIB),
        cost_estimate=cost(50),
        name="dense_backward",
    )(
        lengths, slot_mask[:, None, :], patches, x_zero, a_one, qkv, att, x_one, a_two, probs, logs, columns,
        weights, gains, routers, back, gates, pooled, importance, third,
    )


def shard_moves(n_blocks):
    span = 2 * n_blocks
    moves = []
    for step in range(span):
        pairs = []
        for place in range(QUAD * n_blocks):
            for core in range(2):
                target = (place + step) % span
                src = place * 2 + core
                dst = (target // 2 * QUAD + 2 * core + target % 2) * 2 + place // span
                pairs.append((src, dst))
        moves.append(pairs)
    return moves


def swap_cores(value):
    return lax.ppermute(value, "c", [(0, 1), (1, 0)])


def fetch_experts(expert_in, expert_out, n_blocks):
    place = lax.axis_index("g") * QUAD + lax.axis_index("r")
    odd = lax.rem(place, 2) == 1
    both = jnp.stack([expert_in, expert_out], 1).astype(jnp.bfloat16)
    ordered = [jnp.where(odd, both[1], both[0]), jnp.where(odd, both[0], both[1])]
    return [
        lax.ppermute(ordered[step % 2], ("g", "r", "c"), pairs)
        for step, pairs in enumerate(shard_moves(n_blocks))
    ]


def return_experts(parts, n_blocks):
    place = lax.axis_index("g") * QUAD + lax.axis_index("r")
    odd = lax.rem(place, 2) == 1
    sums = [None, None]
    for step, pairs in enumerate(shard_moves(n_blocks)):
        back = lax.ppermute(parts[step], ("g", "r", "c"), [(dst, src) for src, dst in pairs])
        back = back.astype(jnp.float32)
        sums[step % 2] = back if sums[step % 2] is None else sums[step % 2] + back
    zero, one = jnp.where(odd, sums[1], sums[0]), jnp.where(odd, sums[0], sums[1])
    return jnp.stack([zero[0], one[0]]), jnp.stack([zero[1], one[1]])


def body(
    patches,
    lengths,
    slot_mask,
    expert_picks,
    priority_rank,
    class_labels,
    dense_weights,
    dense_first,
    dense_second,
    dense_average,
    router_weights,
    router_first,
    router_second,
    router_average,
    norm_params,
    norm_first,
    norm_second,
    norm_average,
    expert_in,
    in_first,
    in_second,
    in_average,
    expert_out,
    out_first,
    out_second,
    out_average,
    head_weights,
    head_first,
    head_second,
    head_average,
):
    n_blocks = lax.axis_size("g")
    sizes = {name: lax.axis_size(name) for name in ALL}
    rows_own, n_experts = router_weights.shape
    n_tail = max(8, n_experts)
    tail = jnp.zeros((n_tail, dense_weights.shape[2]), jnp.float32)
    tail = tail.at[:6, :rows_own].set(norm_params)
    tail = tail.at[:n_experts, 128 : 128 + rows_own].set(router_weights.T)
    rows_here, n_slots_row = slot_mask.shape
    tokens, model_width = patches.shape
    n_images = lengths.shape[0] * lengths.shape[1]
    capacity = (21 * tokens * TOP + 20 * n_experts - 1) // (20 * n_experts)
    padded = round_up(capacity, 16)
    layer_b, gain_rows, router_t, columns = gather_weights(
        sizes,
        (lengths.shape[1], n_experts, capacity, padded),
        dense_weights,
        tail,
        expert_picks,
        priority_rank,
        slot_mask,
        lengths,
    )
    expert_in_now, expert_out_now, layer_b = lax.optimization_barrier((expert_in, expert_out, layer_b))
    own_chunks = fetch_experts(expert_in_now, expert_out_now, n_blocks)
    own_half = jnp.concatenate(own_chunks, 1)
    other_half = swap_cores(own_half)
    x_zero, a_one, qkv, att_out, x_one, a_two, router_probs, logs, pooled, part_importance = (
        dense_forward(
            n_experts, lengths, slot_mask, patches, layer_b, gain_rows, router_t, columns
        )
    )
    arrived, details = dispatch(sizes, n_experts, padded, a_two, router_probs, columns)
    activated, slope, result, part_pooled = expert_forward(
        arrived, details, own_half, other_half, 4 * n_blocks
    )
    g_head, d_pooled_all, d_pooled, g_norm_three, local_loss, total_importance = head_step(
        sizes,
        n_images,
        part_pooled,
        pooled,
        part_importance,
        gain_rows,
        head_weights,
        class_labels,
    )
    d_back, back_gate, *grads = expert_backward(
        sizes, arrived, details, d_pooled_all, result, slope, activated, own_half, other_half
    )
    g_one, g_two = return_experts(grads, n_blocks)
    blocks = dense_backward(
        sizes,
        n_experts,
        padded,
        rows_own,
        lengths,
        slot_mask,
        patches,
        (x_zero, a_one, qkv, att_out, x_one, a_two, router_probs, logs),
        columns,
        layer_b,
        gain_rows,
        router_t,
        d_back,
        back_gate,
        d_pooled,
        total_importance,
        g_norm_three,
    )
    reduced = scatter_dense(sizes, blocks)
    n_dense = dense_weights.shape[0] * rows_own
    g_layers = reduced[:n_dense].reshape(-1, rows_own, model_width)
    g_norms = reduced[n_dense : n_dense + 6, :rows_own]
    g_router = reduced[n_dense : n_dense + n_experts, 128 : 128 + rows_own].T
    importance = total_importance[0, :n_experts]
    local_loss = local_loss[0, 0]
    centre = jnp.mean(importance)
    spread = jnp.mean((importance - centre) ** 2)
    squares = (
        jnp.sum(g_layers * g_layers) + jnp.sum(g_router * g_router) + jnp.sum(g_norms * g_norms)
    )
    squares = squares + jnp.sum(g_one * g_one) + jnp.sum(g_two * g_two) + jnp.sum(g_head * g_head)
    line = lax.broadcasted_iota(jnp.int32, (8, 128), 0)
    all_sums = share_sums(sizes, jnp.where(line == 0, local_loss, squares))
    loss_sum, square_sum = all_sums[0, 0], all_sums[1, 0]
    grad_norm = jnp.sqrt(square_sum)
    factor = jnp.minimum(1.0, clip_limit / grad_norm)
    loss_value = loss_sum + aux_weight * spread / (centre * centre)
    dense_out = adam_update(
        dense_weights, dense_first, dense_second, dense_average, g_layers, factor, base_rate
    )
    router_out = adam_update(
        router_weights, router_first, router_second, router_average, g_router, factor, base_rate
    )
    norm_out = adam_update(
        norm_params, norm_first, norm_second, norm_average, g_norms, factor, norm_rate
    )
    in_out = adam_update(expert_in, in_first, in_second, in_average, g_one, factor, base_rate)
    out_out = adam_update(expert_out, out_first, out_second, out_average, g_two, factor, base_rate)
    head_out = adam_update(
        head_weights, head_first, head_second, head_average, g_head, factor, base_rate
    )
    return (
        loss_value,
        importance,
        grad_norm,
        *dense_out,
        *router_out,
        *norm_out,
        *in_out,
        *out_out,
        *head_out,
    )


def solution(mesh):
    n_dp, n_expert = mesh.shape["dp"], mesh.shape["expert"]
    shaped = mesh.devices.reshape(n_dp // QUAD, QUAD, n_expert // 2, 2)
    fine = Mesh(shaped, ALL)
    rows = P(ALL, None)
    dense = P(None, ALL, None)
    norms = P(None, ALL)
    experts = P(("x", "c"), ("g", "r"), None)
    placed = (rows,) * 6 + (dense,) * 4 + (rows,) * 4 + (norms,) * 4 + (experts,) * 8 + (rows,) * 4
    results = (
        (P(),) * 3 + (dense,) * 4 + (rows,) * 4 + (norms,) * 4 + (experts,) * 8 + (rows,) * 4
    )
    return jax.shard_map(body, mesh=fine, in_specs=placed, out_specs=results, check_vma=False)
```

```python
import functools
import math

import jax
import jax.numpy as jnp
from jax import lax
from jax.experimental import pallas as pl
from jax.experimental.pallas import tpu as pltpu
from jax.sharding import Mesh
from jax.sharding import PartitionSpec as P

HEADS = 12
TOP = 2
STEP_COUNT = 10
QUAD = 4

high_prec = lax.Precision.HIGHEST
eps_norm = 1e-06
aux_weight = 0.01
clip_limit = 1.0
base_rate = 0.05
norm_rate = 0.5
beta_first = 0.9
beta_second = 0.999
weight_decay = 0.1
polyak_decay = 0.7
adam_eps = 1e-08
mask_fill = -1e30

ALL = ("g", "r", "x", "c")
MEMBERS = ("x", "r")


def adam_update(weight, first_state, second_state, average_state, gradient, factor, step_rate):
    clipped = gradient * factor
    first_new = beta_first * first_state + (1.0 - beta_first) * clipped
    second_new = beta_second * second_state + (1.0 - beta_second) * clipped * clipped
    first_hat = first_new / (1.0 - beta_first**STEP_COUNT)
    second_hat = second_new / (1.0 - beta_second**STEP_COUNT)
    weight_new = weight - step_rate * (
        first_hat / (jnp.sqrt(second_hat) + adam_eps) + weight_decay * weight
    )
    average_new = polyak_decay * average_state + (1.0 - polyak_decay) * weight_new
    return (weight_new, first_new, second_new, average_new)


MESH_ID = pl.DeviceIdType.MESH
VMEM = pltpu.VMEM
ANY = pl.ANY
MIB = 1 << 20


def cost(microseconds):
    return pl.CostEstimate(flops=int(microseconds * 1.15e9), bytes_accessed=0, transcendentals=0)


def whole(space=None):
    return pl.BlockSpec(memory_space=space or VMEM)


def round_up(value, step):
    return (value + step - 1) // step * step


class Place:
    def __init__(self, sizes):
        self.G, self.X = sizes["g"], sizes["x"]
        self.Z, self.Y = QUAD, sizes["g"]
        self.chips = self.Z * self.Y * self.X
        spot = lax.axis_index("g") * QUAD + lax.axis_index("r")
        self.z, self.y = lax.div(spot, self.Y), lax.rem(spot, self.Y)
        self.x, self.c = lax.axis_index("x"), lax.axis_index("c")
        self.g, self.r = lax.axis_index("g"), lax.axis_index("r")
        self.chip = spot * self.X + self.x
        self.member = self.x * QUAD + self.r

    def at(self, z=None, y=None, x=None, c=None):
        spot = (self.z if z is None else z) * self.Y + (self.y if y is None else y)
        return {
            "g": lax.div(spot, QUAD),
            "r": lax.rem(spot, QUAD),
            "x": self.x if x is None else x,
            "c": self.c if c is None else c,
        }

    def of_chip(self, chip):
        spot = lax.div(chip, self.X)
        return {
            "g": lax.div(spot, QUAD),
            "r": lax.rem(spot, QUAD),
            "x": lax.rem(chip, self.X),
            "c": self.c,
        }

    def of_member(self, member):
        return {
            "g": self.g,
            "r": lax.rem(member, QUAD),
            "x": lax.div(member, QUAD),
            "c": self.c,
        }

    def sibling(self):
        return self.at(c=1 - self.c)


def greet(peers):
    barrier = pltpu.get_barrier_semaphore()
    for peer in peers:
        pl.semaphore_signal(barrier, inc=1, device_id=peer, device_id_type=MESH_ID)
    pl.semaphore_wait(barrier, len(peers))


def send(src, dst, send_sem, recv_sem, peer):
    return pltpu.make_async_remote_copy(
        src_ref=src,
        dst_ref=dst,
        send_sem=send_sem,
        recv_sem=recv_sem,
        device_id=peer,
        device_id_type=MESH_ID,
    )


def others(me, count):
    return [lax.rem(me + step, count) for step in range(1, count)]


def grid_peers(at):
    peers = [at.at(z=z) for z in others(at.z, at.Z)]
    peers += [at.at(y=y) for y in others(at.y, at.Y)]
    peers += [at.at(x=x) for x in others(at.x, at.X)]
    return peers + [at.sibling()]


def gather_kernel(
    sizes, rows, mats, routing, dense_ref, tail_ref, pick_ref, rank_ref, mask_ref, length_ref,
    w_ref, gain_ref, router_ref, col_ref, land, *sems
):
    at = Place(sizes)
    Z, Y, X = at.Z, at.Y, at.X
    depth = land.shape[4]
    cut = depth // 2 // 16 * 16
    first, second = pl.ds(0, cut), pl.ds(cut, depth - cut)
    z_out, z_in, ya_out, ya_in, xb_out, xb_in, xa_out, xa_in, yb_out, yb_in, c_out, c_in = sems
    block = jnp.concatenate([dense_ref[...].reshape(mats * rows, -1), tail_ref[...]], 0)
    if block.shape[0] < depth:
        block = jnp.pad(block, ((0, depth - block.shape[0]), (0, 0)))
    mine = land.at[at.c, at.z, at.x, at.y]
    mine[...] = block.astype(jnp.bfloat16)
    greet(grid_peers(at))
    started = []

    def begin(copy):
        copy.start()
        started.append(copy)

    order = [at.z] + [lax.rem(at.z + k, Z) for k in (1, 3, 2)]
    for z in order[1:]:
        begin(send(mine, mine, z_out.at[z], z_in.at[at.z], at.at(z=z)))

    def one(z):
        part = land.at[at.c, z, at.x, at.y]
        for y in others(at.y, Y):
            begin(send(part.at[first], part.at[first], ya_out.at[z, y], ya_in.at[z, at.y], at.at(y=y)))
        for x in others(at.x, X):
            begin(send(part.at[second], part.at[second], xb_out.at[z, x], xb_in.at[z, at.x], at.at(x=x)))

    def two(z):
        for y in others(at.y, Y):
            part = land.at[at.c, z, at.x, y, first]
            send(part, part, ya_out.at[z, y], ya_in.at[z, y], at.at(y=y)).wait_recv()
        line = land.at[at.c, z, at.x, :, first]
        for x in others(at.x, X):
            begin(send(line, line, xa_out.at[z, x], xa_in.at[z, at.x], at.at(x=x)))
        for x in others(at.x, X):
            part = land.at[at.c, z, x, at.y, second]
            send(part, part, xb_out.at[z, x], xb_in.at[z, x], at.at(x=x)).wait_recv()
        line = land.at[at.c, z, :, at.y, second]
        for y in others(at.y, Y):
            begin(send(line, line, yb_out.at[z, y], yb_in.at[z, at.y], at.at(y=y)))

    def three(z):
        for x in others(at.x, X):
            line = land.at[at.c, z, x, :, first]
            send(line, line, xa_out.at[z, x], xa_in.at[z, x], at.at(x=x)).wait_recv()
        for y in others(at.y, Y):
            line = land.at[at.c, z, :, y, second]
            send(line, line, yb_out.at[z, y], yb_in.at[z, y], at.at(y=y)).wait_recv()
        plane = land.at[at.c, z]
        begin(send(plane, plane, c_out.at[z], c_in.at[z], at.sibling()))

    for step in range(Z + 2):
        if step < Z:
            if step > 0:
                z = order[step]
                part = land.at[at.c, z, at.x, at.y]
                send(part, part, z_out.at[z], z_in.at[z], at.at(z=z)).wait_recv()
            one(order[step])
        if step == 0:
            col_ref[...] = route_math(*routing, pick_ref, rank_ref, mask_ref, length_ref)
        if 0 <= step - 1 < Z:
            two(order[step - 1])
        if 0 <= step - 2 < Z:
            three(order[step - 2])
    for z in order:
        plane = land.at[1 - at.c, z]
        send(plane, plane, c_out.at[z], c_in.at[z], at.sibling()).wait_recv()
    for copy in started:
        copy.wait_send()
    chips = [(z, y, x) for z in range(Z) for y in range(Y) for x in range(X)]
    cores = [(c, z, x, y) for z, y, x in chips for c in range(2)]
    group = 16 // math.gcd(16, rows)
    for start in range(0, len(cores), group):
        for mat in range(mats):
            w_ref[mat, start * rows : (start + group) * rows] = jnp.concatenate(
                [land[spot][mat * rows : (mat + 1) * rows] for spot in cores[start : start + group]], 0
            )
    base, count = mats * rows, tail_ref.shape[0]
    tails = [land[spot][base : base + count].astype(jnp.float32) for spot in cores]
    gain_ref[...] = jnp.concatenate([tail[:8, :rows] for tail in tails], 1)
    router_ref[...] = jnp.concatenate([tail[:, 128 : 128 + rows] for tail in tails], 1)


def gather_weights(sizes, routing, dense, tail, picks, ranks, slot_mask, lengths):
    mats, rows, width = dense.shape
    count = tail.shape[0]
    depth = round_up(mats * rows + count, 16)
    Z, Y, X = QUAD, sizes["g"], sizes["x"]
    dma = pltpu.SemaphoreType.DMA
    by_y, by_x = dma((Z, Y)), dma((Z, X))
    return pl.pallas_call(
        functools.partial(gather_kernel, sizes, rows, mats, routing),
        out_shape=(
            jax.ShapeDtypeStruct((mats, width, width), jnp.bfloat16),
            jax.ShapeDtypeStruct((8, width), jnp.float32),
            jax.ShapeDtypeStruct((count, width), jnp.float32),
            jax.ShapeDtypeStruct((picks.shape[0], 128), jnp.float32),
        ),
        in_specs=[whole()] * 6,
        out_specs=(whole(),) * 4,
        scratch_shapes=[VMEM((2, Z, X, Y, depth, width), jnp.bfloat16), dma((Z,)), dma((Z,))]
        + [by_y, by_y, by_x, by_x, by_x, by_x, by_y, by_y, dma((Z,)), dma((Z,))],
        compiler_params=pltpu.CompilerParams(
            collective_id=1, has_side_effects=True, vmem_limit_bytes=48 * MIB
        ),
        cost_estimate=cost(44),
        name="gather_weights",
    )(dense, tail, picks, ranks, slot_mask, lengths)


def scatter_kernel(sizes, g_ref, out_ref, hold, sib, got_xa, got_yb, got_ya, got_xb, got_z, *sems):
    at = Place(sizes)
    Z, Y, X = at.Z, at.Y, at.X
    depth = g_ref.shape[4]
    cut = depth // 2 // 16 * 16
    first, second = pl.ds(0, cut), pl.ds(cut, depth - cut)
    c_out, c_in, xa_out, xa_in, yb_out, yb_in, ya_out, ya_in, xb_out, xb_in, z_out, z_in = sems
    greet(grid_peers(at))
    started = []

    def begin(copy):
        copy.start()
        started.append(copy)

    wide = lambda value: value.astype(jnp.float32)
    order = [lax.rem(at.z + k, Z) for k in (2, 1, 3)] + [at.z]
    for z in order:
        begin(send(g_ref.at[1 - at.c, z], sib.at[z], c_out.at[z], c_in.at[z], at.sibling()))

    def one(z):
        send(sib.at[z], sib.at[z], c_out.at[z], c_in.at[z], at.sibling()).wait_recv()
        hold[z] = (wide(g_ref[at.c, z]) + wide(sib[z])).astype(jnp.bfloat16)
        for x in others(at.x, X):
            begin(send(hold.at[z, x, :, first], got_xa.at[z, at.x], xa_out.at[z, x], xa_in.at[z, at.x], at.at(x=x)))
        for y in others(at.y, Y):
            begin(send(hold.at[z, :, y, second], got_yb.at[z, at.y], yb_out.at[z, y], yb_in.at[z, at.y], at.at(y=y)))

    def two(z):
        total = wide(hold[z, at.x, :, first])
        for x in others(at.x, X):
            send(got_xa.at[z, x], got_xa.at[z, x], xa_out.at[z, x], xa_in.at[z, x], at.at(x=x)).wait_recv()
            total = total + wide(got_xa[z, x])
        hold[z, at.x, :, first] = total.astype(jnp.bfloat16)
        for y in others(at.y, Y):
            begin(send(hold.at[z, at.x, y, first], got_ya.at[z, at.y], ya_out.at[z, y], ya_in.at[z, at.y], at.at(y=y)))
        total = wide(hold[z, :, at.y, second])
        for y in others(at.y, Y):
            send(got_yb.at[z, y], got_yb.at[z, y], yb_out.at[z, y], yb_in.at[z, y], at.at(y=y)).wait_recv()
            total = total + wide(got_yb[z, y])
        hold[z, :, at.y, second] = total.astype(jnp.bfloat16)
        for x in others(at.x, X):
            begin(send(hold.at[z, x, at.y, second], got_xb.at[z, at.x], xb_out.at[z, x], xb_in.at[z, at.x], at.at(x=x)))

    def three(z, last):
        total = wide(hold[z, at.x, at.y, first])
        for y in others(at.y, Y):
            send(got_ya.at[z, y], got_ya.at[z, y], ya_out.at[z, y], ya_in.at[z, y], at.at(y=y)).wait_recv()
            total = total + wide(got_ya[z, y])
        rest = wide(hold[z, at.x, at.y, second])
        for x in others(at.x, X):
            send(got_xb.at[z, x], got_xb.at[z, x], xb_out.at[z, x], xb_in.at[z, x], at.at(x=x)).wait_recv()
            rest = rest + wide(got_xb[z, x])
        if last:
            out_ref[first] = total
            out_ref[second] = rest
            return
        mine = hold.at[z, at.x, at.y]
        mine[first] = total.astype(jnp.bfloat16)
        mine[second] = rest.astype(jnp.bfloat16)
        begin(send(mine, got_z.at[at.z], z_out.at[z], z_in.at[at.z], at.at(z=z)))

    for step in range(Z + 2):
        if step < Z:
            one(order[step])
        if 0 <= step - 1 < Z:
            two(order[step - 1])
        if 0 <= step - 2 < Z:
            three(order[step - 2], step - 2 == Z - 1)
    for z in order[:-1]:
        send(got_z.at[z], got_z.at[z], z_out.at[z], z_in.at[z], at.at(z=z)).wait_recv()
        out_ref[...] += wide(got_z[z])
    for copy in started:
        copy.wait_send()


def scatter_dense(sizes, blocks):
    unused, Z, X, Y, depth, width = blocks.shape
    dma = pltpu.SemaphoreType.DMA
    by_y, by_x, by_z = dma((Z, Y)), dma((Z, X)), dma((Z,))
    cut = depth // 2 // 16 * 16
    half = jnp.bfloat16
    return pl.pallas_call(
        functools.partial(scatter_kernel, sizes),
        out_shape=jax.ShapeDtypeStruct((depth, width), jnp.float32),
        in_specs=[whole()],
        out_specs=whole(),
        scratch_shapes=[
            VMEM((Z, X, Y, depth, width), half),
            VMEM((Z, X, Y, depth, width), half),
            VMEM((Z, X, Y, cut, width), half),
            VMEM((Z, Y, X, depth - cut, width), half),
            VMEM((Z, Y, cut, width), half),
            VMEM((Z, X, depth - cut, width), half),
            VMEM((Z, depth, width), half),
        ]
        + [by_z, by_z, by_x, by_x, by_y, by_y, by_y, by_y, by_x, by_x, by_z, by_z],
        compiler_params=pltpu.CompilerParams(
            collective_id=2, has_side_effects=True, vmem_limit_bytes=48 * MIB
        ),
        cost_estimate=cost(45),
        name="scatter_dense",
    )(blocks)


def sums_kernel(sizes, in_ref, out_ref, land, out_sem, in_sem):
    at = Place(sizes)
    count = 2 * at.chips
    me = at.chip * 2 + at.c
    ids = others(me, count)

    def peer(device):
        spot = at.of_chip(lax.div(device, 2))
        spot["c"] = lax.rem(device, 2)
        return spot

    greet([peer(device) for device in ids])
    land[me] = in_ref[...]
    copies = [send(in_ref, land.at[me], out_sem.at[d], in_sem.at[me], peer(d)) for d in ids]
    for copy in copies:
        copy.start()
    for d in ids:
        send(land.at[d], land.at[d], out_sem.at[d], in_sem.at[d], peer(d)).wait_recv()
    out_ref[...] = jnp.sum(land[...], 0)
    for copy in copies:
        copy.wait_send()


def share_sums(sizes, values):
    count = sizes["g"] * QUAD * sizes["x"] * 2
    dma = pltpu.SemaphoreType.DMA
    return pl.pallas_call(
        functools.partial(sums_kernel, sizes),
        out_shape=jax.ShapeDtypeStruct(values.shape, jnp.float32),
        in_specs=[whole()],
        out_specs=whole(),
        scratch_shapes=[VMEM((count, *values.shape), jnp.float32), dma((count,)), dma((count,))],
        compiler_params=pltpu.CompilerParams(collective_id=3, has_side_effects=True),
        cost_estimate=cost(10),
        name="share_sums",
    )(values)


EARLY = 1
IMAGE_PAD = 16


def split_three(value):
    high = value.astype(jnp.bfloat16)
    rest = value - high.astype(jnp.float32)
    middle = rest.astype(jnp.bfloat16)
    return high, middle, (rest - middle.astype(jnp.float32)).astype(jnp.bfloat16)


def dot_f32(left, right, dims):
    return lax.dot_general(left, right, (dims, ((), ())), preferred_element_type=jnp.float32)


NN = ((1,), (0,))
NT = ((1,), (1,))
TN = ((0,), (0,))


def norm_parts(values):
    centre = values - jnp.mean(values, -1, keepdims=True)
    spread = jnp.mean(centre * centre, -1, keepdims=True)
    scale = lax.rsqrt(spread + eps_norm)
    return centre * scale, scale


def norm_back(d_out, scaled, scale, gain):
    pulled = d_out * gain
    return scale * (
        pulled
        - jnp.mean(pulled, -1, keepdims=True)
        - scaled * jnp.mean(pulled * scaled, -1, keepdims=True)
    )


def head_kernel(
    sizes, images, part_ref, own_ref, imp_ref, gain_ref, head_ref, label_ref,
    g_head_ref, d_pool_ref, own_d_ref, g_norm_ref, sums_ref, total_imp_ref,
    in_part, rows, d_rows, d_sib, d_sum, d_in, head_b, labels, d_logits, *sems
):
    at = Place(sizes)
    chips, members = at.chips, QUAD * at.X
    devices = 2 * chips
    p_out, p_in, r_out, r_in, s_out, s_in, d_out, d_in_sem, b_out, b_in = sems
    width = own_ref.shape[1]
    same_core = others(at.chip, chips)
    greet([at.of_chip(chip) for chip in same_core] + [at.sibling()])
    started = []

    def begin(copy):
        copy.start()
        started.append(copy)

    team = others(at.member, members)
    for member in team:
        begin(send(part_ref.at[member], in_part.at[at.member], p_out.at[member], p_in.at[at.member], at.of_member(member)))
    in_part[at.member] = part_ref[at.member]
    head_b[...] = head_ref[...].astype(jnp.bfloat16)
    wide = devices * IMAGE_PAD
    spot = lax.broadcasted_iota(jnp.int32, (label_ref.shape[1], wide), 1)
    given = lax.broadcasted_iota(jnp.int32, (label_ref.shape[1], wide), 0)
    image = lax.rem(spot, IMAGE_PAD)
    device = lax.rem(lax.div(spot, IMAGE_PAD), chips) * 2 + lax.div(spot, IMAGE_PAD * chips)
    chosen = ((device * images + image == given) & (image < images)).astype(jnp.bfloat16)
    labels[...] = dot_f32(label_ref[...].astype(jnp.float32).astype(jnp.bfloat16), chosen, NN).astype(jnp.bfloat16)
    for member in team:
        send(in_part.at[member], in_part.at[member], p_out.at[member], p_in.at[member], at.of_member(member)).wait_recv()
    pooled = own_ref[...] + jnp.sum(in_part[...], 0)
    scaled, scale = norm_parts(pooled)
    gain, shift = gain_ref[2:3], gain_ref[5:6]
    a_three = scaled * gain + shift
    row = lax.broadcasted_iota(jnp.int32, (IMAGE_PAD, width), 0)
    block = jnp.where(row < images, a_three, 0.0)
    pieces = split_three(imp_ref[0:1])
    for index, piece in enumerate(pieces):
        block = jnp.where(row == images + index, piece.astype(jnp.float32), block)
    rows[at.c, at.chip] = block.astype(jnp.bfloat16)
    mine = rows.at[at.c, at.chip]
    for chip in same_core:
        begin(send(mine, mine, r_out.at[chip], r_in.at[at.chip], at.of_chip(chip)))
    for chip in same_core:
        part = rows.at[at.c, chip]
        send(part, part, r_out.at[chip], r_in.at[chip], at.of_chip(chip)).wait_recv()
    begin(send(rows.at[at.c], rows.at[at.c], s_out.at[0], s_in.at[0], at.sibling()))
    send(rows.at[1 - at.c], rows.at[1 - at.c], s_out.at[0], s_in.at[0], at.sibling()).wait_recv()
    gathered = rows[...].reshape(wide, width)
    in_block = lax.rem(lax.broadcasted_iota(jnp.int32, (wide, width), 0), IMAGE_PAD)
    total = jnp.sum(jnp.where(in_block >= images, gathered.astype(jnp.float32), 0.0), 0, keepdims=True)
    total_imp_ref[...] = jnp.broadcast_to(total, total_imp_ref.shape)
    gathered = jnp.where(in_block < images, gathered.astype(jnp.float32), 0.0).astype(jnp.bfloat16)
    logits = dot_f32(head_b[...], gathered, NT)
    image = lax.rem(lax.broadcasted_iota(jnp.int32, logits.shape, 1), IMAGE_PAD)
    count = devices * images
    target = labels[...].astype(jnp.float32)
    power = jnp.exp(-jnp.abs(logits))
    loss = jnp.maximum(logits, 0.0) + jnp.log1p(power) - target * logits
    loss = jnp.sum(jnp.where(image < images, loss, 0.0), 1, keepdims=True)
    loss = jnp.sum(loss, 0, keepdims=True) / count
    sums_ref[...] = jnp.broadcast_to(loss, sums_ref.shape)
    chance = jnp.where(logits >= 0.0, 1.0, power) / (1.0 + power)
    d_logits[...] = jnp.where(image < images, (chance - target) / count, 0.0).astype(jnp.bfloat16)
    partial = dot_f32(d_logits[...], head_b[...], TN)
    d_rows[...] = partial.reshape(d_rows.shape).astype(jnp.bfloat16)
    begin(send(d_rows.at[1 - at.c], d_sib, s_out.at[1], s_in.at[1], at.sibling()))
    g_head_ref[...] = dot_f32(d_logits[...], gathered, NN)
    send(d_sib, d_sib, s_out.at[1], s_in.at[1], at.sibling()).wait_recv()
    d_sum[...] = (d_rows[at.c].astype(jnp.float32) + d_sib[...].astype(jnp.float32)).astype(jnp.bfloat16)
    for chip in same_core:
        begin(send(d_sum.at[chip], d_in.at[at.chip], d_out.at[chip], d_in_sem.at[at.chip], at.of_chip(chip)))
    d_in[at.chip] = d_sum[at.chip]
    for chip in same_core:
        send(d_in.at[chip], d_in.at[chip], d_out.at[chip], d_in_sem.at[chip], at.of_chip(chip)).wait_recv()
    d_norm = jnp.sum(d_in[...].astype(jnp.float32), 0)
    d_norm = jnp.where(row < images, d_norm, 0.0)
    d_pooled = norm_back(d_norm, scaled, scale, gain)
    d_pooled = jnp.where(row < images, d_pooled, 0.0)
    d_gain = jnp.sum(d_norm * scaled, 0, keepdims=True)
    d_shift = jnp.sum(d_norm, 0, keepdims=True)
    line = lax.broadcasted_iota(jnp.int32, g_norm_ref.shape, 0)
    g_norm_ref[...] = jnp.where(line == 2, d_gain, jnp.where(line == 5, d_shift, 0.0))
    own_d_ref[...] = d_pooled
    d_pool_ref[at.member] = d_pooled
    mine = d_pool_ref.at[at.member]
    for member in team:
        begin(send(own_d_ref, mine, b_out.at[member], b_in.at[at.member], at.of_member(member)))
    for member in team:
        part = d_pool_ref.at[member]
        send(part, part, b_out.at[member], b_in.at[member], at.of_member(member)).wait_recv()
    for copy in started:
        copy.wait_send()


def head_step(sizes, images, part, own, imp, gains, head, label):
    members = QUAD * sizes["x"]
    chips = members * sizes["g"]
    classes, width = head.shape
    wide = 2 * chips * IMAGE_PAD
    dma = pltpu.SemaphoreType.DMA
    by_member, by_chip = dma((members,)), dma((chips,))
    f32, half = jnp.float32, jnp.bfloat16
    blocks = (chips, IMAGE_PAD, width)
    return pl.pallas_call(
        functools.partial(head_kernel, sizes, images),
        out_shape=(
            jax.ShapeDtypeStruct((classes, width), f32),
            jax.ShapeDtypeStruct((members, IMAGE_PAD, width), f32),
            jax.ShapeDtypeStruct((IMAGE_PAD, width), f32),
            jax.ShapeDtypeStruct((8, width), f32),
            jax.ShapeDtypeStruct((8, 128), f32),
            jax.ShapeDtypeStruct((8, width), f32),
        ),
        in_specs=[whole()] * 6,
        out_specs=(whole(),) * 6,
        scratch_shapes=[
            VMEM((members, IMAGE_PAD, width), f32),
            VMEM((2, *blocks), half),
            VMEM((2, *blocks), half),
            VMEM(blocks, half),
            VMEM(blocks, half),
            VMEM(blocks, half),
            VMEM((classes, width), half),
            VMEM((classes, wide), half),
            VMEM((classes, wide), half),
        ]
        + [by_member, by_member, by_chip, by_chip, dma((2,)), dma((2,)), by_chip, by_chip]
        + [by_member, by_member],
        compiler_params=pltpu.CompilerParams(
            collective_id=4, has_side_effects=True, vmem_limit_bytes=56 * MIB
        ),
        cost_estimate=cost(42),
        name="head_step",
    )(part, own, imp, gains, head, label)


def route_math(per_image, n_experts, capacity, padded, pick_ref, rank_ref, mask_ref, length_ref):
    rows_here, span = mask_ref.shape
    tokens = rows_here * span
    valid = mask_ref[...].astype(jnp.float32)
    lengths = length_ref[...]
    position = lax.broadcasted_iota(jnp.int32, (rows_here, span), 1)
    segment = jnp.zeros((rows_here, span), jnp.int32)
    bound = jnp.zeros((rows_here, 1), jnp.int32)
    for image in range(per_image):
        bound = bound + lengths[:, image : image + 1]
        segment = segment + jnp.where(position >= bound, 1, 0)
    pool = jnp.zeros_like(valid)
    for image in range(per_image):
        member = jnp.where(segment == image, valid, 0.0)
        pool = pool + member / jnp.maximum(jnp.sum(member, 1, keepdims=True), 1.0)
    line = lax.broadcasted_iota(jnp.int32, (rows_here, span), 0)
    image = (segment + per_image * line).astype(jnp.float32)

    def flat(value):
        return jnp.concatenate([value[i : i + 1] for i in range(rows_here)], 1)

    rank_row = rank_ref[...].astype(jnp.float32)
    table = jnp.concatenate([flat(valid), flat(pool), flat(image), rank_row], 0)
    table = jnp.concatenate([table, jnp.zeros((124, tokens), jnp.float32)], 0).T
    valid_col, pool_col, image_col, rank_col = (table[:, i : i + 1] for i in range(4))
    picks = pick_ref[...]
    pick_one, pick_two = picks[:, 0:1], picks[:, 1:2]
    lane = lax.broadcasted_iota(jnp.int32, (tokens, 128), 1)
    in_first, in_second = lane < n_experts, (lane >= n_experts) & (lane < 2 * n_experts)
    hot = jnp.where(in_first & (pick_one == lane), valid_col, 0.0)
    hot = hot + jnp.where(in_second & (pick_two == lane - n_experts), valid_col, 0.0)
    shifted = jnp.where(in_second & (pick_one == lane - n_experts), valid_col, 0.0)
    before = jnp.where(rank_row < rank_col, 1.0, 0.0).astype(jnp.bfloat16)
    ahead = dot_f32(before, hot.astype(jnp.bfloat16), NN) + jnp.sum(shifted, 0, keepdims=True)
    counted = hot * ahead
    pos_one = jnp.sum(jnp.where(in_first, counted, 0.0), 1, keepdims=True)
    pos_two = jnp.sum(jnp.where(in_second, counted, 0.0), 1, keepdims=True)

    def place(pick, pos):
        kept = (valid_col > 0.0) & (pos < capacity)
        return jnp.where(kept, pick.astype(jnp.float32) * padded + pos, -1.0)

    columns = (
        place(pick_one, pos_one),
        place(pick_two, pos_two),
        valid_col,
        pool_col,
        image_col,
        pick_one.astype(jnp.float32),
        pick_two.astype(jnp.float32),
    )
    result = jnp.zeros((tokens, 128), jnp.float32)
    for index, column in enumerate(columns):
        result = jnp.where(lane == index, column, result)
    return result


def lane_mask(shape, left):
    lane = lax.broadcasted_iota(jnp.int32, shape, 1)
    return lane < 64 if left else lane >= 64


def allowed_slots(lengths, row, images, valid_row, span):
    query = lax.broadcasted_iota(jnp.int32, (span, span), 0)
    key = lax.broadcasted_iota(jnp.int32, (span, span), 1)
    bound = 0
    query_seg, key_seg = jnp.zeros((span, span), jnp.int32), jnp.zeros((span, span), jnp.int32)
    for image in range(images):
        bound = bound + lengths[row, image]
        query_seg = query_seg + jnp.where(query >= bound, 1, 0)
        key_seg = key_seg + jnp.where(key >= bound, 1, 0)
    return (query_seg == key_seg) & ((valid_row > 0) | (query == key))


def dense_forward_kernel(
    n_experts, images, length_ref, mask_ref, patch_ref, w_ref, gain_ref, router_ref, col_ref,
    x_zero_ref, a_one_ref, qkv_ref, att_ref, x_one_ref, a_two_ref, prob_ref, lse_ref, pool_ref, imp_ref
):
    row = pl.program_id(0)
    span, width = patch_ref.shape
    x_zero = dot_f32(patch_ref[...], w_ref[0], NN)
    x_zero_ref[...] = x_zero
    a_one = (norm_parts(x_zero)[0] * gain_ref[0:1] + gain_ref[3:4]).astype(jnp.bfloat16)
    a_one_ref[...] = a_one
    for part in range(3):
        qkv_ref[:, part * width : (part + 1) * width] = dot_f32(a_one, w_ref[1 + part], NN).astype(
            jnp.bfloat16
        )
    open_to = allowed_slots(length_ref, row, images, mask_ref[0], span)
    lane = lax.broadcasted_iota(jnp.int32, (span, 128), 1)
    logs = jnp.zeros((span, 128), jnp.float32)
    for pair in range(width // 128):
        query, key, value = (
            qkv_ref[:, part * width + pair * 128 : part * width + (pair + 1) * 128]
            for part in range(3)
        )
        outs = []
        for side in range(2):
            held = jnp.where((lane < 64) == (side == 0), query, jnp.zeros_like(query))
            scores = jnp.where(open_to, dot_f32(held, key, NT) * 64**-0.5, mask_fill)
            top = jnp.max(scores, 1, keepdims=True)
            powers = jnp.exp(scores - top)
            total = jnp.sum(powers, 1, keepdims=True)
            probs = (powers * (1.0 / total)).astype(jnp.bfloat16)
            outs.append(dot_f32(probs, value, NN))
            logs = jnp.where(lane == 2 * pair + side, top + jnp.log(total), logs)
        att_ref[:, pair * 128 : (pair + 1) * 128] = jnp.where(lane < 64, outs[0], outs[1]).astype(
            jnp.bfloat16
        )
    lse_ref[...] = logs
    x_one = x_zero + dot_f32(att_ref[...], w_ref[4], NN)
    x_one_ref[...] = x_one
    a_two = (norm_parts(x_one)[0] * gain_ref[1:2] + gain_ref[4:5]).astype(jnp.bfloat16)
    a_two_ref[...] = a_two
    routers = router_ref[...].astype(jnp.bfloat16)
    if routers.shape[0] < 128:
        routers = jnp.concatenate(
            [routers, jnp.zeros((128 - routers.shape[0], width), jnp.bfloat16)], 0
        )
    logits = jnp.where(lane < n_experts, dot_f32(a_two, routers, NT), mask_fill)
    powers = jnp.exp(logits - jnp.max(logits, 1, keepdims=True))
    probs = powers / jnp.sum(powers, 1, keepdims=True)
    prob_ref[...] = probs

    @pl.when(row == 0)
    def _():
        pool_ref[...] = jnp.zeros_like(pool_ref)
        imp_ref[...] = jnp.zeros_like(imp_ref)

    valid, pool, image = col_ref[:, 2:3], col_ref[:, 3:4], col_ref[:, 4:5]
    imp_ref[0:1, 0:128] += jnp.sum(probs * valid, 0, keepdims=True)
    line = lax.broadcasted_iota(jnp.int32, pool_ref.shape, 0)
    for index in range(images):
        number = row * images + index
        weight = jnp.where(image == number.astype(jnp.float32), pool, 0.0)
        pooled = jnp.sum(x_one * weight, 0, keepdims=True)
        pool_ref[...] = jnp.where(line == number, pooled, pool_ref[...])


def dense_forward(n_experts, lengths, slot_mask, patches, weights, gains, routers, columns):
    rows_here, span = slot_mask.shape
    tokens, width = patches.shape
    f32, half = jnp.float32, jnp.bfloat16

    def block(wide):
        return pl.BlockSpec((span, wide), lambda i: (i, 0))

    def out(wide, kind):
        return jax.ShapeDtypeStruct((tokens, wide), kind)

    def fixed(shape):
        return pl.BlockSpec(shape, lambda i: (0, 0))

    return pl.pallas_call(
        functools.partial(dense_forward_kernel, n_experts, lengths.shape[1]),
        grid=(rows_here,),
        out_shape=(
            out(width, f32), out(width, half), out(3 * width, half), out(width, half),
            out(width, f32), out(width, half), out(128, f32), out(128, f32),
            jax.ShapeDtypeStruct((IMAGE_PAD, width), f32), jax.ShapeDtypeStruct((8, width), f32),
        ),
        in_specs=[
            whole(pltpu.SMEM), pl.BlockSpec((1, 1, span), lambda i: (i, 0, 0)), block(width),
            whole(), whole(), whole(), block(128),
        ],
        out_specs=(
            block(width), block(width), block(3 * width), block(width), block(width), block(width),
            block(128), block(128), fixed((IMAGE_PAD, width)), fixed((8, width)),
        ),
        compiler_params=pltpu.CompilerParams(vmem_limit_bytes=48 * MIB),
        cost_estimate=cost(25),
        name="dense_forward",
    )(lengths, slot_mask[:, None, :], patches, weights, gains, routers, columns)


def dispatch_kernel(
    sizes, n_experts, padded, a_two_ref, prob_ref, col_ref, rows_ref, detail_ref,
    send_rows, send_detail, places, own_sem, r_out, r_in, m_out, m_in
):
    at = Place(sizes)
    tokens = a_two_ref.shape[0]
    team = others(at.member, n_experts)
    greet([at.of_member(member) for member in team])
    columns = col_ref[...]
    places[...] = columns.T[:8]
    lane = lax.broadcasted_iota(jnp.int32, (tokens, 128), 1)
    kind, expert = lax.div(lane, n_experts), lax.rem(lane, n_experts).astype(jnp.float32)
    slot_lane = lax.broadcasted_iota(jnp.int32, (tokens, send_detail.shape[2]), 1).astype(jnp.float32)
    pool, image = columns[:, 3:4], columns[:, 4:5]
    details = None
    for choice in range(2):
        slot, pick = columns[:, choice : choice + 1], columns[:, 5 + choice : 6 + choice]
        hot = (expert == pick) & (slot >= 0.0)
        gate = jnp.sum(jnp.where(hot & (kind == 0), prob_ref[...], 0.0), 1, keepdims=True)
        values = jnp.zeros((tokens, 128), jnp.float32)
        pieces = [*split_three(gate), *split_three(pool), image]
        for index, piece in enumerate(pieces):
            values = jnp.where(kind == index, piece.astype(jnp.float32), values)
        values = jnp.where(hot, values, 0.0).astype(jnp.bfloat16)
        spot = jnp.where(slot >= 0.0, slot - pick * padded, -1.0)
        chosen = jnp.where(spot == slot_lane, 1.0, 0.0).astype(jnp.bfloat16)
        found = dot_f32(values, chosen, TN)
        details = found if details is None else details + found
    n = n_experts
    gates = details[0:n] + details[n : 2 * n] + details[2 * n : 3 * n]
    pools = details[3 * n : 4 * n] + details[4 * n : 5 * n] + details[5 * n : 6 * n]
    images = details[6 * n : 7 * n]
    for index in range(n):
        for spot, value in enumerate((gates, pools, images)):
            send_detail[index, spot : spot + 1] = value[index : index + 1]
        send_detail[index, 3:8] = jnp.zeros((5, send_detail.shape[2]), jnp.float32)

    def rows_of(member):
        slots = lax.broadcasted_iota(jnp.int32, (padded, tokens), 0) + member * padded
        slots = slots.astype(jnp.float32)
        match = (slots == places[0:1]) | (slots == places[1:2])
        match = jnp.where(match, 1.0, 0.0).astype(jnp.bfloat16)
        send_rows[member] = dot_f32(match, a_two_ref[...], NN).astype(jnp.bfloat16)

    def row_copy(member, source):
        return send(
            send_rows.at[member], rows_ref.at[source], r_out.at[member], r_in.at[source], at.of_member(member)
        )

    def detail_copy(member, source):
        return send(
            send_detail.at[member], detail_ref.at[source], m_out.at[member], m_in.at[source], at.of_member(member)
        )

    def step(index, carry):
        member = lax.rem(at.member + index, n_experts)
        rows_of(member)
        row_copy(member, at.member).start()
        detail_copy(member, at.member).start()
        return carry

    lax.fori_loop(1, n_experts, step, 0)
    rows_of(at.member)
    keep_rows = pltpu.make_async_copy(send_rows.at[at.member], rows_ref.at[at.member], own_sem.at[0])
    keep_detail = pltpu.make_async_copy(send_detail.at[at.member], detail_ref.at[at.member], own_sem.at[1])
    keep_rows.start()
    keep_detail.start()
    for member in team:
        row_copy(member, member).wait_recv()
        detail_copy(member, member).wait_recv()
    for member in team:
        row_copy(member, at.member).wait_send()
        detail_copy(member, at.member).wait_send()
    keep_rows.wait()
    keep_detail.wait()


def dispatch(sizes, n_experts, padded, a_two, probs, columns):
    tokens, width = a_two.shape
    lanes = round_up(padded, 128)
    dma = pltpu.SemaphoreType.DMA
    each = dma((n_experts,))
    return pl.pallas_call(
        functools.partial(dispatch_kernel, sizes, n_experts, padded),
        out_shape=(
            jax.ShapeDtypeStruct((n_experts, padded, width), jnp.bfloat16),
            jax.ShapeDtypeStruct((n_experts, 8, lanes), jnp.float32),
        ),
        in_specs=[whole()] * 3,
        out_specs=(whole(ANY), whole(ANY)),
        scratch_shapes=[
            VMEM((n_experts, padded, width), jnp.bfloat16),
            VMEM((n_experts, 8, lanes), jnp.float32),
            VMEM((8, tokens), jnp.float32),
            dma((2,)), each, each, each, each,
        ],
        compiler_params=pltpu.CompilerParams(
            collective_id=5, has_side_effects=True, vmem_limit_bytes=48 * MIB
        ),
        cost_estimate=cost(50),
        name="dispatch",
    )(a_two, probs, columns)


def image_hot(detail, padded):
    image = detail[2:3, :padded]
    line = lax.broadcasted_iota(jnp.int32, (IMAGE_PAD, padded), 0).astype(jnp.float32)
    return line == image


TILE = 32


def tiles(count):
    return [slice(start, min(start + TILE, count)) for start in range(0, count, TILE)]


def expert_forward_kernel(sizes, padded, rows_ref, detail_ref, *refs):
    at = Place(sizes)
    half = len(refs) - 11
    chunks = refs[:half]
    act_ref, slope_ref, y_ref, part_ref, other_ref = refs[half : half + 5]
    weights, total, own_sem, s_out, s_in, keep_sem = refs[half + 5 :]
    many, unused, width = rows_ref.shape
    count = many * padded
    turn, block = pl.program_id(0), pl.program_id(1)

    def own_copy(index):
        return pltpu.make_async_copy(chunks[index], weights.at[0, index], own_sem.at[index])

    def swap_copy(index):
        return send(
            chunks[index], weights.at[1, index], s_out.at[index], s_in.at[index], at.sibling()
        )

    def keep_copy():
        return pltpu.make_async_copy(weights.at[1], other_ref, keep_sem.at[0])

    @pl.when((turn == 0) & (block == 0))
    def _():
        for index in range(half):
            own_copy(index).start()
        greet([at.sibling()])
        for index in range(half):
            swap_copy(index).start()
        for index in range(half):
            own_copy(index).wait()

    @pl.when((turn == 1) & (block == 0))
    def _():
        for index in range(half):
            swap_copy(index).wait_recv()
        keep_copy().start()

    rows = rows_ref[...].reshape(count, width)
    for index in range(half):
        hidden_all = dot_f32(rows, weights[turn, index, 0], NT)
        for spot in tiles(count):
            hidden = hidden_all[spot]
            square = hidden * hidden
            curve = jnp.tanh(hidden * (0.7978845608 + 0.7978845608 * 0.044715 * square))
            upper = 0.5 + 0.5 * curve
            gelu = hidden * upper
            slope = upper + gelu * (1.0 - upper) * (
                2.0 * 0.7978845608 + 6.0 * 0.7978845608 * 0.044715 * square
            )
            act_ref[index, spot] = gelu.astype(jnp.bfloat16)
            slope_ref[index, spot] = slope.astype(jnp.bfloat16)
    acts = jnp.concatenate([act_ref[index] for index in range(half)], 1)
    ends = jnp.concatenate([weights[turn, index, 1] for index in range(half)], 0)
    found = dot_f32(acts, ends, NN)
    span = pl.ds(pl.multiple_of(block * count, 16), count)

    @pl.when(turn == 0)
    def _():
        total[span] = found

    @pl.when(turn == 1)
    def _():
        result = (total[span] + found).astype(jnp.bfloat16)
        y_ref[...] = result.reshape(many, padded, width)
        for source in range(many):
            detail = detail_ref[source]
            weight = detail[0:1, :padded] * detail[1:2, :padded]
            shares = jnp.where(image_hot(detail, padded), weight, 0.0)
            pieces = jnp.concatenate(split_three(shares), 0)
            sums = dot_f32(pieces, result[source * padded : (source + 1) * padded], NN)
            part_ref[source] = (
                sums[:IMAGE_PAD] + sums[IMAGE_PAD : 2 * IMAGE_PAD] + sums[2 * IMAGE_PAD :]
            )

    @pl.when((turn == 1) & (block == pl.num_programs(1) - 1))
    def _():
        for index in range(half):
            swap_copy(index).wait_send()
        keep_copy().wait()


def expert_forward(sizes, rows, details, chunks):
    sources, padded, width = rows.shape
    half = len(chunks)
    part = chunks[0].shape[1]
    many = max(1, 576 // padded)
    lanes = details.shape[2]
    kind = jnp.bfloat16
    dma = pltpu.SemaphoreType.DMA

    def by_source(*shape):
        return pl.BlockSpec((many, *shape), lambda t, i: (i, 0, 0))

    def late(*shape):
        return pl.BlockSpec((many, *shape), lambda t, i: (i * t, 0, 0))

    flat = pl.BlockSpec((half, many * padded, part), lambda t, i: (t, i, 0))
    return pl.pallas_call(
        functools.partial(expert_forward_kernel, sizes, padded),
        grid=(2, sources // many),
        out_shape=(
            jax.ShapeDtypeStruct((2 * half, sources * padded, part), kind),
            jax.ShapeDtypeStruct((2 * half, sources * padded, part), kind),
            jax.ShapeDtypeStruct((sources, padded, width), kind),
            jax.ShapeDtypeStruct((sources, IMAGE_PAD, width), jnp.float32),
            jax.ShapeDtypeStruct((half, 2, part, width), kind),
        ),
        in_specs=[by_source(padded, width), by_source(8, lanes)] + [whole(ANY)] * half,
        out_specs=(flat, flat, late(padded, width), late(IMAGE_PAD, width), whole(ANY)),
        scratch_shapes=[
            VMEM((2, half, 2, part, width), kind),
            VMEM((sources * padded, width), jnp.float32),
            dma((half,)), dma((half,)), dma((half,)), dma((1,)),
        ],
        compiler_params=pltpu.CompilerParams(
            collective_id=7, has_side_effects=True, vmem_limit_bytes=56 * MIB
        ),
        cost_estimate=cost(40),
        name="expert_forward",
    )(rows, details, *chunks)


def expert_backward_kernel(
    sizes, padded, rows_ref, detail_ref, pool_ref, y_ref, slope_ref, act_ref, other_ref, *refs
):
    at = Place(sizes)
    sources, unused, width = rows_ref.shape
    chunks, unused, part = slope_ref.shape
    half = chunks // 2
    own_refs, refs = refs[:half], refs[half:]
    back_ref, gate_ref, *outs = refs[: 2 + half]
    d_hidden, d_rows, send_rows, send_gate, send_grad, got_grad = refs[2 + half : 8 + half]
    own_sem, r_out, r_in, m_out, m_in, g_out, g_in, g_keep = refs[8 + half :]
    many = y_ref.shape[0]
    rounds = sources // many
    step = pl.program_id(0)
    team = others(at.member, sources)

    def row_copy(member, source):
        return send(
            send_rows.at[member], back_ref.at[source], r_out.at[member], r_in.at[source], at.of_member(member)
        )

    def gate_copy(member, source):
        return send(
            send_gate.at[member], gate_ref.at[source], m_out.at[member], m_in.at[source], at.of_member(member)
        )

    def keep_copies():
        return (
            pltpu.make_async_copy(send_rows.at[at.member], back_ref.at[at.member], own_sem.at[0]),
            pltpu.make_async_copy(send_gate.at[at.member], gate_ref.at[at.member], own_sem.at[1]),
        )

    def grad_copy(index):
        return send(
            send_grad.at[index], got_grad.at[index], g_out.at[index], g_in.at[index], at.sibling()
        )

    def out_copy(index):
        return pltpu.make_async_copy(got_grad.at[index], outs[index], g_keep.at[index])

    @pl.when(step == 0)
    def _():
        greet([at.of_member(member) for member in team] + [at.sibling()])

    @pl.when(step < rounds)
    def _():
        block = lax.rem(lax.div(at.member, many) + 1 + step, rounds)
        d_out = []
        for index in range(many):
            source = block * many + index
            detail = detail_ref[source]
            hot = image_hot(detail, padded)
            hots = jnp.where(hot, 1.0, 0.0).astype(jnp.bfloat16)
            pools = jnp.concatenate(split_three(pool_ref[source]), 0)
            wide = dot_f32(jnp.concatenate([hots] * 3, 0), pools, TN)
            lanes = detail.shape[1]
            upright = jnp.concatenate([detail, jnp.zeros((120, lanes), jnp.float32)], 0).T
            gate, pool = upright[:padded, 0:1], upright[:padded, 1:2]
            d_out.append((gate * (pool * wide)).astype(jnp.bfloat16))
            along = dot_f32(pools, y_ref[index], NT)
            along = along[:IMAGE_PAD] + along[IMAGE_PAD : 2 * IMAGE_PAD] + along[2 * IMAGE_PAD :]
            d_gate = jnp.sum(jnp.where(hot, along, 0.0), 0, keepdims=True) * detail[1:2, :padded]
            send_gate[source] = jnp.zeros(detail.shape, jnp.float32)
            send_gate[source, 0:1, :padded] = d_gate
        d_out = jnp.concatenate(d_out, 0)
        count = many * padded
        span = pl.ds(pl.multiple_of(block * count, 16), count)
        d_rows[span] = d_out

        def weight(index, which):
            return own_refs[index][which] if index < half else other_ref[index - half, which]

        for index in range(chunks):
            d_act = dot_f32(d_out, weight(index, 1), NT)
            for spot in tiles(count):
                rows_now = pl.ds(pl.multiple_of(block * count + spot.start, 16), spot.stop - spot.start)
                d_hidden[index, rows_now] = (
                    d_act[spot] * slope_ref[index, spot].astype(jnp.float32)
                ).astype(jnp.bfloat16)
        d_hids = jnp.concatenate([d_hidden[index, span] for index in range(chunks)], 1)
        starts = jnp.concatenate([weight(index, 0) for index in range(chunks)], 0)
        total = dot_f32(d_hids, starts, NN)
        total = total.astype(jnp.bfloat16)
        for index in range(many):
            source = block * many + index
            send_rows[source] = total[index * padded : (index + 1) * padded]

            @pl.when(source != at.member)
            def _():
                row_copy(source, at.member).start()
                gate_copy(source, at.member).start()

            @pl.when(source == at.member)
            def _():
                for copy in keep_copies():
                    copy.start()

    @pl.when(step >= rounds)
    def _():
        index = step - rounds
        chunk = lax.rem(index + half, chunks)
        rows = rows_ref[...].reshape(sources * padded, width)
        g_one = dot_f32(d_hidden[chunk], rows, TN)
        g_two = dot_f32(act_ref[0], d_rows[...], TN)

        @pl.when(index < half)
        def _():
            send_grad[index, 0] = g_one.astype(jnp.bfloat16)
            send_grad[index, 1] = g_two.astype(jnp.bfloat16)
            grad_copy(index).start()

        @pl.when(index >= half)
        def _():
            spot = index - half
            grad_copy(spot).wait_recv()
            got_grad[spot, 0] = (got_grad[spot, 0].astype(jnp.float32) + g_one).astype(jnp.bfloat16)
            got_grad[spot, 1] = (got_grad[spot, 1].astype(jnp.float32) + g_two).astype(jnp.bfloat16)

        for spot in range(half):

            @pl.when(index == spot + half)
            def _():
                out_copy(spot).start()

    @pl.when(step == rounds + chunks - 1)
    def _():
        for member in team:
            row_copy(member, member).wait_recv()
            gate_copy(member, member).wait_recv()
        for member in team:
            row_copy(member, at.member).wait_send()
            gate_copy(member, at.member).wait_send()
        for copy in keep_copies():
            copy.wait()
        for spot in range(half):
            grad_copy(spot).wait_send()
            out_copy(spot).wait()


def expert_backward(sizes, rows, details, pools, results, slopes, acts, chunks_own, other):
    sources, padded, width = rows.shape
    chunks, count, part = acts.shape
    many = max(1, (288 if part % 128 else 576) // padded)
    rounds, half = sources // many, chunks // 2
    lanes = details.shape[2]
    kind = jnp.bfloat16
    dma = pltpu.SemaphoreType.DMA
    each, parts = dma((sources,)), dma((half,))

    def block_of(step):
        member = lax.axis_index("x") * QUAD + lax.axis_index("r")
        return lax.rem(lax.div(member, many) + 1 + jnp.minimum(step, rounds - 1), rounds)

    def chunk_of(step):
        return lax.rem(jnp.maximum(step - rounds, 0) + half, chunks)

    return pl.pallas_call(
        functools.partial(expert_backward_kernel, sizes, padded),
        grid=(rounds + chunks,),
        out_shape=(
            jax.ShapeDtypeStruct((sources, padded, width), kind),
            jax.ShapeDtypeStruct((sources, 8, lanes), jnp.float32),
        )
        + (jax.ShapeDtypeStruct((2, part, width), kind),) * half,
        in_specs=[
            whole(), whole(), whole(),
            pl.BlockSpec((many, padded, width), lambda i: (block_of(i), 0, 0)),
            pl.BlockSpec((chunks, many * padded, part), lambda i: (0, block_of(i), 0)),
            pl.BlockSpec((1, count, part), lambda i: (chunk_of(i), 0, 0)),
        ]
        + [whole()] * (1 + half),
        out_specs=(whole(ANY),) * (2 + half),
        scratch_shapes=[
            VMEM((chunks, count, part), kind),
            VMEM((count, width), kind),
            VMEM((sources, padded, width), kind),
            VMEM((sources, 8, lanes), jnp.float32),
            VMEM((half, 2, part, width), kind),
            VMEM((half, 2, part, width), kind),
            dma((2,)), each, each, each, each, parts, parts, parts,
        ],
        compiler_params=pltpu.CompilerParams(
            collective_id=6, has_side_effects=True, vmem_limit_bytes=62 * MIB
        ),
        cost_estimate=cost(65),
        name="expert_backward",
    )(rows, details, pools, results, slopes, acts, other, *chunks_own)


def dense_backward_kernel(
    sizes, n_experts, images, padded, length_ref, mask_ref, patch_ref, x_zero_ref, a_one_ref, qkv_ref, att_ref,
    x_one_ref, a_two_ref, prob_ref, lse_ref, col_ref, w_ref, gain_ref, router_ref, back_ref, gate_ref,
    pool_ref, imp_ref, third_ref, out_ref, grads, g_router, g_norm, d_qkv
):
    row = pl.program_id(0)
    span, width = patch_ref.shape
    mats, rows = grads.shape[0], width // (8 * sizes["g"] * sizes["x"])

    @pl.when(row == 0)
    def _():
        grads[...] = jnp.zeros_like(grads)
        g_router[...] = jnp.zeros_like(g_router)
        g_norm[...] = third_ref[...]

    columns = col_ref[...]
    slot_one, slot_two = columns[:, 0:1], columns[:, 1:2]
    count = n_experts * padded
    slot = lax.broadcasted_iota(jnp.int32, (span, count), 1).astype(jnp.float32)
    match = jnp.where((slot == slot_one) | (slot == slot_two), 1.0, 0.0).astype(jnp.bfloat16)
    d_a_two = dot_f32(match, back_ref[...].reshape(count, width), NN)
    lanes = gate_ref.shape[2]
    spot = lax.broadcasted_iota(jnp.int32, (span, lanes), 1)
    inside = spot < padded
    spot = spot.astype(jnp.float32)
    found_one, found_two = jnp.zeros((span, lanes), jnp.float32), jnp.zeros((span, lanes), jnp.float32)
    for expert in range(n_experts):
        line = jnp.broadcast_to(gate_ref[expert, 0:1], (span, lanes))
        found_one = jnp.where(inside & (spot == slot_one - expert * padded), line, found_one)
        found_two = jnp.where(inside & (spot == slot_two - expert * padded), line, found_two)
    d_gate_one = jnp.sum(found_one, 1, keepdims=True)
    d_gate_two = jnp.sum(found_two, 1, keepdims=True)
    lane = lax.broadcasted_iota(jnp.int32, (span, 128), 1)
    number = lane.astype(jnp.float32)
    valid, pool, image = columns[:, 2:3], columns[:, 3:4], columns[:, 4:5]
    head = lax.broadcasted_iota(jnp.int32, (1, 128), 1) < n_experts
    importance = imp_ref[0:1, 0:128]
    centre = jnp.sum(jnp.where(head, importance, 0.0), 1, keepdims=True) / n_experts
    away = jnp.where(head, importance - centre, 0.0)
    spread = jnp.sum(away * away, 1, keepdims=True) / n_experts
    d_imp = aux_weight * (
        2.0 * away / (n_experts * centre * centre)
        - 2.0 * spread / (n_experts * centre * centre * centre)
    )
    d_probs = valid * d_imp
    d_probs = d_probs + jnp.where(number == columns[:, 5:6], d_gate_one, 0.0)
    d_probs = d_probs + jnp.where(number == columns[:, 6:7], d_gate_two, 0.0)
    probs = prob_ref[...]
    d_router = (probs * (d_probs - jnp.sum(probs * d_probs, 1, keepdims=True))).astype(jnp.bfloat16)
    g_router[...] += dot_f32(d_router, a_two_ref[...], TN)
    routers = router_ref[...].astype(jnp.bfloat16)
    if routers.shape[0] < 128:
        routers = jnp.concatenate(
            [routers, jnp.zeros((128 - routers.shape[0], width), jnp.bfloat16)], 0
        )
    d_a_two = d_a_two + dot_f32(d_router, routers, NN)
    scaled, scale = norm_parts(x_one_ref[...])
    g_norm[1:2] += jnp.sum(d_a_two * scaled, 0, keepdims=True)
    g_norm[4:5] += jnp.sum(d_a_two, 0, keepdims=True)
    d_x_one = norm_back(d_a_two, scaled, scale, gain_ref[1:2])
    for index in range(images):
        place = row * images + index
        weight = jnp.where(image == place.astype(jnp.float32), pool, 0.0)
        d_x_one = d_x_one + weight * pool_ref[pl.ds(place, 1)]
    d_att = d_x_one.astype(jnp.bfloat16)
    grads[4] += dot_f32(att_ref[...], d_att, TN)
    d_out = dot_f32(d_att, w_ref[4], NT).astype(jnp.bfloat16)
    open_to = allowed_slots(length_ref, row, images, mask_ref[0], span)
    logs = lse_ref[...]
    for pair in range(width // 128):
        query, key, value = (
            qkv_ref[:, part * width + pair * 128 : part * width + (pair + 1) * 128]
            for part in range(3)
        )
        d_pair = d_out[:, pair * 128 : (pair + 1) * 128]
        found = []
        for side in range(2):
            left = (lane < 64) == (side == 0)
            held = jnp.where(left, query, jnp.zeros_like(query))
            scores = jnp.where(open_to, dot_f32(held, key, NT) * 64**-0.5, mask_fill)
            total = logs[:, 2 * pair + side : 2 * pair + side + 1]
            chance = jnp.exp(scores - total)
            d_held = jnp.where(left, d_pair, jnp.zeros_like(d_pair))
            d_chance = dot_f32(d_held, value, NT)
            d_value = dot_f32(chance.astype(jnp.bfloat16), d_pair, TN)
            d_scores = chance * (d_chance - jnp.sum(chance * d_chance, 1, keepdims=True))
            d_scores = d_scores.astype(jnp.bfloat16)
            d_query = dot_f32(d_scores, key, NN) * 64**-0.5
            d_key = dot_f32(d_scores, query, TN) * 64**-0.5
            found.append((d_query, d_key, d_value))
        for part in range(3):
            d_qkv[:, part * width + pair * 128 : part * width + (pair + 1) * 128] = jnp.where(
                lane < 64, found[0][part], found[1][part]
            ).astype(jnp.bfloat16)
    d_a_one = None
    for part in range(3):
        piece = d_qkv[:, part * width : (part + 1) * width]
        grads[1 + part] += dot_f32(a_one_ref[...], piece, TN)
        found = dot_f32(piece, w_ref[1 + part], NT)
        d_a_one = found if d_a_one is None else d_a_one + found
    scaled, scale = norm_parts(x_zero_ref[...])
    g_norm[0:1] += jnp.sum(d_a_one * scaled, 0, keepdims=True)
    g_norm[3:4] += jnp.sum(d_a_one, 0, keepdims=True)
    d_x_zero = norm_back(d_a_one, scaled, scale, gain_ref[0:1]) + d_x_one
    grads[0] += dot_f32(patch_ref[...], d_x_zero.astype(jnp.bfloat16), TN)

    @pl.when(row == pl.num_programs(0) - 1)
    def _():
        Z, Y, X = QUAD, sizes["g"], sizes["x"]
        tall = max(8, n_experts)
        norms = g_norm[...]
        if tall > 8:
            norms = jnp.concatenate([norms, jnp.zeros((tall - 8, width), jnp.float32)], 0)
        router_grads = g_router[:tall]
        depth = out_ref.shape[4]
        device = 0
        for z in range(Z):
            for y in range(Y):
                for x in range(X):
                    for c in range(2):
                        spot = slice(device * rows, (device + 1) * rows)
                        blank = jnp.zeros((tall, 128 - rows), jnp.float32)
                        tail = [norms[:, spot], blank, router_grads[:, spot], blank]
                        tail.append(jnp.zeros((tall, width - 256), jnp.float32))
                        pieces = [grads[mat, spot] for mat in range(mats)]
                        pieces.append(jnp.concatenate(tail, 1))
                        left = depth - mats * rows - tall
                        if left:
                            pieces.append(jnp.zeros((left, width), jnp.float32))
                        out_ref[c, z, x, y] = jnp.concatenate(pieces, 0).astype(jnp.bfloat16)
                        device += 1


def dense_backward(
    sizes, n_experts, padded, rows_own, lengths, slot_mask, patches, kept, columns, weights, gains, routers, back,
    gates, pooled, importance, third
):
    rows_here, span = slot_mask.shape
    tokens, width = patches.shape
    mats = weights.shape[0]
    depth = round_up(mats * rows_own + max(8, n_experts), 16)
    x_zero, a_one, qkv, att, x_one, a_two, probs, logs = kept

    def block(wide):
        return pl.BlockSpec((span, wide), lambda i: (i, 0))

    return pl.pallas_call(
        functools.partial(dense_backward_kernel, sizes, n_experts, lengths.shape[1], padded),
        grid=(rows_here,),
        out_shape=jax.ShapeDtypeStruct(
            (2, QUAD, sizes["x"], sizes["g"], depth, width), jnp.bfloat16
        ),
        in_specs=[
            whole(pltpu.SMEM), pl.BlockSpec((1, 1, span), lambda i: (i, 0, 0)), block(width),
            block(width), block(width), block(3 * width), block(width), block(width), block(width),
            block(128), block(128), block(128),
        ]
        + [whole()] * 8,
        out_specs=whole(),
        scratch_shapes=[
            VMEM((mats, width, width), jnp.float32),
            VMEM((128, width), jnp.float32),
            VMEM((8, width), jnp.float32),
            VMEM((span, 3 * width), jnp.bfloat16),
        ],
        compiler_params=pltpu.CompilerParams(vmem_limit_bytes=60 * MIB),
        cost_estimate=cost(50),
        name="dense_backward",
    )(
        lengths, slot_mask[:, None, :], patches, x_zero, a_one, qkv, att, x_one, a_two, probs, logs, columns,
        weights, gains, routers, back, gates, pooled, importance, third,
    )


def shard_moves(n_blocks):
    span = 2 * n_blocks
    moves = []
    for step in range(span):
        pairs = []
        for place in range(QUAD * n_blocks):
            for core in range(2):
                target = (place + step) % span
                src = place * 2 + core
                dst = (target // 2 * QUAD + 2 * core + target % 2) * 2 + place // span
                pairs.append((src, dst))
        moves.append(pairs)
    return moves


def order_shards(expert_in, expert_out):
    place = lax.axis_index("g") * QUAD + lax.axis_index("r")
    odd = lax.rem(place, 2) == 1
    both = jnp.stack([expert_in, expert_out], 1).astype(jnp.bfloat16)
    return [jnp.where(odd, both[1], both[0]), jnp.where(odd, both[0], both[1])]


def fetch_experts(shards, n_blocks, steps):
    moves = shard_moves(n_blocks)
    return [lax.ppermute(shards[step % 2], ("g", "r", "c"), moves[step]) for step in steps]


def return_experts(parts, n_blocks):
    place = lax.axis_index("g") * QUAD + lax.axis_index("r")
    odd = lax.rem(place, 2) == 1
    sums = [None, None]
    for step, pairs in enumerate(shard_moves(n_blocks)):
        back = lax.ppermute(parts[step], ("g", "r", "c"), [(dst, src) for src, dst in pairs])
        back = back.astype(jnp.float32)
        sums[step % 2] = back if sums[step % 2] is None else sums[step % 2] + back
    zero, one = jnp.where(odd, sums[1], sums[0]), jnp.where(odd, sums[0], sums[1])
    return jnp.stack([zero[0], one[0]]), jnp.stack([zero[1], one[1]])


def body(
    patches,
    lengths,
    slot_mask,
    expert_picks,
    priority_rank,
    class_labels,
    dense_weights,
    dense_first,
    dense_second,
    dense_average,
    router_weights,
    router_first,
    router_second,
    router_average,
    norm_params,
    norm_first,
    norm_second,
    norm_average,
    expert_in,
    in_first,
    in_second,
    in_average,
    expert_out,
    out_first,
    out_second,
    out_average,
    head_weights,
    head_first,
    head_second,
    head_average,
):
    n_blocks = lax.axis_size("g")
    sizes = {name: lax.axis_size(name) for name in ALL}
    rows_own, n_experts = router_weights.shape
    n_tail = max(8, n_experts)
    tail = jnp.zeros((n_tail, dense_weights.shape[2]), jnp.float32)
    tail = tail.at[:6, :rows_own].set(norm_params)
    tail = tail.at[:n_experts, 128 : 128 + rows_own].set(router_weights.T)
    rows_here, n_slots_row = slot_mask.shape
    tokens, model_width = patches.shape
    n_images = lengths.shape[0] * lengths.shape[1]
    capacity = (21 * tokens * TOP + 20 * n_experts - 1) // (20 * n_experts)
    padded = round_up(capacity, 16)
    shards = order_shards(expert_in, expert_out)
    own_chunks = fetch_experts(shards, n_blocks, range(EARLY))
    layer_b, gain_rows, router_t, columns = gather_weights(
        sizes,
        (lengths.shape[1], n_experts, capacity, padded),
        dense_weights,
        tail,
        expert_picks,
        priority_rank,
        slot_mask,
        lengths,
    )
    shards, layer_b = lax.optimization_barrier((shards, layer_b))
    own_chunks += fetch_experts(shards, n_blocks, range(EARLY, 2 * n_blocks))
    x_zero, a_one, qkv, att_out, x_one, a_two, router_probs, logs, pooled, part_importance = (
        dense_forward(
            n_experts, lengths, slot_mask, patches, layer_b, gain_rows, router_t, columns
        )
    )
    arrived, details = dispatch(sizes, n_experts, padded, a_two, router_probs, columns)
    activated, slope, result, part_pooled, other_chunks = expert_forward(
        sizes, arrived, details, own_chunks
    )
    g_head, d_pooled_all, d_pooled, g_norm_three, local_loss, total_importance = head_step(
        sizes,
        n_images,
        part_pooled,
        pooled,
        part_importance,
        gain_rows,
        head_weights,
        class_labels,
    )
    d_back, back_gate, *grads = expert_backward(
        sizes, arrived, details, d_pooled_all, result, slope, activated, own_chunks, other_chunks
    )
    g_one, g_two = return_experts(grads, n_blocks)
    blocks = dense_backward(
        sizes,
        n_experts,
        padded,
        rows_own,
        lengths,
        slot_mask,
        patches,
        (x_zero, a_one, qkv, att_out, x_one, a_two, router_probs, logs),
        columns,
        layer_b,
        gain_rows,
        router_t,
        d_back,
        back_gate,
        d_pooled,
        total_importance,
        g_norm_three,
    )
    reduced = scatter_dense(sizes, blocks)
    n_dense = dense_weights.shape[0] * rows_own
    g_layers = reduced[:n_dense].reshape(-1, rows_own, model_width)
    g_norms = reduced[n_dense : n_dense + 6, :rows_own]
    g_router = reduced[n_dense : n_dense + n_experts, 128 : 128 + rows_own].T
    importance = total_importance[0, :n_experts]
    local_loss = local_loss[0, 0]
    centre = jnp.mean(importance)
    spread = jnp.mean((importance - centre) ** 2)
    squares = (
        jnp.sum(g_layers * g_layers) + jnp.sum(g_router * g_router) + jnp.sum(g_norms * g_norms)
    )
    squares = squares + jnp.sum(g_one * g_one) + jnp.sum(g_two * g_two) + jnp.sum(g_head * g_head)
    line = lax.broadcasted_iota(jnp.int32, (8, 128), 0)
    all_sums = share_sums(sizes, jnp.where(line == 0, local_loss, squares))
    loss_sum, square_sum = all_sums[0, 0], all_sums[1, 0]
    grad_norm = jnp.sqrt(square_sum)
    factor = jnp.minimum(1.0, clip_limit / grad_norm)
    loss_value = loss_sum + aux_weight * spread / (centre * centre)
    dense_out = adam_update(
        dense_weights, dense_first, dense_second, dense_average, g_layers, factor, base_rate
    )
    router_out = adam_update(
        router_weights, router_first, router_second, router_average, g_router, factor, base_rate
    )
    norm_out = adam_update(
        norm_params, norm_first, norm_second, norm_average, g_norms, factor, norm_rate
    )
    in_out = adam_update(expert_in, in_first, in_second, in_average, g_one, factor, base_rate)
    out_out = adam_update(expert_out, out_first, out_second, out_average, g_two, factor, base_rate)
    head_out = adam_update(
        head_weights, head_first, head_second, head_average, g_head, factor, base_rate
    )
    return (
        loss_value,
        importance,
        grad_norm,
        *dense_out,
        *router_out,
        *norm_out,
        *in_out,
        *out_out,
        *head_out,
    )


def solution(mesh):
    n_dp, n_expert = mesh.shape["dp"], mesh.shape["expert"]
    shaped = mesh.devices.reshape(n_dp // QUAD, QUAD, n_expert // 2, 2)
    fine = Mesh(shaped, ALL)
    rows = P(ALL, None)
    dense = P(None, ALL, None)
    norms = P(None, ALL)
    experts = P(("x", "c"), ("g", "r"), None)
    placed = (rows,) * 6 + (dense,) * 4 + (rows,) * 4 + (norms,) * 4 + (experts,) * 8 + (rows,) * 4
    results = (
        (P(),) * 3 + (dense,) * 4 + (rows,) * 4 + (norms,) * 4 + (experts,) * 8 + (rows,) * 4
    )
    return jax.shard_map(body, mesh=fine, in_specs=placed, out_specs=results, check_vma=False)
```

```python
import functools
import math

import jax
import jax.numpy as jnp
from jax import lax
from jax.experimental import pallas as pl
from jax.experimental.pallas import tpu as pltpu
from jax.sharding import Mesh
from jax.sharding import PartitionSpec as P

HEADS = 12
TOP = 2
STEP_COUNT = 10
QUAD = 4

high_prec = lax.Precision.HIGHEST
eps_norm = 1e-06
aux_weight = 0.01
clip_limit = 1.0
base_rate = 0.05
norm_rate = 0.5
beta_first = 0.9
beta_second = 0.999
weight_decay = 0.1
polyak_decay = 0.7
adam_eps = 1e-08
mask_fill = -1e30

ALL = ("g", "r", "x", "c")
MEMBERS = ("x", "r")


def adam_update(weight, first_state, second_state, average_state, gradient, factor, step_rate):
    clipped = gradient * factor
    first_new = beta_first * first_state + (1.0 - beta_first) * clipped
    second_new = beta_second * second_state + (1.0 - beta_second) * clipped * clipped
    first_hat = first_new / (1.0 - beta_first**STEP_COUNT)
    second_hat = second_new / (1.0 - beta_second**STEP_COUNT)
    weight_new = weight - step_rate * (
        first_hat / (jnp.sqrt(second_hat) + adam_eps) + weight_decay * weight
    )
    average_new = polyak_decay * average_state + (1.0 - polyak_decay) * weight_new
    return (weight_new, first_new, second_new, average_new)


MESH_ID = pl.DeviceIdType.MESH
VMEM = pltpu.VMEM
ANY = pl.ANY
MIB = 1 << 20


def cost(microseconds):
    return pl.CostEstimate(flops=int(microseconds * 1.15e9), bytes_accessed=0, transcendentals=0)


def whole(space=None):
    return pl.BlockSpec(memory_space=space or VMEM)


def round_up(value, step):
    return (value + step - 1) // step * step


class Place:
    def __init__(self, sizes):
        self.G, self.X = sizes["g"], sizes["x"]
        self.Z, self.Y = QUAD, sizes["g"]
        self.chips = self.Z * self.Y * self.X
        spot = lax.axis_index("g") * QUAD + lax.axis_index("r")
        self.z, self.y = lax.div(spot, self.Y), lax.rem(spot, self.Y)
        self.x, self.c = lax.axis_index("x"), lax.axis_index("c")
        self.g, self.r = lax.axis_index("g"), lax.axis_index("r")
        self.chip = spot * self.X + self.x
        self.member = self.x * QUAD + self.r

    def at(self, z=None, y=None, x=None, c=None):
        spot = (self.z if z is None else z) * self.Y + (self.y if y is None else y)
        return {
            "g": lax.div(spot, QUAD),
            "r": lax.rem(spot, QUAD),
            "x": self.x if x is None else x,
            "c": self.c if c is None else c,
        }

    def of_chip(self, chip):
        spot = lax.div(chip, self.X)
        return {
            "g": lax.div(spot, QUAD),
            "r": lax.rem(spot, QUAD),
            "x": lax.rem(chip, self.X),
            "c": self.c,
        }

    def of_member(self, member):
        return {
            "g": self.g,
            "r": lax.rem(member, QUAD),
            "x": lax.div(member, QUAD),
            "c": self.c,
        }

    def sibling(self):
        return self.at(c=1 - self.c)


def greet(peers):
    barrier = pltpu.get_barrier_semaphore()
    for peer in peers:
        pl.semaphore_signal(barrier, inc=1, device_id=peer, device_id_type=MESH_ID)
    pl.semaphore_wait(barrier, len(peers))


def send(src, dst, send_sem, recv_sem, peer):
    return pltpu.make_async_remote_copy(
        src_ref=src,
        dst_ref=dst,
        send_sem=send_sem,
        recv_sem=recv_sem,
        device_id=peer,
        device_id_type=MESH_ID,
    )


def others(me, count):
    return [lax.rem(me + step, count) for step in range(1, count)]


def grid_peers(at):
    peers = [at.at(z=z) for z in others(at.z, at.Z)]
    peers += [at.at(y=y) for y in others(at.y, at.Y)]
    peers += [at.at(x=x) for x in others(at.x, at.X)]
    return peers + [at.sibling()]


def gather_kernel(
    sizes, rows, mats, routing, dense_ref, tail_ref, pick_ref, rank_ref, mask_ref, length_ref,
    w_ref, gain_ref, router_ref, col_ref, land, *sems
):
    at = Place(sizes)
    Z, Y, X = at.Z, at.Y, at.X
    depth = land.shape[4]
    cut = depth // 2 // 16 * 16
    first, second = pl.ds(0, cut), pl.ds(cut, depth - cut)
    z_out, z_in, ya_out, ya_in, xb_out, xb_in, xa_out, xa_in, yb_out, yb_in, c_out, c_in = sems
    block = jnp.concatenate([dense_ref[...].reshape(mats * rows, -1), tail_ref[...]], 0)
    if block.shape[0] < depth:
        block = jnp.pad(block, ((0, depth - block.shape[0]), (0, 0)))
    mine = land.at[at.c, at.z, at.x, at.y]
    mine[...] = block.astype(jnp.bfloat16)
    greet(grid_peers(at))
    started = []

    def begin(copy):
        copy.start()
        started.append(copy)

    order = [at.z] + [lax.rem(at.z + k, Z) for k in (1, 3, 2)]
    for z in order[1:]:
        begin(send(mine, mine, z_out.at[z], z_in.at[at.z], at.at(z=z)))

    def one(z):
        part = land.at[at.c, z, at.x, at.y]
        for y in others(at.y, Y):
            begin(send(part.at[first], part.at[first], ya_out.at[z, y], ya_in.at[z, at.y], at.at(y=y)))
        for x in others(at.x, X):
            begin(send(part.at[second], part.at[second], xb_out.at[z, x], xb_in.at[z, at.x], at.at(x=x)))

    def two(z):
        for y in others(at.y, Y):
            part = land.at[at.c, z, at.x, y, first]
            send(part, part, ya_out.at[z, y], ya_in.at[z, y], at.at(y=y)).wait_recv()
        line = land.at[at.c, z, at.x, :, first]
        for x in others(at.x, X):
            begin(send(line, line, xa_out.at[z, x], xa_in.at[z, at.x], at.at(x=x)))
        for x in others(at.x, X):
            part = land.at[at.c, z, x, at.y, second]
            send(part, part, xb_out.at[z, x], xb_in.at[z, x], at.at(x=x)).wait_recv()
        line = land.at[at.c, z, :, at.y, second]
        for y in others(at.y, Y):
            begin(send(line, line, yb_out.at[z, y], yb_in.at[z, at.y], at.at(y=y)))

    def three(z):
        for x in others(at.x, X):
            line = land.at[at.c, z, x, :, first]
            send(line, line, xa_out.at[z, x], xa_in.at[z, x], at.at(x=x)).wait_recv()
        for y in others(at.y, Y):
            line = land.at[at.c, z, :, y, second]
            send(line, line, yb_out.at[z, y], yb_in.at[z, y], at.at(y=y)).wait_recv()
        plane = land.at[at.c, z]
        begin(send(plane, plane, c_out.at[z], c_in.at[z], at.sibling()))

    for step in range(Z + 2):
        if step < Z:
            if step > 0:
                z = order[step]
                part = land.at[at.c, z, at.x, at.y]
                send(part, part, z_out.at[z], z_in.at[z], at.at(z=z)).wait_recv()
            one(order[step])
        if step == 0:
            col_ref[...] = route_math(*routing, pick_ref, rank_ref, mask_ref, length_ref)
        if 0 <= step - 1 < Z:
            two(order[step - 1])
        if 0 <= step - 2 < Z:
            three(order[step - 2])
    for z in order:
        plane = land.at[1 - at.c, z]
        send(plane, plane, c_out.at[z], c_in.at[z], at.sibling()).wait_recv()
    for copy in started:
        copy.wait_send()
    chips = [(z, y, x) for z in range(Z) for y in range(Y) for x in range(X)]
    cores = [(c, z, x, y) for z, y, x in chips for c in range(2)]
    group = 16 // math.gcd(16, rows)
    for start in range(0, len(cores), group):
        for mat in range(mats):
            w_ref[mat, start * rows : (start + group) * rows] = jnp.concatenate(
                [land[spot][mat * rows : (mat + 1) * rows] for spot in cores[start : start + group]], 0
            )
    base, count = mats * rows, tail_ref.shape[0]
    tails = [land[spot][base : base + count].astype(jnp.float32) for spot in cores]
    gain_ref[...] = jnp.concatenate([tail[:8, :rows] for tail in tails], 1)
    router_ref[...] = jnp.concatenate([tail[:, 128 : 128 + rows] for tail in tails], 1)


def gather_weights(sizes, routing, dense, tail, picks, ranks, slot_mask, lengths):
    mats, rows, width = dense.shape
    count = tail.shape[0]
    depth = round_up(mats * rows + count, 16)
    Z, Y, X = QUAD, sizes["g"], sizes["x"]
    dma = pltpu.SemaphoreType.DMA
    by_y, by_x = dma((Z, Y)), dma((Z, X))
    return pl.pallas_call(
        functools.partial(gather_kernel, sizes, rows, mats, routing),
        out_shape=(
            jax.ShapeDtypeStruct((mats, width, width), jnp.bfloat16),
            jax.ShapeDtypeStruct((8, width), jnp.float32),
            jax.ShapeDtypeStruct((count, width), jnp.float32),
            jax.ShapeDtypeStruct((picks.shape[0], 128), jnp.float32),
        ),
        in_specs=[whole()] * 6,
        out_specs=(whole(),) * 4,
        scratch_shapes=[VMEM((2, Z, X, Y, depth, width), jnp.bfloat16), dma((Z,)), dma((Z,))]
        + [by_y, by_y, by_x, by_x, by_x, by_x, by_y, by_y, dma((Z,)), dma((Z,))],
        compiler_params=pltpu.CompilerParams(
            collective_id=1, has_side_effects=True, vmem_limit_bytes=48 * MIB
        ),
        cost_estimate=cost(44),
        name="gather_weights",
    )(dense, tail, picks, ranks, slot_mask, lengths)


def total_square(value):
    return jnp.sum(jnp.sum(value * value, 0, keepdims=True), 1, keepdims=True)


def scatter_kernel(sizes, g_ref, out_ref, square_ref, hold, sib, got_xa, got_yb, got_ya, got_xb, got_z, *sems):
    at = Place(sizes)
    Z, Y, X = at.Z, at.Y, at.X
    depth = g_ref.shape[4]
    cut = depth // 2 // 16 * 16
    first, second = pl.ds(0, cut), pl.ds(cut, depth - cut)
    c_out, c_in, xa_out, xa_in, yb_out, yb_in, ya_out, ya_in, xb_out, xb_in, z_out, z_in = sems
    greet(grid_peers(at))
    started = []

    def begin(copy):
        copy.start()
        started.append(copy)

    wide = lambda value: value.astype(jnp.float32)
    order = [lax.rem(at.z + k, Z) for k in (2, 1, 3)] + [at.z]
    for z in order:
        begin(send(g_ref.at[1 - at.c, z], sib.at[z], c_out.at[z], c_in.at[z], at.sibling()))

    def one(z):
        send(sib.at[z], sib.at[z], c_out.at[z], c_in.at[z], at.sibling()).wait_recv()
        hold[z] = (wide(g_ref[at.c, z]) + wide(sib[z])).astype(jnp.bfloat16)
        for x in others(at.x, X):
            begin(send(hold.at[z, x, :, first], got_xa.at[z, at.x], xa_out.at[z, x], xa_in.at[z, at.x], at.at(x=x)))
        for y in others(at.y, Y):
            begin(send(hold.at[z, :, y, second], got_yb.at[z, at.y], yb_out.at[z, y], yb_in.at[z, at.y], at.at(y=y)))

    def two(z):
        total = wide(hold[z, at.x, :, first])
        for x in others(at.x, X):
            send(got_xa.at[z, x], got_xa.at[z, x], xa_out.at[z, x], xa_in.at[z, x], at.at(x=x)).wait_recv()
            total = total + wide(got_xa[z, x])
        hold[z, at.x, :, first] = total.astype(jnp.bfloat16)
        for y in others(at.y, Y):
            begin(send(hold.at[z, at.x, y, first], got_ya.at[z, at.y], ya_out.at[z, y], ya_in.at[z, at.y], at.at(y=y)))
        total = wide(hold[z, :, at.y, second])
        for y in others(at.y, Y):
            send(got_yb.at[z, y], got_yb.at[z, y], yb_out.at[z, y], yb_in.at[z, y], at.at(y=y)).wait_recv()
            total = total + wide(got_yb[z, y])
        hold[z, :, at.y, second] = total.astype(jnp.bfloat16)
        for x in others(at.x, X):
            begin(send(hold.at[z, x, at.y, second], got_xb.at[z, at.x], xb_out.at[z, x], xb_in.at[z, at.x], at.at(x=x)))

    def three(z, last):
        total = wide(hold[z, at.x, at.y, first])
        for y in others(at.y, Y):
            send(got_ya.at[z, y], got_ya.at[z, y], ya_out.at[z, y], ya_in.at[z, y], at.at(y=y)).wait_recv()
            total = total + wide(got_ya[z, y])
        rest = wide(hold[z, at.x, at.y, second])
        for x in others(at.x, X):
            send(got_xb.at[z, x], got_xb.at[z, x], xb_out.at[z, x], xb_in.at[z, x], at.at(x=x)).wait_recv()
            rest = rest + wide(got_xb[z, x])
        if last:
            out_ref[first] = total
            out_ref[second] = rest
            return
        mine = hold.at[z, at.x, at.y]
        mine[first] = total.astype(jnp.bfloat16)
        mine[second] = rest.astype(jnp.bfloat16)
        begin(send(mine, got_z.at[at.z], z_out.at[z], z_in.at[at.z], at.at(z=z)))

    for step in range(Z + 2):
        if step < Z:
            one(order[step])
        if 0 <= step - 1 < Z:
            two(order[step - 1])
        if 0 <= step - 2 < Z:
            three(order[step - 2], step - 2 == Z - 1)
    for z in order[:-1]:
        send(got_z.at[z], got_z.at[z], z_out.at[z], z_in.at[z], at.at(z=z)).wait_recv()
        out_ref[...] += wide(got_z[z])
    square_ref[...] = jnp.broadcast_to(total_square(out_ref[...]), square_ref.shape)
    for copy in started:
        copy.wait_send()


def scatter_dense(sizes, blocks):
    unused, Z, X, Y, depth, width = blocks.shape
    dma = pltpu.SemaphoreType.DMA
    by_y, by_x, by_z = dma((Z, Y)), dma((Z, X)), dma((Z,))
    cut = depth // 2 // 16 * 16
    half = jnp.bfloat16
    return pl.pallas_call(
        functools.partial(scatter_kernel, sizes),
        out_shape=(
            jax.ShapeDtypeStruct((depth, width), jnp.float32),
            jax.ShapeDtypeStruct((8, 128), jnp.float32),
        ),
        in_specs=[whole()],
        out_specs=(whole(), whole()),
        scratch_shapes=[
            VMEM((Z, X, Y, depth, width), half),
            VMEM((Z, X, Y, depth, width), half),
            VMEM((Z, X, Y, cut, width), half),
            VMEM((Z, Y, X, depth - cut, width), half),
            VMEM((Z, Y, cut, width), half),
            VMEM((Z, X, depth - cut, width), half),
            VMEM((Z, depth, width), half),
        ]
        + [by_z, by_z, by_x, by_x, by_y, by_y, by_y, by_y, by_x, by_x, by_z, by_z],
        compiler_params=pltpu.CompilerParams(
            collective_id=2, has_side_effects=True, vmem_limit_bytes=48 * MIB
        ),
        cost_estimate=cost(45),
        name="scatter_dense",
    )(blocks)


def finish_kernel(sizes, n_experts, head_ref, dense_ref, imp_ref, *refs):
    at = Place(sizes)
    many = len(refs) - 7
    parts = refs[:many]
    first_ref, second_ref, out_ref, land, own, out_sem, in_sem = refs[many:]
    count = 2 * at.chips
    me = at.chip * 2 + at.c
    ids = others(me, count)

    def peer(device):
        spot = at.of_chip(lax.div(device, 2))
        spot["c"] = lax.rem(device, 2)
        return spot

    greet([peer(device) for device in ids])
    place = lax.rem(at.g * QUAD + at.r, 2)
    square = dense_ref[0:1, 0:1] + head_ref[1:2, 0:1]
    for parity in range(2):
        expert = place if parity == 0 else 1 - place
        for index, ref in enumerate((first_ref, second_ref)):
            total = None
            for step in range(parity, many, 2):
                found = parts[step][index].astype(jnp.float32)
                total = found if total is None else total + found
            ref[expert] = total
            square = square + total_square(total)
    line = lax.broadcasted_iota(jnp.int32, own.shape, 0)
    own[...] = jnp.where(line == 0, head_ref[0:1, 0:1], jnp.where(line == 1, square, 0.0))
    land[me] = own[...]
    copies = [send(own, land.at[me], out_sem.at[d], in_sem.at[me], peer(d)) for d in ids]
    for copy in copies:
        copy.start()
    importance = imp_ref[0:1, 0:128]
    head = lax.broadcasted_iota(jnp.int32, (1, 128), 1) < n_experts
    centre = jnp.sum(jnp.where(head, importance, 0.0), 1, keepdims=True) / n_experts
    away = jnp.where(head, importance - centre, 0.0)
    spread = jnp.sum(away * away, 1, keepdims=True) / n_experts
    balance = aux_weight * spread / (centre * centre)
    for d in ids:
        send(land.at[d], land.at[d], out_sem.at[d], in_sem.at[d], peer(d)).wait_recv()
    sums = jnp.sum(land[...], 0)
    norm = jnp.sqrt(sums[1:2, 0:1])
    factor = jnp.minimum(1.0, clip_limit / norm)
    loss = sums[0:1, 0:1] + balance
    out_ref[...] = jnp.where(line == 0, loss, jnp.where(line == 1, norm, factor))
    for copy in copies:
        copy.wait_send()


def finish(sizes, n_experts, parts, head_sums, dense_sums, importance):
    devices = sizes["g"] * QUAD * sizes["x"] * 2
    unused, rows, width = parts[0].shape
    dma = pltpu.SemaphoreType.DMA
    grads = jax.ShapeDtypeStruct((2, rows, width), jnp.float32)
    return pl.pallas_call(
        functools.partial(finish_kernel, sizes, n_experts),
        out_shape=(grads, grads, jax.ShapeDtypeStruct((8, 128), jnp.float32)),
        in_specs=[whole()] * (3 + len(parts)),
        out_specs=(whole(),) * 3,
        scratch_shapes=[
            VMEM((devices, 8, 128), jnp.float32),
            VMEM((8, 128), jnp.float32),
            dma((devices,)),
            dma((devices,)),
        ],
        compiler_params=pltpu.CompilerParams(
            collective_id=3, has_side_effects=True, vmem_limit_bytes=48 * MIB
        ),
        cost_estimate=cost(10),
        name="finish",
    )(head_sums, dense_sums, importance, *parts)


EARLY = 0
IMAGE_PAD = 16


def split_three(value):
    high = value.astype(jnp.bfloat16)
    rest = value - high.astype(jnp.float32)
    middle = rest.astype(jnp.bfloat16)
    return high, middle, (rest - middle.astype(jnp.float32)).astype(jnp.bfloat16)


def dot_f32(left, right, dims):
    return lax.dot_general(left, right, (dims, ((), ())), preferred_element_type=jnp.float32)


NN = ((1,), (0,))
NT = ((1,), (1,))
TN = ((0,), (0,))


def norm_parts(values):
    centre = values - jnp.mean(values, -1, keepdims=True)
    spread = jnp.mean(centre * centre, -1, keepdims=True)
    scale = lax.rsqrt(spread + eps_norm)
    return centre * scale, scale


def norm_back(d_out, scaled, scale, gain):
    pulled = d_out * gain
    return scale * (
        pulled
        - jnp.mean(pulled, -1, keepdims=True)
        - scaled * jnp.mean(pulled * scaled, -1, keepdims=True)
    )


def head_kernel(
    sizes, images, part_ref, own_ref, imp_ref, gain_ref, head_ref, label_ref,
    g_head_ref, d_pool_ref, own_d_ref, g_norm_ref, sums_ref, total_imp_ref,
    in_part, rows, d_rows, d_sib, d_sum, d_in, head_b, labels, d_logits, *sems
):
    at = Place(sizes)
    chips, members = at.chips, QUAD * at.X
    devices = 2 * chips
    p_out, p_in, r_out, r_in, s_out, s_in, d_out, d_in_sem, b_out, b_in = sems
    width = own_ref.shape[1]
    same_core = others(at.chip, chips)
    greet([at.of_chip(chip) for chip in same_core] + [at.sibling()])
    started = []

    def begin(copy):
        copy.start()
        started.append(copy)

    team = others(at.member, members)
    for member in team:
        begin(send(part_ref.at[member], in_part.at[at.member], p_out.at[member], p_in.at[at.member], at.of_member(member)))
    in_part[at.member] = part_ref[at.member]
    head_b[...] = head_ref[...].astype(jnp.bfloat16)
    wide = devices * IMAGE_PAD
    spot = lax.broadcasted_iota(jnp.int32, (label_ref.shape[1], wide), 1)
    given = lax.broadcasted_iota(jnp.int32, (label_ref.shape[1], wide), 0)
    image = lax.rem(spot, IMAGE_PAD)
    device = lax.rem(lax.div(spot, IMAGE_PAD), chips) * 2 + lax.div(spot, IMAGE_PAD * chips)
    chosen = ((device * images + image == given) & (image < images)).astype(jnp.bfloat16)
    labels[...] = dot_f32(label_ref[...].astype(jnp.float32).astype(jnp.bfloat16), chosen, NN).astype(jnp.bfloat16)
    for member in team:
        send(in_part.at[member], in_part.at[member], p_out.at[member], p_in.at[member], at.of_member(member)).wait_recv()
    pooled = own_ref[...] + jnp.sum(in_part[...], 0)
    scaled, scale = norm_parts(pooled)
    gain, shift = gain_ref[2:3], gain_ref[5:6]
    a_three = scaled * gain + shift
    row = lax.broadcasted_iota(jnp.int32, (IMAGE_PAD, width), 0)
    block = jnp.where(row < images, a_three, 0.0)
    pieces = split_three(imp_ref[0:1])
    for index, piece in enumerate(pieces):
        block = jnp.where(row == images + index, piece.astype(jnp.float32), block)
    rows[at.c, at.chip] = block.astype(jnp.bfloat16)
    mine = rows.at[at.c, at.chip]
    for chip in same_core:
        begin(send(mine, mine, r_out.at[chip], r_in.at[at.chip], at.of_chip(chip)))
    for chip in same_core:
        part = rows.at[at.c, chip]
        send(part, part, r_out.at[chip], r_in.at[chip], at.of_chip(chip)).wait_recv()
    begin(send(rows.at[at.c], rows.at[at.c], s_out.at[0], s_in.at[0], at.sibling()))
    send(rows.at[1 - at.c], rows.at[1 - at.c], s_out.at[0], s_in.at[0], at.sibling()).wait_recv()
    gathered = rows[...].reshape(wide, width)
    in_block = lax.rem(lax.broadcasted_iota(jnp.int32, (wide, width), 0), IMAGE_PAD)
    total = jnp.sum(jnp.where(in_block >= images, gathered.astype(jnp.float32), 0.0), 0, keepdims=True)
    total_imp_ref[...] = jnp.broadcast_to(total, total_imp_ref.shape)
    gathered = jnp.where(in_block < images, gathered.astype(jnp.float32), 0.0).astype(jnp.bfloat16)
    logits = dot_f32(head_b[...], gathered, NT)
    image = lax.rem(lax.broadcasted_iota(jnp.int32, logits.shape, 1), IMAGE_PAD)
    count = devices * images
    target = labels[...].astype(jnp.float32)
    power = jnp.exp(-jnp.abs(logits))
    loss = jnp.maximum(logits, 0.0) + jnp.log1p(power) - target * logits
    loss = jnp.sum(jnp.where(image < images, loss, 0.0), 1, keepdims=True)
    loss = jnp.sum(loss, 0, keepdims=True) / count
    chance = jnp.where(logits >= 0.0, 1.0, power) / (1.0 + power)
    d_logits[...] = jnp.where(image < images, (chance - target) / count, 0.0).astype(jnp.bfloat16)
    partial = dot_f32(d_logits[...], head_b[...], TN)
    d_rows[...] = partial.reshape(d_rows.shape).astype(jnp.bfloat16)
    begin(send(d_rows.at[1 - at.c], d_sib, s_out.at[1], s_in.at[1], at.sibling()))
    g_head = dot_f32(d_logits[...], gathered, NN)
    g_head_ref[...] = g_head
    line = lax.broadcasted_iota(jnp.int32, sums_ref.shape, 0)
    sums_ref[...] = jnp.where(line == 0, loss, jnp.where(line == 1, total_square(g_head), 0.0))
    send(d_sib, d_sib, s_out.at[1], s_in.at[1], at.sibling()).wait_recv()
    d_sum[...] = (d_rows[at.c].astype(jnp.float32) + d_sib[...].astype(jnp.float32)).astype(jnp.bfloat16)
    for chip in same_core:
        begin(send(d_sum.at[chip], d_in.at[at.chip], d_out.at[chip], d_in_sem.at[at.chip], at.of_chip(chip)))
    d_in[at.chip] = d_sum[at.chip]
    for chip in same_core:
        send(d_in.at[chip], d_in.at[chip], d_out.at[chip], d_in_sem.at[chip], at.of_chip(chip)).wait_recv()
    d_norm = jnp.sum(d_in[...].astype(jnp.float32), 0)
    d_norm = jnp.where(row < images, d_norm, 0.0)
    d_pooled = norm_back(d_norm, scaled, scale, gain)
    d_pooled = jnp.where(row < images, d_pooled, 0.0)
    d_gain = jnp.sum(d_norm * scaled, 0, keepdims=True)
    d_shift = jnp.sum(d_norm, 0, keepdims=True)
    line = lax.broadcasted_iota(jnp.int32, g_norm_ref.shape, 0)
    g_norm_ref[...] = jnp.where(line == 2, d_gain, jnp.where(line == 5, d_shift, 0.0))
    own_d_ref[...] = d_pooled
    d_pool_ref[at.member] = d_pooled
    mine = d_pool_ref.at[at.member]
    for member in team:
        begin(send(own_d_ref, mine, b_out.at[member], b_in.at[at.member], at.of_member(member)))
    for member in team:
        part = d_pool_ref.at[member]
        send(part, part, b_out.at[member], b_in.at[member], at.of_member(member)).wait_recv()
    for copy in started:
        copy.wait_send()


def head_step(sizes, images, part, own, imp, gains, head, label):
    members = QUAD * sizes["x"]
    chips = members * sizes["g"]
    classes, width = head.shape
    wide = 2 * chips * IMAGE_PAD
    dma = pltpu.SemaphoreType.DMA
    by_member, by_chip = dma((members,)), dma((chips,))
    f32, half = jnp.float32, jnp.bfloat16
    blocks = (chips, IMAGE_PAD, width)
    return pl.pallas_call(
        functools.partial(head_kernel, sizes, images),
        out_shape=(
            jax.ShapeDtypeStruct((classes, width), f32),
            jax.ShapeDtypeStruct((members, IMAGE_PAD, width), f32),
            jax.ShapeDtypeStruct((IMAGE_PAD, width), f32),
            jax.ShapeDtypeStruct((8, width), f32),
            jax.ShapeDtypeStruct((8, 128), f32),
            jax.ShapeDtypeStruct((8, width), f32),
        ),
        in_specs=[whole()] * 6,
        out_specs=(whole(),) * 6,
        scratch_shapes=[
            VMEM((members, IMAGE_PAD, width), f32),
            VMEM((2, *blocks), half),
            VMEM((2, *blocks), half),
            VMEM(blocks, half),
            VMEM(blocks, half),
            VMEM(blocks, half),
            VMEM((classes, width), half),
            VMEM((classes, wide), half),
            VMEM((classes, wide), half),
        ]
        + [by_member, by_member, by_chip, by_chip, dma((2,)), dma((2,)), by_chip, by_chip]
        + [by_member, by_member],
        compiler_params=pltpu.CompilerParams(
            collective_id=4, has_side_effects=True, vmem_limit_bytes=56 * MIB
        ),
        cost_estimate=cost(42),
        name="head_step",
    )(part, own, imp, gains, head, label)


def route_math(per_image, n_experts, capacity, padded, pick_ref, rank_ref, mask_ref, length_ref):
    rows_here, span = mask_ref.shape
    tokens = rows_here * span
    valid = mask_ref[...].astype(jnp.float32)
    lengths = length_ref[...]
    position = lax.broadcasted_iota(jnp.int32, (rows_here, span), 1)
    segment = jnp.zeros((rows_here, span), jnp.int32)
    bound = jnp.zeros((rows_here, 1), jnp.int32)
    for image in range(per_image):
        bound = bound + lengths[:, image : image + 1]
        segment = segment + jnp.where(position >= bound, 1, 0)
    pool = jnp.zeros_like(valid)
    for image in range(per_image):
        member = jnp.where(segment == image, valid, 0.0)
        pool = pool + member / jnp.maximum(jnp.sum(member, 1, keepdims=True), 1.0)
    line = lax.broadcasted_iota(jnp.int32, (rows_here, span), 0)
    image = (segment + per_image * line).astype(jnp.float32)

    def flat(value):
        return jnp.concatenate([value[i : i + 1] for i in range(rows_here)], 1)

    rank_row = rank_ref[...].astype(jnp.float32)
    table = jnp.concatenate([flat(valid), flat(pool), flat(image), rank_row], 0)
    table = jnp.concatenate([table, jnp.zeros((124, tokens), jnp.float32)], 0).T
    valid_col, pool_col, image_col, rank_col = (table[:, i : i + 1] for i in range(4))
    picks = pick_ref[...]
    pick_one, pick_two = picks[:, 0:1], picks[:, 1:2]
    lane = lax.broadcasted_iota(jnp.int32, (tokens, 128), 1)
    in_first, in_second = lane < n_experts, (lane >= n_experts) & (lane < 2 * n_experts)
    hot = jnp.where(in_first & (pick_one == lane), valid_col, 0.0)
    hot = hot + jnp.where(in_second & (pick_two == lane - n_experts), valid_col, 0.0)
    shifted = jnp.where(in_second & (pick_one == lane - n_experts), valid_col, 0.0)
    before = jnp.where(rank_row < rank_col, 1.0, 0.0).astype(jnp.bfloat16)
    ahead = dot_f32(before, hot.astype(jnp.bfloat16), NN) + jnp.sum(shifted, 0, keepdims=True)
    counted = hot * ahead
    pos_one = jnp.sum(jnp.where(in_first, counted, 0.0), 1, keepdims=True)
    pos_two = jnp.sum(jnp.where(in_second, counted, 0.0), 1, keepdims=True)

    def place(pick, pos):
        kept = (valid_col > 0.0) & (pos < capacity)
        return jnp.where(kept, pick.astype(jnp.float32) * padded + pos, -1.0)

    columns = (
        place(pick_one, pos_one),
        place(pick_two, pos_two),
        valid_col,
        pool_col,
        image_col,
        pick_one.astype(jnp.float32),
        pick_two.astype(jnp.float32),
    )
    result = jnp.zeros((tokens, 128), jnp.float32)
    for index, column in enumerate(columns):
        result = jnp.where(lane == index, column, result)
    return result


def lane_mask(shape, left):
    lane = lax.broadcasted_iota(jnp.int32, shape, 1)
    return lane < 64 if left else lane >= 64


def allowed_slots(lengths, row, images, valid_row, span):
    query = lax.broadcasted_iota(jnp.int32, (span, span), 0)
    key = lax.broadcasted_iota(jnp.int32, (span, span), 1)
    bound = 0
    query_seg, key_seg = jnp.zeros((span, span), jnp.int32), jnp.zeros((span, span), jnp.int32)
    for image in range(images):
        bound = bound + lengths[row, image]
        query_seg = query_seg + jnp.where(query >= bound, 1, 0)
        key_seg = key_seg + jnp.where(key >= bound, 1, 0)
    return (query_seg == key_seg) & ((valid_row > 0) | (query == key))


def dense_forward_kernel(
    n_experts, images, length_ref, mask_ref, patch_ref, w_ref, gain_ref, router_ref, col_ref,
    x_zero_ref, a_one_ref, qkv_ref, att_ref, x_one_ref, a_two_ref, prob_ref, lse_ref, pool_ref, imp_ref
):
    row = pl.program_id(0)
    span, width = patch_ref.shape
    x_zero = dot_f32(patch_ref[...], w_ref[0], NN)
    x_zero_ref[...] = x_zero
    a_one = (norm_parts(x_zero)[0] * gain_ref[0:1] + gain_ref[3:4]).astype(jnp.bfloat16)
    a_one_ref[...] = a_one
    for part in range(3):
        qkv_ref[:, part * width : (part + 1) * width] = dot_f32(a_one, w_ref[1 + part], NN).astype(
            jnp.bfloat16
        )
    open_to = allowed_slots(length_ref, row, images, mask_ref[0], span)
    lane = lax.broadcasted_iota(jnp.int32, (span, 128), 1)
    logs = jnp.zeros((span, 128), jnp.float32)
    for pair in range(width // 128):
        query, key, value = (
            qkv_ref[:, part * width + pair * 128 : part * width + (pair + 1) * 128]
            for part in range(3)
        )
        outs = []
        for side in range(2):
            held = jnp.where((lane < 64) == (side == 0), query, jnp.zeros_like(query))
            scores = jnp.where(open_to, dot_f32(held, key, NT) * 64**-0.5, mask_fill)
            top = jnp.max(scores, 1, keepdims=True)
            powers = jnp.exp(scores - top)
            total = jnp.sum(powers, 1, keepdims=True)
            probs = (powers * (1.0 / total)).astype(jnp.bfloat16)
            outs.append(dot_f32(probs, value, NN))
            logs = jnp.where(lane == 2 * pair + side, top + jnp.log(total), logs)
        att_ref[:, pair * 128 : (pair + 1) * 128] = jnp.where(lane < 64, outs[0], outs[1]).astype(
            jnp.bfloat16
        )
    lse_ref[...] = logs
    x_one = x_zero + dot_f32(att_ref[...], w_ref[4], NN)
    x_one_ref[...] = x_one
    a_two = (norm_parts(x_one)[0] * gain_ref[1:2] + gain_ref[4:5]).astype(jnp.bfloat16)
    a_two_ref[...] = a_two
    routers = router_ref[...].astype(jnp.bfloat16)
    if routers.shape[0] < 128:
        routers = jnp.concatenate(
            [routers, jnp.zeros((128 - routers.shape[0], width), jnp.bfloat16)], 0
        )
    logits = jnp.where(lane < n_experts, dot_f32(a_two, routers, NT), mask_fill)
    powers = jnp.exp(logits - jnp.max(logits, 1, keepdims=True))
    probs = powers / jnp.sum(powers, 1, keepdims=True)
    prob_ref[...] = probs

    @pl.when(row == 0)
    def _():
        pool_ref[...] = jnp.zeros_like(pool_ref)
        imp_ref[...] = jnp.zeros_like(imp_ref)

    valid, pool, image = col_ref[:, 2:3], col_ref[:, 3:4], col_ref[:, 4:5]
    imp_ref[0:1, 0:128] += jnp.sum(probs * valid, 0, keepdims=True)
    line = lax.broadcasted_iota(jnp.int32, pool_ref.shape, 0)
    for index in range(images):
        number = row * images + index
        weight = jnp.where(image == number.astype(jnp.float32), pool, 0.0)
        pooled = jnp.sum(x_one * weight, 0, keepdims=True)
        pool_ref[...] = jnp.where(line == number, pooled, pool_ref[...])


def dense_forward(n_experts, lengths, slot_mask, patches, weights, gains, routers, columns):
    rows_here, span = slot_mask.shape
    tokens, width = patches.shape
    f32, half = jnp.float32, jnp.bfloat16

    def block(wide):
        return pl.BlockSpec((span, wide), lambda i: (i, 0))

    def out(wide, kind):
        return jax.ShapeDtypeStruct((tokens, wide), kind)

    def fixed(shape):
        return pl.BlockSpec(shape, lambda i: (0, 0))

    return pl.pallas_call(
        functools.partial(dense_forward_kernel, n_experts, lengths.shape[1]),
        grid=(rows_here,),
        out_shape=(
            out(width, f32), out(width, half), out(3 * width, half), out(width, half),
            out(width, f32), out(width, half), out(128, f32), out(128, f32),
            jax.ShapeDtypeStruct((IMAGE_PAD, width), f32), jax.ShapeDtypeStruct((8, width), f32),
        ),
        in_specs=[
            whole(pltpu.SMEM), pl.BlockSpec((1, 1, span), lambda i: (i, 0, 0)), block(width),
            whole(), whole(), whole(), block(128),
        ],
        out_specs=(
            block(width), block(width), block(3 * width), block(width), block(width), block(width),
            block(128), block(128), fixed((IMAGE_PAD, width)), fixed((8, width)),
        ),
        compiler_params=pltpu.CompilerParams(vmem_limit_bytes=48 * MIB),
        cost_estimate=cost(25),
        name="dense_forward",
    )(lengths, slot_mask[:, None, :], patches, weights, gains, routers, columns)


def dispatch_kernel(
    sizes, n_experts, padded, a_two_ref, prob_ref, col_ref, rows_ref, detail_ref,
    send_rows, send_detail, places, own_sem, r_out, r_in, m_out, m_in
):
    at = Place(sizes)
    tokens = a_two_ref.shape[0]
    team = others(at.member, n_experts)
    greet([at.of_member(member) for member in team])
    columns = col_ref[...]
    places[...] = columns.T[:8]
    lane = lax.broadcasted_iota(jnp.int32, (tokens, 128), 1)
    kind, expert = lax.div(lane, n_experts), lax.rem(lane, n_experts).astype(jnp.float32)
    slot_lane = lax.broadcasted_iota(jnp.int32, (tokens, send_detail.shape[2]), 1).astype(jnp.float32)
    pool, image = columns[:, 3:4], columns[:, 4:5]
    details = None
    for choice in range(2):
        slot, pick = columns[:, choice : choice + 1], columns[:, 5 + choice : 6 + choice]
        hot = (expert == pick) & (slot >= 0.0)
        gate = jnp.sum(jnp.where(hot & (kind == 0), prob_ref[...], 0.0), 1, keepdims=True)
        values = jnp.zeros((tokens, 128), jnp.float32)
        pieces = [*split_three(gate), *split_three(pool), image]
        for index, piece in enumerate(pieces):
            values = jnp.where(kind == index, piece.astype(jnp.float32), values)
        values = jnp.where(hot, values, 0.0).astype(jnp.bfloat16)
        spot = jnp.where(slot >= 0.0, slot - pick * padded, -1.0)
        chosen = jnp.where(spot == slot_lane, 1.0, 0.0).astype(jnp.bfloat16)
        found = dot_f32(values, chosen, TN)
        details = found if details is None else details + found
    n = n_experts
    gates = details[0:n] + details[n : 2 * n] + details[2 * n : 3 * n]
    pools = details[3 * n : 4 * n] + details[4 * n : 5 * n] + details[5 * n : 6 * n]
    images = details[6 * n : 7 * n]
    for index in range(n):
        for spot, value in enumerate((gates, pools, images)):
            send_detail[index, spot : spot + 1] = value[index : index + 1]
        send_detail[index, 3:8] = jnp.zeros((5, send_detail.shape[2]), jnp.float32)

    def rows_of(member):
        slots = lax.broadcasted_iota(jnp.int32, (padded, tokens), 0) + member * padded
        slots = slots.astype(jnp.float32)
        match = (slots == places[0:1]) | (slots == places[1:2])
        match = jnp.where(match, 1.0, 0.0).astype(jnp.bfloat16)
        send_rows[member] = dot_f32(match, a_two_ref[...], NN).astype(jnp.bfloat16)

    def row_copy(member, source):
        return send(
            send_rows.at[member], rows_ref.at[source], r_out.at[member], r_in.at[source], at.of_member(member)
        )

    def detail_copy(member, source):
        return send(
            send_detail.at[member], detail_ref.at[source], m_out.at[member], m_in.at[source], at.of_member(member)
        )

    def step(index, carry):
        member = lax.rem(at.member + index, n_experts)
        rows_of(member)
        row_copy(member, at.member).start()
        detail_copy(member, at.member).start()
        return carry

    lax.fori_loop(1, n_experts, step, 0)
    rows_of(at.member)
    keep_rows = pltpu.make_async_copy(send_rows.at[at.member], rows_ref.at[at.member], own_sem.at[0])
    keep_detail = pltpu.make_async_copy(send_detail.at[at.member], detail_ref.at[at.member], own_sem.at[1])
    keep_rows.start()
    keep_detail.start()
    for member in team:
        row_copy(member, member).wait_recv()
        detail_copy(member, member).wait_recv()
    for member in team:
        row_copy(member, at.member).wait_send()
        detail_copy(member, at.member).wait_send()
    keep_rows.wait()
    keep_detail.wait()


def dispatch(sizes, n_experts, padded, a_two, probs, columns):
    tokens, width = a_two.shape
    lanes = round_up(padded, 128)
    dma = pltpu.SemaphoreType.DMA
    each = dma((n_experts,))
    return pl.pallas_call(
        functools.partial(dispatch_kernel, sizes, n_experts, padded),
        out_shape=(
            jax.ShapeDtypeStruct((n_experts, padded, width), jnp.bfloat16),
            jax.ShapeDtypeStruct((n_experts, 8, lanes), jnp.float32),
        ),
        in_specs=[whole()] * 3,
        out_specs=(whole(ANY), whole(ANY)),
        scratch_shapes=[
            VMEM((n_experts, padded, width), jnp.bfloat16),
            VMEM((n_experts, 8, lanes), jnp.float32),
            VMEM((8, tokens), jnp.float32),
            dma((2,)), each, each, each, each,
        ],
        compiler_params=pltpu.CompilerParams(
            collective_id=5, has_side_effects=True, vmem_limit_bytes=48 * MIB
        ),
        cost_estimate=cost(50),
        name="dispatch",
    )(a_two, probs, columns)


def image_hot(detail, padded):
    image = detail[2:3, :padded]
    line = lax.broadcasted_iota(jnp.int32, (IMAGE_PAD, padded), 0).astype(jnp.float32)
    return line == image


TILE = 32


def tiles(count):
    return [slice(start, min(start + TILE, count)) for start in range(0, count, TILE)]


def expert_forward_kernel(sizes, padded, rows_ref, detail_ref, *refs):
    at = Place(sizes)
    half = len(refs) - 11
    chunks = refs[:half]
    act_ref, slope_ref, y_ref, part_ref, other_ref = refs[half : half + 5]
    weights, total, own_sem, s_out, s_in, keep_sem = refs[half + 5 :]
    many, unused, width = rows_ref.shape
    count = many * padded
    turn, block = pl.program_id(0), pl.program_id(1)

    def own_copy(index):
        return pltpu.make_async_copy(chunks[index], weights.at[0, index], own_sem.at[index])

    def swap_copy(index):
        return send(
            chunks[index], weights.at[1, index], s_out.at[index], s_in.at[index], at.sibling()
        )

    def keep_copy():
        return pltpu.make_async_copy(weights.at[1], other_ref, keep_sem.at[0])

    @pl.when((turn == 0) & (block == 0))
    def _():
        for index in range(half):
            own_copy(index).start()
        greet([at.sibling()])
        for index in range(half):
            swap_copy(index).start()
        for index in range(half):
            own_copy(index).wait()

    @pl.when((turn == 1) & (block == 0))
    def _():
        for index in range(half):
            swap_copy(index).wait_recv()
        keep_copy().start()

    rows = rows_ref[...].reshape(count, width)
    for index in range(half):
        hidden_all = dot_f32(rows, weights[turn, index, 0], NT)
        for spot in tiles(count):
            hidden = hidden_all[spot]
            square = hidden * hidden
            curve = jnp.tanh(hidden * (0.7978845608 + 0.7978845608 * 0.044715 * square))
            upper = 0.5 + 0.5 * curve
            gelu = hidden * upper
            slope = upper + gelu * (1.0 - upper) * (
                2.0 * 0.7978845608 + 6.0 * 0.7978845608 * 0.044715 * square
            )
            act_ref[index, spot] = gelu.astype(jnp.bfloat16)
            slope_ref[index, spot] = slope.astype(jnp.bfloat16)
    acts = jnp.concatenate([act_ref[index] for index in range(half)], 1)
    ends = jnp.concatenate([weights[turn, index, 1] for index in range(half)], 0)
    found = dot_f32(acts, ends, NN)
    span = pl.ds(pl.multiple_of(block * count, 16), count)

    @pl.when(turn == 0)
    def _():
        total[span] = found

    @pl.when(turn == 1)
    def _():
        result = (total[span] + found).astype(jnp.bfloat16)
        y_ref[...] = result.reshape(many, padded, width)
        for source in range(many):
            detail = detail_ref[source]
            weight = detail[0:1, :padded] * detail[1:2, :padded]
            shares = jnp.where(image_hot(detail, padded), weight, 0.0)
            pieces = jnp.concatenate(split_three(shares), 0)
            sums = dot_f32(pieces, result[source * padded : (source + 1) * padded], NN)
            part_ref[source] = (
                sums[:IMAGE_PAD] + sums[IMAGE_PAD : 2 * IMAGE_PAD] + sums[2 * IMAGE_PAD :]
            )

    @pl.when((turn == 1) & (block == pl.num_programs(1) - 1))
    def _():
        for index in range(half):
            swap_copy(index).wait_send()
        keep_copy().wait()


def expert_forward(sizes, rows, details, chunks):
    sources, padded, width = rows.shape
    half = len(chunks)
    part = chunks[0].shape[1]
    many = max(1, 576 // padded)
    lanes = details.shape[2]
    kind = jnp.bfloat16
    dma = pltpu.SemaphoreType.DMA

    def by_source(*shape):
        return pl.BlockSpec((many, *shape), lambda t, i: (i, 0, 0))

    def late(*shape):
        return pl.BlockSpec((many, *shape), lambda t, i: (i * t, 0, 0))

    flat = pl.BlockSpec((half, many * padded, part), lambda t, i: (t, i, 0))
    return pl.pallas_call(
        functools.partial(expert_forward_kernel, sizes, padded),
        grid=(2, sources // many),
        out_shape=(
            jax.ShapeDtypeStruct((2 * half, sources * padded, part), kind),
            jax.ShapeDtypeStruct((2 * half, sources * padded, part), kind),
            jax.ShapeDtypeStruct((sources, padded, width), kind),
            jax.ShapeDtypeStruct((sources, IMAGE_PAD, width), jnp.float32),
            jax.ShapeDtypeStruct((half, 2, part, width), kind),
        ),
        in_specs=[by_source(padded, width), by_source(8, lanes)] + [whole(ANY)] * half,
        out_specs=(flat, flat, late(padded, width), late(IMAGE_PAD, width), whole(ANY)),
        scratch_shapes=[
            VMEM((2, half, 2, part, width), kind),
            VMEM((sources * padded, width), jnp.float32),
            dma((half,)), dma((half,)), dma((half,)), dma((1,)),
        ],
        compiler_params=pltpu.CompilerParams(
            collective_id=7, has_side_effects=True, vmem_limit_bytes=56 * MIB
        ),
        cost_estimate=cost(40),
        name="expert_forward",
    )(rows, details, *chunks)


def expert_backward_kernel(
    sizes, padded, rows_ref, detail_ref, pool_ref, y_ref, slope_ref, act_ref, other_ref, *refs
):
    at = Place(sizes)
    sources, unused, width = rows_ref.shape
    chunks, unused, part = slope_ref.shape
    half = chunks // 2
    own_refs, refs = refs[:half], refs[half:]
    back_ref, gate_ref, *outs = refs[: 2 + half]
    d_hidden, d_rows, send_rows, send_gate, send_grad, got_grad = refs[2 + half : 8 + half]
    own_sem, r_out, r_in, m_out, m_in, g_out, g_in, g_keep = refs[8 + half :]
    many = y_ref.shape[0]
    rounds = sources // many
    step = pl.program_id(0)
    team = others(at.member, sources)

    def row_copy(member, source):
        return send(
            send_rows.at[member], back_ref.at[source], r_out.at[member], r_in.at[source], at.of_member(member)
        )

    def gate_copy(member, source):
        return send(
            send_gate.at[member], gate_ref.at[source], m_out.at[member], m_in.at[source], at.of_member(member)
        )

    def keep_copies():
        return (
            pltpu.make_async_copy(send_rows.at[at.member], back_ref.at[at.member], own_sem.at[0]),
            pltpu.make_async_copy(send_gate.at[at.member], gate_ref.at[at.member], own_sem.at[1]),
        )

    def grad_copy(index):
        return send(
            send_grad.at[index], got_grad.at[index], g_out.at[index], g_in.at[index], at.sibling()
        )

    def out_copy(index):
        return pltpu.make_async_copy(got_grad.at[index], outs[index], g_keep.at[index])

    @pl.when(step == 0)
    def _():
        greet([at.of_member(member) for member in team] + [at.sibling()])

    @pl.when(step < rounds)
    def _():
        block = lax.rem(lax.div(at.member, many) + 1 + step, rounds)
        d_out = []
        for index in range(many):
            source = block * many + index
            detail = detail_ref[source]
            hot = image_hot(detail, padded)
            hots = jnp.where(hot, 1.0, 0.0).astype(jnp.bfloat16)
            pools = jnp.concatenate(split_three(pool_ref[source]), 0)
            wide = dot_f32(jnp.concatenate([hots] * 3, 0), pools, TN)
            lanes = detail.shape[1]
            upright = jnp.concatenate([detail, jnp.zeros((120, lanes), jnp.float32)], 0).T
            gate, pool = upright[:padded, 0:1], upright[:padded, 1:2]
            d_out.append((gate * (pool * wide)).astype(jnp.bfloat16))
            along = dot_f32(pools, y_ref[index], NT)
            along = along[:IMAGE_PAD] + along[IMAGE_PAD : 2 * IMAGE_PAD] + along[2 * IMAGE_PAD :]
            d_gate = jnp.sum(jnp.where(hot, along, 0.0), 0, keepdims=True) * detail[1:2, :padded]
            send_gate[source] = jnp.zeros(detail.shape, jnp.float32)
            send_gate[source, 0:1, :padded] = d_gate
        d_out = jnp.concatenate(d_out, 0)
        count = many * padded
        span = pl.ds(pl.multiple_of(block * count, 16), count)
        d_rows[span] = d_out

        def weight(index, which):
            return own_refs[index][which] if index < half else other_ref[index - half, which]

        for index in range(chunks):
            d_act = dot_f32(d_out, weight(index, 1), NT)
            for spot in tiles(count):
                rows_now = pl.ds(pl.multiple_of(block * count + spot.start, 16), spot.stop - spot.start)
                d_hidden[index, rows_now] = (
                    d_act[spot] * slope_ref[index, spot].astype(jnp.float32)
                ).astype(jnp.bfloat16)
        d_hids = jnp.concatenate([d_hidden[index, span] for index in range(chunks)], 1)
        starts = jnp.concatenate([weight(index, 0) for index in range(chunks)], 0)
        total = dot_f32(d_hids, starts, NN)
        total = total.astype(jnp.bfloat16)
        for index in range(many):
            source = block * many + index
            send_rows[source] = total[index * padded : (index + 1) * padded]

            @pl.when(source != at.member)
            def _():
                row_copy(source, at.member).start()
                gate_copy(source, at.member).start()

            @pl.when(source == at.member)
            def _():
                for copy in keep_copies():
                    copy.start()

    @pl.when(step >= rounds)
    def _():
        index = step - rounds
        chunk = lax.rem(index + half, chunks)
        rows = rows_ref[...].reshape(sources * padded, width)
        g_one = dot_f32(d_hidden[chunk], rows, TN)
        g_two = dot_f32(act_ref[0], d_rows[...], TN)

        @pl.when(index < half)
        def _():
            send_grad[index, 0] = g_one.astype(jnp.bfloat16)
            send_grad[index, 1] = g_two.astype(jnp.bfloat16)
            grad_copy(index).start()

        @pl.when(index >= half)
        def _():
            spot = index - half
            grad_copy(spot).wait_recv()
            got_grad[spot, 0] = (got_grad[spot, 0].astype(jnp.float32) + g_one).astype(jnp.bfloat16)
            got_grad[spot, 1] = (got_grad[spot, 1].astype(jnp.float32) + g_two).astype(jnp.bfloat16)

        for spot in range(half):

            @pl.when(index == spot + half)
            def _():
                out_copy(spot).start()

    @pl.when(step == rounds + chunks - 1)
    def _():
        for member in team:
            row_copy(member, member).wait_recv()
            gate_copy(member, member).wait_recv()
        for member in team:
            row_copy(member, at.member).wait_send()
            gate_copy(member, at.member).wait_send()
        for copy in keep_copies():
            copy.wait()
        for spot in range(half):
            grad_copy(spot).wait_send()
            out_copy(spot).wait()


def expert_backward(sizes, rows, details, pools, results, slopes, acts, chunks_own, other):
    sources, padded, width = rows.shape
    chunks, count, part = acts.shape
    many = max(1, (288 if part % 128 else 576) // padded)
    rounds, half = sources // many, chunks // 2
    lanes = details.shape[2]
    kind = jnp.bfloat16
    dma = pltpu.SemaphoreType.DMA
    each, parts = dma((sources,)), dma((half,))

    def block_of(step):
        member = lax.axis_index("x") * QUAD + lax.axis_index("r")
        return lax.rem(lax.div(member, many) + 1 + jnp.minimum(step, rounds - 1), rounds)

    def chunk_of(step):
        return lax.rem(jnp.maximum(step - rounds, 0) + half, chunks)

    return pl.pallas_call(
        functools.partial(expert_backward_kernel, sizes, padded),
        grid=(rounds + chunks,),
        out_shape=(
            jax.ShapeDtypeStruct((sources, padded, width), kind),
            jax.ShapeDtypeStruct((sources, 8, lanes), jnp.float32),
        )
        + (jax.ShapeDtypeStruct((2, part, width), kind),) * half,
        in_specs=[
            whole(), whole(), whole(),
            pl.BlockSpec((many, padded, width), lambda i: (block_of(i), 0, 0)),
            pl.BlockSpec((chunks, many * padded, part), lambda i: (0, block_of(i), 0)),
            pl.BlockSpec((1, count, part), lambda i: (chunk_of(i), 0, 0)),
        ]
        + [whole()] * (1 + half),
        out_specs=(whole(ANY),) * (2 + half),
        scratch_shapes=[
            VMEM((chunks, count, part), kind),
            VMEM((count, width), kind),
            VMEM((sources, padded, width), kind),
            VMEM((sources, 8, lanes), jnp.float32),
            VMEM((half, 2, part, width), kind),
            VMEM((half, 2, part, width), kind),
            dma((2,)), each, each, each, each, parts, parts, parts,
        ],
        compiler_params=pltpu.CompilerParams(
            collective_id=6, has_side_effects=True, vmem_limit_bytes=62 * MIB
        ),
        cost_estimate=cost(65),
        name="expert_backward",
    )(rows, details, pools, results, slopes, acts, other, *chunks_own)


def dense_backward_kernel(
    sizes, n_experts, images, padded, length_ref, mask_ref, patch_ref, x_zero_ref, a_one_ref, qkv_ref, att_ref,
    x_one_ref, a_two_ref, prob_ref, lse_ref, col_ref, w_ref, gain_ref, router_ref, back_ref, gate_ref,
    pool_ref, imp_ref, third_ref, out_ref, grads, g_router, g_norm, d_qkv
):
    row = pl.program_id(0)
    span, width = patch_ref.shape
    mats, rows = grads.shape[0], width // (8 * sizes["g"] * sizes["x"])

    @pl.when(row == 0)
    def _():
        grads[...] = jnp.zeros_like(grads)
        g_router[...] = jnp.zeros_like(g_router)
        g_norm[...] = third_ref[...]

    columns = col_ref[...]
    slot_one, slot_two = columns[:, 0:1], columns[:, 1:2]
    count = n_experts * padded
    slot = lax.broadcasted_iota(jnp.int32, (span, count), 1).astype(jnp.float32)
    match = jnp.where((slot == slot_one) | (slot == slot_two), 1.0, 0.0).astype(jnp.bfloat16)
    d_a_two = dot_f32(match, back_ref[...].reshape(count, width), NN)
    lanes = gate_ref.shape[2]
    spot = lax.broadcasted_iota(jnp.int32, (span, lanes), 1)
    inside = spot < padded
    spot = spot.astype(jnp.float32)
    found_one, found_two = jnp.zeros((span, lanes), jnp.float32), jnp.zeros((span, lanes), jnp.float32)
    for expert in range(n_experts):
        line = jnp.broadcast_to(gate_ref[expert, 0:1], (span, lanes))
        found_one = jnp.where(inside & (spot == slot_one - expert * padded), line, found_one)
        found_two = jnp.where(inside & (spot == slot_two - expert * padded), line, found_two)
    d_gate_one = jnp.sum(found_one, 1, keepdims=True)
    d_gate_two = jnp.sum(found_two, 1, keepdims=True)
    lane = lax.broadcasted_iota(jnp.int32, (span, 128), 1)
    number = lane.astype(jnp.float32)
    valid, pool, image = columns[:, 2:3], columns[:, 3:4], columns[:, 4:5]
    head = lax.broadcasted_iota(jnp.int32, (1, 128), 1) < n_experts
    importance = imp_ref[0:1, 0:128]
    centre = jnp.sum(jnp.where(head, importance, 0.0), 1, keepdims=True) / n_experts
    away = jnp.where(head, importance - centre, 0.0)
    spread = jnp.sum(away * away, 1, keepdims=True) / n_experts
    d_imp = aux_weight * (
        2.0 * away / (n_experts * centre * centre)
        - 2.0 * spread / (n_experts * centre * centre * centre)
    )
    d_probs = valid * d_imp
    d_probs = d_probs + jnp.where(number == columns[:, 5:6], d_gate_one, 0.0)
    d_probs = d_probs + jnp.where(number == columns[:, 6:7], d_gate_two, 0.0)
    probs = prob_ref[...]
    d_router = (probs * (d_probs - jnp.sum(probs * d_probs, 1, keepdims=True))).astype(jnp.bfloat16)
    g_router[...] += dot_f32(d_router, a_two_ref[...], TN)
    routers = router_ref[...].astype(jnp.bfloat16)
    if routers.shape[0] < 128:
        routers = jnp.concatenate(
            [routers, jnp.zeros((128 - routers.shape[0], width), jnp.bfloat16)], 0
        )
    d_a_two = d_a_two + dot_f32(d_router, routers, NN)
    scaled, scale = norm_parts(x_one_ref[...])
    g_norm[1:2] += jnp.sum(d_a_two * scaled, 0, keepdims=True)
    g_norm[4:5] += jnp.sum(d_a_two, 0, keepdims=True)
    d_x_one = norm_back(d_a_two, scaled, scale, gain_ref[1:2])
    for index in range(images):
        place = row * images + index
        weight = jnp.where(image == place.astype(jnp.float32), pool, 0.0)
        d_x_one = d_x_one + weight * pool_ref[pl.ds(place, 1)]
    d_att = d_x_one.astype(jnp.bfloat16)
    grads[4] += dot_f32(att_ref[...], d_att, TN)
    d_out = dot_f32(d_att, w_ref[4], NT).astype(jnp.bfloat16)
    open_to = allowed_slots(length_ref, row, images, mask_ref[0], span)
    logs = lse_ref[...]
    for pair in range(width // 128):
        query, key, value = (
            qkv_ref[:, part * width + pair * 128 : part * width + (pair + 1) * 128]
            for part in range(3)
        )
        d_pair = d_out[:, pair * 128 : (pair + 1) * 128]
        found = []
        for side in range(2):
            left = (lane < 64) == (side == 0)
            held = jnp.where(left, query, jnp.zeros_like(query))
            scores = jnp.where(open_to, dot_f32(held, key, NT) * 64**-0.5, mask_fill)
            total = logs[:, 2 * pair + side : 2 * pair + side + 1]
            chance = jnp.exp(scores - total)
            d_held = jnp.where(left, d_pair, jnp.zeros_like(d_pair))
            d_chance = dot_f32(d_held, value, NT)
            d_value = dot_f32(chance.astype(jnp.bfloat16), d_pair, TN)
            d_scores = chance * (d_chance - jnp.sum(chance * d_chance, 1, keepdims=True))
            d_scores = d_scores.astype(jnp.bfloat16)
            d_query = dot_f32(d_scores, key, NN) * 64**-0.5
            d_key = dot_f32(d_scores, query, TN) * 64**-0.5
            found.append((d_query, d_key, d_value))
        for part in range(3):
            d_qkv[:, part * width + pair * 128 : part * width + (pair + 1) * 128] = jnp.where(
                lane < 64, found[0][part], found[1][part]
            ).astype(jnp.bfloat16)
    d_a_one = None
    for part in range(3):
        piece = d_qkv[:, part * width : (part + 1) * width]
        grads[1 + part] += dot_f32(a_one_ref[...], piece, TN)
        found = dot_f32(piece, w_ref[1 + part], NT)
        d_a_one = found if d_a_one is None else d_a_one + found
    scaled, scale = norm_parts(x_zero_ref[...])
    g_norm[0:1] += jnp.sum(d_a_one * scaled, 0, keepdims=True)
    g_norm[3:4] += jnp.sum(d_a_one, 0, keepdims=True)
    d_x_zero = norm_back(d_a_one, scaled, scale, gain_ref[0:1]) + d_x_one
    grads[0] += dot_f32(patch_ref[...], d_x_zero.astype(jnp.bfloat16), TN)

    @pl.when(row == pl.num_programs(0) - 1)
    def _():
        Z, Y, X = QUAD, sizes["g"], sizes["x"]
        tall = max(8, n_experts)
        norms = g_norm[...]
        if tall > 8:
            norms = jnp.concatenate([norms, jnp.zeros((tall - 8, width), jnp.float32)], 0)
        router_grads = g_router[:tall]
        depth = out_ref.shape[4]
        device = 0
        for z in range(Z):
            for y in range(Y):
                for x in range(X):
                    for c in range(2):
                        spot = slice(device * rows, (device + 1) * rows)
                        blank = jnp.zeros((tall, 128 - rows), jnp.float32)
                        tail = [norms[:, spot], blank, router_grads[:, spot], blank]
                        tail.append(jnp.zeros((tall, width - 256), jnp.float32))
                        pieces = [grads[mat, spot] for mat in range(mats)]
                        pieces.append(jnp.concatenate(tail, 1))
                        left = depth - mats * rows - tall
                        if left:
                            pieces.append(jnp.zeros((left, width), jnp.float32))
                        out_ref[c, z, x, y] = jnp.concatenate(pieces, 0).astype(jnp.bfloat16)
                        device += 1


def dense_backward(
    sizes, n_experts, padded, rows_own, lengths, slot_mask, patches, kept, columns, weights, gains, routers, back,
    gates, pooled, importance, third
):
    rows_here, span = slot_mask.shape
    tokens, width = patches.shape
    mats = weights.shape[0]
    depth = round_up(mats * rows_own + max(8, n_experts), 16)
    x_zero, a_one, qkv, att, x_one, a_two, probs, logs = kept

    def block(wide):
        return pl.BlockSpec((span, wide), lambda i: (i, 0))

    return pl.pallas_call(
        functools.partial(dense_backward_kernel, sizes, n_experts, lengths.shape[1], padded),
        grid=(rows_here,),
        out_shape=jax.ShapeDtypeStruct(
            (2, QUAD, sizes["x"], sizes["g"], depth, width), jnp.bfloat16
        ),
        in_specs=[
            whole(pltpu.SMEM), pl.BlockSpec((1, 1, span), lambda i: (i, 0, 0)), block(width),
            block(width), block(width), block(3 * width), block(width), block(width), block(width),
            block(128), block(128), block(128),
        ]
        + [whole()] * 8,
        out_specs=whole(),
        scratch_shapes=[
            VMEM((mats, width, width), jnp.float32),
            VMEM((128, width), jnp.float32),
            VMEM((8, width), jnp.float32),
            VMEM((span, 3 * width), jnp.bfloat16),
        ],
        compiler_params=pltpu.CompilerParams(vmem_limit_bytes=60 * MIB),
        cost_estimate=cost(50),
        name="dense_backward",
    )(
        lengths, slot_mask[:, None, :], patches, x_zero, a_one, qkv, att, x_one, a_two, probs, logs, columns,
        weights, gains, routers, back, gates, pooled, importance, third,
    )


def shard_moves(n_blocks):
    span = 2 * n_blocks
    moves = []
    for step in range(span):
        pairs = []
        for place in range(QUAD * n_blocks):
            for core in range(2):
                target = (place + step) % span
                src = place * 2 + core
                dst = (target // 2 * QUAD + 2 * core + target % 2) * 2 + place // span
                pairs.append((src, dst))
        moves.append(pairs)
    return moves


def order_shards(expert_in, expert_out):
    place = lax.axis_index("g") * QUAD + lax.axis_index("r")
    odd = lax.rem(place, 2) == 1
    both = jnp.stack([expert_in, expert_out], 1).astype(jnp.bfloat16)
    return [jnp.where(odd, both[1], both[0]), jnp.where(odd, both[0], both[1])]


def fetch_experts(shards, n_blocks, steps):
    moves = shard_moves(n_blocks)
    return [lax.ppermute(shards[step % 2], ("g", "r", "c"), moves[step]) for step in steps]


def return_experts(parts, n_blocks):
    return [
        lax.ppermute(part, ("g", "r", "c"), [(dst, src) for src, dst in pairs])
        for part, pairs in zip(parts, shard_moves(n_blocks))
    ]


def body(
    patches,
    lengths,
    slot_mask,
    expert_picks,
    priority_rank,
    class_labels,
    dense_weights,
    dense_first,
    dense_second,
    dense_average,
    router_weights,
    router_first,
    router_second,
    router_average,
    norm_params,
    norm_first,
    norm_second,
    norm_average,
    expert_in,
    in_first,
    in_second,
    in_average,
    expert_out,
    out_first,
    out_second,
    out_average,
    head_weights,
    head_first,
    head_second,
    head_average,
):
    n_blocks = lax.axis_size("g")
    sizes = {name: lax.axis_size(name) for name in ALL}
    rows_own, n_experts = router_weights.shape
    n_tail = max(8, n_experts)
    tail = jnp.zeros((n_tail, dense_weights.shape[2]), jnp.float32)
    tail = tail.at[:6, :rows_own].set(norm_params)
    tail = tail.at[:n_experts, 128 : 128 + rows_own].set(router_weights.T)
    rows_here, n_slots_row = slot_mask.shape
    tokens, model_width = patches.shape
    n_images = lengths.shape[0] * lengths.shape[1]
    capacity = (21 * tokens * TOP + 20 * n_experts - 1) // (20 * n_experts)
    padded = round_up(capacity, 16)
    shards = order_shards(expert_in, expert_out)
    own_chunks = fetch_experts(shards, n_blocks, range(EARLY))
    layer_b, gain_rows, router_t, columns = gather_weights(
        sizes,
        (lengths.shape[1], n_experts, capacity, padded),
        dense_weights,
        tail,
        expert_picks,
        priority_rank,
        slot_mask,
        lengths,
    )
    shards, layer_b = lax.optimization_barrier((shards, layer_b))
    own_chunks += fetch_experts(shards, n_blocks, range(EARLY, 2 * n_blocks))
    x_zero, a_one, qkv, att_out, x_one, a_two, router_probs, logs, pooled, part_importance = (
        dense_forward(
            n_experts, lengths, slot_mask, patches, layer_b, gain_rows, router_t, columns
        )
    )
    arrived, details = dispatch(sizes, n_experts, padded, a_two, router_probs, columns)
    activated, slope, result, part_pooled, other_chunks = expert_forward(
        sizes, arrived, details, own_chunks
    )
    g_head, d_pooled_all, d_pooled, g_norm_three, head_sums, total_importance = head_step(
        sizes,
        n_images,
        part_pooled,
        pooled,
        part_importance,
        gain_rows,
        head_weights,
        class_labels,
    )
    d_back, back_gate, *grads = expert_backward(
        sizes, arrived, details, d_pooled_all, result, slope, activated, own_chunks, other_chunks
    )
    parts = return_experts(grads, n_blocks)
    blocks = dense_backward(
        sizes,
        n_experts,
        padded,
        rows_own,
        lengths,
        slot_mask,
        patches,
        (x_zero, a_one, qkv, att_out, x_one, a_two, router_probs, logs),
        columns,
        layer_b,
        gain_rows,
        router_t,
        d_back,
        back_gate,
        d_pooled,
        total_importance,
        g_norm_three,
    )
    reduced, dense_sums = scatter_dense(sizes, blocks)
    g_one, g_two, totals = finish(
        sizes, n_experts, parts, head_sums, dense_sums, total_importance
    )
    n_dense = dense_weights.shape[0] * rows_own
    g_layers = reduced[:n_dense].reshape(-1, rows_own, model_width)
    g_norms = reduced[n_dense : n_dense + 6, :rows_own]
    g_router = reduced[n_dense : n_dense + n_experts, 128 : 128 + rows_own].T
    importance = total_importance[0, :n_experts]
    loss_value, grad_norm, factor = totals[0, 0], totals[1, 0], totals[2, 0]
    dense_out = adam_update(
        dense_weights, dense_first, dense_second, dense_average, g_layers, factor, base_rate
    )
    router_out = adam_update(
        router_weights, router_first, router_second, router_average, g_router, factor, base_rate
    )
    norm_out = adam_update(
        norm_params, norm_first, norm_second, norm_average, g_norms, factor, norm_rate
    )
    in_out = adam_update(expert_in, in_first, in_second, in_average, g_one, factor, base_rate)
    out_out = adam_update(expert_out, out_first, out_second, out_average, g_two, factor, base_rate)
    head_out = adam_update(
        head_weights, head_first, head_second, head_average, g_head, factor, base_rate
    )
    return (
        loss_value,
        importance,
        grad_norm,
        *dense_out,
        *router_out,
        *norm_out,
        *in_out,
        *out_out,
        *head_out,
    )


def solution(mesh):
    n_dp, n_expert = mesh.shape["dp"], mesh.shape["expert"]
    shaped = mesh.devices.reshape(n_dp // QUAD, QUAD, n_expert // 2, 2)
    fine = Mesh(shaped, ALL)
    rows = P(ALL, None)
    dense = P(None, ALL, None)
    norms = P(None, ALL)
    experts = P(("x", "c"), ("g", "r"), None)
    placed = (rows,) * 6 + (dense,) * 4 + (rows,) * 4 + (norms,) * 4 + (experts,) * 8 + (rows,) * 4
    results = (
        (P(),) * 3 + (dense,) * 4 + (rows,) * 4 + (norms,) * 4 + (experts,) * 8 + (rows,) * 4
    )
    return jax.shard_map(body, mesh=fine, in_specs=placed, out_specs=results, check_vma=False)
```

```python
import functools
import math

import jax
import jax.numpy as jnp
from jax import lax
from jax.experimental import pallas as pl
from jax.experimental.pallas import tpu as pltpu
from jax.sharding import Mesh
from jax.sharding import PartitionSpec as P

HEADS = 12
TOP = 2
STEP_COUNT = 10
QUAD = 4

high_prec = lax.Precision.HIGHEST
eps_norm = 1e-06
aux_weight = 0.01
clip_limit = 1.0
base_rate = 0.05
norm_rate = 0.5
beta_first = 0.9
beta_second = 0.999
weight_decay = 0.1
polyak_decay = 0.7
adam_eps = 1e-08
mask_fill = -1e30

ALL = ("g", "r", "x", "c")
MEMBERS = ("x", "r")


def adam_update(weight, first_state, second_state, average_state, gradient, factor, step_rate):
    clipped = gradient * factor
    first_new = beta_first * first_state + (1.0 - beta_first) * clipped
    second_new = beta_second * second_state + (1.0 - beta_second) * clipped * clipped
    first_hat = first_new / (1.0 - beta_first**STEP_COUNT)
    second_hat = second_new / (1.0 - beta_second**STEP_COUNT)
    weight_new = weight - step_rate * (
        first_hat / (jnp.sqrt(second_hat) + adam_eps) + weight_decay * weight
    )
    average_new = polyak_decay * average_state + (1.0 - polyak_decay) * weight_new
    return (weight_new, first_new, second_new, average_new)


MESH_ID = pl.DeviceIdType.MESH
VMEM = pltpu.VMEM
ANY = pl.ANY
MIB = 1 << 20


def cost(microseconds):
    return pl.CostEstimate(flops=int(microseconds * 1.15e9), bytes_accessed=0, transcendentals=0)


def whole(space=None):
    return pl.BlockSpec(memory_space=space or VMEM)


def round_up(value, step):
    return (value + step - 1) // step * step


class Place:
    def __init__(self, sizes):
        self.G, self.X = sizes["g"], sizes["x"]
        self.Z, self.Y = QUAD, sizes["g"]
        self.chips = self.Z * self.Y * self.X
        spot = lax.axis_index("g") * QUAD + lax.axis_index("r")
        self.z, self.y = lax.div(spot, self.Y), lax.rem(spot, self.Y)
        self.x, self.c = lax.axis_index("x"), lax.axis_index("c")
        self.g, self.r = lax.axis_index("g"), lax.axis_index("r")
        self.chip = spot * self.X + self.x
        self.member = self.x * QUAD + self.r

    def at(self, z=None, y=None, x=None, c=None):
        spot = (self.z if z is None else z) * self.Y + (self.y if y is None else y)
        return {
            "g": lax.div(spot, QUAD),
            "r": lax.rem(spot, QUAD),
            "x": self.x if x is None else x,
            "c": self.c if c is None else c,
        }

    def of_chip(self, chip):
        spot = lax.div(chip, self.X)
        return {
            "g": lax.div(spot, QUAD),
            "r": lax.rem(spot, QUAD),
            "x": lax.rem(chip, self.X),
            "c": self.c,
        }

    def of_member(self, member):
        return {
            "g": self.g,
            "r": lax.rem(member, QUAD),
            "x": lax.div(member, QUAD),
            "c": self.c,
        }

    def sibling(self):
        return self.at(c=1 - self.c)


def greet(peers):
    barrier = pltpu.get_barrier_semaphore()
    for peer in peers:
        pl.semaphore_signal(barrier, inc=1, device_id=peer, device_id_type=MESH_ID)
    pl.semaphore_wait(barrier, len(peers))


def send(src, dst, send_sem, recv_sem, peer):
    return pltpu.make_async_remote_copy(
        src_ref=src,
        dst_ref=dst,
        send_sem=send_sem,
        recv_sem=recv_sem,
        device_id=peer,
        device_id_type=MESH_ID,
    )


def others(me, count):
    return [lax.rem(me + step, count) for step in range(1, count)]


def grid_peers(at):
    peers = [at.at(z=z) for z in others(at.z, at.Z)]
    peers += [at.at(y=y) for y in others(at.y, at.Y)]
    peers += [at.at(x=x) for x in others(at.x, at.X)]
    return peers + [at.sibling()]


def gather_kernel(
    sizes, rows, mats, routing, dense_ref, tail_ref, pick_ref, rank_ref, mask_ref, length_ref,
    w_ref, gain_ref, router_ref, col_ref, land, *sems
):
    at = Place(sizes)
    Z, Y, X = at.Z, at.Y, at.X
    depth = land.shape[4]
    cut = depth // 2 // 16 * 16
    first, second = pl.ds(0, cut), pl.ds(cut, depth - cut)
    z_out, z_in, ya_out, ya_in, xb_out, xb_in, xa_out, xa_in, yb_out, yb_in, c_out, c_in = sems
    block = jnp.concatenate([dense_ref[...].reshape(mats * rows, -1), tail_ref[...]], 0)
    if block.shape[0] < depth:
        block = jnp.pad(block, ((0, depth - block.shape[0]), (0, 0)))
    mine = land.at[at.c, at.z, at.x, at.y]
    mine[...] = block.astype(jnp.bfloat16)
    greet(grid_peers(at))
    started = []

    def begin(copy):
        copy.start()
        started.append(copy)

    order = [at.z] + [lax.rem(at.z + k, Z) for k in (1, 3, 2)]
    for z in order[1:]:
        begin(send(mine, mine, z_out.at[z], z_in.at[at.z], at.at(z=z)))

    def one(z):
        part = land.at[at.c, z, at.x, at.y]
        for y in others(at.y, Y):
            begin(send(part.at[first], part.at[first], ya_out.at[z, y], ya_in.at[z, at.y], at.at(y=y)))
        for x in others(at.x, X):
            begin(send(part.at[second], part.at[second], xb_out.at[z, x], xb_in.at[z, at.x], at.at(x=x)))

    def two(z):
        for y in others(at.y, Y):
            part = land.at[at.c, z, at.x, y, first]
            send(part, part, ya_out.at[z, y], ya_in.at[z, y], at.at(y=y)).wait_recv()
        line = land.at[at.c, z, at.x, :, first]
        for x in others(at.x, X):
            begin(send(line, line, xa_out.at[z, x], xa_in.at[z, at.x], at.at(x=x)))
        for x in others(at.x, X):
            part = land.at[at.c, z, x, at.y, second]
            send(part, part, xb_out.at[z, x], xb_in.at[z, x], at.at(x=x)).wait_recv()
        line = land.at[at.c, z, :, at.y, second]
        for y in others(at.y, Y):
            begin(send(line, line, yb_out.at[z, y], yb_in.at[z, at.y], at.at(y=y)))

    def three(z):
        for x in others(at.x, X):
            line = land.at[at.c, z, x, :, first]
            send(line, line, xa_out.at[z, x], xa_in.at[z, x], at.at(x=x)).wait_recv()
        for y in others(at.y, Y):
            line = land.at[at.c, z, :, y, second]
            send(line, line, yb_out.at[z, y], yb_in.at[z, y], at.at(y=y)).wait_recv()
        plane = land.at[at.c, z]
        begin(send(plane, plane, c_out.at[z], c_in.at[z], at.sibling()))

    for step in range(Z + 2):
        if step < Z:
            if step > 0:
                z = order[step]
                part = land.at[at.c, z, at.x, at.y]
                send(part, part, z_out.at[z], z_in.at[z], at.at(z=z)).wait_recv()
            one(order[step])
        if step == 0:
            col_ref[...] = route_math(*routing, pick_ref, rank_ref, mask_ref, length_ref)
        if 0 <= step - 1 < Z:
            two(order[step - 1])
        if 0 <= step - 2 < Z:
            three(order[step - 2])
    for z in order:
        plane = land.at[1 - at.c, z]
        send(plane, plane, c_out.at[z], c_in.at[z], at.sibling()).wait_recv()
    for copy in started:
        copy.wait_send()
    chips = [(z, y, x) for z in range(Z) for y in range(Y) for x in range(X)]
    cores = [(c, z, x, y) for z, y, x in chips for c in range(2)]
    group = 16 // math.gcd(16, rows)
    for start in range(0, len(cores), group):
        for mat in range(mats):
            w_ref[mat, start * rows : (start + group) * rows] = jnp.concatenate(
                [land[spot][mat * rows : (mat + 1) * rows] for spot in cores[start : start + group]], 0
            )
    base, count = mats * rows, tail_ref.shape[0]
    tails = [land[spot][base : base + count].astype(jnp.float32) for spot in cores]
    gain_ref[...] = jnp.concatenate([tail[:8, :rows] for tail in tails], 1)
    router_ref[...] = jnp.concatenate([tail[:, 128 : 128 + rows] for tail in tails], 1)


def gather_weights(sizes, routing, dense, tail, picks, ranks, slot_mask, lengths):
    mats, rows, width = dense.shape
    count = tail.shape[0]
    depth = round_up(mats * rows + count, 16)
    Z, Y, X = QUAD, sizes["g"], sizes["x"]
    dma = pltpu.SemaphoreType.DMA
    by_y, by_x = dma((Z, Y)), dma((Z, X))
    return pl.pallas_call(
        functools.partial(gather_kernel, sizes, rows, mats, routing),
        out_shape=(
            jax.ShapeDtypeStruct((mats, width, width), jnp.bfloat16),
            jax.ShapeDtypeStruct((8, width), jnp.float32),
            jax.ShapeDtypeStruct((count, width), jnp.float32),
            jax.ShapeDtypeStruct((picks.shape[0], 128), jnp.float32),
        ),
        in_specs=[whole()] * 6,
        out_specs=(whole(),) * 4,
        scratch_shapes=[VMEM((2, Z, X, Y, depth, width), jnp.bfloat16), dma((Z,)), dma((Z,))]
        + [by_y, by_y, by_x, by_x, by_x, by_x, by_y, by_y, dma((Z,)), dma((Z,))],
        compiler_params=pltpu.CompilerParams(
            collective_id=1, has_side_effects=True, vmem_limit_bytes=48 * MIB
        ),
        cost_estimate=cost(44),
        name="gather_weights",
    )(dense, tail, picks, ranks, slot_mask, lengths)


def total_square(value):
    return jnp.sum(jnp.sum(value * value, 0, keepdims=True), 1, keepdims=True)


def scatter_kernel(sizes, g_ref, out_ref, square_ref, hold, sib, got_xa, got_yb, got_ya, got_xb, got_z, *sems):
    at = Place(sizes)
    Z, Y, X = at.Z, at.Y, at.X
    depth = g_ref.shape[4]
    cut = depth // 2 // 16 * 16
    first, second = pl.ds(0, cut), pl.ds(cut, depth - cut)
    c_out, c_in, xa_out, xa_in, yb_out, yb_in, ya_out, ya_in, xb_out, xb_in, z_out, z_in = sems
    greet(grid_peers(at))
    started = []

    def begin(copy):
        copy.start()
        started.append(copy)

    wide = lambda value: value.astype(jnp.float32)
    order = [lax.rem(at.z + k, Z) for k in (2, 1, 3)] + [at.z]
    for z in order:
        begin(send(g_ref.at[1 - at.c, z], sib.at[z], c_out.at[z], c_in.at[z], at.sibling()))

    def one(z):
        send(sib.at[z], sib.at[z], c_out.at[z], c_in.at[z], at.sibling()).wait_recv()
        hold[z] = (wide(g_ref[at.c, z]) + wide(sib[z])).astype(jnp.bfloat16)
        for x in others(at.x, X):
            begin(send(hold.at[z, x, :, first], got_xa.at[z, at.x], xa_out.at[z, x], xa_in.at[z, at.x], at.at(x=x)))
        for y in others(at.y, Y):
            begin(send(hold.at[z, :, y, second], got_yb.at[z, at.y], yb_out.at[z, y], yb_in.at[z, at.y], at.at(y=y)))

    def two(z):
        total = wide(hold[z, at.x, :, first])
        for x in others(at.x, X):
            send(got_xa.at[z, x], got_xa.at[z, x], xa_out.at[z, x], xa_in.at[z, x], at.at(x=x)).wait_recv()
            total = total + wide(got_xa[z, x])
        hold[z, at.x, :, first] = total.astype(jnp.bfloat16)
        for y in others(at.y, Y):
            begin(send(hold.at[z, at.x, y, first], got_ya.at[z, at.y], ya_out.at[z, y], ya_in.at[z, at.y], at.at(y=y)))
        total = wide(hold[z, :, at.y, second])
        for y in others(at.y, Y):
            send(got_yb.at[z, y], got_yb.at[z, y], yb_out.at[z, y], yb_in.at[z, y], at.at(y=y)).wait_recv()
            total = total + wide(got_yb[z, y])
        hold[z, :, at.y, second] = total.astype(jnp.bfloat16)
        for x in others(at.x, X):
            begin(send(hold.at[z, x, at.y, second], got_xb.at[z, at.x], xb_out.at[z, x], xb_in.at[z, at.x], at.at(x=x)))

    def three(z, last):
        total = wide(hold[z, at.x, at.y, first])
        for y in others(at.y, Y):
            send(got_ya.at[z, y], got_ya.at[z, y], ya_out.at[z, y], ya_in.at[z, y], at.at(y=y)).wait_recv()
            total = total + wide(got_ya[z, y])
        rest = wide(hold[z, at.x, at.y, second])
        for x in others(at.x, X):
            send(got_xb.at[z, x], got_xb.at[z, x], xb_out.at[z, x], xb_in.at[z, x], at.at(x=x)).wait_recv()
            rest = rest + wide(got_xb[z, x])
        if last:
            out_ref[first] = total
            out_ref[second] = rest
            return
        mine = hold.at[z, at.x, at.y]
        mine[first] = total.astype(jnp.bfloat16)
        mine[second] = rest.astype(jnp.bfloat16)
        begin(send(mine, got_z.at[at.z], z_out.at[z], z_in.at[at.z], at.at(z=z)))

    for step in range(Z + 2):
        if step < Z:
            one(order[step])
        if 0 <= step - 1 < Z:
            two(order[step - 1])
        if 0 <= step - 2 < Z:
            three(order[step - 2], step - 2 == Z - 1)
    for z in order[:-1]:
        send(got_z.at[z], got_z.at[z], z_out.at[z], z_in.at[z], at.at(z=z)).wait_recv()
        out_ref[...] += wide(got_z[z])
    square_ref[...] = jnp.broadcast_to(total_square(out_ref[...]), square_ref.shape)
    for copy in started:
        copy.wait_send()


def scatter_dense(sizes, blocks):
    unused, Z, X, Y, depth, width = blocks.shape
    dma = pltpu.SemaphoreType.DMA
    by_y, by_x, by_z = dma((Z, Y)), dma((Z, X)), dma((Z,))
    cut = depth // 2 // 16 * 16
    half = jnp.bfloat16
    return pl.pallas_call(
        functools.partial(scatter_kernel, sizes),
        out_shape=(
            jax.ShapeDtypeStruct((depth, width), jnp.float32),
            jax.ShapeDtypeStruct((8, 128), jnp.float32),
        ),
        in_specs=[whole()],
        out_specs=(whole(), whole()),
        scratch_shapes=[
            VMEM((Z, X, Y, depth, width), half),
            VMEM((Z, X, Y, depth, width), half),
            VMEM((Z, X, Y, cut, width), half),
            VMEM((Z, Y, X, depth - cut, width), half),
            VMEM((Z, Y, cut, width), half),
            VMEM((Z, X, depth - cut, width), half),
            VMEM((Z, depth, width), half),
        ]
        + [by_z, by_z, by_x, by_x, by_y, by_y, by_y, by_y, by_x, by_x, by_z, by_z],
        compiler_params=pltpu.CompilerParams(
            collective_id=2, has_side_effects=True, vmem_limit_bytes=28 * MIB
        ),
        cost_estimate=cost(45),
        name="scatter_dense",
    )(blocks)


def finish_kernel(sizes, n_experts, head_ref, dense_ref, imp_ref, *refs):
    at = Place(sizes)
    many = len(refs) - 7
    parts = refs[:many]
    first_ref, second_ref, out_ref, land, own, out_sem, in_sem = refs[many:]
    count = 2 * at.chips
    me = at.chip * 2 + at.c
    ids = others(me, count)

    def peer(device):
        spot = at.of_chip(lax.div(device, 2))
        spot["c"] = lax.rem(device, 2)
        return spot

    greet([peer(device) for device in ids])
    place = lax.rem(at.g * QUAD + at.r, 2)
    square = dense_ref[0:1, 0:1] + head_ref[1:2, 0:1]
    for parity in range(2):
        expert = place if parity == 0 else 1 - place
        for index, ref in enumerate((first_ref, second_ref)):
            total = None
            for step in range(parity, many, 2):
                found = parts[step][index].astype(jnp.float32)
                total = found if total is None else total + found
            ref[expert] = total
            square = square + total_square(total)
    line = lax.broadcasted_iota(jnp.int32, own.shape, 0)
    own[...] = jnp.where(line == 0, head_ref[0:1, 0:1], jnp.where(line == 1, square, 0.0))
    land[me] = own[...]
    copies = [send(own, land.at[me], out_sem.at[d], in_sem.at[me], peer(d)) for d in ids]
    for copy in copies:
        copy.start()
    importance = imp_ref[0:1, 0:128]
    head = lax.broadcasted_iota(jnp.int32, (1, 128), 1) < n_experts
    centre = jnp.sum(jnp.where(head, importance, 0.0), 1, keepdims=True) / n_experts
    away = jnp.where(head, importance - centre, 0.0)
    spread = jnp.sum(away * away, 1, keepdims=True) / n_experts
    balance = aux_weight * spread / (centre * centre)
    for d in ids:
        send(land.at[d], land.at[d], out_sem.at[d], in_sem.at[d], peer(d)).wait_recv()
    sums = jnp.sum(land[...], 0)
    norm = jnp.sqrt(sums[1:2, 0:1])
    factor = jnp.minimum(1.0, clip_limit / norm)
    loss = sums[0:1, 0:1] + balance
    out_ref[...] = jnp.where(line == 0, loss, jnp.where(line == 1, norm, factor))
    for copy in copies:
        copy.wait_send()


def finish(sizes, n_experts, parts, head_sums, dense_sums, importance):
    devices = sizes["g"] * QUAD * sizes["x"] * 2
    unused, rows, width = parts[0].shape
    dma = pltpu.SemaphoreType.DMA
    grads = jax.ShapeDtypeStruct((2, rows, width), jnp.float32)
    return pl.pallas_call(
        functools.partial(finish_kernel, sizes, n_experts),
        out_shape=(grads, grads, jax.ShapeDtypeStruct((8, 128), jnp.float32)),
        in_specs=[whole()] * (3 + len(parts)),
        out_specs=(whole(),) * 3,
        scratch_shapes=[
            VMEM((devices, 8, 128), jnp.float32),
            VMEM((8, 128), jnp.float32),
            dma((devices,)),
            dma((devices,)),
        ],
        compiler_params=pltpu.CompilerParams(
            collective_id=3, has_side_effects=True, vmem_limit_bytes=20 * MIB
        ),
        cost_estimate=cost(10),
        name="finish",
    )(head_sums, dense_sums, importance, *parts)


IMAGE_PAD = 16


def split_three(value):
    high = value.astype(jnp.bfloat16)
    rest = value - high.astype(jnp.float32)
    middle = rest.astype(jnp.bfloat16)
    return high, middle, (rest - middle.astype(jnp.float32)).astype(jnp.bfloat16)


def dot_f32(left, right, dims):
    return lax.dot_general(left, right, (dims, ((), ())), preferred_element_type=jnp.float32)


NN = ((1,), (0,))
NT = ((1,), (1,))
TN = ((0,), (0,))


def norm_parts(values):
    centre = values - jnp.mean(values, -1, keepdims=True)
    spread = jnp.mean(centre * centre, -1, keepdims=True)
    scale = lax.rsqrt(spread + eps_norm)
    return centre * scale, scale


def norm_back(d_out, scaled, scale, gain):
    pulled = d_out * gain
    return scale * (
        pulled
        - jnp.mean(pulled, -1, keepdims=True)
        - scaled * jnp.mean(pulled * scaled, -1, keepdims=True)
    )


def head_kernel(
    sizes, images, part_ref, own_ref, imp_ref, gain_ref, head_ref, label_ref,
    g_head_ref, d_pool_ref, own_d_ref, g_norm_ref, sums_ref, total_imp_ref,
    in_part, rows, d_rows, d_sib, d_sum, d_in, head_b, labels, d_logits, *sems
):
    at = Place(sizes)
    chips, members = at.chips, QUAD * at.X
    devices = 2 * chips
    p_out, p_in, r_out, r_in, s_out, s_in, d_out, d_in_sem, b_out, b_in = sems
    width = own_ref.shape[1]
    same_core = others(at.chip, chips)
    greet([at.of_chip(chip) for chip in same_core] + [at.sibling()])
    started = []

    def begin(copy):
        copy.start()
        started.append(copy)

    team = others(at.member, members)
    for member in team:
        begin(send(part_ref.at[member], in_part.at[at.member], p_out.at[member], p_in.at[at.member], at.of_member(member)))
    in_part[at.member] = part_ref[at.member]
    head_b[...] = head_ref[...].astype(jnp.bfloat16)
    wide = devices * IMAGE_PAD
    spot = lax.broadcasted_iota(jnp.int32, (label_ref.shape[1], wide), 1)
    given = lax.broadcasted_iota(jnp.int32, (label_ref.shape[1], wide), 0)
    image = lax.rem(spot, IMAGE_PAD)
    device = lax.rem(lax.div(spot, IMAGE_PAD), chips) * 2 + lax.div(spot, IMAGE_PAD * chips)
    chosen = ((device * images + image == given) & (image < images)).astype(jnp.bfloat16)
    labels[...] = dot_f32(label_ref[...].astype(jnp.float32).astype(jnp.bfloat16), chosen, NN).astype(jnp.bfloat16)
    for member in team:
        send(in_part.at[member], in_part.at[member], p_out.at[member], p_in.at[member], at.of_member(member)).wait_recv()
    pooled = own_ref[...] + jnp.sum(in_part[...], 0)
    scaled, scale = norm_parts(pooled)
    gain, shift = gain_ref[2:3], gain_ref[5:6]
    a_three = scaled * gain + shift
    row = lax.broadcasted_iota(jnp.int32, (IMAGE_PAD, width), 0)
    block = jnp.where(row < images, a_three, 0.0)
    pieces = split_three(imp_ref[0:1])
    for index, piece in enumerate(pieces):
        block = jnp.where(row == images + index, piece.astype(jnp.float32), block)
    rows[at.c, at.chip] = block.astype(jnp.bfloat16)
    mine = rows.at[at.c, at.chip]
    for chip in same_core:
        begin(send(mine, mine, r_out.at[chip], r_in.at[at.chip], at.of_chip(chip)))
    for chip in same_core:
        part = rows.at[at.c, chip]
        send(part, part, r_out.at[chip], r_in.at[chip], at.of_chip(chip)).wait_recv()
    begin(send(rows.at[at.c], rows.at[at.c], s_out.at[0], s_in.at[0], at.sibling()))
    send(rows.at[1 - at.c], rows.at[1 - at.c], s_out.at[0], s_in.at[0], at.sibling()).wait_recv()
    gathered = rows[...].reshape(wide, width)
    in_block = lax.rem(lax.broadcasted_iota(jnp.int32, (wide, width), 0), IMAGE_PAD)
    total = jnp.sum(jnp.where(in_block >= images, gathered.astype(jnp.float32), 0.0), 0, keepdims=True)
    total_imp_ref[...] = jnp.broadcast_to(total, total_imp_ref.shape)
    gathered = jnp.where(in_block < images, gathered.astype(jnp.float32), 0.0).astype(jnp.bfloat16)
    logits = dot_f32(head_b[...], gathered, NT)
    image = lax.rem(lax.broadcasted_iota(jnp.int32, logits.shape, 1), IMAGE_PAD)
    count = devices * images
    target = labels[...].astype(jnp.float32)
    power = jnp.exp(-jnp.abs(logits))
    loss = jnp.maximum(logits, 0.0) + jnp.log1p(power) - target * logits
    loss = jnp.sum(jnp.where(image < images, loss, 0.0), 1, keepdims=True)
    loss = jnp.sum(loss, 0, keepdims=True) / count
    chance = jnp.where(logits >= 0.0, 1.0, power) / (1.0 + power)
    d_logits[...] = jnp.where(image < images, (chance - target) / count, 0.0).astype(jnp.bfloat16)
    partial = dot_f32(d_logits[...], head_b[...], TN)
    d_rows[...] = partial.reshape(d_rows.shape).astype(jnp.bfloat16)
    begin(send(d_rows.at[1 - at.c], d_sib, s_out.at[1], s_in.at[1], at.sibling()))
    g_head = dot_f32(d_logits[...], gathered, NN)
    g_head_ref[...] = g_head
    line = lax.broadcasted_iota(jnp.int32, sums_ref.shape, 0)
    sums_ref[...] = jnp.where(line == 0, loss, jnp.where(line == 1, total_square(g_head), 0.0))
    send(d_sib, d_sib, s_out.at[1], s_in.at[1], at.sibling()).wait_recv()
    d_sum[...] = (d_rows[at.c].astype(jnp.float32) + d_sib[...].astype(jnp.float32)).astype(jnp.bfloat16)
    for chip in same_core:
        begin(send(d_sum.at[chip], d_in.at[at.chip], d_out.at[chip], d_in_sem.at[at.chip], at.of_chip(chip)))
    d_in[at.chip] = d_sum[at.chip]
    for chip in same_core:
        send(d_in.at[chip], d_in.at[chip], d_out.at[chip], d_in_sem.at[chip], at.of_chip(chip)).wait_recv()
    d_norm = jnp.sum(d_in[...].astype(jnp.float32), 0)
    d_norm = jnp.where(row < images, d_norm, 0.0)
    d_pooled = norm_back(d_norm, scaled, scale, gain)
    d_pooled = jnp.where(row < images, d_pooled, 0.0)
    d_gain = jnp.sum(d_norm * scaled, 0, keepdims=True)
    d_shift = jnp.sum(d_norm, 0, keepdims=True)
    line = lax.broadcasted_iota(jnp.int32, g_norm_ref.shape, 0)
    g_norm_ref[...] = jnp.where(line == 2, d_gain, jnp.where(line == 5, d_shift, 0.0))
    own_d_ref[...] = d_pooled
    d_pool_ref[at.member] = d_pooled
    mine = d_pool_ref.at[at.member]
    for member in team:
        begin(send(own_d_ref, mine, b_out.at[member], b_in.at[at.member], at.of_member(member)))
    for member in team:
        part = d_pool_ref.at[member]
        send(part, part, b_out.at[member], b_in.at[member], at.of_member(member)).wait_recv()
    for copy in started:
        copy.wait_send()


def head_step(sizes, images, part, own, imp, gains, head, label):
    members = QUAD * sizes["x"]
    chips = members * sizes["g"]
    classes, width = head.shape
    wide = 2 * chips * IMAGE_PAD
    dma = pltpu.SemaphoreType.DMA
    by_member, by_chip = dma((members,)), dma((chips,))
    f32, half = jnp.float32, jnp.bfloat16
    blocks = (chips, IMAGE_PAD, width)
    return pl.pallas_call(
        functools.partial(head_kernel, sizes, images),
        out_shape=(
            jax.ShapeDtypeStruct((classes, width), f32),
            jax.ShapeDtypeStruct((members, IMAGE_PAD, width), f32),
            jax.ShapeDtypeStruct((IMAGE_PAD, width), f32),
            jax.ShapeDtypeStruct((8, width), f32),
            jax.ShapeDtypeStruct((8, 128), f32),
            jax.ShapeDtypeStruct((8, width), f32),
        ),
        in_specs=[whole()] * 6,
        out_specs=(whole(),) * 6,
        scratch_shapes=[
            VMEM((members, IMAGE_PAD, width), f32),
            VMEM((2, *blocks), half),
            VMEM((2, *blocks), half),
            VMEM(blocks, half),
            VMEM(blocks, half),
            VMEM(blocks, half),
            VMEM((classes, width), half),
            VMEM((classes, wide), half),
            VMEM((classes, wide), half),
        ]
        + [by_member, by_member, by_chip, by_chip, dma((2,)), dma((2,)), by_chip, by_chip]
        + [by_member, by_member],
        compiler_params=pltpu.CompilerParams(
            collective_id=4, has_side_effects=True, vmem_limit_bytes=56 * MIB
        ),
        cost_estimate=cost(42),
        name="head_step",
    )(part, own, imp, gains, head, label)


def route_math(per_image, n_experts, capacity, padded, pick_ref, rank_ref, mask_ref, length_ref):
    rows_here, span = mask_ref.shape
    tokens = rows_here * span
    valid = mask_ref[...].astype(jnp.float32)
    lengths = length_ref[...]
    position = lax.broadcasted_iota(jnp.int32, (rows_here, span), 1)
    segment = jnp.zeros((rows_here, span), jnp.int32)
    bound = jnp.zeros((rows_here, 1), jnp.int32)
    for image in range(per_image):
        bound = bound + lengths[:, image : image + 1]
        segment = segment + jnp.where(position >= bound, 1, 0)
    pool = jnp.zeros_like(valid)
    for image in range(per_image):
        member = jnp.where(segment == image, valid, 0.0)
        pool = pool + member / jnp.maximum(jnp.sum(member, 1, keepdims=True), 1.0)
    line = lax.broadcasted_iota(jnp.int32, (rows_here, span), 0)
    image = (segment + per_image * line).astype(jnp.float32)

    def flat(value):
        return jnp.concatenate([value[i : i + 1] for i in range(rows_here)], 1)

    rank_row = rank_ref[...].astype(jnp.float32)
    table = jnp.concatenate([flat(valid), flat(pool), flat(image), rank_row], 0)
    table = jnp.concatenate([table, jnp.zeros((124, tokens), jnp.float32)], 0).T
    valid_col, pool_col, image_col, rank_col = (table[:, i : i + 1] for i in range(4))
    picks = pick_ref[...]
    pick_one, pick_two = picks[:, 0:1], picks[:, 1:2]
    lane = lax.broadcasted_iota(jnp.int32, (tokens, 128), 1)
    in_first, in_second = lane < n_experts, (lane >= n_experts) & (lane < 2 * n_experts)
    hot = jnp.where(in_first & (pick_one == lane), valid_col, 0.0)
    hot = hot + jnp.where(in_second & (pick_two == lane - n_experts), valid_col, 0.0)
    shifted = jnp.where(in_second & (pick_one == lane - n_experts), valid_col, 0.0)
    before = jnp.where(rank_row < rank_col, 1.0, 0.0).astype(jnp.bfloat16)
    ahead = dot_f32(before, hot.astype(jnp.bfloat16), NN) + jnp.sum(shifted, 0, keepdims=True)
    counted = hot * ahead
    pos_one = jnp.sum(jnp.where(in_first, counted, 0.0), 1, keepdims=True)
    pos_two = jnp.sum(jnp.where(in_second, counted, 0.0), 1, keepdims=True)

    def place(pick, pos):
        kept = (valid_col > 0.0) & (pos < capacity)
        return jnp.where(kept, pick.astype(jnp.float32) * padded + pos, -1.0)

    columns = (
        place(pick_one, pos_one),
        place(pick_two, pos_two),
        valid_col,
        pool_col,
        image_col,
        pick_one.astype(jnp.float32),
        pick_two.astype(jnp.float32),
    )
    result = jnp.zeros((tokens, 128), jnp.float32)
    for index, column in enumerate(columns):
        result = jnp.where(lane == index, column, result)
    return result


def allowed_slots(lengths, row, images, valid_row, span):
    query = lax.broadcasted_iota(jnp.int32, (span, span), 0)
    key = lax.broadcasted_iota(jnp.int32, (span, span), 1)
    bound = 0
    query_seg, key_seg = jnp.zeros((span, span), jnp.int32), jnp.zeros((span, span), jnp.int32)
    for image in range(images):
        bound = bound + lengths[row, image]
        query_seg = query_seg + jnp.where(query >= bound, 1, 0)
        key_seg = key_seg + jnp.where(key >= bound, 1, 0)
    return (query_seg == key_seg) & ((valid_row > 0) | (query == key))


TILE = 32


def tiles(count):
    return [slice(start, min(start + TILE, count)) for start in range(0, count, TILE)]


class Team:
    def __init__(self, at):
        self.at, self.span = at, 2 * at.G
        self.spot = at.g * QUAD + at.r

    def target(self, step):
        at = self.at
        chosen = lax.rem(self.spot + step, self.span)
        block, index = lax.div(chosen, 2), lax.rem(chosen, 2)
        core = lax.div(self.spot, self.span)
        r = 2 * at.c + index
        own = (block == at.g) & (r == at.r) & (core == at.c)
        return {"g": block, "r": r, "x": at.x, "c": core}, index, own

    def source(self, step):
        at = self.at
        chosen = at.g * 2 + lax.rem(at.r, 2)
        spot = at.c * self.span + lax.rem(chosen - step + self.span, self.span)
        device = {"g": lax.div(spot, QUAD), "r": lax.rem(spot, QUAD), "x": at.x, "c": lax.div(at.r, 2)}
        return device, lax.rem(at.r, 2)

    def peers(self):
        at = self.at
        count = 2 * at.G * QUAD
        me = self.spot * 2 + at.c
        line = []
        for device in others(me, count):
            spot = lax.div(device, 2)
            line.append(
                {"g": lax.div(spot, QUAD), "r": lax.rem(spot, QUAD), "x": at.x, "c": lax.rem(device, 2)}
            )
        for x in others(at.x, at.X):
            line += [{"g": at.g, "r": r, "x": x, "c": at.c} for r in range(QUAD)]
        return line


def image_hot(detail, padded):
    image = detail[2:3, :padded]
    line = lax.broadcasted_iota(jnp.int32, (IMAGE_PAD, padded), 0).astype(jnp.float32)
    return line == image


def forward_kernel(
    sizes, n_experts, images, padded,
    length_ref, mask_ref, patch_ref, w_ref, gain_ref, router_ref, col_ref, shard_ref,
    x_zero_out, a_one_out, qkv_out, att_out, x_one_out, a_two_out, prob_ref, lse_ref, pool_ref, imp_ref,
    rows_out, detail_out, act_out, slope_out, y_out, part_ref, weight_out,
    x_zero_buf, a_one_buf, qkv_buf, att_buf, x_one_buf, a_two_ref, weights, send_rows, send_detail, places,
    rows_in, detail_in, total, act_buf, slope_buf, dense_sem, keep_sem, own_sem,
    w_out, w_in, s_out, s_in, r_out, r_in, m_out, m_in, act_sem, slope_sem
):
    at = Place(sizes)
    team = Team(at)
    half = weights.shape[1]
    span, width = mask_ref.shape[2], patch_ref.shape[1]
    rows_here = mask_ref.shape[0]
    tokens = rows_here * span
    greet(team.peers())

    def shard_copy(step):
        device, index, own = team.target(step)
        return send(
            shard_ref.at[index], weights.at[0, step], w_out.at[step], w_in.at[step], device
        )

    def shard_own(step):
        device, index, own = team.target(step)
        return pltpu.make_async_copy(shard_ref.at[index], weights.at[0, step], w_in.at[step])

    for step in range(half):
        own = team.target(step)[2]

        @pl.when(own)
        def _():
            shard_own(step).start()

        @pl.when(jnp.logical_not(own))
        def _():
            shard_copy(step).start()

    dense = (
        (x_zero_buf, x_zero_out), (a_one_buf, a_one_out), (qkv_buf, qkv_out), (att_buf, att_out), (x_one_buf, x_one_out),
    )

    def dense_copies(row):
        slot = lax.rem(row, 2)
        here = pl.ds(pl.multiple_of(row * span, 16), span)
        return [
            pltpu.make_async_copy(buf.at[slot], out.at[here], dense_sem.at[index, slot])
            for index, (buf, out) in enumerate(dense)
        ]

    pool_ref[...] = jnp.zeros_like(pool_ref)
    imp_ref[...] = jnp.zeros_like(imp_ref)
    routers = router_ref[...].astype(jnp.bfloat16)
    if routers.shape[0] < 128:
        routers = jnp.concatenate(
            [routers, jnp.zeros((128 - routers.shape[0], width), jnp.bfloat16)], 0
        )
    lane = lax.broadcasted_iota(jnp.int32, (span, 128), 1)

    def dense_row(row, carry):
        @pl.when(row >= 2)
        def _():
            for copy in dense_copies(row - 2):
                copy.wait()

        slot = lax.rem(row, 2)
        here = pl.ds(pl.multiple_of(row * span, 16), span)
        x_zero = dot_f32(patch_ref[here], w_ref[0], NN)
        x_zero_buf[slot] = x_zero
        a_one = (norm_parts(x_zero)[0] * gain_ref[0:1] + gain_ref[3:4]).astype(jnp.bfloat16)
        a_one_buf[slot] = a_one
        for part in range(3):
            qkv_buf[slot, :, part * width : (part + 1) * width] = dot_f32(
                a_one, w_ref[1 + part], NN
            ).astype(jnp.bfloat16)
        open_to = allowed_slots(length_ref, row, images, mask_ref[row], span)
        logs = jnp.zeros((span, 128), jnp.float32)
        for pair in range(width // 128):
            query, key, value = (
                qkv_buf[slot, :, part * width + pair * 128 : part * width + (pair + 1) * 128]
                for part in range(3)
            )
            outs = []
            for side in range(2):
                held = jnp.where((lane < 64) == (side == 0), query, jnp.zeros_like(query))
                scores = jnp.where(open_to, dot_f32(held, key, NT) * 64**-0.5, mask_fill)
                top = jnp.max(scores, 1, keepdims=True)
                powers = jnp.exp(scores - top)
                whole_sum = jnp.sum(powers, 1, keepdims=True)
                probs = (powers * (1.0 / whole_sum)).astype(jnp.bfloat16)
                outs.append(dot_f32(probs, value, NN))
                logs = jnp.where(lane == 2 * pair + side, top + jnp.log(whole_sum), logs)
            att_buf[slot, :, pair * 128 : (pair + 1) * 128] = jnp.where(
                lane < 64, outs[0], outs[1]
            ).astype(jnp.bfloat16)
        lse_ref[here] = logs
        x_one = x_zero + dot_f32(att_buf[slot], w_ref[4], NN)
        x_one_buf[slot] = x_one
        a_two = (norm_parts(x_one)[0] * gain_ref[1:2] + gain_ref[4:5]).astype(jnp.bfloat16)
        a_two_ref[here] = a_two
        logits = jnp.where(lane < n_experts, dot_f32(a_two, routers, NT), mask_fill)
        powers = jnp.exp(logits - jnp.max(logits, 1, keepdims=True))
        probs = powers / jnp.sum(powers, 1, keepdims=True)
        prob_ref[here] = probs
        columns = col_ref[here]
        valid, pool, image = columns[:, 2:3], columns[:, 3:4], columns[:, 4:5]
        imp_ref[0:1, 0:128] += jnp.sum(probs * valid, 0, keepdims=True)
        line = lax.broadcasted_iota(jnp.int32, pool_ref.shape, 0)
        for index in range(images):
            number = row * images + index
            weight = jnp.where(image == number.astype(jnp.float32), pool, 0.0)
            pooled = jnp.sum(x_one * weight, 0, keepdims=True)
            pool_ref[...] = jnp.where(line == number, pooled, pool_ref[...])
        for copy in dense_copies(row):
            copy.start()
        return carry

    lax.fori_loop(0, rows_here, dense_row, 0)

    columns = col_ref[...]
    places[...] = columns.T[:8]
    lane = lax.broadcasted_iota(jnp.int32, (tokens, 128), 1)
    kind, expert = lax.div(lane, n_experts), lax.rem(lane, n_experts).astype(jnp.float32)
    slot_lane = lax.broadcasted_iota(jnp.int32, (tokens, send_detail.shape[2]), 1).astype(jnp.float32)
    pool, image = columns[:, 3:4], columns[:, 4:5]
    details = None
    for choice in range(2):
        slot, pick = columns[:, choice : choice + 1], columns[:, 5 + choice : 6 + choice]
        hot = (expert == pick) & (slot >= 0.0)
        gate = jnp.sum(jnp.where(hot & (kind == 0), prob_ref[...], 0.0), 1, keepdims=True)
        values = jnp.zeros((tokens, 128), jnp.float32)
        pieces = [*split_three(gate), *split_three(pool), image]
        for index, piece in enumerate(pieces):
            values = jnp.where(kind == index, piece.astype(jnp.float32), values)
        values = jnp.where(hot, values, 0.0).astype(jnp.bfloat16)
        spot = jnp.where(slot >= 0.0, slot - pick * padded, -1.0)
        chosen = jnp.where(spot == slot_lane, 1.0, 0.0).astype(jnp.bfloat16)
        found = dot_f32(values, chosen, TN)
        details = found if details is None else details + found
    n = n_experts
    gates = details[0:n] + details[n : 2 * n] + details[2 * n : 3 * n]
    pools = details[3 * n : 4 * n] + details[4 * n : 5 * n] + details[5 * n : 6 * n]
    numbers = details[6 * n : 7 * n]
    for index in range(n):
        for spot, value in enumerate((gates, pools, numbers)):
            send_detail[index, spot : spot + 1] = value[index : index + 1]
        send_detail[index, 3:8] = jnp.zeros((5, send_detail.shape[2]), jnp.float32)

    def rows_of(member):
        slots = lax.broadcasted_iota(jnp.int32, (padded, tokens), 0) + member * padded
        slots = slots.astype(jnp.float32)
        match = (slots == places[0:1]) | (slots == places[1:2])
        match = jnp.where(match, 1.0, 0.0).astype(jnp.bfloat16)
        return dot_f32(match, a_two_ref[...], NN).astype(jnp.bfloat16)

    def row_copy(member, source):
        return send(
            send_rows.at[member], rows_in.at[source], r_out.at[member], r_in.at[source], at.of_member(member)
        )

    def detail_copy(member, source):
        return send(
            send_detail.at[member], detail_in.at[source], m_out.at[member], m_in.at[source], at.of_member(member)
        )

    def dispatch_step(index, carry):
        member = lax.rem(at.member + index, n_experts)
        send_rows[member] = rows_of(member)
        row_copy(member, at.member).start()
        detail_copy(member, at.member).start()
        return carry

    lax.fori_loop(1, n_experts, dispatch_step, 0)
    rows_in[at.member] = rows_of(at.member)
    detail_in[at.member] = send_detail[at.member]
    a_two_copy = pltpu.make_async_copy(a_two_ref, a_two_out, keep_sem.at[0])
    a_two_copy.start()
    for row in range(max(rows_here - 2, 0), rows_here):
        for copy in dense_copies(row):
            copy.wait()

    def swap_copy(index):
        return send(
            weights.at[0, index], weights.at[1, index], s_out.at[index], s_in.at[index], at.sibling()
        )

    for step in range(half):
        device, index, own = team.target(step)

        @pl.when(own)
        def _():
            shard_own(step).wait()

        @pl.when(jnp.logical_not(own))
        def _():
            shard_copy(step).wait_recv()

        swap_copy(step).start()

    many = act_buf.shape[2] // padded
    count = many * padded
    rounds = n_experts // many
    part = act_buf.shape[3]

    def hidden_copies(index):
        slot, turn = lax.rem(index, 2), lax.div(index, rounds)
        block = block_of(index)
        here = pl.ds(pl.multiple_of(block * count, 16), count)
        there = pl.ds(turn * half, half)
        return (
            pltpu.make_async_copy(act_buf.at[slot], act_out.at[there, here], act_sem.at[slot]),
            pltpu.make_async_copy(slope_buf.at[slot], slope_out.at[there, here], slope_sem.at[slot]),
        )

    def block_of(index):
        return lax.rem(lax.div(at.member, many) + index, rounds)

    def expert_step(index, carry):
        slot, turn = lax.rem(index, 2), lax.div(index, rounds)
        block = block_of(index)

        @pl.when(turn == 0)
        def _():
            for spot in range(many):
                source = block * many + spot

                @pl.when(source != at.member)
                def _():
                    row_copy(source, source).wait_recv()
                    detail_copy(source, source).wait_recv()

        @pl.when(index == rounds)
        def _():
            for step in range(half):
                swap_copy(step).wait_recv()

        @pl.when(index >= 2)
        def _():
            for copy in hidden_copies(index - 2):
                copy.wait()

        rows = rows_in[pl.ds(block * many, many)].reshape(count, width)
        for chunk in range(half):
            hidden_all = dot_f32(rows, weights[turn, chunk, 0], NT)
            for spot in tiles(count):
                hidden = hidden_all[spot]
                square = hidden * hidden
                curve = jnp.tanh(hidden * (0.7978845608 + 0.7978845608 * 0.044715 * square))
                upper = 0.5 + 0.5 * curve
                gelu = hidden * upper
                slope = upper + gelu * (1.0 - upper) * (
                    2.0 * 0.7978845608 + 6.0 * 0.7978845608 * 0.044715 * square
                )
                act_buf[slot, chunk, spot] = gelu.astype(jnp.bfloat16)
                slope_buf[slot, chunk, spot] = slope.astype(jnp.bfloat16)
        for copy in hidden_copies(index):
            copy.start()
        acts = jnp.concatenate([act_buf[slot, chunk] for chunk in range(half)], 1)
        ends = jnp.concatenate([weights[turn, chunk, 1] for chunk in range(half)], 0)
        found = dot_f32(acts, ends, NN)
        here = pl.ds(pl.multiple_of(block * count, 16), count)

        @pl.when(turn == 0)
        def _():
            total[here] = found

        @pl.when(turn == 1)
        def _():
            result = (total[here] + found).astype(jnp.bfloat16)
            for spot in range(many):
                source = block * many + spot
                mine = result[spot * padded : (spot + 1) * padded]
                send_rows[source] = mine
                detail = detail_in[source]
                weight = detail[0:1, :padded] * detail[1:2, :padded]
                shares = jnp.where(image_hot(detail, padded), weight, 0.0)
                pieces = jnp.concatenate(split_three(shares), 0)
                sums = dot_f32(pieces, mine, NN)
                part_ref[source] = (
                    sums[:IMAGE_PAD] + sums[IMAGE_PAD : 2 * IMAGE_PAD] + sums[2 * IMAGE_PAD :]
                )

        @pl.when(index == rounds - 1)
        def _():
            for member in others(at.member, n_experts):
                row_copy(member, at.member).wait_send()
                detail_copy(member, at.member).wait_send()

        return carry

    lax.fori_loop(0, 2 * rounds, expert_step, 0)
    keeps = [
        pltpu.make_async_copy(rows_in, rows_out, keep_sem.at[1]),
        pltpu.make_async_copy(detail_in, detail_out, keep_sem.at[2]),
        pltpu.make_async_copy(send_rows, y_out, keep_sem.at[3]),
        pltpu.make_async_copy(weights, weight_out, keep_sem.at[4]),
    ]
    for copy in keeps:
        copy.start()
    for index in range(2 * rounds - 2, 2 * rounds):
        for copy in hidden_copies(index):
            copy.wait()
    for step in range(half):
        own = team.target(step)[2]
        swap_copy(step).wait_send()

        @pl.when(jnp.logical_not(own))
        def _():
            shard_copy(step).wait_send()

    a_two_copy.wait()
    for copy in keeps:
        copy.wait()


def forward(sizes, n_experts, padded, lengths, slot_mask, patches, weights, gains, routers, columns, shards):
    rows_here, span = slot_mask.shape
    tokens, width = patches.shape
    part = shards.shape[2]
    half = 2 * sizes["g"]
    lanes = round_up(padded, 128)
    many = max(1, 576 // padded)
    count = n_experts * padded
    f32, kind = jnp.float32, jnp.bfloat16
    dma = pltpu.SemaphoreType.DMA
    each, parts, two = dma((n_experts,)), dma((half,)), dma((2,))

    def out(wide, dtype):
        return jax.ShapeDtypeStruct((tokens, wide), dtype)

    hidden = jax.ShapeDtypeStruct((2 * half, count, part), kind)
    rows = (n_experts, padded, width)
    return pl.pallas_call(
        functools.partial(forward_kernel, sizes, n_experts, lengths.shape[1], padded),
        out_shape=(
            out(width, f32), out(width, kind), out(3 * width, kind), out(width, kind), out(width, f32),
            out(width, kind), out(128, f32), out(128, f32),
            jax.ShapeDtypeStruct((IMAGE_PAD, width), f32), jax.ShapeDtypeStruct((8, width), f32),
            jax.ShapeDtypeStruct(rows, kind), jax.ShapeDtypeStruct((n_experts, 8, lanes), f32),
            hidden, hidden, jax.ShapeDtypeStruct(rows, kind),
            jax.ShapeDtypeStruct((n_experts, IMAGE_PAD, width), f32),
            jax.ShapeDtypeStruct((2, half, 2, part, width), kind),
        ),
        in_specs=[whole(pltpu.SMEM)] + [whole()] * 6 + [whole(ANY)],
        out_specs=(whole(ANY),) * 6 + (whole(),) * 4 + (whole(ANY),) * 5 + (whole(), whole(ANY)),
        scratch_shapes=[
            VMEM((2, span, width), f32), VMEM((2, span, width), kind), VMEM((2, span, 3 * width), kind),
            VMEM((2, span, width), kind), VMEM((2, span, width), f32), VMEM((tokens, width), kind),
            VMEM((2, half, 2, part, width), kind), VMEM(rows, kind), VMEM((n_experts, 8, lanes), f32),
            VMEM((8, tokens), f32), VMEM(rows, kind), VMEM((n_experts, 8, lanes), f32),
            VMEM((count, width), f32), VMEM((2, half, many * padded, part), kind),
            VMEM((2, half, many * padded, part), kind), dma((5, 2)), dma((5,)), two,
            parts, parts, parts, parts, each, each, each, each, two, two,
        ],
        compiler_params=pltpu.CompilerParams(
            collective_id=5, has_side_effects=True, vmem_limit_bytes=60 * MIB
        ),
        cost_estimate=cost(120),
        name="forward",
    )(lengths, slot_mask[:, None, :], patches, weights, gains, routers, columns, shards)


def expert_backward_kernel(
    sizes, padded, rows_ref, detail_ref, pool_ref, y_ref, slope_ref, act_ref, weight_ref, *refs
):
    at = Place(sizes)
    sources, unused, width = rows_ref.shape
    chunks, unused, part = slope_ref.shape
    half = chunks // 2
    back_ref, gate_ref, *outs = refs[: 2 + half]
    d_hidden, d_rows, send_rows, send_gate, send_grad, got_grad = refs[2 + half : 8 + half]
    own_sem, r_out, r_in, m_out, m_in, g_out, g_in, g_keep = refs[8 + half :]
    many = y_ref.shape[0]
    rounds = sources // many
    step = pl.program_id(0)
    team = others(at.member, sources)

    def row_copy(member, source):
        return send(
            send_rows.at[member], back_ref.at[source], r_out.at[member], r_in.at[source], at.of_member(member)
        )

    def gate_copy(member, source):
        return send(
            send_gate.at[member], gate_ref.at[source], m_out.at[member], m_in.at[source], at.of_member(member)
        )

    def keep_copies():
        return (
            pltpu.make_async_copy(send_rows.at[at.member], back_ref.at[at.member], own_sem.at[0]),
            pltpu.make_async_copy(send_gate.at[at.member], gate_ref.at[at.member], own_sem.at[1]),
        )

    def grad_copy(index):
        return send(
            send_grad.at[index], got_grad.at[index], g_out.at[index], g_in.at[index], at.sibling()
        )

    def out_copy(index):
        return pltpu.make_async_copy(got_grad.at[index], outs[index], g_keep.at[index])

    @pl.when(step == 0)
    def _():
        greet([at.of_member(member) for member in team] + [at.sibling()])

    @pl.when(step < rounds)
    def _():
        block = lax.rem(lax.div(at.member, many) + 1 + step, rounds)
        d_out = []
        for index in range(many):
            source = block * many + index
            detail = detail_ref[source]
            hot = image_hot(detail, padded)
            hots = jnp.where(hot, 1.0, 0.0).astype(jnp.bfloat16)
            pools = jnp.concatenate(split_three(pool_ref[source]), 0)
            wide = dot_f32(jnp.concatenate([hots] * 3, 0), pools, TN)
            lanes = detail.shape[1]
            upright = jnp.concatenate([detail, jnp.zeros((120, lanes), jnp.float32)], 0).T
            gate, pool = upright[:padded, 0:1], upright[:padded, 1:2]
            d_out.append((gate * (pool * wide)).astype(jnp.bfloat16))
            along = dot_f32(pools, y_ref[index], NT)
            along = along[:IMAGE_PAD] + along[IMAGE_PAD : 2 * IMAGE_PAD] + along[2 * IMAGE_PAD :]
            d_gate = jnp.sum(jnp.where(hot, along, 0.0), 0, keepdims=True) * detail[1:2, :padded]
            send_gate[source] = jnp.zeros(detail.shape, jnp.float32)
            send_gate[source, 0:1, :padded] = d_gate
        d_out = jnp.concatenate(d_out, 0)
        count = many * padded
        span = pl.ds(pl.multiple_of(block * count, 16), count)
        d_rows[span] = d_out

        def weight(index, which):
            return weight_ref[index // half, index % half, which]

        for index in range(chunks):
            d_act = dot_f32(d_out, weight(index, 1), NT)
            for spot in tiles(count):
                rows_now = pl.ds(pl.multiple_of(block * count + spot.start, 16), spot.stop - spot.start)
                d_hidden[index, rows_now] = (
                    d_act[spot] * slope_ref[index, spot].astype(jnp.float32)
                ).astype(jnp.bfloat16)
        d_hids = jnp.concatenate([d_hidden[index, span] for index in range(chunks)], 1)
        starts = jnp.concatenate([weight(index, 0) for index in range(chunks)], 0)
        total = dot_f32(d_hids, starts, NN)
        total = total.astype(jnp.bfloat16)
        for index in range(many):
            source = block * many + index
            send_rows[source] = total[index * padded : (index + 1) * padded]

            @pl.when(source != at.member)
            def _():
                row_copy(source, at.member).start()
                gate_copy(source, at.member).start()

            @pl.when(source == at.member)
            def _():
                for copy in keep_copies():
                    copy.start()

    @pl.when(step >= rounds)
    def _():
        index = step - rounds
        chunk = lax.rem(index + half, chunks)
        rows = rows_ref[...].reshape(sources * padded, width)
        g_one = dot_f32(d_hidden[chunk], rows, TN)
        g_two = dot_f32(act_ref[0], d_rows[...], TN)

        @pl.when(index < half)
        def _():
            send_grad[index, 0] = g_one.astype(jnp.bfloat16)
            send_grad[index, 1] = g_two.astype(jnp.bfloat16)
            grad_copy(index).start()

        @pl.when(index >= half)
        def _():
            spot = index - half
            grad_copy(spot).wait_recv()
            got_grad[spot, 0] = (got_grad[spot, 0].astype(jnp.float32) + g_one).astype(jnp.bfloat16)
            got_grad[spot, 1] = (got_grad[spot, 1].astype(jnp.float32) + g_two).astype(jnp.bfloat16)

        for spot in range(half):

            @pl.when(index == spot + half)
            def _():
                out_copy(spot).start()

    @pl.when(step == rounds + chunks - 1)
    def _():
        for member in team:
            row_copy(member, member).wait_recv()
            gate_copy(member, member).wait_recv()
        for member in team:
            row_copy(member, at.member).wait_send()
            gate_copy(member, at.member).wait_send()
        for copy in keep_copies():
            copy.wait()
        for spot in range(half):
            grad_copy(spot).wait_send()
            out_copy(spot).wait()


def expert_backward(sizes, rows, details, pools, results, slopes, acts, weights):
    sources, padded, width = rows.shape
    chunks, count, part = acts.shape
    many = max(1, (288 if part % 128 else 576) // padded)
    rounds, half = sources // many, chunks // 2
    lanes = details.shape[2]
    kind = jnp.bfloat16
    dma = pltpu.SemaphoreType.DMA
    each, parts = dma((sources,)), dma((half,))

    def block_of(step):
        member = lax.axis_index("x") * QUAD + lax.axis_index("r")
        return lax.rem(lax.div(member, many) + 1 + jnp.minimum(step, rounds - 1), rounds)

    def chunk_of(step):
        return lax.rem(jnp.maximum(step - rounds, 0) + half, chunks)

    return pl.pallas_call(
        functools.partial(expert_backward_kernel, sizes, padded),
        grid=(rounds + chunks,),
        out_shape=(
            jax.ShapeDtypeStruct((sources, padded, width), kind),
            jax.ShapeDtypeStruct((sources, 8, lanes), jnp.float32),
        )
        + (jax.ShapeDtypeStruct((2, part, width), kind),) * half,
        in_specs=[
            whole(), whole(), whole(),
            pl.BlockSpec((many, padded, width), lambda i: (block_of(i), 0, 0)),
            pl.BlockSpec((chunks, many * padded, part), lambda i: (0, block_of(i), 0)),
            pl.BlockSpec((1, count, part), lambda i: (chunk_of(i), 0, 0)),
        ]
        + [whole()],
        out_specs=(whole(ANY),) * (2 + half),
        scratch_shapes=[
            VMEM((chunks, count, part), kind),
            VMEM((count, width), kind),
            VMEM((sources, padded, width), kind),
            VMEM((sources, 8, lanes), jnp.float32),
            VMEM((half, 2, part, width), kind),
            VMEM((half, 2, part, width), kind),
            dma((2,)), each, each, each, each, parts, parts, parts,
        ],
        compiler_params=pltpu.CompilerParams(
            collective_id=6, has_side_effects=True, vmem_limit_bytes=62 * MIB
        ),
        cost_estimate=cost(65),
        name="expert_backward",
    )(rows, details, pools, results, slopes, acts, weights)


def dense_backward_kernel(
    sizes, n_experts, images, padded, length_ref, mask_ref, patch_ref, x_zero_ref, a_one_ref, qkv_ref, att_ref,
    x_one_ref, a_two_ref, prob_ref, lse_ref, col_ref, w_ref, gain_ref, router_ref, back_ref, gate_ref,
    pool_ref, imp_ref, third_ref, out_ref, grads, g_router, g_norm, d_qkv
):
    row = pl.program_id(0)
    span, width = patch_ref.shape
    mats, rows = grads.shape[0], width // (8 * sizes["g"] * sizes["x"])

    @pl.when(row == 0)
    def _():
        grads[...] = jnp.zeros_like(grads)
        g_router[...] = jnp.zeros_like(g_router)
        g_norm[...] = third_ref[...]

    columns = col_ref[...]
    slot_one, slot_two = columns[:, 0:1], columns[:, 1:2]
    count = n_experts * padded
    slot = lax.broadcasted_iota(jnp.int32, (span, count), 1).astype(jnp.float32)
    match = jnp.where((slot == slot_one) | (slot == slot_two), 1.0, 0.0).astype(jnp.bfloat16)
    d_a_two = dot_f32(match, back_ref[...].reshape(count, width), NN)
    lanes = gate_ref.shape[2]
    spot = lax.broadcasted_iota(jnp.int32, (span, lanes), 1)
    inside = spot < padded
    spot = spot.astype(jnp.float32)
    found_one, found_two = jnp.zeros((span, lanes), jnp.float32), jnp.zeros((span, lanes), jnp.float32)
    for expert in range(n_experts):
        line = jnp.broadcast_to(gate_ref[expert, 0:1], (span, lanes))
        found_one = jnp.where(inside & (spot == slot_one - expert * padded), line, found_one)
        found_two = jnp.where(inside & (spot == slot_two - expert * padded), line, found_two)
    d_gate_one = jnp.sum(found_one, 1, keepdims=True)
    d_gate_two = jnp.sum(found_two, 1, keepdims=True)
    lane = lax.broadcasted_iota(jnp.int32, (span, 128), 1)
    number = lane.astype(jnp.float32)
    valid, pool, image = columns[:, 2:3], columns[:, 3:4], columns[:, 4:5]
    head = lax.broadcasted_iota(jnp.int32, (1, 128), 1) < n_experts
    importance = imp_ref[0:1, 0:128]
    centre = jnp.sum(jnp.where(head, importance, 0.0), 1, keepdims=True) / n_experts
    away = jnp.where(head, importance - centre, 0.0)
    spread = jnp.sum(away * away, 1, keepdims=True) / n_experts
    d_imp = aux_weight * (
        2.0 * away / (n_experts * centre * centre)
        - 2.0 * spread / (n_experts * centre * centre * centre)
    )
    d_probs = valid * d_imp
    d_probs = d_probs + jnp.where(number == columns[:, 5:6], d_gate_one, 0.0)
    d_probs = d_probs + jnp.where(number == columns[:, 6:7], d_gate_two, 0.0)
    probs = prob_ref[...]
    d_router = (probs * (d_probs - jnp.sum(probs * d_probs, 1, keepdims=True))).astype(jnp.bfloat16)
    g_router[...] += dot_f32(d_router, a_two_ref[...], TN)
    routers = router_ref[...].astype(jnp.bfloat16)
    if routers.shape[0] < 128:
        routers = jnp.concatenate(
            [routers, jnp.zeros((128 - routers.shape[0], width), jnp.bfloat16)], 0
        )
    d_a_two = d_a_two + dot_f32(d_router, routers, NN)
    scaled, scale = norm_parts(x_one_ref[...])
    g_norm[1:2] += jnp.sum(d_a_two * scaled, 0, keepdims=True)
    g_norm[4:5] += jnp.sum(d_a_two, 0, keepdims=True)
    d_x_one = norm_back(d_a_two, scaled, scale, gain_ref[1:2])
    for index in range(images):
        place = row * images + index
        weight = jnp.where(image == place.astype(jnp.float32), pool, 0.0)
        d_x_one = d_x_one + weight * pool_ref[pl.ds(place, 1)]
    d_att = d_x_one.astype(jnp.bfloat16)
    grads[4] += dot_f32(att_ref[...], d_att, TN)
    d_out = dot_f32(d_att, w_ref[4], NT).astype(jnp.bfloat16)
    open_to = allowed_slots(length_ref, row, images, mask_ref[0], span)
    logs = lse_ref[...]
    for pair in range(width // 128):
        query, key, value = (
            qkv_ref[:, part * width + pair * 128 : part * width + (pair + 1) * 128]
            for part in range(3)
        )
        d_pair = d_out[:, pair * 128 : (pair + 1) * 128]
        found = []
        for side in range(2):
            left = (lane < 64) == (side == 0)
            held = jnp.where(left, query, jnp.zeros_like(query))
            scores = jnp.where(open_to, dot_f32(held, key, NT) * 64**-0.5, mask_fill)
            total = logs[:, 2 * pair + side : 2 * pair + side + 1]
            chance = jnp.exp(scores - total)
            d_held = jnp.where(left, d_pair, jnp.zeros_like(d_pair))
            d_chance = dot_f32(d_held, value, NT)
            d_value = dot_f32(chance.astype(jnp.bfloat16), d_pair, TN)
            d_scores = chance * (d_chance - jnp.sum(chance * d_chance, 1, keepdims=True))
            d_scores = d_scores.astype(jnp.bfloat16)
            d_query = dot_f32(d_scores, key, NN) * 64**-0.5
            d_key = dot_f32(d_scores, query, TN) * 64**-0.5
            found.append((d_query, d_key, d_value))
        for part in range(3):
            d_qkv[:, part * width + pair * 128 : part * width + (pair + 1) * 128] = jnp.where(
                lane < 64, found[0][part], found[1][part]
            ).astype(jnp.bfloat16)
    d_a_one = None
    for part in range(3):
        piece = d_qkv[:, part * width : (part + 1) * width]
        grads[1 + part] += dot_f32(a_one_ref[...], piece, TN)
        found = dot_f32(piece, w_ref[1 + part], NT)
        d_a_one = found if d_a_one is None else d_a_one + found
    scaled, scale = norm_parts(x_zero_ref[...])
    g_norm[0:1] += jnp.sum(d_a_one * scaled, 0, keepdims=True)
    g_norm[3:4] += jnp.sum(d_a_one, 0, keepdims=True)
    d_x_zero = norm_back(d_a_one, scaled, scale, gain_ref[0:1]) + d_x_one
    grads[0] += dot_f32(patch_ref[...], d_x_zero.astype(jnp.bfloat16), TN)

    @pl.when(row == pl.num_programs(0) - 1)
    def _():
        Z, Y, X = QUAD, sizes["g"], sizes["x"]
        tall = max(8, n_experts)
        norms = g_norm[...]
        if tall > 8:
            norms = jnp.concatenate([norms, jnp.zeros((tall - 8, width), jnp.float32)], 0)
        router_grads = g_router[:tall]
        depth = out_ref.shape[4]
        device = 0
        for z in range(Z):
            for y in range(Y):
                for x in range(X):
                    for c in range(2):
                        spot = slice(device * rows, (device + 1) * rows)
                        blank = jnp.zeros((tall, 128 - rows), jnp.float32)
                        tail = [norms[:, spot], blank, router_grads[:, spot], blank]
                        tail.append(jnp.zeros((tall, width - 256), jnp.float32))
                        pieces = [grads[mat, spot] for mat in range(mats)]
                        pieces.append(jnp.concatenate(tail, 1))
                        left = depth - mats * rows - tall
                        if left:
                            pieces.append(jnp.zeros((left, width), jnp.float32))
                        out_ref[c, z, x, y] = jnp.concatenate(pieces, 0).astype(jnp.bfloat16)
                        device += 1


def dense_backward(
    sizes, n_experts, padded, rows_own, lengths, slot_mask, patches, kept, columns, weights, gains, routers, back,
    gates, pooled, importance, third
):
    rows_here, span = slot_mask.shape
    tokens, width = patches.shape
    mats = weights.shape[0]
    depth = round_up(mats * rows_own + max(8, n_experts), 16)
    x_zero, a_one, qkv, att, x_one, a_two, probs, logs = kept

    def block(wide):
        return pl.BlockSpec((span, wide), lambda i: (i, 0))

    return pl.pallas_call(
        functools.partial(dense_backward_kernel, sizes, n_experts, lengths.shape[1], padded),
        grid=(rows_here,),
        out_shape=jax.ShapeDtypeStruct(
            (2, QUAD, sizes["x"], sizes["g"], depth, width), jnp.bfloat16
        ),
        in_specs=[
            whole(pltpu.SMEM), pl.BlockSpec((1, 1, span), lambda i: (i, 0, 0)), block(width),
            block(width), block(width), block(3 * width), block(width), block(width), block(width),
            block(128), block(128), block(128),
        ]
        + [whole()] * 8,
        out_specs=whole(),
        scratch_shapes=[
            VMEM((mats, width, width), jnp.float32),
            VMEM((128, width), jnp.float32),
            VMEM((8, width), jnp.float32),
            VMEM((span, 3 * width), jnp.bfloat16),
        ],
        compiler_params=pltpu.CompilerParams(vmem_limit_bytes=60 * MIB),
        cost_estimate=cost(50),
        name="dense_backward",
    )(
        lengths, slot_mask[:, None, :], patches, x_zero, a_one, qkv, att, x_one, a_two, probs, logs, columns,
        weights, gains, routers, back, gates, pooled, importance, third,
    )


def shard_moves(n_blocks):
    span = 2 * n_blocks
    moves = []
    for step in range(span):
        pairs = []
        for place in range(QUAD * n_blocks):
            for core in range(2):
                target = (place + step) % span
                src = place * 2 + core
                dst = (target // 2 * QUAD + 2 * core + target % 2) * 2 + place // span
                pairs.append((src, dst))
        moves.append(pairs)
    return moves


def return_experts(parts, n_blocks):
    return [
        lax.ppermute(part, ("g", "r", "c"), [(dst, src) for src, dst in pairs])
        for part, pairs in zip(parts, shard_moves(n_blocks))
    ]


def body(
    patches,
    lengths,
    slot_mask,
    expert_picks,
    priority_rank,
    class_labels,
    dense_weights,
    dense_first,
    dense_second,
    dense_average,
    router_weights,
    router_first,
    router_second,
    router_average,
    norm_params,
    norm_first,
    norm_second,
    norm_average,
    expert_in,
    in_first,
    in_second,
    in_average,
    expert_out,
    out_first,
    out_second,
    out_average,
    head_weights,
    head_first,
    head_second,
    head_average,
):
    n_blocks = lax.axis_size("g")
    sizes = {name: lax.axis_size(name) for name in ALL}
    rows_own, n_experts = router_weights.shape
    n_tail = max(8, n_experts)
    tail = jnp.zeros((n_tail, dense_weights.shape[2]), jnp.float32)
    tail = tail.at[:6, :rows_own].set(norm_params)
    tail = tail.at[:n_experts, 128 : 128 + rows_own].set(router_weights.T)
    rows_here, n_slots_row = slot_mask.shape
    tokens, model_width = patches.shape
    n_images = lengths.shape[0] * lengths.shape[1]
    capacity = (21 * tokens * TOP + 20 * n_experts - 1) // (20 * n_experts)
    padded = round_up(capacity, 16)
    layer_b, gain_rows, router_t, columns = gather_weights(
        sizes,
        (lengths.shape[1], n_experts, capacity, padded),
        dense_weights,
        tail,
        expert_picks,
        priority_rank,
        slot_mask,
        lengths,
    )
    shards = jnp.stack([expert_in, expert_out], 1).astype(jnp.bfloat16)
    (
        x_zero, a_one, qkv, att_out, x_one, a_two, router_probs, logs, pooled, part_importance,
        arrived, details, activated, slope, result, part_pooled, expert_weights
    ) = forward(
        sizes, n_experts, padded, lengths, slot_mask, patches, layer_b, gain_rows, router_t, columns, shards
    )
    g_head, d_pooled_all, d_pooled, g_norm_three, head_sums, total_importance = head_step(
        sizes,
        n_images,
        part_pooled,
        pooled,
        part_importance,
        gain_rows,
        head_weights,
        class_labels,
    )
    d_back, back_gate, *grads = expert_backward(
        sizes, arrived, details, d_pooled_all, result, slope, activated, expert_weights
    )
    parts = return_experts(grads, n_blocks)
    blocks = dense_backward(
        sizes,
        n_experts,
        padded,
        rows_own,
        lengths,
        slot_mask,
        patches,
        (x_zero, a_one, qkv, att_out, x_one, a_two, router_probs, logs),
        columns,
        layer_b,
        gain_rows,
        router_t,
        d_back,
        back_gate,
        d_pooled,
        total_importance,
        g_norm_three,
    )
    reduced, dense_sums = scatter_dense(sizes, blocks)
    g_one, g_two, totals = finish(
        sizes, n_experts, parts, head_sums, dense_sums, total_importance
    )
    n_dense = dense_weights.shape[0] * rows_own
    g_layers = reduced[:n_dense].reshape(-1, rows_own, model_width)
    g_norms = reduced[n_dense : n_dense + 6, :rows_own]
    g_router = reduced[n_dense : n_dense + n_experts, 128 : 128 + rows_own].T
    importance = total_importance[0, :n_experts]
    loss_value, grad_norm, factor = totals[0, 0], totals[1, 0], totals[2, 0]
    dense_out = adam_update(
        dense_weights, dense_first, dense_second, dense_average, g_layers, factor, base_rate
    )
    router_out = adam_update(
        router_weights, router_first, router_second, router_average, g_router, factor, base_rate
    )
    norm_out = adam_update(
        norm_params, norm_first, norm_second, norm_average, g_norms, factor, norm_rate
    )
    in_out = adam_update(expert_in, in_first, in_second, in_average, g_one, factor, base_rate)
    out_out = adam_update(expert_out, out_first, out_second, out_average, g_two, factor, base_rate)
    head_out = adam_update(
        head_weights, head_first, head_second, head_average, g_head, factor, base_rate
    )
    return (
        loss_value,
        importance,
        grad_norm,
        *dense_out,
        *router_out,
        *norm_out,
        *in_out,
        *out_out,
        *head_out,
    )


def solution(mesh):
    n_dp, n_expert = mesh.shape["dp"], mesh.shape["expert"]
    shaped = mesh.devices.reshape(n_dp // QUAD, QUAD, n_expert // 2, 2)
    fine = Mesh(shaped, ALL)
    rows = P(ALL, None)
    dense = P(None, ALL, None)
    norms = P(None, ALL)
    experts = P(("x", "c"), ("g", "r"), None)
    placed = (rows,) * 6 + (dense,) * 4 + (rows,) * 4 + (norms,) * 4 + (experts,) * 8 + (rows,) * 4
    results = (
        (P(),) * 3 + (dense,) * 4 + (rows,) * 4 + (norms,) * 4 + (experts,) * 8 + (rows,) * 4
    )
    return jax.shard_map(body, mesh=fine, in_specs=placed, out_specs=results, check_vma=False)
```

```python
import functools
import math

import jax
import jax.numpy as jnp
from jax import lax
from jax.experimental import pallas as pl
from jax.experimental.pallas import tpu as pltpu
from jax.sharding import Mesh
from jax.sharding import PartitionSpec as P

HEADS = 12
TOP = 2
STEP_COUNT = 10
QUAD = 4

high_prec = lax.Precision.HIGHEST
eps_norm = 1e-06
aux_weight = 0.01
clip_limit = 1.0
base_rate = 0.05
norm_rate = 0.5
beta_first = 0.9
beta_second = 0.999
weight_decay = 0.1
polyak_decay = 0.7
adam_eps = 1e-08
mask_fill = -1e30

ALL = ("g", "r", "x", "c")
MEMBERS = ("x", "r")


def adam_update(weight, first_state, second_state, average_state, gradient, factor, step_rate):
    clipped = gradient * factor
    first_new = beta_first * first_state + (1.0 - beta_first) * clipped
    second_new = beta_second * second_state + (1.0 - beta_second) * clipped * clipped
    first_hat = first_new / (1.0 - beta_first**STEP_COUNT)
    second_hat = second_new / (1.0 - beta_second**STEP_COUNT)
    weight_new = weight - step_rate * (
        first_hat / (jnp.sqrt(second_hat) + adam_eps) + weight_decay * weight
    )
    average_new = polyak_decay * average_state + (1.0 - polyak_decay) * weight_new
    return (weight_new, first_new, second_new, average_new)


MESH_ID = pl.DeviceIdType.MESH
VMEM = pltpu.VMEM
ANY = pl.ANY
MIB = 1 << 20


def cost(microseconds):
    return pl.CostEstimate(flops=int(microseconds * 1.15e9), bytes_accessed=0, transcendentals=0)


def whole(space=None):
    return pl.BlockSpec(memory_space=space or VMEM)


def round_up(value, step):
    return (value + step - 1) // step * step


class Place:
    def __init__(self, sizes):
        self.G, self.X = sizes["g"], sizes["x"]
        self.Z, self.Y = QUAD, sizes["g"]
        self.chips = self.Z * self.Y * self.X
        spot = lax.axis_index("g") * QUAD + lax.axis_index("r")
        self.z, self.y = lax.div(spot, self.Y), lax.rem(spot, self.Y)
        self.x, self.c = lax.axis_index("x"), lax.axis_index("c")
        self.g, self.r = lax.axis_index("g"), lax.axis_index("r")
        self.chip = spot * self.X + self.x
        self.member = self.x * QUAD + self.r

    def at(self, z=None, y=None, x=None, c=None):
        spot = (self.z if z is None else z) * self.Y + (self.y if y is None else y)
        return {
            "g": lax.div(spot, QUAD),
            "r": lax.rem(spot, QUAD),
            "x": self.x if x is None else x,
            "c": self.c if c is None else c,
        }

    def of_chip(self, chip):
        spot = lax.div(chip, self.X)
        return {
            "g": lax.div(spot, QUAD),
            "r": lax.rem(spot, QUAD),
            "x": lax.rem(chip, self.X),
            "c": self.c,
        }

    def of_member(self, member):
        return {
            "g": self.g,
            "r": lax.rem(member, QUAD),
            "x": lax.div(member, QUAD),
            "c": self.c,
        }

    def sibling(self):
        return self.at(c=1 - self.c)


def greet(peers):
    barrier = pltpu.get_barrier_semaphore()
    for peer in peers:
        pl.semaphore_signal(barrier, inc=1, device_id=peer, device_id_type=MESH_ID)
    pl.semaphore_wait(barrier, len(peers))


def send(src, dst, send_sem, recv_sem, peer):
    return pltpu.make_async_remote_copy(
        src_ref=src,
        dst_ref=dst,
        send_sem=send_sem,
        recv_sem=recv_sem,
        device_id=peer,
        device_id_type=MESH_ID,
    )


def others(me, count):
    return [lax.rem(me + step, count) for step in range(1, count)]


def grid_peers(at):
    peers = [at.at(z=z) for z in others(at.z, at.Z)]
    peers += [at.at(y=y) for y in others(at.y, at.Y)]
    peers += [at.at(x=x) for x in others(at.x, at.X)]
    return peers + [at.sibling()]


def gather_kernel(
    sizes, rows, mats, routing, dense_ref, tail_ref, pick_ref, rank_ref, mask_ref, length_ref,
    w_ref, gain_ref, router_ref, col_ref, land, *sems
):
    at = Place(sizes)
    Z, Y, X = at.Z, at.Y, at.X
    depth = land.shape[4]
    cut = depth // 2 // 16 * 16
    first, second = pl.ds(0, cut), pl.ds(cut, depth - cut)
    z_out, z_in, ya_out, ya_in, xb_out, xb_in, xa_out, xa_in, yb_out, yb_in, c_out, c_in = sems
    block = jnp.concatenate([dense_ref[...].reshape(mats * rows, -1), tail_ref[...]], 0)
    if block.shape[0] < depth:
        block = jnp.pad(block, ((0, depth - block.shape[0]), (0, 0)))
    mine = land.at[at.c, at.z, at.x, at.y]
    mine[...] = block.astype(jnp.bfloat16)
    greet(grid_peers(at))
    started = []

    def begin(copy):
        copy.start()
        started.append(copy)

    order = [at.z] + [lax.rem(at.z + k, Z) for k in (1, 3, 2)]
    for z in order[1:]:
        begin(send(mine, mine, z_out.at[z], z_in.at[at.z], at.at(z=z)))

    def one(z):
        part = land.at[at.c, z, at.x, at.y]
        for y in others(at.y, Y):
            begin(send(part.at[first], part.at[first], ya_out.at[z, y], ya_in.at[z, at.y], at.at(y=y)))
        for x in others(at.x, X):
            begin(send(part.at[second], part.at[second], xb_out.at[z, x], xb_in.at[z, at.x], at.at(x=x)))

    def two(z):
        for y in others(at.y, Y):
            part = land.at[at.c, z, at.x, y, first]
            send(part, part, ya_out.at[z, y], ya_in.at[z, y], at.at(y=y)).wait_recv()
        line = land.at[at.c, z, at.x, :, first]
        for x in others(at.x, X):
            begin(send(line, line, xa_out.at[z, x], xa_in.at[z, at.x], at.at(x=x)))
        for x in others(at.x, X):
            part = land.at[at.c, z, x, at.y, second]
            send(part, part, xb_out.at[z, x], xb_in.at[z, x], at.at(x=x)).wait_recv()
        line = land.at[at.c, z, :, at.y, second]
        for y in others(at.y, Y):
            begin(send(line, line, yb_out.at[z, y], yb_in.at[z, at.y], at.at(y=y)))

    def three(z):
        for x in others(at.x, X):
            line = land.at[at.c, z, x, :, first]
            send(line, line, xa_out.at[z, x], xa_in.at[z, x], at.at(x=x)).wait_recv()
        for y in others(at.y, Y):
            line = land.at[at.c, z, :, y, second]
            send(line, line, yb_out.at[z, y], yb_in.at[z, y], at.at(y=y)).wait_recv()
        plane = land.at[at.c, z]
        begin(send(plane, plane, c_out.at[z], c_in.at[z], at.sibling()))

    for step in range(Z + 2):
        if step < Z:
            if step > 0:
                z = order[step]
                part = land.at[at.c, z, at.x, at.y]
                send(part, part, z_out.at[z], z_in.at[z], at.at(z=z)).wait_recv()
            one(order[step])
        if step == 0:
            col_ref[...] = route_math(*routing, pick_ref, rank_ref, mask_ref, length_ref)
        if 0 <= step - 1 < Z:
            two(order[step - 1])
        if 0 <= step - 2 < Z:
            three(order[step - 2])
    for z in order:
        plane = land.at[1 - at.c, z]
        send(plane, plane, c_out.at[z], c_in.at[z], at.sibling()).wait_recv()
    for copy in started:
        copy.wait_send()
    chips = [(z, y, x) for z in range(Z) for y in range(Y) for x in range(X)]
    cores = [(c, z, x, y) for z, y, x in chips for c in range(2)]
    group = 16 // math.gcd(16, rows)
    for start in range(0, len(cores), group):
        for mat in range(mats):
            w_ref[mat, start * rows : (start + group) * rows] = jnp.concatenate(
                [land[spot][mat * rows : (mat + 1) * rows] for spot in cores[start : start + group]], 0
            )
    base, count = mats * rows, tail_ref.shape[0]
    tails = [land[spot][base : base + count].astype(jnp.float32) for spot in cores]
    gain_ref[...] = jnp.concatenate([tail[:8, :rows] for tail in tails], 1)
    router_ref[...] = jnp.concatenate([tail[:, 128 : 128 + rows] for tail in tails], 1)


def gather_weights(sizes, routing, dense, tail, picks, ranks, slot_mask, lengths):
    mats, rows, width = dense.shape
    count = tail.shape[0]
    depth = round_up(mats * rows + count, 16)
    Z, Y, X = QUAD, sizes["g"], sizes["x"]
    dma = pltpu.SemaphoreType.DMA
    by_y, by_x = dma((Z, Y)), dma((Z, X))
    return pl.pallas_call(
        functools.partial(gather_kernel, sizes, rows, mats, routing),
        out_shape=(
            jax.ShapeDtypeStruct((mats, width, width), jnp.bfloat16),
            jax.ShapeDtypeStruct((8, width), jnp.float32),
            jax.ShapeDtypeStruct((count, width), jnp.float32),
            jax.ShapeDtypeStruct((picks.shape[0], 128), jnp.float32),
        ),
        in_specs=[whole()] * 6,
        out_specs=(whole(),) * 4,
        scratch_shapes=[VMEM((2, Z, X, Y, depth, width), jnp.bfloat16), dma((Z,)), dma((Z,))]
        + [by_y, by_y, by_x, by_x, by_x, by_x, by_y, by_y, dma((Z,)), dma((Z,))],
        compiler_params=pltpu.CompilerParams(
            collective_id=1, has_side_effects=True, vmem_limit_bytes=48 * MIB
        ),
        cost_estimate=cost(44),
        name="gather_weights",
    )(dense, tail, picks, ranks, slot_mask, lengths)


def total_square(value):
    return jnp.sum(jnp.sum(value * value, 0, keepdims=True), 1, keepdims=True)


def scatter_kernel(sizes, g_ref, out_ref, square_ref, hold, sib, got_xa, got_yb, got_ya, got_xb, got_z, *sems):
    at = Place(sizes)
    Z, Y, X = at.Z, at.Y, at.X
    depth = g_ref.shape[4]
    cut = depth // 2 // 16 * 16
    first, second = pl.ds(0, cut), pl.ds(cut, depth - cut)
    c_out, c_in, xa_out, xa_in, yb_out, yb_in, ya_out, ya_in, xb_out, xb_in, z_out, z_in = sems
    greet(grid_peers(at))
    started = []

    def begin(copy):
        copy.start()
        started.append(copy)

    wide = lambda value: value.astype(jnp.float32)
    order = [lax.rem(at.z + k, Z) for k in (2, 1, 3)] + [at.z]
    for z in order:
        begin(send(g_ref.at[1 - at.c, z], sib.at[z], c_out.at[z], c_in.at[z], at.sibling()))

    def one(z):
        send(sib.at[z], sib.at[z], c_out.at[z], c_in.at[z], at.sibling()).wait_recv()
        hold[z] = (wide(g_ref[at.c, z]) + wide(sib[z])).astype(jnp.bfloat16)
        for x in others(at.x, X):
            begin(send(hold.at[z, x, :, first], got_xa.at[z, at.x], xa_out.at[z, x], xa_in.at[z, at.x], at.at(x=x)))
        for y in others(at.y, Y):
            begin(send(hold.at[z, :, y, second], got_yb.at[z, at.y], yb_out.at[z, y], yb_in.at[z, at.y], at.at(y=y)))

    def two(z):
        total = wide(hold[z, at.x, :, first])
        for x in others(at.x, X):
            send(got_xa.at[z, x], got_xa.at[z, x], xa_out.at[z, x], xa_in.at[z, x], at.at(x=x)).wait_recv()
            total = total + wide(got_xa[z, x])
        hold[z, at.x, :, first] = total.astype(jnp.bfloat16)
        for y in others(at.y, Y):
            begin(send(hold.at[z, at.x, y, first], got_ya.at[z, at.y], ya_out.at[z, y], ya_in.at[z, at.y], at.at(y=y)))
        total = wide(hold[z, :, at.y, second])
        for y in others(at.y, Y):
            send(got_yb.at[z, y], got_yb.at[z, y], yb_out.at[z, y], yb_in.at[z, y], at.at(y=y)).wait_recv()
            total = total + wide(got_yb[z, y])
        hold[z, :, at.y, second] = total.astype(jnp.bfloat16)
        for x in others(at.x, X):
            begin(send(hold.at[z, x, at.y, second], got_xb.at[z, at.x], xb_out.at[z, x], xb_in.at[z, at.x], at.at(x=x)))

    def three(z, last):
        total = wide(hold[z, at.x, at.y, first])
        for y in others(at.y, Y):
            send(got_ya.at[z, y], got_ya.at[z, y], ya_out.at[z, y], ya_in.at[z, y], at.at(y=y)).wait_recv()
            total = total + wide(got_ya[z, y])
        rest = wide(hold[z, at.x, at.y, second])
        for x in others(at.x, X):
            send(got_xb.at[z, x], got_xb.at[z, x], xb_out.at[z, x], xb_in.at[z, x], at.at(x=x)).wait_recv()
            rest = rest + wide(got_xb[z, x])
        if last:
            out_ref[first] = total
            out_ref[second] = rest
            return
        mine = hold.at[z, at.x, at.y]
        mine[first] = total.astype(jnp.bfloat16)
        mine[second] = rest.astype(jnp.bfloat16)
        begin(send(mine, got_z.at[at.z], z_out.at[z], z_in.at[at.z], at.at(z=z)))

    for step in range(Z + 2):
        if step < Z:
            one(order[step])
        if 0 <= step - 1 < Z:
            two(order[step - 1])
        if 0 <= step - 2 < Z:
            three(order[step - 2], step - 2 == Z - 1)
    for z in order[:-1]:
        send(got_z.at[z], got_z.at[z], z_out.at[z], z_in.at[z], at.at(z=z)).wait_recv()
        out_ref[...] += wide(got_z[z])
    square_ref[...] = jnp.broadcast_to(total_square(out_ref[...]), square_ref.shape)
    for copy in started:
        copy.wait_send()


def scatter_dense(sizes, blocks):
    unused, Z, X, Y, depth, width = blocks.shape
    dma = pltpu.SemaphoreType.DMA
    by_y, by_x, by_z = dma((Z, Y)), dma((Z, X)), dma((Z,))
    cut = depth // 2 // 16 * 16
    half = jnp.bfloat16
    return pl.pallas_call(
        functools.partial(scatter_kernel, sizes),
        out_shape=(
            jax.ShapeDtypeStruct((depth, width), jnp.float32),
            jax.ShapeDtypeStruct((8, 128), jnp.float32),
        ),
        in_specs=[whole()],
        out_specs=(whole(), whole()),
        scratch_shapes=[
            VMEM((Z, X, Y, depth, width), half),
            VMEM((Z, X, Y, depth, width), half),
            VMEM((Z, X, Y, cut, width), half),
            VMEM((Z, Y, X, depth - cut, width), half),
            VMEM((Z, Y, cut, width), half),
            VMEM((Z, X, depth - cut, width), half),
            VMEM((Z, depth, width), half),
        ]
        + [by_z, by_z, by_x, by_x, by_y, by_y, by_y, by_y, by_x, by_x, by_z, by_z],
        compiler_params=pltpu.CompilerParams(
            collective_id=2, has_side_effects=True, vmem_limit_bytes=28 * MIB
        ),
        cost_estimate=cost(45),
        name="scatter_dense",
    )(blocks)


def finish_kernel(sizes, n_experts, head_ref, dense_ref, imp_ref, *refs):
    at = Place(sizes)
    many = len(refs) - 7
    parts = refs[:many]
    first_ref, second_ref, out_ref, land, own, out_sem, in_sem = refs[many:]
    count = 2 * at.chips
    me = at.chip * 2 + at.c
    ids = others(me, count)

    def peer(device):
        spot = at.of_chip(lax.div(device, 2))
        spot["c"] = lax.rem(device, 2)
        return spot

    greet([peer(device) for device in ids])
    place = lax.rem(at.g * QUAD + at.r, 2)
    square = dense_ref[0:1, 0:1] + head_ref[1:2, 0:1]
    for parity in range(2):
        expert = place if parity == 0 else 1 - place
        for index, ref in enumerate((first_ref, second_ref)):
            total = None
            for step in range(parity, many, 2):
                found = parts[step][index].astype(jnp.float32)
                total = found if total is None else total + found
            ref[expert] = total
            square = square + total_square(total)
    line = lax.broadcasted_iota(jnp.int32, own.shape, 0)
    own[...] = jnp.where(line == 0, head_ref[0:1, 0:1], jnp.where(line == 1, square, 0.0))
    land[me] = own[...]
    copies = [send(own, land.at[me], out_sem.at[d], in_sem.at[me], peer(d)) for d in ids]
    for copy in copies:
        copy.start()
    importance = imp_ref[0:1, 0:128]
    head = lax.broadcasted_iota(jnp.int32, (1, 128), 1) < n_experts
    centre = jnp.sum(jnp.where(head, importance, 0.0), 1, keepdims=True) / n_experts
    away = jnp.where(head, importance - centre, 0.0)
    spread = jnp.sum(away * away, 1, keepdims=True) / n_experts
    balance = aux_weight * spread / (centre * centre)
    for d in ids:
        send(land.at[d], land.at[d], out_sem.at[d], in_sem.at[d], peer(d)).wait_recv()
    sums = jnp.sum(land[...], 0)
    norm = jnp.sqrt(sums[1:2, 0:1])
    factor = jnp.minimum(1.0, clip_limit / norm)
    loss = sums[0:1, 0:1] + balance
    out_ref[...] = jnp.where(line == 0, loss, jnp.where(line == 1, norm, factor))
    for copy in copies:
        copy.wait_send()


def finish(sizes, n_experts, parts, head_sums, dense_sums, importance):
    devices = sizes["g"] * QUAD * sizes["x"] * 2
    unused, rows, width = parts[0].shape
    dma = pltpu.SemaphoreType.DMA
    grads = jax.ShapeDtypeStruct((2, rows, width), jnp.float32)
    return pl.pallas_call(
        functools.partial(finish_kernel, sizes, n_experts),
        out_shape=(grads, grads, jax.ShapeDtypeStruct((8, 128), jnp.float32)),
        in_specs=[whole()] * (3 + len(parts)),
        out_specs=(whole(),) * 3,
        scratch_shapes=[
            VMEM((devices, 8, 128), jnp.float32),
            VMEM((8, 128), jnp.float32),
            dma((devices,)),
            dma((devices,)),
        ],
        compiler_params=pltpu.CompilerParams(
            collective_id=3, has_side_effects=True, vmem_limit_bytes=20 * MIB
        ),
        cost_estimate=cost(10),
        name="finish",
    )(head_sums, dense_sums, importance, *parts)


IMAGE_PAD = 16


def split_three(value):
    high = value.astype(jnp.bfloat16)
    rest = value - high.astype(jnp.float32)
    middle = rest.astype(jnp.bfloat16)
    return high, middle, (rest - middle.astype(jnp.float32)).astype(jnp.bfloat16)


def dot_f32(left, right, dims):
    return lax.dot_general(left, right, (dims, ((), ())), preferred_element_type=jnp.float32)


NN = ((1,), (0,))
NT = ((1,), (1,))
TN = ((0,), (0,))


def norm_parts(values):
    centre = values - jnp.mean(values, -1, keepdims=True)
    spread = jnp.mean(centre * centre, -1, keepdims=True)
    scale = lax.rsqrt(spread + eps_norm)
    return centre * scale, scale


def norm_back(d_out, scaled, scale, gain):
    pulled = d_out * gain
    return scale * (
        pulled
        - jnp.mean(pulled, -1, keepdims=True)
        - scaled * jnp.mean(pulled * scaled, -1, keepdims=True)
    )


def head_kernel(
    sizes, images, part_ref, own_ref, imp_ref, gain_ref, head_ref, label_ref,
    g_head_ref, d_pool_ref, own_d_ref, g_norm_ref, sums_ref, total_imp_ref,
    in_part, rows, d_rows, d_sib, d_sum, d_in, head_b, labels, d_logits, *sems
):
    at = Place(sizes)
    chips, members = at.chips, QUAD * at.X
    devices = 2 * chips
    p_out, p_in, r_out, r_in, s_out, s_in, d_out, d_in_sem, b_out, b_in = sems
    width = own_ref.shape[1]
    same_core = others(at.chip, chips)
    greet([at.of_chip(chip) for chip in same_core] + [at.sibling()])
    started = []

    def begin(copy):
        copy.start()
        started.append(copy)

    team = others(at.member, members)
    for member in team:
        begin(send(part_ref.at[member], in_part.at[at.member], p_out.at[member], p_in.at[at.member], at.of_member(member)))
    in_part[at.member] = part_ref[at.member]
    head_b[...] = head_ref[...].astype(jnp.bfloat16)
    wide = devices * IMAGE_PAD
    spot = lax.broadcasted_iota(jnp.int32, (label_ref.shape[1], wide), 1)
    given = lax.broadcasted_iota(jnp.int32, (label_ref.shape[1], wide), 0)
    image = lax.rem(spot, IMAGE_PAD)
    device = lax.rem(lax.div(spot, IMAGE_PAD), chips) * 2 + lax.div(spot, IMAGE_PAD * chips)
    chosen = ((device * images + image == given) & (image < images)).astype(jnp.bfloat16)
    labels[...] = dot_f32(label_ref[...].astype(jnp.float32).astype(jnp.bfloat16), chosen, NN).astype(jnp.bfloat16)
    for member in team:
        send(in_part.at[member], in_part.at[member], p_out.at[member], p_in.at[member], at.of_member(member)).wait_recv()
    pooled = own_ref[...] + jnp.sum(in_part[...], 0)
    scaled, scale = norm_parts(pooled)
    gain, shift = gain_ref[2:3], gain_ref[5:6]
    a_three = scaled * gain + shift
    row = lax.broadcasted_iota(jnp.int32, (IMAGE_PAD, width), 0)
    block = jnp.where(row < images, a_three, 0.0)
    pieces = split_three(imp_ref[0:1])
    for index, piece in enumerate(pieces):
        block = jnp.where(row == images + index, piece.astype(jnp.float32), block)
    rows[at.c, at.chip] = block.astype(jnp.bfloat16)
    mine = rows.at[at.c, at.chip]
    for chip in same_core:
        begin(send(mine, mine, r_out.at[chip], r_in.at[at.chip], at.of_chip(chip)))
    for chip in same_core:
        part = rows.at[at.c, chip]
        send(part, part, r_out.at[chip], r_in.at[chip], at.of_chip(chip)).wait_recv()
    begin(send(rows.at[at.c], rows.at[at.c], s_out.at[0], s_in.at[0], at.sibling()))
    send(rows.at[1 - at.c], rows.at[1 - at.c], s_out.at[0], s_in.at[0], at.sibling()).wait_recv()
    gathered = rows[...].reshape(wide, width)
    in_block = lax.rem(lax.broadcasted_iota(jnp.int32, (wide, width), 0), IMAGE_PAD)
    total = jnp.sum(jnp.where(in_block >= images, gathered.astype(jnp.float32), 0.0), 0, keepdims=True)
    total_imp_ref[...] = jnp.broadcast_to(total, total_imp_ref.shape)
    gathered = jnp.where(in_block < images, gathered.astype(jnp.float32), 0.0).astype(jnp.bfloat16)
    logits = dot_f32(head_b[...], gathered, NT)
    image = lax.rem(lax.broadcasted_iota(jnp.int32, logits.shape, 1), IMAGE_PAD)
    count = devices * images
    target = labels[...].astype(jnp.float32)
    power = jnp.exp(-jnp.abs(logits))
    loss = jnp.maximum(logits, 0.0) + jnp.log1p(power) - target * logits
    loss = jnp.sum(jnp.where(image < images, loss, 0.0), 1, keepdims=True)
    loss = jnp.sum(loss, 0, keepdims=True) / count
    chance = jnp.where(logits >= 0.0, 1.0, power) / (1.0 + power)
    d_logits[...] = jnp.where(image < images, (chance - target) / count, 0.0).astype(jnp.bfloat16)
    partial = dot_f32(d_logits[...], head_b[...], TN)
    d_rows[...] = partial.reshape(d_rows.shape).astype(jnp.bfloat16)
    begin(send(d_rows.at[1 - at.c], d_sib, s_out.at[1], s_in.at[1], at.sibling()))
    g_head = dot_f32(d_logits[...], gathered, NN)
    g_head_ref[...] = g_head
    line = lax.broadcasted_iota(jnp.int32, sums_ref.shape, 0)
    sums_ref[...] = jnp.where(line == 0, loss, jnp.where(line == 1, total_square(g_head), 0.0))
    send(d_sib, d_sib, s_out.at[1], s_in.at[1], at.sibling()).wait_recv()
    d_sum[...] = (d_rows[at.c].astype(jnp.float32) + d_sib[...].astype(jnp.float32)).astype(jnp.bfloat16)
    for chip in same_core:
        begin(send(d_sum.at[chip], d_in.at[at.chip], d_out.at[chip], d_in_sem.at[at.chip], at.of_chip(chip)))
    d_in[at.chip] = d_sum[at.chip]
    for chip in same_core:
        send(d_in.at[chip], d_in.at[chip], d_out.at[chip], d_in_sem.at[chip], at.of_chip(chip)).wait_recv()
    d_norm = jnp.sum(d_in[...].astype(jnp.float32), 0)
    d_norm = jnp.where(row < images, d_norm, 0.0)
    d_pooled = norm_back(d_norm, scaled, scale, gain)
    d_pooled = jnp.where(row < images, d_pooled, 0.0)
    d_gain = jnp.sum(d_norm * scaled, 0, keepdims=True)
    d_shift = jnp.sum(d_norm, 0, keepdims=True)
    line = lax.broadcasted_iota(jnp.int32, g_norm_ref.shape, 0)
    g_norm_ref[...] = jnp.where(line == 2, d_gain, jnp.where(line == 5, d_shift, 0.0))
    own_d_ref[...] = d_pooled
    d_pool_ref[at.member] = d_pooled
    mine = d_pool_ref.at[at.member]
    for member in team:
        begin(send(own_d_ref, mine, b_out.at[member], b_in.at[at.member], at.of_member(member)))
    for member in team:
        part = d_pool_ref.at[member]
        send(part, part, b_out.at[member], b_in.at[member], at.of_member(member)).wait_recv()
    for copy in started:
        copy.wait_send()


def head_step(sizes, images, part, own, imp, gains, head, label):
    members = QUAD * sizes["x"]
    chips = members * sizes["g"]
    classes, width = head.shape
    wide = 2 * chips * IMAGE_PAD
    dma = pltpu.SemaphoreType.DMA
    by_member, by_chip = dma((members,)), dma((chips,))
    f32, half = jnp.float32, jnp.bfloat16
    blocks = (chips, IMAGE_PAD, width)
    return pl.pallas_call(
        functools.partial(head_kernel, sizes, images),
        out_shape=(
            jax.ShapeDtypeStruct((classes, width), f32),
            jax.ShapeDtypeStruct((members, IMAGE_PAD, width), f32),
            jax.ShapeDtypeStruct((IMAGE_PAD, width), f32),
            jax.ShapeDtypeStruct((8, width), f32),
            jax.ShapeDtypeStruct((8, 128), f32),
            jax.ShapeDtypeStruct((8, width), f32),
        ),
        in_specs=[whole()] * 6,
        out_specs=(whole(),) * 6,
        scratch_shapes=[
            VMEM((members, IMAGE_PAD, width), f32),
            VMEM((2, *blocks), half),
            VMEM((2, *blocks), half),
            VMEM(blocks, half),
            VMEM(blocks, half),
            VMEM(blocks, half),
            VMEM((classes, width), half),
            VMEM((classes, wide), half),
            VMEM((classes, wide), half),
        ]
        + [by_member, by_member, by_chip, by_chip, dma((2,)), dma((2,)), by_chip, by_chip]
        + [by_member, by_member],
        compiler_params=pltpu.CompilerParams(
            collective_id=4, has_side_effects=True, vmem_limit_bytes=56 * MIB
        ),
        cost_estimate=cost(42),
        name="head_step",
    )(part, own, imp, gains, head, label)


def route_math(per_image, n_experts, capacity, padded, pick_ref, rank_ref, mask_ref, length_ref):
    rows_here, span = mask_ref.shape
    tokens = rows_here * span
    valid = mask_ref[...].astype(jnp.float32)
    lengths = length_ref[...]
    position = lax.broadcasted_iota(jnp.int32, (rows_here, span), 1)
    segment = jnp.zeros((rows_here, span), jnp.int32)
    bound = jnp.zeros((rows_here, 1), jnp.int32)
    for image in range(per_image):
        bound = bound + lengths[:, image : image + 1]
        segment = segment + jnp.where(position >= bound, 1, 0)
    pool = jnp.zeros_like(valid)
    for image in range(per_image):
        member = jnp.where(segment == image, valid, 0.0)
        pool = pool + member / jnp.maximum(jnp.sum(member, 1, keepdims=True), 1.0)
    line = lax.broadcasted_iota(jnp.int32, (rows_here, span), 0)
    image = (segment + per_image * line).astype(jnp.float32)

    def flat(value):
        return jnp.concatenate([value[i : i + 1] for i in range(rows_here)], 1)

    rank_row = rank_ref[...].astype(jnp.float32)
    table = jnp.concatenate([flat(valid), flat(pool), flat(image), rank_row], 0)
    table = jnp.concatenate([table, jnp.zeros((124, tokens), jnp.float32)], 0).T
    valid_col, pool_col, image_col, rank_col = (table[:, i : i + 1] for i in range(4))
    picks = pick_ref[...]
    pick_one, pick_two = picks[:, 0:1], picks[:, 1:2]
    lane = lax.broadcasted_iota(jnp.int32, (tokens, 128), 1)
    in_first, in_second = lane < n_experts, (lane >= n_experts) & (lane < 2 * n_experts)
    hot = jnp.where(in_first & (pick_one == lane), valid_col, 0.0)
    hot = hot + jnp.where(in_second & (pick_two == lane - n_experts), valid_col, 0.0)
    shifted = jnp.where(in_second & (pick_one == lane - n_experts), valid_col, 0.0)
    before = jnp.where(rank_row < rank_col, 1.0, 0.0).astype(jnp.bfloat16)
    ahead = dot_f32(before, hot.astype(jnp.bfloat16), NN) + jnp.sum(shifted, 0, keepdims=True)
    counted = hot * ahead
    pos_one = jnp.sum(jnp.where(in_first, counted, 0.0), 1, keepdims=True)
    pos_two = jnp.sum(jnp.where(in_second, counted, 0.0), 1, keepdims=True)

    def place(pick, pos):
        kept = (valid_col > 0.0) & (pos < capacity)
        return jnp.where(kept, pick.astype(jnp.float32) * padded + pos, -1.0)

    columns = (
        place(pick_one, pos_one),
        place(pick_two, pos_two),
        valid_col,
        pool_col,
        image_col,
        pick_one.astype(jnp.float32),
        pick_two.astype(jnp.float32),
    )
    result = jnp.zeros((tokens, 128), jnp.float32)
    for index, column in enumerate(columns):
        result = jnp.where(lane == index, column, result)
    return result


def allowed_slots(lengths, row, images, valid_row, span):
    query = lax.broadcasted_iota(jnp.int32, (span, span), 0)
    key = lax.broadcasted_iota(jnp.int32, (span, span), 1)
    bound = 0
    query_seg, key_seg = jnp.zeros((span, span), jnp.int32), jnp.zeros((span, span), jnp.int32)
    for image in range(images):
        bound = bound + lengths[row, image]
        query_seg = query_seg + jnp.where(query >= bound, 1, 0)
        key_seg = key_seg + jnp.where(key >= bound, 1, 0)
    return (query_seg == key_seg) & ((valid_row > 0) | (query == key))


TILE = 32


def tiles(count):
    return [slice(start, min(start + TILE, count)) for start in range(0, count, TILE)]


class Team:
    def __init__(self, at):
        self.at, self.span = at, 2 * at.G
        self.spot = at.g * QUAD + at.r

    def target(self, step):
        at = self.at
        chosen = lax.rem(self.spot + step, self.span)
        block, index = lax.div(chosen, 2), lax.rem(chosen, 2)
        core = lax.div(self.spot, self.span)
        r = 2 * at.c + index
        own = (block == at.g) & (r == at.r) & (core == at.c)
        return {"g": block, "r": r, "x": at.x, "c": core}, index, own

    def source(self, step):
        at = self.at
        chosen = at.g * 2 + lax.rem(at.r, 2)
        spot = at.c * self.span + lax.rem(chosen - step + self.span, self.span)
        device = {"g": lax.div(spot, QUAD), "r": lax.rem(spot, QUAD), "x": at.x, "c": lax.div(at.r, 2)}
        return device, lax.rem(at.r, 2)

    def peers(self):
        at = self.at
        count = 2 * at.G * QUAD
        me = self.spot * 2 + at.c
        line = []
        for device in others(me, count):
            spot = lax.div(device, 2)
            line.append(
                {"g": lax.div(spot, QUAD), "r": lax.rem(spot, QUAD), "x": at.x, "c": lax.rem(device, 2)}
            )
        for x in others(at.x, at.X):
            line += [{"g": at.g, "r": r, "x": x, "c": at.c} for r in range(QUAD)]
        return line


def image_hot(detail, padded):
    image = detail[2:3, :padded]
    line = lax.broadcasted_iota(jnp.int32, (IMAGE_PAD, padded), 0).astype(jnp.float32)
    return line == image


def forward_kernel(
    sizes, n_experts, images, padded,
    length_ref, mask_ref, patch_ref, w_ref, gain_ref, router_ref, col_ref, shard_ref,
    x_zero_out, a_one_out, qkv_out, att_out, x_one_out, a_two_out, prob_ref, lse_ref, pool_ref, imp_ref,
    rows_out, detail_out, act_out, slope_out, y_out, part_ref, weight_out,
    x_zero_buf, a_one_buf, qkv_buf, att_buf, x_one_buf, a_two_ref, weights, send_rows, send_detail, places,
    rows_in, detail_in, total, act_buf, slope_buf, dense_sem, keep_sem, own_sem,
    w_out, w_in, s_out, s_in, r_out, r_in, m_out, m_in, act_sem, slope_sem
):
    at = Place(sizes)
    team = Team(at)
    half = weights.shape[1]
    early, middle = half // 2, half * 3 // 4
    span, width = mask_ref.shape[2], patch_ref.shape[1]
    rows_here = mask_ref.shape[0]
    tokens = rows_here * span
    greet(team.peers())

    def spot_of(step, side=0):
        return step // early, side * early + step % early

    def swap_copy(step):
        return send(
            weights.at[spot_of(step)], weights.at[spot_of(step, 1)], s_out.at[step], s_in.at[step], at.sibling()
        )

    def shard_copy(step):
        device, index, own = team.target(step)
        return send(
            shard_ref.at[index], weights.at[spot_of(step)], w_out.at[step], w_in.at[step], device
        )

    def shard_own(step):
        device, index, own = team.target(step)
        return pltpu.make_async_copy(shard_ref.at[index], weights.at[spot_of(step)], w_in.at[step])

    def shard_starts(steps):
        for step in steps:
            own = team.target(step)[2]

            @pl.when(own)
            def _():
                shard_own(step).start()

            @pl.when(jnp.logical_not(own))
            def _():
                shard_copy(step).start()

    def shard_waits(steps):
        for step in steps:
            own = team.target(step)[2]

            @pl.when(own)
            def _():
                shard_own(step).wait()

            @pl.when(jnp.logical_not(own))
            def _():
                shard_copy(step).wait_recv()

            swap_copy(step).start()

    shard_starts(range(early))

    dense = (
        (x_zero_buf, x_zero_out), (a_one_buf, a_one_out), (qkv_buf, qkv_out), (att_buf, att_out), (x_one_buf, x_one_out),
    )

    def dense_copies(row):
        slot = lax.rem(row, 2)
        here = pl.ds(pl.multiple_of(row * span, 16), span)
        return [
            pltpu.make_async_copy(buf.at[slot], out.at[here], dense_sem.at[index, slot])
            for index, (buf, out) in enumerate(dense)
        ]

    pool_ref[...] = jnp.zeros_like(pool_ref)
    imp_ref[...] = jnp.zeros_like(imp_ref)
    routers = router_ref[...].astype(jnp.bfloat16)
    if routers.shape[0] < 128:
        routers = jnp.concatenate(
            [routers, jnp.zeros((128 - routers.shape[0], width), jnp.bfloat16)], 0
        )
    lane = lax.broadcasted_iota(jnp.int32, (span, 128), 1)

    def dense_row(row, carry):
        @pl.when(row >= 2)
        def _():
            for copy in dense_copies(row - 2):
                copy.wait()

        slot = lax.rem(row, 2)
        here = pl.ds(pl.multiple_of(row * span, 16), span)
        x_zero = dot_f32(patch_ref[here], w_ref[0], NN)
        x_zero_buf[slot] = x_zero
        a_one = (norm_parts(x_zero)[0] * gain_ref[0:1] + gain_ref[3:4]).astype(jnp.bfloat16)
        a_one_buf[slot] = a_one
        for part in range(3):
            qkv_buf[slot, :, part * width : (part + 1) * width] = dot_f32(
                a_one, w_ref[1 + part], NN
            ).astype(jnp.bfloat16)
        open_to = allowed_slots(length_ref, row, images, mask_ref[row], span)
        logs = jnp.zeros((span, 128), jnp.float32)
        for pair in range(width // 128):
            query, key, value = (
                qkv_buf[slot, :, part * width + pair * 128 : part * width + (pair + 1) * 128]
                for part in range(3)
            )
            outs = []
            for side in range(2):
                held = jnp.where((lane < 64) == (side == 0), query, jnp.zeros_like(query))
                scores = jnp.where(open_to, dot_f32(held, key, NT) * 64**-0.5, mask_fill)
                top = jnp.max(scores, 1, keepdims=True)
                powers = jnp.exp(scores - top)
                whole_sum = jnp.sum(powers, 1, keepdims=True)
                probs = (powers * (1.0 / whole_sum)).astype(jnp.bfloat16)
                outs.append(dot_f32(probs, value, NN))
                logs = jnp.where(lane == 2 * pair + side, top + jnp.log(whole_sum), logs)
            att_buf[slot, :, pair * 128 : (pair + 1) * 128] = jnp.where(
                lane < 64, outs[0], outs[1]
            ).astype(jnp.bfloat16)
        lse_ref[here] = logs
        x_one = x_zero + dot_f32(att_buf[slot], w_ref[4], NN)
        x_one_buf[slot] = x_one
        a_two = (norm_parts(x_one)[0] * gain_ref[1:2] + gain_ref[4:5]).astype(jnp.bfloat16)
        a_two_ref[here] = a_two
        logits = jnp.where(lane < n_experts, dot_f32(a_two, routers, NT), mask_fill)
        powers = jnp.exp(logits - jnp.max(logits, 1, keepdims=True))
        probs = powers / jnp.sum(powers, 1, keepdims=True)
        prob_ref[here] = probs
        columns = col_ref[here]
        valid, pool, image = columns[:, 2:3], columns[:, 3:4], columns[:, 4:5]
        imp_ref[0:1, 0:128] += jnp.sum(probs * valid, 0, keepdims=True)
        line = lax.broadcasted_iota(jnp.int32, pool_ref.shape, 0)
        for index in range(images):
            number = row * images + index
            weight = jnp.where(image == number.astype(jnp.float32), pool, 0.0)
            pooled = jnp.sum(x_one * weight, 0, keepdims=True)
            pool_ref[...] = jnp.where(line == number, pooled, pool_ref[...])
        for copy in dense_copies(row):
            copy.start()
        return carry

    lax.fori_loop(0, rows_here, dense_row, 0)

    columns = col_ref[...]
    places[...] = columns.T[:8]
    lane = lax.broadcasted_iota(jnp.int32, (tokens, 128), 1)
    kind, expert = lax.div(lane, n_experts), lax.rem(lane, n_experts).astype(jnp.float32)
    slot_lane = lax.broadcasted_iota(jnp.int32, (tokens, send_detail.shape[2]), 1).astype(jnp.float32)
    pool, image = columns[:, 3:4], columns[:, 4:5]
    details = None
    for choice in range(2):
        slot, pick = columns[:, choice : choice + 1], columns[:, 5 + choice : 6 + choice]
        hot = (expert == pick) & (slot >= 0.0)
        gate = jnp.sum(jnp.where(hot & (kind == 0), prob_ref[...], 0.0), 1, keepdims=True)
        values = jnp.zeros((tokens, 128), jnp.float32)
        pieces = [*split_three(gate), *split_three(pool), image]
        for index, piece in enumerate(pieces):
            values = jnp.where(kind == index, piece.astype(jnp.float32), values)
        values = jnp.where(hot, values, 0.0).astype(jnp.bfloat16)
        spot = jnp.where(slot >= 0.0, slot - pick * padded, -1.0)
        chosen = jnp.where(spot == slot_lane, 1.0, 0.0).astype(jnp.bfloat16)
        found = dot_f32(values, chosen, TN)
        details = found if details is None else details + found
    n = n_experts
    gates = details[0:n] + details[n : 2 * n] + details[2 * n : 3 * n]
    pools = details[3 * n : 4 * n] + details[4 * n : 5 * n] + details[5 * n : 6 * n]
    numbers = details[6 * n : 7 * n]
    for index in range(n):
        for spot, value in enumerate((gates, pools, numbers)):
            send_detail[index, spot : spot + 1] = value[index : index + 1]
        send_detail[index, 3:8] = jnp.zeros((5, send_detail.shape[2]), jnp.float32)

    def rows_of(member):
        slots = lax.broadcasted_iota(jnp.int32, (padded, tokens), 0) + member * padded
        slots = slots.astype(jnp.float32)
        match = (slots == places[0:1]) | (slots == places[1:2])
        match = jnp.where(match, 1.0, 0.0).astype(jnp.bfloat16)
        return dot_f32(match, a_two_ref[...], NN).astype(jnp.bfloat16)

    def row_copy(member, source):
        return send(
            send_rows.at[member], rows_in.at[source], r_out.at[member], r_in.at[source], at.of_member(member)
        )

    def detail_copy(member, source):
        return send(
            send_detail.at[member], detail_in.at[source], m_out.at[member], m_in.at[source], at.of_member(member)
        )

    def dispatch_step(index, carry):
        member = lax.rem(at.member + index, n_experts)
        send_rows[member] = rows_of(member)
        row_copy(member, at.member).start()
        detail_copy(member, at.member).start()
        return carry

    lax.fori_loop(1, n_experts, dispatch_step, 0)
    shard_starts(range(early, middle))
    rows_in[at.member] = rows_of(at.member)
    detail_in[at.member] = send_detail[at.member]
    a_two_copy = pltpu.make_async_copy(a_two_ref, a_two_out, keep_sem.at[0])
    a_two_copy.start()
    for row in range(max(rows_here - 2, 0), rows_here):
        for copy in dense_copies(row):
            copy.wait()

    shard_waits(range(early))
    for step in range(early):
        swap_copy(step).wait_recv()

    many = act_buf.shape[2] // padded
    count = many * padded
    rounds = n_experts // many
    part = act_buf.shape[3]

    def hidden_copies(index):
        slot, turn = lax.rem(index, 2), lax.div(index, rounds)
        block = block_of(index)
        here = pl.ds(pl.multiple_of(block * count, 16), count)
        there = pl.ds(turn * half, half)
        return (
            pltpu.make_async_copy(act_buf.at[slot], act_out.at[there, here], act_sem.at[slot]),
            pltpu.make_async_copy(slope_buf.at[slot], slope_out.at[there, here], slope_sem.at[slot]),
        )

    def block_of(index):
        return lax.rem(lax.div(at.member, many) + index, rounds)

    def expert_step(index, carry):
        slot, turn = lax.rem(index, 2), lax.div(index, rounds)
        block = block_of(index)

        @pl.when(turn == 0)
        def _():
            for spot in range(many):
                source = block * many + spot

                @pl.when(source != at.member)
                def _():
                    row_copy(source, source).wait_recv()
                    detail_copy(source, source).wait_recv()

        @pl.when(index == 0)
        def _():
            shard_starts(range(middle, half))

        @pl.when(index == rounds)
        def _():
            shard_waits(range(early, half))

        @pl.when(index >= 2)
        def _():
            for copy in hidden_copies(index - 2):
                copy.wait()

        rows = rows_in[pl.ds(block * many, many)].reshape(count, width)
        for chunk in range(half):
            if chunk == early:

                @pl.when(index == rounds)
                def _():
                    for step in range(early, half):
                        swap_copy(step).wait_recv()

            hidden_all = dot_f32(rows, weights[turn, chunk, 0], NT)
            for spot in tiles(count):
                hidden = hidden_all[spot]
                square = hidden * hidden
                curve = jnp.tanh(hidden * (0.7978845608 + 0.7978845608 * 0.044715 * square))
                upper = 0.5 + 0.5 * curve
                gelu = hidden * upper
                slope = upper + gelu * (1.0 - upper) * (
                    2.0 * 0.7978845608 + 6.0 * 0.7978845608 * 0.044715 * square
                )
                act_buf[slot, chunk, spot] = gelu.astype(jnp.bfloat16)
                slope_buf[slot, chunk, spot] = slope.astype(jnp.bfloat16)
        for copy in hidden_copies(index):
            copy.start()
        acts = jnp.concatenate([act_buf[slot, chunk] for chunk in range(half)], 1)
        ends = jnp.concatenate([weights[turn, chunk, 1] for chunk in range(half)], 0)
        found = dot_f32(acts, ends, NN)
        here = pl.ds(pl.multiple_of(block * count, 16), count)

        @pl.when(turn == 0)
        def _():
            total[here] = found

        @pl.when(turn == 1)
        def _():
            result = (total[here] + found).astype(jnp.bfloat16)
            for spot in range(many):
                source = block * many + spot
                mine = result[spot * padded : (spot + 1) * padded]
                send_rows[source] = mine
                detail = detail_in[source]
                weight = detail[0:1, :padded] * detail[1:2, :padded]
                shares = jnp.where(image_hot(detail, padded), weight, 0.0)
                pieces = jnp.concatenate(split_three(shares), 0)
                sums = dot_f32(pieces, mine, NN)
                part_ref[source] = (
                    sums[:IMAGE_PAD] + sums[IMAGE_PAD : 2 * IMAGE_PAD] + sums[2 * IMAGE_PAD :]
                )

        @pl.when(index == rounds - 1)
        def _():
            for member in others(at.member, n_experts):
                row_copy(member, at.member).wait_send()
                detail_copy(member, at.member).wait_send()

        return carry

    lax.fori_loop(0, 2 * rounds, expert_step, 0)
    keeps = [
        pltpu.make_async_copy(rows_in, rows_out, keep_sem.at[1]),
        pltpu.make_async_copy(detail_in, detail_out, keep_sem.at[2]),
        pltpu.make_async_copy(send_rows, y_out, keep_sem.at[3]),
        pltpu.make_async_copy(weights, weight_out, keep_sem.at[4]),
    ]
    for copy in keeps:
        copy.start()
    for index in range(2 * rounds - 2, 2 * rounds):
        for copy in hidden_copies(index):
            copy.wait()
    for step in range(half):
        own = team.target(step)[2]
        swap_copy(step).wait_send()

        @pl.when(jnp.logical_not(own))
        def _():
            shard_copy(step).wait_send()

    a_two_copy.wait()
    for copy in keeps:
        copy.wait()


def forward(sizes, n_experts, padded, lengths, slot_mask, patches, weights, gains, routers, columns, shards):
    rows_here, span = slot_mask.shape
    tokens, width = patches.shape
    part = shards.shape[2]
    half = 2 * sizes["g"]
    lanes = round_up(padded, 128)
    many = max(1, 576 // padded)
    count = n_experts * padded
    f32, kind = jnp.float32, jnp.bfloat16
    dma = pltpu.SemaphoreType.DMA
    each, parts, two = dma((n_experts,)), dma((half,)), dma((2,))

    def out(wide, dtype):
        return jax.ShapeDtypeStruct((tokens, wide), dtype)

    hidden = jax.ShapeDtypeStruct((2 * half, count, part), kind)
    rows = (n_experts, padded, width)
    return pl.pallas_call(
        functools.partial(forward_kernel, sizes, n_experts, lengths.shape[1], padded),
        out_shape=(
            out(width, f32), out(width, kind), out(3 * width, kind), out(width, kind), out(width, f32),
            out(width, kind), out(128, f32), out(128, f32),
            jax.ShapeDtypeStruct((IMAGE_PAD, width), f32), jax.ShapeDtypeStruct((8, width), f32),
            jax.ShapeDtypeStruct(rows, kind), jax.ShapeDtypeStruct((n_experts, 8, lanes), f32),
            hidden, hidden, jax.ShapeDtypeStruct(rows, kind),
            jax.ShapeDtypeStruct((n_experts, IMAGE_PAD, width), f32),
            jax.ShapeDtypeStruct((2, half, 2, part, width), kind),
        ),
        in_specs=[whole(pltpu.SMEM)] + [whole()] * 6 + [whole(ANY)],
        out_specs=(whole(ANY),) * 6 + (whole(),) * 4 + (whole(ANY),) * 5 + (whole(), whole(ANY)),
        scratch_shapes=[
            VMEM((2, span, width), f32), VMEM((2, span, width), kind), VMEM((2, span, 3 * width), kind),
            VMEM((2, span, width), kind), VMEM((2, span, width), f32), VMEM((tokens, width), kind),
            VMEM((2, half, 2, part, width), kind), VMEM(rows, kind), VMEM((n_experts, 8, lanes), f32),
            VMEM((8, tokens), f32), VMEM(rows, kind), VMEM((n_experts, 8, lanes), f32),
            VMEM((count, width), f32), VMEM((2, half, many * padded, part), kind),
            VMEM((2, half, many * padded, part), kind), dma((5, 2)), dma((5,)), two,
            parts, parts, parts, parts, each, each, each, each, two, two,
        ],
        compiler_params=pltpu.CompilerParams(
            collective_id=5, has_side_effects=True, vmem_limit_bytes=60 * MIB
        ),
        cost_estimate=cost(120),
        name="forward",
    )(lengths, slot_mask[:, None, :], patches, weights, gains, routers, columns, shards)


def chunk_at(index, half):
    early = half // 2
    step = lax.rem(index, half)
    side = jnp.where(index < half, early, 0)
    return lax.div(step, early) * half + side + lax.rem(step, early)


def expert_backward_kernel(
    sizes, padded, rows_ref, detail_ref, pool_ref, y_ref, slope_ref, act_ref, weight_ref, *refs
):
    at = Place(sizes)
    sources, unused, width = rows_ref.shape
    chunks, unused, part = slope_ref.shape
    half = chunks // 2
    back_ref, gate_ref, *outs = refs[: 2 + half]
    d_hidden, d_rows, send_rows, send_gate, send_grad, got_grad = refs[2 + half : 8 + half]
    own_sem, r_out, r_in, m_out, m_in, g_out, g_in, g_keep = refs[8 + half :]
    many = y_ref.shape[0]
    rounds = sources // many
    step = pl.program_id(0)
    team = others(at.member, sources)

    def row_copy(member, source):
        return send(
            send_rows.at[member], back_ref.at[source], r_out.at[member], r_in.at[source], at.of_member(member)
        )

    def gate_copy(member, source):
        return send(
            send_gate.at[member], gate_ref.at[source], m_out.at[member], m_in.at[source], at.of_member(member)
        )

    def keep_copies():
        return (
            pltpu.make_async_copy(send_rows.at[at.member], back_ref.at[at.member], own_sem.at[0]),
            pltpu.make_async_copy(send_gate.at[at.member], gate_ref.at[at.member], own_sem.at[1]),
        )

    def grad_copy(index):
        return send(
            send_grad.at[index], got_grad.at[index], g_out.at[index], g_in.at[index], at.sibling()
        )

    def out_copy(index):
        return pltpu.make_async_copy(got_grad.at[index], outs[index], g_keep.at[index])

    @pl.when(step == 0)
    def _():
        greet([at.of_member(member) for member in team] + [at.sibling()])

    @pl.when(step < rounds)
    def _():
        block = lax.rem(lax.div(at.member, many) + 1 + step, rounds)
        d_out = []
        for index in range(many):
            source = block * many + index
            detail = detail_ref[source]
            hot = image_hot(detail, padded)
            hots = jnp.where(hot, 1.0, 0.0).astype(jnp.bfloat16)
            pools = jnp.concatenate(split_three(pool_ref[source]), 0)
            wide = dot_f32(jnp.concatenate([hots] * 3, 0), pools, TN)
            lanes = detail.shape[1]
            upright = jnp.concatenate([detail, jnp.zeros((120, lanes), jnp.float32)], 0).T
            gate, pool = upright[:padded, 0:1], upright[:padded, 1:2]
            d_out.append((gate * (pool * wide)).astype(jnp.bfloat16))
            along = dot_f32(pools, y_ref[index], NT)
            along = along[:IMAGE_PAD] + along[IMAGE_PAD : 2 * IMAGE_PAD] + along[2 * IMAGE_PAD :]
            d_gate = jnp.sum(jnp.where(hot, along, 0.0), 0, keepdims=True) * detail[1:2, :padded]
            send_gate[source] = jnp.zeros(detail.shape, jnp.float32)
            send_gate[source, 0:1, :padded] = d_gate
        d_out = jnp.concatenate(d_out, 0)
        count = many * padded
        span = pl.ds(pl.multiple_of(block * count, 16), count)
        d_rows[span] = d_out

        def weight(index, which):
            return weight_ref[index // half, index % half, which]

        for index in range(chunks):
            d_act = dot_f32(d_out, weight(index, 1), NT)
            for spot in tiles(count):
                rows_now = pl.ds(pl.multiple_of(block * count + spot.start, 16), spot.stop - spot.start)
                d_hidden[index, rows_now] = (
                    d_act[spot] * slope_ref[index, spot].astype(jnp.float32)
                ).astype(jnp.bfloat16)
        d_hids = jnp.concatenate([d_hidden[index, span] for index in range(chunks)], 1)
        starts = jnp.concatenate([weight(index, 0) for index in range(chunks)], 0)
        total = dot_f32(d_hids, starts, NN)
        total = total.astype(jnp.bfloat16)
        for index in range(many):
            source = block * many + index
            send_rows[source] = total[index * padded : (index + 1) * padded]

            @pl.when(source != at.member)
            def _():
                row_copy(source, at.member).start()
                gate_copy(source, at.member).start()

            @pl.when(source == at.member)
            def _():
                for copy in keep_copies():
                    copy.start()

    @pl.when(step >= rounds)
    def _():
        index = step - rounds
        chunk = chunk_at(index, half)
        rows = rows_ref[...].reshape(sources * padded, width)
        g_one = dot_f32(d_hidden[chunk], rows, TN)
        g_two = dot_f32(act_ref[0], d_rows[...], TN)

        @pl.when(index < half)
        def _():
            send_grad[index, 0] = g_one.astype(jnp.bfloat16)
            send_grad[index, 1] = g_two.astype(jnp.bfloat16)
            grad_copy(index).start()

        @pl.when(index >= half)
        def _():
            spot = index - half
            grad_copy(spot).wait_recv()
            got_grad[spot, 0] = (got_grad[spot, 0].astype(jnp.float32) + g_one).astype(jnp.bfloat16)
            got_grad[spot, 1] = (got_grad[spot, 1].astype(jnp.float32) + g_two).astype(jnp.bfloat16)

        for spot in range(half):

            @pl.when(index == spot + half)
            def _():
                out_copy(spot).start()

    @pl.when(step == rounds + chunks - 1)
    def _():
        for member in team:
            row_copy(member, member).wait_recv()
            gate_copy(member, member).wait_recv()
        for member in team:
            row_copy(member, at.member).wait_send()
            gate_copy(member, at.member).wait_send()
        for copy in keep_copies():
            copy.wait()
        for spot in range(half):
            grad_copy(spot).wait_send()
            out_copy(spot).wait()


def expert_backward(sizes, rows, details, pools, results, slopes, acts, weights):
    sources, padded, width = rows.shape
    chunks, count, part = acts.shape
    many = max(1, (288 if part % 128 else 576) // padded)
    rounds, half = sources // many, chunks // 2
    lanes = details.shape[2]
    kind = jnp.bfloat16
    dma = pltpu.SemaphoreType.DMA
    each, parts = dma((sources,)), dma((half,))

    def block_of(step):
        member = lax.axis_index("x") * QUAD + lax.axis_index("r")
        return lax.rem(lax.div(member, many) + 1 + jnp.minimum(step, rounds - 1), rounds)

    def chunk_of(step):
        return chunk_at(jnp.maximum(step - rounds, 0), half)

    return pl.pallas_call(
        functools.partial(expert_backward_kernel, sizes, padded),
        grid=(rounds + chunks,),
        out_shape=(
            jax.ShapeDtypeStruct((sources, padded, width), kind),
            jax.ShapeDtypeStruct((sources, 8, lanes), jnp.float32),
        )
        + (jax.ShapeDtypeStruct((2, part, width), kind),) * half,
        in_specs=[
            whole(), whole(), whole(),
            pl.BlockSpec((many, padded, width), lambda i: (block_of(i), 0, 0)),
            pl.BlockSpec((chunks, many * padded, part), lambda i: (0, block_of(i), 0)),
            pl.BlockSpec((1, count, part), lambda i: (chunk_of(i), 0, 0)),
        ]
        + [whole()],
        out_specs=(whole(ANY),) * (2 + half),
        scratch_shapes=[
            VMEM((chunks, count, part), kind),
            VMEM((count, width), kind),
            VMEM((sources, padded, width), kind),
            VMEM((sources, 8, lanes), jnp.float32),
            VMEM((half, 2, part, width), kind),
            VMEM((half, 2, part, width), kind),
            dma((2,)), each, each, each, each, parts, parts, parts,
        ],
        compiler_params=pltpu.CompilerParams(
            collective_id=6, has_side_effects=True, vmem_limit_bytes=62 * MIB
        ),
        cost_estimate=cost(65),
        name="expert_backward",
    )(rows, details, pools, results, slopes, acts, weights)


def dense_backward_kernel(
    sizes, n_experts, images, padded, length_ref, mask_ref, patch_ref, x_zero_ref, a_one_ref, qkv_ref, att_ref,
    x_one_ref, a_two_ref, prob_ref, lse_ref, col_ref, w_ref, gain_ref, router_ref, back_ref, gate_ref,
    pool_ref, imp_ref, third_ref, out_ref, grads, g_router, g_norm, d_qkv
):
    row = pl.program_id(0)
    span, width = patch_ref.shape
    mats, rows = grads.shape[0], width // (8 * sizes["g"] * sizes["x"])

    @pl.when(row == 0)
    def _():
        grads[...] = jnp.zeros_like(grads)
        g_router[...] = jnp.zeros_like(g_router)
        g_norm[...] = third_ref[...]

    columns = col_ref[...]
    slot_one, slot_two = columns[:, 0:1], columns[:, 1:2]
    count = n_experts * padded
    slot = lax.broadcasted_iota(jnp.int32, (span, count), 1).astype(jnp.float32)
    match = jnp.where((slot == slot_one) | (slot == slot_two), 1.0, 0.0).astype(jnp.bfloat16)
    d_a_two = dot_f32(match, back_ref[...].reshape(count, width), NN)
    lanes = gate_ref.shape[2]
    spot = lax.broadcasted_iota(jnp.int32, (span, lanes), 1)
    inside = spot < padded
    spot = spot.astype(jnp.float32)
    found_one, found_two = jnp.zeros((span, lanes), jnp.float32), jnp.zeros((span, lanes), jnp.float32)
    for expert in range(n_experts):
        line = jnp.broadcast_to(gate_ref[expert, 0:1], (span, lanes))
        found_one = jnp.where(inside & (spot == slot_one - expert * padded), line, found_one)
        found_two = jnp.where(inside & (spot == slot_two - expert * padded), line, found_two)
    d_gate_one = jnp.sum(found_one, 1, keepdims=True)
    d_gate_two = jnp.sum(found_two, 1, keepdims=True)
    lane = lax.broadcasted_iota(jnp.int32, (span, 128), 1)
    number = lane.astype(jnp.float32)
    valid, pool, image = columns[:, 2:3], columns[:, 3:4], columns[:, 4:5]
    head = lax.broadcasted_iota(jnp.int32, (1, 128), 1) < n_experts
    importance = imp_ref[0:1, 0:128]
    centre = jnp.sum(jnp.where(head, importance, 0.0), 1, keepdims=True) / n_experts
    away = jnp.where(head, importance - centre, 0.0)
    spread = jnp.sum(away * away, 1, keepdims=True) / n_experts
    d_imp = aux_weight * (
        2.0 * away / (n_experts * centre * centre)
        - 2.0 * spread / (n_experts * centre * centre * centre)
    )
    d_probs = valid * d_imp
    d_probs = d_probs + jnp.where(number == columns[:, 5:6], d_gate_one, 0.0)
    d_probs = d_probs + jnp.where(number == columns[:, 6:7], d_gate_two, 0.0)
    probs = prob_ref[...]
    d_router = (probs * (d_probs - jnp.sum(probs * d_probs, 1, keepdims=True))).astype(jnp.bfloat16)
    g_router[...] += dot_f32(d_router, a_two_ref[...], TN)
    routers = router_ref[...].astype(jnp.bfloat16)
    if routers.shape[0] < 128:
        routers = jnp.concatenate(
            [routers, jnp.zeros((128 - routers.shape[0], width), jnp.bfloat16)], 0
        )
    d_a_two = d_a_two + dot_f32(d_router, routers, NN)
    scaled, scale = norm_parts(x_one_ref[...])
    g_norm[1:2] += jnp.sum(d_a_two * scaled, 0, keepdims=True)
    g_norm[4:5] += jnp.sum(d_a_two, 0, keepdims=True)
    d_x_one = norm_back(d_a_two, scaled, scale, gain_ref[1:2])
    for index in range(images):
        place = row * images + index
        weight = jnp.where(image == place.astype(jnp.float32), pool, 0.0)
        d_x_one = d_x_one + weight * pool_ref[pl.ds(place, 1)]
    d_att = d_x_one.astype(jnp.bfloat16)
    grads[4] += dot_f32(att_ref[...], d_att, TN)
    d_out = dot_f32(d_att, w_ref[4], NT).astype(jnp.bfloat16)
    open_to = allowed_slots(length_ref, row, images, mask_ref[0], span)
    logs = lse_ref[...]
    for pair in range(width // 128):
        query, key, value = (
            qkv_ref[:, part * width + pair * 128 : part * width + (pair + 1) * 128]
            for part in range(3)
        )
        d_pair = d_out[:, pair * 128 : (pair + 1) * 128]
        found = []
        for side in range(2):
            left = (lane < 64) == (side == 0)
            held = jnp.where(left, query, jnp.zeros_like(query))
            scores = jnp.where(open_to, dot_f32(held, key, NT) * 64**-0.5, mask_fill)
            total = logs[:, 2 * pair + side : 2 * pair + side + 1]
            chance = jnp.exp(scores - total)
            d_held = jnp.where(left, d_pair, jnp.zeros_like(d_pair))
            d_chance = dot_f32(d_held, value, NT)
            d_value = dot_f32(chance.astype(jnp.bfloat16), d_pair, TN)
            d_scores = chance * (d_chance - jnp.sum(chance * d_chance, 1, keepdims=True))
            d_scores = d_scores.astype(jnp.bfloat16)
            d_query = dot_f32(d_scores, key, NN) * 64**-0.5
            d_key = dot_f32(d_scores, query, TN) * 64**-0.5
            found.append((d_query, d_key, d_value))
        for part in range(3):
            d_qkv[:, part * width + pair * 128 : part * width + (pair + 1) * 128] = jnp.where(
                lane < 64, found[0][part], found[1][part]
            ).astype(jnp.bfloat16)
    d_a_one = None
    for part in range(3):
        piece = d_qkv[:, part * width : (part + 1) * width]
        grads[1 + part] += dot_f32(a_one_ref[...], piece, TN)
        found = dot_f32(piece, w_ref[1 + part], NT)
        d_a_one = found if d_a_one is None else d_a_one + found
    scaled, scale = norm_parts(x_zero_ref[...])
    g_norm[0:1] += jnp.sum(d_a_one * scaled, 0, keepdims=True)
    g_norm[3:4] += jnp.sum(d_a_one, 0, keepdims=True)
    d_x_zero = norm_back(d_a_one, scaled, scale, gain_ref[0:1]) + d_x_one
    grads[0] += dot_f32(patch_ref[...], d_x_zero.astype(jnp.bfloat16), TN)

    @pl.when(row == pl.num_programs(0) - 1)
    def _():
        Z, Y, X = QUAD, sizes["g"], sizes["x"]
        tall = max(8, n_experts)
        norms = g_norm[...]
        if tall > 8:
            norms = jnp.concatenate([norms, jnp.zeros((tall - 8, width), jnp.float32)], 0)
        router_grads = g_router[:tall]
        depth = out_ref.shape[4]
        device = 0
        for z in range(Z):
            for y in range(Y):
                for x in range(X):
                    for c in range(2):
                        spot = slice(device * rows, (device + 1) * rows)
                        blank = jnp.zeros((tall, 128 - rows), jnp.float32)
                        tail = [norms[:, spot], blank, router_grads[:, spot], blank]
                        tail.append(jnp.zeros((tall, width - 256), jnp.float32))
                        pieces = [grads[mat, spot] for mat in range(mats)]
                        pieces.append(jnp.concatenate(tail, 1))
                        left = depth - mats * rows - tall
                        if left:
                            pieces.append(jnp.zeros((left, width), jnp.float32))
                        out_ref[c, z, x, y] = jnp.concatenate(pieces, 0).astype(jnp.bfloat16)
                        device += 1


def dense_backward(
    sizes, n_experts, padded, rows_own, lengths, slot_mask, patches, kept, columns, weights, gains, routers, back,
    gates, pooled, importance, third
):
    rows_here, span = slot_mask.shape
    tokens, width = patches.shape
    mats = weights.shape[0]
    depth = round_up(mats * rows_own + max(8, n_experts), 16)
    x_zero, a_one, qkv, att, x_one, a_two, probs, logs = kept

    def block(wide):
        return pl.BlockSpec((span, wide), lambda i: (i, 0))

    return pl.pallas_call(
        functools.partial(dense_backward_kernel, sizes, n_experts, lengths.shape[1], padded),
        grid=(rows_here,),
        out_shape=jax.ShapeDtypeStruct(
            (2, QUAD, sizes["x"], sizes["g"], depth, width), jnp.bfloat16
        ),
        in_specs=[
            whole(pltpu.SMEM), pl.BlockSpec((1, 1, span), lambda i: (i, 0, 0)), block(width),
            block(width), block(width), block(3 * width), block(width), block(width), block(width),
            block(128), block(128), block(128),
        ]
        + [whole()] * 8,
        out_specs=whole(),
        scratch_shapes=[
            VMEM((mats, width, width), jnp.float32),
            VMEM((128, width), jnp.float32),
            VMEM((8, width), jnp.float32),
            VMEM((span, 3 * width), jnp.bfloat16),
        ],
        compiler_params=pltpu.CompilerParams(vmem_limit_bytes=60 * MIB),
        cost_estimate=cost(50),
        name="dense_backward",
    )(
        lengths, slot_mask[:, None, :], patches, x_zero, a_one, qkv, att, x_one, a_two, probs, logs, columns,
        weights, gains, routers, back, gates, pooled, importance, third,
    )


def shard_moves(n_blocks):
    span = 2 * n_blocks
    moves = []
    for step in range(span):
        pairs = []
        for place in range(QUAD * n_blocks):
            for core in range(2):
                target = (place + step) % span
                src = place * 2 + core
                dst = (target // 2 * QUAD + 2 * core + target % 2) * 2 + place // span
                pairs.append((src, dst))
        moves.append(pairs)
    return moves


def return_experts(parts, n_blocks):
    return [
        lax.ppermute(part, ("g", "r", "c"), [(dst, src) for src, dst in pairs])
        for part, pairs in zip(parts, shard_moves(n_blocks))
    ]


def body(
    patches,
    lengths,
    slot_mask,
    expert_picks,
    priority_rank,
    class_labels,
    dense_weights,
    dense_first,
    dense_second,
    dense_average,
    router_weights,
    router_first,
    router_second,
    router_average,
    norm_params,
    norm_first,
    norm_second,
    norm_average,
    expert_in,
    in_first,
    in_second,
    in_average,
    expert_out,
    out_first,
    out_second,
    out_average,
    head_weights,
    head_first,
    head_second,
    head_average,
):
    n_blocks = lax.axis_size("g")
    sizes = {name: lax.axis_size(name) for name in ALL}
    rows_own, n_experts = router_weights.shape
    n_tail = max(8, n_experts)
    tail = jnp.zeros((n_tail, dense_weights.shape[2]), jnp.float32)
    tail = tail.at[:6, :rows_own].set(norm_params)
    tail = tail.at[:n_experts, 128 : 128 + rows_own].set(router_weights.T)
    rows_here, n_slots_row = slot_mask.shape
    tokens, model_width = patches.shape
    n_images = lengths.shape[0] * lengths.shape[1]
    capacity = (21 * tokens * TOP + 20 * n_experts - 1) // (20 * n_experts)
    padded = round_up(capacity, 16)
    layer_b, gain_rows, router_t, columns = gather_weights(
        sizes,
        (lengths.shape[1], n_experts, capacity, padded),
        dense_weights,
        tail,
        expert_picks,
        priority_rank,
        slot_mask,
        lengths,
    )
    shards = jnp.stack([expert_in, expert_out], 1).astype(jnp.bfloat16)
    (
        x_zero, a_one, qkv, att_out, x_one, a_two, router_probs, logs, pooled, part_importance,
        arrived, details, activated, slope, result, part_pooled, expert_weights
    ) = forward(
        sizes, n_experts, padded, lengths, slot_mask, patches, layer_b, gain_rows, router_t, columns, shards
    )
    g_head, d_pooled_all, d_pooled, g_norm_three, head_sums, total_importance = head_step(
        sizes,
        n_images,
        part_pooled,
        pooled,
        part_importance,
        gain_rows,
        head_weights,
        class_labels,
    )
    d_back, back_gate, *grads = expert_backward(
        sizes, arrived, details, d_pooled_all, result, slope, activated, expert_weights
    )
    parts = return_experts(grads, n_blocks)
    blocks = dense_backward(
        sizes,
        n_experts,
        padded,
        rows_own,
        lengths,
        slot_mask,
        patches,
        (x_zero, a_one, qkv, att_out, x_one, a_two, router_probs, logs),
        columns,
        layer_b,
        gain_rows,
        router_t,
        d_back,
        back_gate,
        d_pooled,
        total_importance,
        g_norm_three,
    )
    reduced, dense_sums = scatter_dense(sizes, blocks)
    g_one, g_two, totals = finish(
        sizes, n_experts, parts, head_sums, dense_sums, total_importance
    )
    n_dense = dense_weights.shape[0] * rows_own
    g_layers = reduced[:n_dense].reshape(-1, rows_own, model_width)
    g_norms = reduced[n_dense : n_dense + 6, :rows_own]
    g_router = reduced[n_dense : n_dense + n_experts, 128 : 128 + rows_own].T
    importance = total_importance[0, :n_experts]
    loss_value, grad_norm, factor = totals[0, 0], totals[1, 0], totals[2, 0]
    dense_out = adam_update(
        dense_weights, dense_first, dense_second, dense_average, g_layers, factor, base_rate
    )
    router_out = adam_update(
        router_weights, router_first, router_second, router_average, g_router, factor, base_rate
    )
    norm_out = adam_update(
        norm_params, norm_first, norm_second, norm_average, g_norms, factor, norm_rate
    )
    in_out = adam_update(expert_in, in_first, in_second, in_average, g_one, factor, base_rate)
    out_out = adam_update(expert_out, out_first, out_second, out_average, g_two, factor, base_rate)
    head_out = adam_update(
        head_weights, head_first, head_second, head_average, g_head, factor, base_rate
    )
    return (
        loss_value,
        importance,
        grad_norm,
        *dense_out,
        *router_out,
        *norm_out,
        *in_out,
        *out_out,
        *head_out,
    )


def solution(mesh):
    n_dp, n_expert = mesh.shape["dp"], mesh.shape["expert"]
    shaped = mesh.devices.reshape(n_dp // QUAD, QUAD, n_expert // 2, 2)
    fine = Mesh(shaped, ALL)
    rows = P(ALL, None)
    dense = P(None, ALL, None)
    norms = P(None, ALL)
    experts = P(("x", "c"), ("g", "r"), None)
    placed = (rows,) * 6 + (dense,) * 4 + (rows,) * 4 + (norms,) * 4 + (experts,) * 8 + (rows,) * 4
    results = (
        (P(),) * 3 + (dense,) * 4 + (rows,) * 4 + (norms,) * 4 + (experts,) * 8 + (rows,) * 4
    )
    return jax.shard_map(body, mesh=fine, in_specs=placed, out_specs=results, check_vma=False)
```

```python
import functools
import math

import jax
import jax.numpy as jnp
from jax import lax
from jax.experimental import pallas as pl
from jax.experimental.pallas import tpu as pltpu
from jax.sharding import Mesh
from jax.sharding import PartitionSpec as P

HEADS = 12
TOP = 2
STEP_COUNT = 10
QUAD = 4

high_prec = lax.Precision.HIGHEST
eps_norm = 1e-06
aux_weight = 0.01
clip_limit = 1.0
base_rate = 0.05
norm_rate = 0.5
beta_first = 0.9
beta_second = 0.999
weight_decay = 0.1
polyak_decay = 0.7
adam_eps = 1e-08
mask_fill = -1e30

ALL = ("g", "r", "x", "c")
MEMBERS = ("x", "r")


def adam_update(weight, first_state, second_state, average_state, gradient, factor, step_rate):
    clipped = gradient * factor
    first_new = beta_first * first_state + (1.0 - beta_first) * clipped
    second_new = beta_second * second_state + (1.0 - beta_second) * clipped * clipped
    first_hat = first_new / (1.0 - beta_first**STEP_COUNT)
    second_hat = second_new / (1.0 - beta_second**STEP_COUNT)
    weight_new = weight - step_rate * (
        first_hat / (jnp.sqrt(second_hat) + adam_eps) + weight_decay * weight
    )
    average_new = polyak_decay * average_state + (1.0 - polyak_decay) * weight_new
    return (weight_new, first_new, second_new, average_new)


MESH_ID = pl.DeviceIdType.MESH
VMEM = pltpu.VMEM
ANY = pl.ANY
MIB = 1 << 20


def cost(microseconds):
    return pl.CostEstimate(flops=int(microseconds * 1.15e9), bytes_accessed=0, transcendentals=0)


def whole(space=None):
    return pl.BlockSpec(memory_space=space or VMEM)


def round_up(value, step):
    return (value + step - 1) // step * step


class Place:
    def __init__(self, sizes):
        self.G, self.X = sizes["g"], sizes["x"]
        self.Z, self.Y = QUAD, sizes["g"]
        self.chips = self.Z * self.Y * self.X
        spot = lax.axis_index("g") * QUAD + lax.axis_index("r")
        self.z, self.y = lax.div(spot, self.Y), lax.rem(spot, self.Y)
        self.x, self.c = lax.axis_index("x"), lax.axis_index("c")
        self.g, self.r = lax.axis_index("g"), lax.axis_index("r")
        self.chip = spot * self.X + self.x
        self.member = self.x * QUAD + self.r

    def at(self, z=None, y=None, x=None, c=None):
        spot = (self.z if z is None else z) * self.Y + (self.y if y is None else y)
        return {
            "g": lax.div(spot, QUAD),
            "r": lax.rem(spot, QUAD),
            "x": self.x if x is None else x,
            "c": self.c if c is None else c,
        }

    def of_chip(self, chip):
        spot = lax.div(chip, self.X)
        return {
            "g": lax.div(spot, QUAD),
            "r": lax.rem(spot, QUAD),
            "x": lax.rem(chip, self.X),
            "c": self.c,
        }

    def of_member(self, member):
        return {
            "g": self.g,
            "r": lax.rem(member, QUAD),
            "x": lax.div(member, QUAD),
            "c": self.c,
        }

    def sibling(self):
        return self.at(c=1 - self.c)


def greet(peers):
    barrier = pltpu.get_barrier_semaphore()
    for peer in peers:
        pl.semaphore_signal(barrier, inc=1, device_id=peer, device_id_type=MESH_ID)
    pl.semaphore_wait(barrier, len(peers))


def send(src, dst, send_sem, recv_sem, peer):
    return pltpu.make_async_remote_copy(
        src_ref=src,
        dst_ref=dst,
        send_sem=send_sem,
        recv_sem=recv_sem,
        device_id=peer,
        device_id_type=MESH_ID,
    )


def others(me, count):
    return [lax.rem(me + step, count) for step in range(1, count)]


def grid_peers(at):
    peers = [at.at(z=z) for z in others(at.z, at.Z)]
    peers += [at.at(y=y) for y in others(at.y, at.Y)]
    peers += [at.at(x=x) for x in others(at.x, at.X)]
    return peers + [at.sibling()]


def gather_dense(at, rows, mats, count, land, sems, started, beside, idle):
    Z, Y, X = at.Z, at.Y, at.X
    depth = land.shape[4]
    cut = depth // 2 // 16 * 16
    first, second = pl.ds(0, cut), pl.ds(cut, depth - cut)
    z_out, z_in, ya_out, ya_in, xb_out, xb_in, xa_out, xa_in, yb_out, yb_in, c_out, c_in = sems
    mine = land.at[at.c, at.z, at.x, at.y]

    def begin(copy):
        copy.start()
        started.append(copy)

    order = [at.z] + [lax.rem(at.z + k, Z) for k in (1, 3, 2)]
    for z in order[1:]:
        begin(send(mine, mine, z_out.at[z], z_in.at[at.z], at.at(z=z)))

    def one(z):
        part = land.at[at.c, z, at.x, at.y]
        for y in others(at.y, Y):
            begin(send(part.at[first], part.at[first], ya_out.at[z, y], ya_in.at[z, at.y], at.at(y=y)))
        for x in others(at.x, X):
            begin(send(part.at[second], part.at[second], xb_out.at[z, x], xb_in.at[z, at.x], at.at(x=x)))

    def two(z):
        for y in others(at.y, Y):
            part = land.at[at.c, z, at.x, y, first]
            send(part, part, ya_out.at[z, y], ya_in.at[z, y], at.at(y=y)).wait_recv()
        line = land.at[at.c, z, at.x, :, first]
        for x in others(at.x, X):
            begin(send(line, line, xa_out.at[z, x], xa_in.at[z, at.x], at.at(x=x)))
        for x in others(at.x, X):
            part = land.at[at.c, z, x, at.y, second]
            send(part, part, xb_out.at[z, x], xb_in.at[z, x], at.at(x=x)).wait_recv()
        line = land.at[at.c, z, :, at.y, second]
        for y in others(at.y, Y):
            begin(send(line, line, yb_out.at[z, y], yb_in.at[z, at.y], at.at(y=y)))

    def three(z):
        for x in others(at.x, X):
            line = land.at[at.c, z, x, :, first]
            send(line, line, xa_out.at[z, x], xa_in.at[z, x], at.at(x=x)).wait_recv()
        for y in others(at.y, Y):
            line = land.at[at.c, z, :, y, second]
            send(line, line, yb_out.at[z, y], yb_in.at[z, y], at.at(y=y)).wait_recv()
        plane = land.at[at.c, z]
        begin(send(plane, plane, c_out.at[z], c_in.at[z], at.sibling()))

    for step in range(Z + 2):
        if step < Z:
            if step > 0:
                z = order[step]
                part = land.at[at.c, z, at.x, at.y]
                send(part, part, z_out.at[z], z_in.at[z], at.at(z=z)).wait_recv()
            one(order[step])
        if step == 0:
            beside()
        if step == Z - 1:
            idle()
        if 0 <= step - 1 < Z:
            two(order[step - 1])
        if 0 <= step - 2 < Z:
            three(order[step - 2])
    for z in order:
        plane = land.at[1 - at.c, z]
        send(plane, plane, c_out.at[z], c_in.at[z], at.sibling()).wait_recv()


def assemble_dense(at, rows, mats, count, land, w_ref, gain_ref, router_ref):
    chips = [(z, y, x) for z in range(at.Z) for y in range(at.Y) for x in range(at.X)]
    cores = [(c, z, x, y) for z, y, x in chips for c in range(2)]
    group = 16 // math.gcd(16, rows)
    for start in range(0, len(cores), group):
        for mat in range(mats):
            w_ref[mat, start * rows : (start + group) * rows] = jnp.concatenate(
                [land[spot][mat * rows : (mat + 1) * rows] for spot in cores[start : start + group]], 0
            )
    base = mats * rows
    tails = [land[spot][base : base + count].astype(jnp.float32) for spot in cores]
    gain_ref[...] = jnp.concatenate([tail[:8, :rows] for tail in tails], 1)
    router_ref[...] = jnp.concatenate([tail[:, 128 : 128 + rows] for tail in tails], 1)


def total_square(value):
    return jnp.sum(jnp.sum(value * value, 0, keepdims=True), 1, keepdims=True)


def scatter_kernel(sizes, g_ref, out_ref, square_ref, hold, sib, got_xa, got_yb, got_ya, got_xb, got_z, *sems):
    at = Place(sizes)
    Z, Y, X = at.Z, at.Y, at.X
    depth = g_ref.shape[4]
    cut = depth // 2 // 16 * 16
    first, second = pl.ds(0, cut), pl.ds(cut, depth - cut)
    c_out, c_in, xa_out, xa_in, yb_out, yb_in, ya_out, ya_in, xb_out, xb_in, z_out, z_in = sems
    greet(grid_peers(at))
    started = []

    def begin(copy):
        copy.start()
        started.append(copy)

    wide = lambda value: value.astype(jnp.float32)
    order = [lax.rem(at.z + k, Z) for k in (2, 1, 3)] + [at.z]
    for z in order:
        begin(send(g_ref.at[1 - at.c, z], sib.at[z], c_out.at[z], c_in.at[z], at.sibling()))

    def one(z):
        send(sib.at[z], sib.at[z], c_out.at[z], c_in.at[z], at.sibling()).wait_recv()
        hold[z] = (wide(g_ref[at.c, z]) + wide(sib[z])).astype(jnp.bfloat16)
        for x in others(at.x, X):
            begin(send(hold.at[z, x, :, first], got_xa.at[z, at.x], xa_out.at[z, x], xa_in.at[z, at.x], at.at(x=x)))
        for y in others(at.y, Y):
            begin(send(hold.at[z, :, y, second], got_yb.at[z, at.y], yb_out.at[z, y], yb_in.at[z, at.y], at.at(y=y)))

    def two(z):
        total = wide(hold[z, at.x, :, first])
        for x in others(at.x, X):
            send(got_xa.at[z, x], got_xa.at[z, x], xa_out.at[z, x], xa_in.at[z, x], at.at(x=x)).wait_recv()
            total = total + wide(got_xa[z, x])
        hold[z, at.x, :, first] = total.astype(jnp.bfloat16)
        for y in others(at.y, Y):
            begin(send(hold.at[z, at.x, y, first], got_ya.at[z, at.y], ya_out.at[z, y], ya_in.at[z, at.y], at.at(y=y)))
        total = wide(hold[z, :, at.y, second])
        for y in others(at.y, Y):
            send(got_yb.at[z, y], got_yb.at[z, y], yb_out.at[z, y], yb_in.at[z, y], at.at(y=y)).wait_recv()
            total = total + wide(got_yb[z, y])
        hold[z, :, at.y, second] = total.astype(jnp.bfloat16)
        for x in others(at.x, X):
            begin(send(hold.at[z, x, at.y, second], got_xb.at[z, at.x], xb_out.at[z, x], xb_in.at[z, at.x], at.at(x=x)))

    def three(z, last):
        total = wide(hold[z, at.x, at.y, first])
        for y in others(at.y, Y):
            send(got_ya.at[z, y], got_ya.at[z, y], ya_out.at[z, y], ya_in.at[z, y], at.at(y=y)).wait_recv()
            total = total + wide(got_ya[z, y])
        rest = wide(hold[z, at.x, at.y, second])
        for x in others(at.x, X):
            send(got_xb.at[z, x], got_xb.at[z, x], xb_out.at[z, x], xb_in.at[z, x], at.at(x=x)).wait_recv()
            rest = rest + wide(got_xb[z, x])
        if last:
            out_ref[first] = total
            out_ref[second] = rest
            return
        mine = hold.at[z, at.x, at.y]
        mine[first] = total.astype(jnp.bfloat16)
        mine[second] = rest.astype(jnp.bfloat16)
        begin(send(mine, got_z.at[at.z], z_out.at[z], z_in.at[at.z], at.at(z=z)))

    for step in range(Z + 2):
        if step < Z:
            one(order[step])
        if 0 <= step - 1 < Z:
            two(order[step - 1])
        if 0 <= step - 2 < Z:
            three(order[step - 2], step - 2 == Z - 1)
    for z in order[:-1]:
        send(got_z.at[z], got_z.at[z], z_out.at[z], z_in.at[z], at.at(z=z)).wait_recv()
        out_ref[...] += wide(got_z[z])
    square_ref[...] = jnp.broadcast_to(total_square(out_ref[...]), square_ref.shape)
    for copy in started:
        copy.wait_send()


def scatter_dense(sizes, blocks):
    unused, Z, X, Y, depth, width = blocks.shape
    dma = pltpu.SemaphoreType.DMA
    by_y, by_x, by_z = dma((Z, Y)), dma((Z, X)), dma((Z,))
    cut = depth // 2 // 16 * 16
    half = jnp.bfloat16
    return pl.pallas_call(
        functools.partial(scatter_kernel, sizes),
        out_shape=(
            jax.ShapeDtypeStruct((depth, width), jnp.float32),
            jax.ShapeDtypeStruct((8, 128), jnp.float32),
        ),
        in_specs=[whole()],
        out_specs=(whole(), whole()),
        scratch_shapes=[
            VMEM((Z, X, Y, depth, width), half),
            VMEM((Z, X, Y, depth, width), half),
            VMEM((Z, X, Y, cut, width), half),
            VMEM((Z, Y, X, depth - cut, width), half),
            VMEM((Z, Y, cut, width), half),
            VMEM((Z, X, depth - cut, width), half),
            VMEM((Z, depth, width), half),
        ]
        + [by_z, by_z, by_x, by_x, by_y, by_y, by_y, by_y, by_x, by_x, by_z, by_z],
        compiler_params=pltpu.CompilerParams(
            collective_id=2, has_side_effects=True, vmem_limit_bytes=28 * MIB
        ),
        cost_estimate=cost(45),
        name="scatter_dense",
    )(blocks)


def finish_kernel(sizes, n_experts, head_ref, dense_ref, imp_ref, *refs):
    at = Place(sizes)
    many = len(refs) - 7
    parts = refs[:many]
    first_ref, second_ref, out_ref, land, own, out_sem, in_sem = refs[many:]
    count = 2 * at.chips
    me = at.chip * 2 + at.c
    ids = others(me, count)

    def peer(device):
        spot = at.of_chip(lax.div(device, 2))
        spot["c"] = lax.rem(device, 2)
        return spot

    greet([peer(device) for device in ids])
    place = lax.rem(at.g * QUAD + at.r, 2)
    square = dense_ref[0:1, 0:1] + head_ref[1:2, 0:1]
    for parity in range(2):
        expert = place if parity == 0 else 1 - place
        for index, ref in enumerate((first_ref, second_ref)):
            total = None
            for step in range(parity * many // 2, (parity + 1) * many // 2):
                found = parts[step][index].astype(jnp.float32)
                total = found if total is None else total + found
            ref[expert] = total
            square = square + total_square(total)
    line = lax.broadcasted_iota(jnp.int32, own.shape, 0)
    own[...] = jnp.where(line == 0, head_ref[0:1, 0:1], jnp.where(line == 1, square, 0.0))
    land[me] = own[...]
    copies = [send(own, land.at[me], out_sem.at[d], in_sem.at[me], peer(d)) for d in ids]
    for copy in copies:
        copy.start()
    importance = imp_ref[0:1, 0:128]
    head = lax.broadcasted_iota(jnp.int32, (1, 128), 1) < n_experts
    centre = jnp.sum(jnp.where(head, importance, 0.0), 1, keepdims=True) / n_experts
    away = jnp.where(head, importance - centre, 0.0)
    spread = jnp.sum(away * away, 1, keepdims=True) / n_experts
    balance = aux_weight * spread / (centre * centre)
    for d in ids:
        send(land.at[d], land.at[d], out_sem.at[d], in_sem.at[d], peer(d)).wait_recv()
    sums = jnp.sum(land[...], 0)
    norm = jnp.sqrt(sums[1:2, 0:1])
    factor = jnp.minimum(1.0, clip_limit / norm)
    loss = sums[0:1, 0:1] + balance
    out_ref[...] = jnp.where(line == 0, loss, jnp.where(line == 1, norm, factor))
    for copy in copies:
        copy.wait_send()


def finish(sizes, n_experts, parts, head_sums, dense_sums, importance):
    devices = sizes["g"] * QUAD * sizes["x"] * 2
    unused, rows, width = parts[0].shape
    dma = pltpu.SemaphoreType.DMA
    grads = jax.ShapeDtypeStruct((2, rows, width), jnp.float32)
    return pl.pallas_call(
        functools.partial(finish_kernel, sizes, n_experts),
        out_shape=(grads, grads, jax.ShapeDtypeStruct((8, 128), jnp.float32)),
        in_specs=[whole()] * (3 + len(parts)),
        out_specs=(whole(),) * 3,
        scratch_shapes=[
            VMEM((devices, 8, 128), jnp.float32),
            VMEM((8, 128), jnp.float32),
            dma((devices,)),
            dma((devices,)),
        ],
        compiler_params=pltpu.CompilerParams(
            collective_id=3, has_side_effects=True, vmem_limit_bytes=20 * MIB
        ),
        cost_estimate=cost(10),
        name="finish",
    )(head_sums, dense_sums, importance, *parts)


IMAGE_PAD = 16


def split_three(value):
    high = value.astype(jnp.bfloat16)
    rest = value - high.astype(jnp.float32)
    middle = rest.astype(jnp.bfloat16)
    return high, middle, (rest - middle.astype(jnp.float32)).astype(jnp.bfloat16)


def dot_f32(left, right, dims):
    return lax.dot_general(left, right, (dims, ((), ())), preferred_element_type=jnp.float32)


NN = ((1,), (0,))
NT = ((1,), (1,))
TN = ((0,), (0,))


def norm_parts(values):
    centre = values - jnp.mean(values, -1, keepdims=True)
    spread = jnp.mean(centre * centre, -1, keepdims=True)
    scale = lax.rsqrt(spread + eps_norm)
    return centre * scale, scale


def norm_back(d_out, scaled, scale, gain):
    pulled = d_out * gain
    return scale * (
        pulled
        - jnp.mean(pulled, -1, keepdims=True)
        - scaled * jnp.mean(pulled * scaled, -1, keepdims=True)
    )


def head_kernel(
    sizes, images, part_ref, own_ref, imp_ref, gain_ref, head_ref, label_ref,
    g_head_ref, d_pool_ref, own_d_ref, g_norm_ref, sums_ref, total_imp_ref,
    in_part, rows, d_rows, d_sib, d_sum, d_in, head_b, labels, d_logits, *sems
):
    at = Place(sizes)
    chips, members = at.chips, QUAD * at.X
    devices = 2 * chips
    p_out, p_in, r_out, r_in, s_out, s_in, d_out, d_in_sem, b_out, b_in = sems
    width = own_ref.shape[1]
    same_core = others(at.chip, chips)
    greet([at.of_chip(chip) for chip in same_core] + [at.sibling()])
    started = []

    def begin(copy):
        copy.start()
        started.append(copy)

    team = others(at.member, members)
    for member in team:
        begin(send(part_ref.at[member], in_part.at[at.member], p_out.at[member], p_in.at[at.member], at.of_member(member)))
    in_part[at.member] = part_ref[at.member]
    head_b[...] = head_ref[...].astype(jnp.bfloat16)
    wide = devices * IMAGE_PAD
    spot = lax.broadcasted_iota(jnp.int32, (label_ref.shape[1], wide), 1)
    given = lax.broadcasted_iota(jnp.int32, (label_ref.shape[1], wide), 0)
    image = lax.rem(spot, IMAGE_PAD)
    device = lax.rem(lax.div(spot, IMAGE_PAD), chips) * 2 + lax.div(spot, IMAGE_PAD * chips)
    chosen = ((device * images + image == given) & (image < images)).astype(jnp.bfloat16)
    labels[...] = dot_f32(label_ref[...].astype(jnp.float32).astype(jnp.bfloat16), chosen, NN).astype(jnp.bfloat16)
    for member in team:
        send(in_part.at[member], in_part.at[member], p_out.at[member], p_in.at[member], at.of_member(member)).wait_recv()
    pooled = own_ref[...] + jnp.sum(in_part[...], 0)
    scaled, scale = norm_parts(pooled)
    gain, shift = gain_ref[2:3], gain_ref[5:6]
    a_three = scaled * gain + shift
    row = lax.broadcasted_iota(jnp.int32, (IMAGE_PAD, width), 0)
    block = jnp.where(row < images, a_three, 0.0)
    pieces = split_three(imp_ref[0:1])
    for index, piece in enumerate(pieces):
        block = jnp.where(row == images + index, piece.astype(jnp.float32), block)
    rows[at.c, at.chip] = block.astype(jnp.bfloat16)
    mine = rows.at[at.c, at.chip]
    for chip in same_core:
        begin(send(mine, mine, r_out.at[chip], r_in.at[at.chip], at.of_chip(chip)))
    for chip in same_core:
        part = rows.at[at.c, chip]
        send(part, part, r_out.at[chip], r_in.at[chip], at.of_chip(chip)).wait_recv()
    begin(send(rows.at[at.c], rows.at[at.c], s_out.at[0], s_in.at[0], at.sibling()))
    send(rows.at[1 - at.c], rows.at[1 - at.c], s_out.at[0], s_in.at[0], at.sibling()).wait_recv()
    gathered = rows[...].reshape(wide, width)
    in_block = lax.rem(lax.broadcasted_iota(jnp.int32, (wide, width), 0), IMAGE_PAD)
    total = jnp.sum(jnp.where(in_block >= images, gathered.astype(jnp.float32), 0.0), 0, keepdims=True)
    total_imp_ref[...] = jnp.broadcast_to(total, total_imp_ref.shape)
    gathered = jnp.where(in_block < images, gathered.astype(jnp.float32), 0.0).astype(jnp.bfloat16)
    logits = dot_f32(head_b[...], gathered, NT)
    image = lax.rem(lax.broadcasted_iota(jnp.int32, logits.shape, 1), IMAGE_PAD)
    count = devices * images
    target = labels[...].astype(jnp.float32)
    power = jnp.exp(-jnp.abs(logits))
    loss = jnp.maximum(logits, 0.0) + jnp.log1p(power) - target * logits
    loss = jnp.sum(jnp.where(image < images, loss, 0.0), 1, keepdims=True)
    loss = jnp.sum(loss, 0, keepdims=True) / count
    chance = jnp.where(logits >= 0.0, 1.0, power) / (1.0 + power)
    d_logits[...] = jnp.where(image < images, (chance - target) / count, 0.0).astype(jnp.bfloat16)
    partial = dot_f32(d_logits[...], head_b[...], TN)
    d_rows[...] = partial.reshape(d_rows.shape).astype(jnp.bfloat16)
    begin(send(d_rows.at[1 - at.c], d_sib, s_out.at[1], s_in.at[1], at.sibling()))
    g_head = dot_f32(d_logits[...], gathered, NN)
    g_head_ref[...] = g_head
    line = lax.broadcasted_iota(jnp.int32, sums_ref.shape, 0)
    sums_ref[...] = jnp.where(line == 0, loss, jnp.where(line == 1, total_square(g_head), 0.0))
    send(d_sib, d_sib, s_out.at[1], s_in.at[1], at.sibling()).wait_recv()
    d_sum[...] = (d_rows[at.c].astype(jnp.float32) + d_sib[...].astype(jnp.float32)).astype(jnp.bfloat16)
    for chip in same_core:
        begin(send(d_sum.at[chip], d_in.at[at.chip], d_out.at[chip], d_in_sem.at[at.chip], at.of_chip(chip)))
    d_in[at.chip] = d_sum[at.chip]
    for chip in same_core:
        send(d_in.at[chip], d_in.at[chip], d_out.at[chip], d_in_sem.at[chip], at.of_chip(chip)).wait_recv()
    d_norm = jnp.sum(d_in[...].astype(jnp.float32), 0)
    d_norm = jnp.where(row < images, d_norm, 0.0)
    d_pooled = norm_back(d_norm, scaled, scale, gain)
    d_pooled = jnp.where(row < images, d_pooled, 0.0)
    d_gain = jnp.sum(d_norm * scaled, 0, keepdims=True)
    d_shift = jnp.sum(d_norm, 0, keepdims=True)
    line = lax.broadcasted_iota(jnp.int32, g_norm_ref.shape, 0)
    g_norm_ref[...] = jnp.where(line == 2, d_gain, jnp.where(line == 5, d_shift, 0.0))
    own_d_ref[...] = d_pooled
    d_pool_ref[at.member] = d_pooled
    mine = d_pool_ref.at[at.member]
    for member in team:
        begin(send(own_d_ref, mine, b_out.at[member], b_in.at[at.member], at.of_member(member)))
    for member in team:
        part = d_pool_ref.at[member]
        send(part, part, b_out.at[member], b_in.at[member], at.of_member(member)).wait_recv()
    for copy in started:
        copy.wait_send()


def head_step(sizes, images, part, own, imp, gains, head, label):
    members = QUAD * sizes["x"]
    chips = members * sizes["g"]
    classes, width = head.shape
    wide = 2 * chips * IMAGE_PAD
    dma = pltpu.SemaphoreType.DMA
    by_member, by_chip = dma((members,)), dma((chips,))
    f32, half = jnp.float32, jnp.bfloat16
    blocks = (chips, IMAGE_PAD, width)
    return pl.pallas_call(
        functools.partial(head_kernel, sizes, images),
        out_shape=(
            jax.ShapeDtypeStruct((classes, width), f32),
            jax.ShapeDtypeStruct((members, IMAGE_PAD, width), f32),
            jax.ShapeDtypeStruct((IMAGE_PAD, width), f32),
            jax.ShapeDtypeStruct((8, width), f32),
            jax.ShapeDtypeStruct((8, 128), f32),
            jax.ShapeDtypeStruct((8, width), f32),
        ),
        in_specs=[whole()] * 6,
        out_specs=(whole(),) * 6,
        scratch_shapes=[
            VMEM((members, IMAGE_PAD, width), f32),
            VMEM((2, *blocks), half),
            VMEM((2, *blocks), half),
            VMEM(blocks, half),
            VMEM(blocks, half),
            VMEM(blocks, half),
            VMEM((classes, width), half),
            VMEM((classes, wide), half),
            VMEM((classes, wide), half),
        ]
        + [by_member, by_member, by_chip, by_chip, dma((2,)), dma((2,)), by_chip, by_chip]
        + [by_member, by_member],
        compiler_params=pltpu.CompilerParams(
            collective_id=4, has_side_effects=True, vmem_limit_bytes=56 * MIB
        ),
        cost_estimate=cost(42),
        name="head_step",
    )(part, own, imp, gains, head, label)


def route_math(per_image, n_experts, capacity, padded, pick_ref, rank_ref, mask_ref, length_ref):
    rows_here, span = mask_ref.shape
    tokens = rows_here * span
    valid = mask_ref[...].astype(jnp.float32)
    lengths = length_ref[...]
    position = lax.broadcasted_iota(jnp.int32, (rows_here, span), 1)
    segment = jnp.zeros((rows_here, span), jnp.int32)
    bound = jnp.zeros((rows_here, 1), jnp.int32)
    for image in range(per_image):
        bound = bound + lengths[:, image : image + 1]
        segment = segment + jnp.where(position >= bound, 1, 0)
    pool = jnp.zeros_like(valid)
    for image in range(per_image):
        member = jnp.where(segment == image, valid, 0.0)
        pool = pool + member / jnp.maximum(jnp.sum(member, 1, keepdims=True), 1.0)
    line = lax.broadcasted_iota(jnp.int32, (rows_here, span), 0)
    image = (segment + per_image * line).astype(jnp.float32)

    def flat(value):
        return jnp.concatenate([value[i : i + 1] for i in range(rows_here)], 1)

    rank_row = rank_ref[...].astype(jnp.float32)
    picks = pick_ref[...].astype(jnp.float32)
    table = jnp.concatenate([flat(valid), flat(pool), flat(image), rank_row, picks], 0)
    table = jnp.concatenate([table, jnp.zeros((122, tokens), jnp.float32)], 0).T
    valid_col, pool_col, image_col, rank_col, pick_one, pick_two = (
        table[:, i : i + 1] for i in range(6)
    )
    lane = lax.broadcasted_iota(jnp.int32, (tokens, 128), 1)
    in_first, in_second = lane < n_experts, (lane >= n_experts) & (lane < 2 * n_experts)
    number = lane.astype(jnp.float32)
    hot = jnp.where(in_first & (pick_one == number), valid_col, 0.0)
    hot = hot + jnp.where(in_second & (pick_two == number - n_experts), valid_col, 0.0)
    shifted = jnp.where(in_second & (pick_one == number - n_experts), valid_col, 0.0)
    before = jnp.where(rank_row < rank_col, 1.0, 0.0).astype(jnp.bfloat16)
    ahead = dot_f32(before, hot.astype(jnp.bfloat16), NN) + jnp.sum(shifted, 0, keepdims=True)
    counted = hot * ahead
    pos_one = jnp.sum(jnp.where(in_first, counted, 0.0), 1, keepdims=True)
    pos_two = jnp.sum(jnp.where(in_second, counted, 0.0), 1, keepdims=True)

    def place(pick, pos):
        kept = (valid_col > 0.0) & (pos < capacity)
        return jnp.where(kept, pick * padded + pos, -1.0)

    columns = (
        place(pick_one, pos_one),
        place(pick_two, pos_two),
        valid_col,
        pool_col,
        image_col,
        pick_one,
        pick_two,
    )
    result = jnp.zeros((tokens, 128), jnp.float32)
    for index, column in enumerate(columns):
        result = jnp.where(lane == index, column, result)
    return result


def allowed_slots(lengths, row, images, valid_row, span):
    query = lax.broadcasted_iota(jnp.int32, (span, span), 0)
    key = lax.broadcasted_iota(jnp.int32, (span, span), 1)
    bound = 0
    query_seg, key_seg = jnp.zeros((span, span), jnp.int32), jnp.zeros((span, span), jnp.int32)
    for image in range(images):
        bound = bound + lengths[row, image]
        query_seg = query_seg + jnp.where(query >= bound, 1, 0)
        key_seg = key_seg + jnp.where(key >= bound, 1, 0)
    return (query_seg == key_seg) & ((valid_row > 0) | (query == key))


TILE = 32


def tiles(count):
    return [slice(start, min(start + TILE, count)) for start in range(0, count, TILE)]


def step_order(blocks):
    return [*range(0, 2 * blocks, 2), *range(1, 2 * blocks, 2)]


class Team:
    def __init__(self, at):
        self.at, self.span = at, 2 * at.G
        self.spot = at.g * QUAD + at.r

    def target(self, step):
        at = self.at
        chosen = lax.rem(self.spot + step_order(at.G)[step], self.span)
        block, index = lax.div(chosen, 2), lax.rem(chosen, 2)
        core = lax.div(self.spot, self.span)
        r = 2 * at.c + index
        own = (block == at.g) & (r == at.r) & (core == at.c)
        return {"g": block, "r": r, "x": at.x, "c": core}, index, own

    def peers(self):
        at = self.at
        count = 2 * at.G * QUAD
        me = self.spot * 2 + at.c
        line = []
        for device in others(me, count):
            spot = lax.div(device, 2)
            line.append(
                {"g": lax.div(spot, QUAD), "r": lax.rem(spot, QUAD), "x": at.x, "c": lax.rem(device, 2)}
            )
        for x in others(at.x, at.X):
            line += [{"g": at.g, "r": r, "x": x, "c": at.c} for r in range(QUAD)]
        return line


def image_hot(detail, padded):
    image = detail[2:3, :padded]
    line = lax.broadcasted_iota(jnp.int32, (IMAGE_PAD, padded), 0).astype(jnp.float32)
    return line == image


def forward_kernel(
    sizes, n_experts, images, padded,
    length_ref, lengths_ref, mask_ref, pick_ref, rank_ref, patch_ref, dense_ref, norm_ref, routing_ref, in_ref, out_ref,
    w_keep, gain_ref, router_ref, col_ref, x_zero_out, a_one_out, qkv_out, att_out, x_one_out, a_two_out, prob_ref, lse_ref, pool_ref, imp_ref,
    rows_out, detail_out, act_out, slope_out, y_out, part_ref, weight_out,
    land, w_ref, shard_ref, x_zero_buf, a_one_buf, qkv_buf, att_buf, x_one_buf, a_two_ref, weights, send_rows, send_detail, places,
    rows_in, detail_in, total, act_buf, slope_buf, dense_sem, keep_sem, own_sem,
    w_out, w_in, s_out, s_in, r_out, r_in, m_out, m_in, act_sem, slope_sem, cast_sem, *gather_sems
):
    at = Place(sizes)
    team = Team(at)
    half = weights.shape[1]
    early = half // 2
    rows_here, span = mask_ref.shape
    width = patch_ref.shape[1]
    tokens = rows_here * span
    mats, rows_own, unused = dense_ref.shape
    tall = router_ref.shape[0]
    capacity = (21 * tokens * TOP + 20 * n_experts - 1) // (20 * n_experts)

    part_rows = shard_ref.shape[2]
    casts = [
        pltpu.make_async_copy(ref.at[expert], total.at[pl.ds((index * 2 + expert) * part_rows, part_rows)], cast_sem.at[index, expert])
        for index, ref in enumerate((in_ref, out_ref))
        for expert in range(2)
    ]
    for copy in casts:
        copy.start()
    depth = land.shape[4]
    routing = routing_ref[...]
    routing = jnp.concatenate([routing, jnp.zeros((rows_own, 128 - n_experts), jnp.float32)], 1)
    routing = jnp.concatenate([routing, jnp.zeros((128 - rows_own, 128), jnp.float32)], 0).T
    norms = norm_ref[...]
    norms = jnp.concatenate([norms, jnp.zeros((norms.shape[0], 128 - rows_own), jnp.float32)], 1)
    norms = jnp.concatenate([norms, jnp.zeros((tall - norms.shape[0], 128), jnp.float32)], 0)
    tail = jnp.concatenate(
        [norms, routing[:tall], jnp.zeros((tall, width - 256), jnp.float32)], 1
    )
    block = jnp.concatenate([dense_ref[...].reshape(mats * rows_own, width), tail], 0)
    if block.shape[0] < depth:
        block = jnp.concatenate(
            [block, jnp.zeros((depth - block.shape[0], width), jnp.float32)], 0
        )
    land[at.c, at.z, at.x, at.y] = block.astype(jnp.bfloat16)
    greet(team.peers() + grid_peers(at))

    def spot_of(step, side=0):
        return step // early, side * early + step % early

    def swap_copy(step):
        return send(
            weights.at[spot_of(step)], weights.at[spot_of(step, 1)], s_out.at[step], s_in.at[step], at.sibling()
        )

    def shard_copy(step):
        device, index, own = team.target(step)
        return send(
            shard_ref.at[index], weights.at[spot_of(step)], w_out.at[step], w_in.at[step], device
        )

    def shard_own(step):
        device, index, own = team.target(step)
        return pltpu.make_async_copy(shard_ref.at[index], weights.at[spot_of(step)], w_in.at[step])

    def shard_starts(steps):
        for step in steps:
            own = team.target(step)[2]

            @pl.when(own)
            def _():
                shard_own(step).start()

            @pl.when(jnp.logical_not(own))
            def _():
                shard_copy(step).start()

    def shard_waits(steps):
        for step in steps:
            own = team.target(step)[2]

            @pl.when(own)
            def _():
                shard_own(step).wait()

            @pl.when(jnp.logical_not(own))
            def _():
                shard_copy(step).wait_recv()

            swap_copy(step).start()

    def beside_gather():
        col_ref[...] = route_math(
            images, n_experts, capacity, padded, pick_ref, rank_ref, mask_ref, lengths_ref
        )
        for copy in casts:
            copy.wait()
        for index in range(2):
            for expert in range(2):
                here = pl.ds((index * 2 + expert) * part_rows, part_rows)
                shard_ref[expert, index] = total[here].astype(jnp.bfloat16)

    gathers = []
    gather_dense(
        at, rows_own, mats, tall, land, gather_sems, gathers, beside_gather, lambda: shard_starts(range(early))
    )
    shard_starts(range(early, half))
    assemble_dense(at, rows_own, mats, tall, land, w_ref, gain_ref, router_ref)
    w_copy = pltpu.make_async_copy(w_ref, w_keep, keep_sem.at[5])
    w_copy.start()

    dense = (
        (x_zero_buf, x_zero_out), (a_one_buf, a_one_out), (qkv_buf, qkv_out), (att_buf, att_out), (x_one_buf, x_one_out),
    )

    def dense_copy(row, index):
        here = pl.ds(pl.multiple_of(row * span, 16), span)
        buf, out = dense[index]
        return pltpu.make_async_copy(buf, out.at[here], dense_sem.at[index])

    def keep_dense(row, index, value):
        @pl.when(row > 0)
        def _():
            dense_copy(row - 1, index).wait()

        dense[index][0][...] = value
        dense_copy(row, index).start()

    pool_ref[...] = jnp.zeros_like(pool_ref)
    imp_ref[...] = jnp.zeros_like(imp_ref)
    routers = router_ref[...].astype(jnp.bfloat16)
    if routers.shape[0] < 128:
        routers = jnp.concatenate(
            [routers, jnp.zeros((128 - routers.shape[0], width), jnp.bfloat16)], 0
        )
    lane = lax.broadcasted_iota(jnp.int32, (span, 128), 1)

    def dense_row(row, carry):
        here = pl.ds(pl.multiple_of(row * span, 16), span)
        x_zero = dot_f32(patch_ref[here], w_ref[0], NN)
        keep_dense(row, 0, x_zero)
        a_one = (norm_parts(x_zero)[0] * gain_ref[0:1] + gain_ref[3:4]).astype(jnp.bfloat16)
        keep_dense(row, 1, a_one)

        @pl.when(row > 0)
        def _():
            dense_copy(row - 1, 2).wait()

        for part in range(3):
            qkv_buf[:, part * width : (part + 1) * width] = dot_f32(
                a_one, w_ref[1 + part], NN
            ).astype(jnp.bfloat16)
        dense_copy(row, 2).start()
        open_to = allowed_slots(length_ref, row, images, mask_ref[pl.ds(row, 1)], span)
        logs = jnp.zeros((span, 128), jnp.float32)

        @pl.when(row > 0)
        def _():
            dense_copy(row - 1, 3).wait()

        for pair in range(width // 128):
            query, key, value = (
                qkv_buf[:, part * width + pair * 128 : part * width + (pair + 1) * 128]
                for part in range(3)
            )
            outs = []
            for side in range(2):
                held = jnp.where((lane < 64) == (side == 0), query, jnp.zeros_like(query))
                scores = jnp.where(open_to, dot_f32(held, key, NT) * 64**-0.5, mask_fill)
                top = jnp.max(scores, 1, keepdims=True)
                powers = jnp.exp(scores - top)
                whole_sum = jnp.sum(powers, 1, keepdims=True)
                probs = (powers * (1.0 / whole_sum)).astype(jnp.bfloat16)
                outs.append(dot_f32(probs, value, NN))
                logs = jnp.where(lane == 2 * pair + side, top + jnp.log(whole_sum), logs)
            att_buf[:, pair * 128 : (pair + 1) * 128] = jnp.where(
                lane < 64, outs[0], outs[1]
            ).astype(jnp.bfloat16)
        lse_ref[here] = logs
        dense_copy(row, 3).start()
        x_one = x_zero + dot_f32(att_buf[...], w_ref[4], NN)
        keep_dense(row, 4, x_one)
        a_two = (norm_parts(x_one)[0] * gain_ref[1:2] + gain_ref[4:5]).astype(jnp.bfloat16)
        a_two_ref[here] = a_two
        logits = jnp.where(lane < n_experts, dot_f32(a_two, routers, NT), mask_fill)
        powers = jnp.exp(logits - jnp.max(logits, 1, keepdims=True))
        probs = powers / jnp.sum(powers, 1, keepdims=True)
        prob_ref[here] = probs
        columns = col_ref[here]
        valid, pool, image = columns[:, 2:3], columns[:, 3:4], columns[:, 4:5]
        imp_ref[0:1, 0:128] += jnp.sum(probs * valid, 0, keepdims=True)
        line = lax.broadcasted_iota(jnp.int32, pool_ref.shape, 0)
        for index in range(images):
            number = row * images + index
            weight = jnp.where(image == number.astype(jnp.float32), pool, 0.0)
            pooled = jnp.sum(x_one * weight, 0, keepdims=True)
            pool_ref[...] = jnp.where(line == number, pooled, pool_ref[...])
        return carry

    lax.fori_loop(0, rows_here, dense_row, 0)

    columns = col_ref[...]
    places[...] = columns.T[:8]
    lane = lax.broadcasted_iota(jnp.int32, (tokens, 128), 1)
    kind, expert = lax.div(lane, n_experts), lax.rem(lane, n_experts).astype(jnp.float32)
    slot_lane = lax.broadcasted_iota(jnp.int32, (tokens, send_detail.shape[2]), 1).astype(jnp.float32)
    pool, image = columns[:, 3:4], columns[:, 4:5]
    details = None
    for choice in range(2):
        slot, pick = columns[:, choice : choice + 1], columns[:, 5 + choice : 6 + choice]
        hot = (expert == pick) & (slot >= 0.0)
        gate = jnp.sum(jnp.where(hot & (kind == 0), prob_ref[...], 0.0), 1, keepdims=True)
        values = jnp.zeros((tokens, 128), jnp.float32)
        pieces = [*split_three(gate), *split_three(pool), image]
        for index, piece in enumerate(pieces):
            values = jnp.where(kind == index, piece.astype(jnp.float32), values)
        values = jnp.where(hot, values, 0.0).astype(jnp.bfloat16)
        spot = jnp.where(slot >= 0.0, slot - pick * padded, -1.0)
        chosen = jnp.where(spot == slot_lane, 1.0, 0.0).astype(jnp.bfloat16)
        found = dot_f32(values, chosen, TN)
        details = found if details is None else details + found
    n = n_experts
    gates = details[0:n] + details[n : 2 * n] + details[2 * n : 3 * n]
    pools = details[3 * n : 4 * n] + details[4 * n : 5 * n] + details[5 * n : 6 * n]
    numbers = details[6 * n : 7 * n]
    for index in range(n):
        for spot, value in enumerate((gates, pools, numbers)):
            send_detail[index, spot : spot + 1] = value[index : index + 1]
        send_detail[index, 3:8] = jnp.zeros((5, send_detail.shape[2]), jnp.float32)

    def rows_of(member):
        slots = lax.broadcasted_iota(jnp.int32, (padded, tokens), 0) + member * padded
        slots = slots.astype(jnp.float32)
        match = (slots == places[0:1]) | (slots == places[1:2])
        match = jnp.where(match, 1.0, 0.0).astype(jnp.bfloat16)
        return dot_f32(match, a_two_ref[...], NN).astype(jnp.bfloat16)

    def row_copy(member, source):
        return send(
            send_rows.at[member], rows_in.at[source], r_out.at[member], r_in.at[source], at.of_member(member)
        )

    def detail_copy(member, source):
        return send(
            send_detail.at[member], detail_in.at[source], m_out.at[member], m_in.at[source], at.of_member(member)
        )

    def dispatch_step(index, carry):
        member = lax.rem(at.member + index, n_experts)
        send_rows[member] = rows_of(member)
        row_copy(member, at.member).start()
        detail_copy(member, at.member).start()
        return carry

    lax.fori_loop(1, n_experts, dispatch_step, 0)
    rows_in[at.member] = rows_of(at.member)
    detail_in[at.member] = send_detail[at.member]
    a_two_copy = pltpu.make_async_copy(a_two_ref, a_two_out, keep_sem.at[0])
    a_two_copy.start()
    for index in range(len(dense)):
        dense_copy(rows_here - 1, index).wait()

    shard_waits(range(early))
    for step in range(early):
        swap_copy(step).wait_recv()

    many = act_buf.shape[1] // padded
    count = many * padded
    rounds = n_experts // many

    def hidden_copies(index, chunk):
        block, turn = block_of(index), lax.div(index, rounds)
        here = pl.ds(pl.multiple_of(block * count, 16), count)
        there = turn * half + chunk
        return (
            pltpu.make_async_copy(act_buf.at[chunk], act_out.at[there, here], act_sem.at[chunk]),
            pltpu.make_async_copy(slope_buf.at[chunk], slope_out.at[there, here], slope_sem.at[chunk]),
        )

    def block_of(index):
        return lax.rem(lax.div(at.member, many) + index, rounds)

    def expert_step(index, carry):
        turn = lax.div(index, rounds)
        block = block_of(index)

        @pl.when(turn == 0)
        def _():
            for spot in range(many):
                source = block * many + spot

                @pl.when(source != at.member)
                def _():
                    row_copy(source, source).wait_recv()
                    detail_copy(source, source).wait_recv()

        @pl.when(index == rounds)
        def _():
            shard_waits(range(early, half))

        rows = rows_in[pl.ds(block * many, many)].reshape(count, width)
        for chunk in range(half):
            if chunk == early:

                @pl.when(index == rounds)
                def _():
                    for step in range(early, half):
                        swap_copy(step).wait_recv()
                    keeps[2].start()

            hidden_all = dot_f32(rows, weights[turn, chunk, 0], NT)

            @pl.when(index > 0)
            def _():
                for copy in hidden_copies(index - 1, chunk):
                    copy.wait()

            for spot in tiles(count):
                hidden = hidden_all[spot]
                square = hidden * hidden
                curve = jnp.tanh(hidden * (0.7978845608 + 0.7978845608 * 0.044715 * square))
                upper = 0.5 + 0.5 * curve
                gelu = hidden * upper
                slope = upper + gelu * (1.0 - upper) * (
                    2.0 * 0.7978845608 + 6.0 * 0.7978845608 * 0.044715 * square
                )
                act_buf[chunk, spot] = gelu.astype(jnp.bfloat16)
                slope_buf[chunk, spot] = slope.astype(jnp.bfloat16)
            for copy in hidden_copies(index, chunk):
                copy.start()
        acts = jnp.concatenate([act_buf[chunk] for chunk in range(half)], 1)
        ends = jnp.concatenate([weights[turn, chunk, 1] for chunk in range(half)], 0)
        found = dot_f32(acts, ends, NN)
        here = pl.ds(pl.multiple_of(block * count, 16), count)

        @pl.when(turn == 0)
        def _():
            total[here] = found

        @pl.when(turn == 1)
        def _():
            result = (total[here] + found).astype(jnp.bfloat16)
            for spot in range(many):
                source = block * many + spot
                mine = result[spot * padded : (spot + 1) * padded]
                send_rows[source] = mine
                detail = detail_in[source]
                weight = detail[0:1, :padded] * detail[1:2, :padded]
                shares = jnp.where(image_hot(detail, padded), weight, 0.0)
                pieces = jnp.concatenate(split_three(shares), 0)
                sums = dot_f32(pieces, mine, NN)
                part_ref[source] = (
                    sums[:IMAGE_PAD] + sums[IMAGE_PAD : 2 * IMAGE_PAD] + sums[2 * IMAGE_PAD :]
                )

        @pl.when(index == rounds - 1)
        def _():
            for member in others(at.member, n_experts):
                row_copy(member, at.member).wait_send()
                detail_copy(member, at.member).wait_send()
            for copy in keeps[:2]:
                copy.start()

        return carry

    keeps = [
        pltpu.make_async_copy(rows_in, rows_out, keep_sem.at[1]),
        pltpu.make_async_copy(detail_in, detail_out, keep_sem.at[2]),
        pltpu.make_async_copy(weights, weight_out, keep_sem.at[4]),
        pltpu.make_async_copy(send_rows, y_out, keep_sem.at[3]),
    ]
    lax.fori_loop(0, 2 * rounds, expert_step, 0)
    keeps[3].start()
    for chunk in range(half):
        for copy in hidden_copies(2 * rounds - 1, chunk):
            copy.wait()
    for step in range(half):
        own = team.target(step)[2]
        swap_copy(step).wait_send()

        @pl.when(jnp.logical_not(own))
        def _():
            shard_copy(step).wait_send()

    a_two_copy.wait()
    w_copy.wait()
    for copy in keeps:
        copy.wait()
    for copy in gathers:
        copy.wait_send()


def forward(sizes, n_experts, padded, lengths, slot_mask, picks, ranks, patches, dense, norms, routers, expert_in, expert_out):
    rows_here, span = slot_mask.shape
    tokens, width = patches.shape
    part = expert_in.shape[1]
    mats, rows_own, unused = dense.shape
    tall = max(8, n_experts)
    depth = round_up(mats * rows_own + tall, 16)
    Z, Y, X = QUAD, sizes["g"], sizes["x"]
    half = 2 * sizes["g"]
    lanes = round_up(padded, 128)
    many = max(1, (144 if part % 128 else 576) // padded)
    count = n_experts * padded
    f32, kind = jnp.float32, jnp.bfloat16
    dma = pltpu.SemaphoreType.DMA
    each, parts, two = dma((n_experts,)), dma((half,)), dma((2,))
    by_y, by_x, by_z = dma((Z, Y)), dma((Z, X)), dma((Z,))

    def out(wide, dtype):
        return jax.ShapeDtypeStruct((tokens, wide), dtype)

    hidden = jax.ShapeDtypeStruct((2 * half, count, part), kind)
    rows = (n_experts, padded, width)
    return pl.pallas_call(
        functools.partial(forward_kernel, sizes, n_experts, lengths.shape[1], padded),
        out_shape=(
            jax.ShapeDtypeStruct((mats, width, width), kind), jax.ShapeDtypeStruct((8, width), f32),
            jax.ShapeDtypeStruct((tall, width), f32), out(128, f32),
            out(width, f32), out(width, kind), out(3 * width, kind), out(width, kind), out(width, f32),
            out(width, kind), out(128, f32), out(128, f32),
            jax.ShapeDtypeStruct((IMAGE_PAD, width), f32), jax.ShapeDtypeStruct((8, width), f32),
            jax.ShapeDtypeStruct(rows, kind), jax.ShapeDtypeStruct((n_experts, 8, lanes), f32),
            hidden, hidden, jax.ShapeDtypeStruct(rows, kind),
            jax.ShapeDtypeStruct((n_experts, IMAGE_PAD, width), f32),
            jax.ShapeDtypeStruct((2, half, 2, part, width), kind),
        ),
        in_specs=[whole(pltpu.SMEM)] + [whole()] * 8 + [whole(ANY)] * 2,
        out_specs=(whole(ANY), whole(), whole(), whole()) + (whole(ANY),) * 6 + (whole(),) * 4 + (whole(ANY),) * 5 + (whole(), whole(ANY)),
        scratch_shapes=[
            VMEM((2, Z, X, Y, depth, width), kind), VMEM((mats, width, width), kind), VMEM((2, 2, part, width), kind),
            VMEM((span, width), f32), VMEM((span, width), kind), VMEM((span, 3 * width), kind),
            VMEM((span, width), kind), VMEM((span, width), f32), VMEM((tokens, width), kind),
            VMEM((2, half, 2, part, width), kind), VMEM(rows, kind), VMEM((n_experts, 8, lanes), f32),
            VMEM((8, tokens), f32), VMEM(rows, kind), VMEM((n_experts, 8, lanes), f32),
            VMEM((count, width), f32), VMEM((half, many * padded, part), kind),
            VMEM((half, many * padded, part), kind), dma((5,)), dma((6,)), two,
            parts, parts, parts, parts, each, each, each, each, parts, parts, dma((2, 2)),
            by_z, by_z, by_y, by_y, by_x, by_x, by_x, by_x, by_y, by_y, by_z, by_z,
        ],
        compiler_params=pltpu.CompilerParams(
            collective_id=5, has_side_effects=True, vmem_limit_bytes=62 * MIB
        ),
        cost_estimate=cost(120),
        name="forward",
    )(lengths, lengths, slot_mask, picks.T, ranks, patches, dense, norms, routers, expert_in, expert_out)


def chunk_at(index, half):
    early = half // 2
    step = lax.rem(index, half)
    side = jnp.where(index < half, early, 0)
    return lax.div(step, early) * half + side + lax.rem(step, early)


def expert_backward_kernel(
    sizes, padded, rows_ref, detail_ref, pool_ref, y_ref, slope_ref, act_ref, weight_ref, *refs
):
    at = Place(sizes)
    sources, unused, width = rows_ref.shape
    chunks, unused, part = slope_ref.shape
    half = chunks // 2
    back_ref, gate_ref, *outs = refs[: 2 + half]
    d_hidden, d_rows, send_rows, send_gate, send_grad, got_grad = refs[2 + half : 8 + half]
    own_sem, r_out, r_in, m_out, m_in, g_out, g_in, g_keep = refs[8 + half :]
    many = y_ref.shape[0]
    rounds = sources // many
    step = pl.program_id(0)
    team = others(at.member, sources)

    def row_copy(member, source):
        return send(
            send_rows.at[member], back_ref.at[source], r_out.at[member], r_in.at[source], at.of_member(member)
        )

    def gate_copy(member, source):
        return send(
            send_gate.at[member], gate_ref.at[source], m_out.at[member], m_in.at[source], at.of_member(member)
        )

    def keep_copies():
        return (
            pltpu.make_async_copy(send_rows.at[at.member], back_ref.at[at.member], own_sem.at[0]),
            pltpu.make_async_copy(send_gate.at[at.member], gate_ref.at[at.member], own_sem.at[1]),
        )

    def grad_copy(index):
        return send(
            send_grad.at[index], got_grad.at[index], g_out.at[index], g_in.at[index], at.sibling()
        )

    def out_copy(index):
        return pltpu.make_async_copy(got_grad.at[index], outs[index], g_keep.at[index])

    @pl.when(step == 0)
    def _():
        greet([at.of_member(member) for member in team] + [at.sibling()])

    @pl.when(step < rounds)
    def _():
        block = lax.rem(lax.div(at.member, many) + 1 + step, rounds)
        d_out = []
        for index in range(many):
            source = block * many + index
            detail = detail_ref[source]
            hot = image_hot(detail, padded)
            hots = jnp.where(hot, 1.0, 0.0).astype(jnp.bfloat16)
            pools = jnp.concatenate(split_three(pool_ref[source]), 0)
            wide = dot_f32(jnp.concatenate([hots] * 3, 0), pools, TN)
            lanes = detail.shape[1]
            upright = jnp.concatenate([detail, jnp.zeros((120, lanes), jnp.float32)], 0).T
            gate, pool = upright[:padded, 0:1], upright[:padded, 1:2]
            d_out.append((gate * (pool * wide)).astype(jnp.bfloat16))
            along = dot_f32(pools, y_ref[index], NT)
            along = along[:IMAGE_PAD] + along[IMAGE_PAD : 2 * IMAGE_PAD] + along[2 * IMAGE_PAD :]
            d_gate = jnp.sum(jnp.where(hot, along, 0.0), 0, keepdims=True) * detail[1:2, :padded]
            send_gate[source] = jnp.zeros(detail.shape, jnp.float32)
            send_gate[source, 0:1, :padded] = d_gate
        d_out = jnp.concatenate(d_out, 0)
        count = many * padded
        span = pl.ds(pl.multiple_of(block * count, 16), count)
        d_rows[span] = d_out

        def weight(index, which):
            return weight_ref[index // half, index % half, which]

        for index in range(chunks):
            d_act = dot_f32(d_out, weight(index, 1), NT)
            for spot in tiles(count):
                rows_now = pl.ds(pl.multiple_of(block * count + spot.start, 16), spot.stop - spot.start)
                d_hidden[index, rows_now] = (
                    d_act[spot] * slope_ref[index, spot].astype(jnp.float32)
                ).astype(jnp.bfloat16)
        d_hids = jnp.concatenate([d_hidden[index, span] for index in range(chunks)], 1)
        starts = jnp.concatenate([weight(index, 0) for index in range(chunks)], 0)
        total = dot_f32(d_hids, starts, NN)
        total = total.astype(jnp.bfloat16)
        for index in range(many):
            source = block * many + index
            send_rows[source] = total[index * padded : (index + 1) * padded]

            @pl.when(source != at.member)
            def _():
                row_copy(source, at.member).start()
                gate_copy(source, at.member).start()

            @pl.when(source == at.member)
            def _():
                for copy in keep_copies():
                    copy.start()

    @pl.when(step >= rounds)
    def _():
        index = step - rounds
        chunk = chunk_at(index, half)
        rows = rows_ref[...].reshape(sources * padded, width)
        g_one = dot_f32(d_hidden[chunk], rows, TN)
        g_two = dot_f32(act_ref[0], d_rows[...], TN)

        @pl.when(index < half)
        def _():
            send_grad[index, 0] = g_one.astype(jnp.bfloat16)
            send_grad[index, 1] = g_two.astype(jnp.bfloat16)
            grad_copy(index).start()

        @pl.when(index >= half)
        def _():
            spot = index - half
            grad_copy(spot).wait_recv()
            got_grad[spot, 0] = (got_grad[spot, 0].astype(jnp.float32) + g_one).astype(jnp.bfloat16)
            got_grad[spot, 1] = (got_grad[spot, 1].astype(jnp.float32) + g_two).astype(jnp.bfloat16)

        for spot in range(half):

            @pl.when(index == spot + half)
            def _():
                out_copy(spot).start()

    @pl.when(step == rounds + chunks - 1)
    def _():
        for member in team:
            row_copy(member, member).wait_recv()
            gate_copy(member, member).wait_recv()
        for member in team:
            row_copy(member, at.member).wait_send()
            gate_copy(member, at.member).wait_send()
        for copy in keep_copies():
            copy.wait()
        for spot in range(half):
            grad_copy(spot).wait_send()
            out_copy(spot).wait()


def expert_backward(sizes, rows, details, pools, results, slopes, acts, weights):
    sources, padded, width = rows.shape
    chunks, count, part = acts.shape
    many = max(1, (288 if part % 128 else 576) // padded)
    rounds, half = sources // many, chunks // 2
    lanes = details.shape[2]
    kind = jnp.bfloat16
    dma = pltpu.SemaphoreType.DMA
    each, parts = dma((sources,)), dma((half,))

    def block_of(step):
        member = lax.axis_index("x") * QUAD + lax.axis_index("r")
        return lax.rem(lax.div(member, many) + 1 + jnp.minimum(step, rounds - 1), rounds)

    def chunk_of(step):
        return chunk_at(jnp.maximum(step - rounds, 0), half)

    return pl.pallas_call(
        functools.partial(expert_backward_kernel, sizes, padded),
        grid=(rounds + chunks,),
        out_shape=(
            jax.ShapeDtypeStruct((sources, padded, width), kind),
            jax.ShapeDtypeStruct((sources, 8, lanes), jnp.float32),
        )
        + (jax.ShapeDtypeStruct((2, part, width), kind),) * half,
        in_specs=[
            whole(), whole(), whole(),
            pl.BlockSpec((many, padded, width), lambda i: (block_of(i), 0, 0)),
            pl.BlockSpec((chunks, many * padded, part), lambda i: (0, block_of(i), 0)),
            pl.BlockSpec((1, count, part), lambda i: (chunk_of(i), 0, 0)),
        ]
        + [whole()],
        out_specs=(whole(ANY),) * (2 + half),
        scratch_shapes=[
            VMEM((chunks, count, part), kind),
            VMEM((count, width), kind),
            VMEM((sources, padded, width), kind),
            VMEM((sources, 8, lanes), jnp.float32),
            VMEM((half, 2, part, width), kind),
            VMEM((half, 2, part, width), kind),
            dma((2,)), each, each, each, each, parts, parts, parts,
        ],
        compiler_params=pltpu.CompilerParams(
            collective_id=6, has_side_effects=True, vmem_limit_bytes=62 * MIB
        ),
        cost_estimate=cost(65),
        name="expert_backward",
    )(rows, details, pools, results, slopes, acts, weights)


def dense_backward_kernel(
    sizes, n_experts, images, padded, length_ref, mask_ref, patch_ref, x_zero_ref, a_one_ref, qkv_ref, att_ref,
    x_one_ref, a_two_ref, prob_ref, lse_ref, col_ref, w_ref, gain_ref, router_ref, back_ref, gate_ref,
    pool_ref, imp_ref, third_ref, out_ref, grads, g_router, g_norm, d_qkv
):
    row = pl.program_id(0)
    span, width = patch_ref.shape
    mats, rows = grads.shape[0], width // (8 * sizes["g"] * sizes["x"])

    @pl.when(row == 0)
    def _():
        grads[...] = jnp.zeros_like(grads)
        g_router[...] = jnp.zeros_like(g_router)
        g_norm[...] = third_ref[...]

    columns = col_ref[...]
    slot_one, slot_two = columns[:, 0:1], columns[:, 1:2]
    count = n_experts * padded
    slot = lax.broadcasted_iota(jnp.int32, (span, count), 1).astype(jnp.float32)
    match = jnp.where((slot == slot_one) | (slot == slot_two), 1.0, 0.0).astype(jnp.bfloat16)
    d_a_two = dot_f32(match, back_ref[...].reshape(count, width), NN)
    lanes = gate_ref.shape[2]
    spot = lax.broadcasted_iota(jnp.int32, (span, lanes), 1)
    inside = spot < padded
    spot = spot.astype(jnp.float32)
    found_one, found_two = jnp.zeros((span, lanes), jnp.float32), jnp.zeros((span, lanes), jnp.float32)
    for expert in range(n_experts):
        line = jnp.broadcast_to(gate_ref[expert, 0:1], (span, lanes))
        found_one = jnp.where(inside & (spot == slot_one - expert * padded), line, found_one)
        found_two = jnp.where(inside & (spot == slot_two - expert * padded), line, found_two)
    d_gate_one = jnp.sum(found_one, 1, keepdims=True)
    d_gate_two = jnp.sum(found_two, 1, keepdims=True)
    lane = lax.broadcasted_iota(jnp.int32, (span, 128), 1)
    number = lane.astype(jnp.float32)
    valid, pool, image = columns[:, 2:3], columns[:, 3:4], columns[:, 4:5]
    head = lax.broadcasted_iota(jnp.int32, (1, 128), 1) < n_experts
    importance = imp_ref[0:1, 0:128]
    centre = jnp.sum(jnp.where(head, importance, 0.0), 1, keepdims=True) / n_experts
    away = jnp.where(head, importance - centre, 0.0)
    spread = jnp.sum(away * away, 1, keepdims=True) / n_experts
    d_imp = aux_weight * (
        2.0 * away / (n_experts * centre * centre)
        - 2.0 * spread / (n_experts * centre * centre * centre)
    )
    d_probs = valid * d_imp
    d_probs = d_probs + jnp.where(number == columns[:, 5:6], d_gate_one, 0.0)
    d_probs = d_probs + jnp.where(number == columns[:, 6:7], d_gate_two, 0.0)
    probs = prob_ref[...]
    d_router = (probs * (d_probs - jnp.sum(probs * d_probs, 1, keepdims=True))).astype(jnp.bfloat16)
    g_router[...] += dot_f32(d_router, a_two_ref[...], TN)
    routers = router_ref[...].astype(jnp.bfloat16)
    if routers.shape[0] < 128:
        routers = jnp.concatenate(
            [routers, jnp.zeros((128 - routers.shape[0], width), jnp.bfloat16)], 0
        )
    d_a_two = d_a_two + dot_f32(d_router, routers, NN)
    scaled, scale = norm_parts(x_one_ref[...])
    g_norm[1:2] += jnp.sum(d_a_two * scaled, 0, keepdims=True)
    g_norm[4:5] += jnp.sum(d_a_two, 0, keepdims=True)
    d_x_one = norm_back(d_a_two, scaled, scale, gain_ref[1:2])
    for index in range(images):
        place = row * images + index
        weight = jnp.where(image == place.astype(jnp.float32), pool, 0.0)
        d_x_one = d_x_one + weight * pool_ref[pl.ds(place, 1)]
    d_att = d_x_one.astype(jnp.bfloat16)
    grads[4] += dot_f32(att_ref[...], d_att, TN)
    d_out = dot_f32(d_att, w_ref[4], NT).astype(jnp.bfloat16)
    open_to = allowed_slots(length_ref, row, images, mask_ref[0], span)
    logs = lse_ref[...]
    for pair in range(width // 128):
        query, key, value = (
            qkv_ref[:, part * width + pair * 128 : part * width + (pair + 1) * 128]
            for part in range(3)
        )
        d_pair = d_out[:, pair * 128 : (pair + 1) * 128]
        found = []
        for side in range(2):
            left = (lane < 64) == (side == 0)
            held = jnp.where(left, query, jnp.zeros_like(query))
            scores = jnp.where(open_to, dot_f32(held, key, NT) * 64**-0.5, mask_fill)
            total = logs[:, 2 * pair + side : 2 * pair + side + 1]
            chance = jnp.exp(scores - total)
            d_held = jnp.where(left, d_pair, jnp.zeros_like(d_pair))
            d_chance = dot_f32(d_held, value, NT)
            d_value = dot_f32(chance.astype(jnp.bfloat16), d_pair, TN)
            d_scores = chance * (d_chance - jnp.sum(chance * d_chance, 1, keepdims=True))
            d_scores = d_scores.astype(jnp.bfloat16)
            d_query = dot_f32(d_scores, key, NN) * 64**-0.5
            d_key = dot_f32(d_scores, query, TN) * 64**-0.5
            found.append((d_query, d_key, d_value))
        for part in range(3):
            d_qkv[:, part * width + pair * 128 : part * width + (pair + 1) * 128] = jnp.where(
                lane < 64, found[0][part], found[1][part]
            ).astype(jnp.bfloat16)
    d_a_one = None
    for part in range(3):
        piece = d_qkv[:, part * width : (part + 1) * width]
        grads[1 + part] += dot_f32(a_one_ref[...], piece, TN)
        found = dot_f32(piece, w_ref[1 + part], NT)
        d_a_one = found if d_a_one is None else d_a_one + found
    scaled, scale = norm_parts(x_zero_ref[...])
    g_norm[0:1] += jnp.sum(d_a_one * scaled, 0, keepdims=True)
    g_norm[3:4] += jnp.sum(d_a_one, 0, keepdims=True)
    d_x_zero = norm_back(d_a_one, scaled, scale, gain_ref[0:1]) + d_x_one
    grads[0] += dot_f32(patch_ref[...], d_x_zero.astype(jnp.bfloat16), TN)

    @pl.when(row == pl.num_programs(0) - 1)
    def _():
        Z, Y, X = QUAD, sizes["g"], sizes["x"]
        tall = max(8, n_experts)
        norms = g_norm[...]
        if tall > 8:
            norms = jnp.concatenate([norms, jnp.zeros((tall - 8, width), jnp.float32)], 0)
        router_grads = g_router[:tall]
        depth = out_ref.shape[4]
        device = 0
        for z in range(Z):
            for y in range(Y):
                for x in range(X):
                    for c in range(2):
                        spot = slice(device * rows, (device + 1) * rows)
                        blank = jnp.zeros((tall, 128 - rows), jnp.float32)
                        tail = [norms[:, spot], blank, router_grads[:, spot], blank]
                        tail.append(jnp.zeros((tall, width - 256), jnp.float32))
                        pieces = [grads[mat, spot] for mat in range(mats)]
                        pieces.append(jnp.concatenate(tail, 1))
                        left = depth - mats * rows - tall
                        if left:
                            pieces.append(jnp.zeros((left, width), jnp.float32))
                        out_ref[c, z, x, y] = jnp.concatenate(pieces, 0).astype(jnp.bfloat16)
                        device += 1


def dense_backward(
    sizes, n_experts, padded, rows_own, lengths, slot_mask, patches, kept, columns, weights, gains, routers, back,
    gates, pooled, importance, third
):
    rows_here, span = slot_mask.shape
    tokens, width = patches.shape
    mats = weights.shape[0]
    depth = round_up(mats * rows_own + max(8, n_experts), 16)
    x_zero, a_one, qkv, att, x_one, a_two, probs, logs = kept

    def block(wide):
        return pl.BlockSpec((span, wide), lambda i: (i, 0))

    return pl.pallas_call(
        functools.partial(dense_backward_kernel, sizes, n_experts, lengths.shape[1], padded),
        grid=(rows_here,),
        out_shape=jax.ShapeDtypeStruct(
            (2, QUAD, sizes["x"], sizes["g"], depth, width), jnp.bfloat16
        ),
        in_specs=[
            whole(pltpu.SMEM), pl.BlockSpec((1, 1, span), lambda i: (i, 0, 0)), block(width),
            block(width), block(width), block(3 * width), block(width), block(width), block(width),
            block(128), block(128), block(128),
        ]
        + [whole()] * 8,
        out_specs=whole(),
        scratch_shapes=[
            VMEM((mats, width, width), jnp.float32),
            VMEM((128, width), jnp.float32),
            VMEM((8, width), jnp.float32),
            VMEM((span, 3 * width), jnp.bfloat16),
        ],
        compiler_params=pltpu.CompilerParams(vmem_limit_bytes=60 * MIB),
        cost_estimate=cost(50),
        name="dense_backward",
    )(
        lengths, slot_mask[:, None, :], patches, x_zero, a_one, qkv, att, x_one, a_two, probs, logs, columns,
        weights, gains, routers, back, gates, pooled, importance, third,
    )


def shard_moves(n_blocks):
    span = 2 * n_blocks
    moves = []
    for step in step_order(n_blocks):
        pairs = []
        for place in range(QUAD * n_blocks):
            for core in range(2):
                target = (place + step) % span
                src = place * 2 + core
                dst = (target // 2 * QUAD + 2 * core + target % 2) * 2 + place // span
                pairs.append((src, dst))
        moves.append(pairs)
    return moves


def return_experts(parts, n_blocks):
    return [
        lax.ppermute(part, ("g", "r", "c"), [(dst, src) for src, dst in pairs])
        for part, pairs in zip(parts, shard_moves(n_blocks))
    ]


def body(
    patches,
    lengths,
    slot_mask,
    expert_picks,
    priority_rank,
    class_labels,
    dense_weights,
    dense_first,
    dense_second,
    dense_average,
    router_weights,
    router_first,
    router_second,
    router_average,
    norm_params,
    norm_first,
    norm_second,
    norm_average,
    expert_in,
    in_first,
    in_second,
    in_average,
    expert_out,
    out_first,
    out_second,
    out_average,
    head_weights,
    head_first,
    head_second,
    head_average,
):
    n_blocks = lax.axis_size("g")
    sizes = {name: lax.axis_size(name) for name in ALL}
    rows_own, n_experts = router_weights.shape
    rows_here, n_slots_row = slot_mask.shape
    tokens, model_width = patches.shape
    n_images = lengths.shape[0] * lengths.shape[1]
    capacity = (21 * tokens * TOP + 20 * n_experts - 1) // (20 * n_experts)
    padded = round_up(capacity, 16)
    (
        layer_b, gain_rows, router_t, columns,
        x_zero, a_one, qkv, att_out, x_one, a_two, router_probs, logs, pooled, part_importance,
        arrived, details, activated, slope, result, part_pooled, expert_weights
    ) = forward(
        sizes, n_experts, padded, lengths, slot_mask, expert_picks, priority_rank, patches, dense_weights, norm_params,
        router_weights, expert_in, expert_out
    )
    g_head, d_pooled_all, d_pooled, g_norm_three, head_sums, total_importance = head_step(
        sizes,
        n_images,
        part_pooled,
        pooled,
        part_importance,
        gain_rows,
        head_weights,
        class_labels,
    )
    d_back, back_gate, *grads = expert_backward(
        sizes, arrived, details, d_pooled_all, result, slope, activated, expert_weights
    )
    parts = return_experts(grads, n_blocks)
    blocks = dense_backward(
        sizes,
        n_experts,
        padded,
        rows_own,
        lengths,
        slot_mask,
        patches,
        (x_zero, a_one, qkv, att_out, x_one, a_two, router_probs, logs),
        columns,
        layer_b,
        gain_rows,
        router_t,
        d_back,
        back_gate,
        d_pooled,
        total_importance,
        g_norm_three,
    )
    reduced, dense_sums = scatter_dense(sizes, blocks)
    g_one, g_two, totals = finish(
        sizes, n_experts, parts, head_sums, dense_sums, total_importance
    )
    n_dense = dense_weights.shape[0] * rows_own
    g_layers = reduced[:n_dense].reshape(-1, rows_own, model_width)
    g_norms = reduced[n_dense : n_dense + 6, :rows_own]
    g_router = reduced[n_dense : n_dense + n_experts, 128 : 128 + rows_own].T
    importance = total_importance[0, :n_experts]
    loss_value, grad_norm, factor = totals[0, 0], totals[1, 0], totals[2, 0]
    dense_out = adam_update(
        dense_weights, dense_first, dense_second, dense_average, g_layers, factor, base_rate
    )
    router_out = adam_update(
        router_weights, router_first, router_second, router_average, g_router, factor, base_rate
    )
    norm_out = adam_update(
        norm_params, norm_first, norm_second, norm_average, g_norms, factor, norm_rate
    )
    in_out = adam_update(expert_in, in_first, in_second, in_average, g_one, factor, base_rate)
    out_out = adam_update(expert_out, out_first, out_second, out_average, g_two, factor, base_rate)
    head_out = adam_update(
        head_weights, head_first, head_second, head_average, g_head, factor, base_rate
    )
    return (
        loss_value,
        importance,
        grad_norm,
        *dense_out,
        *router_out,
        *norm_out,
        *in_out,
        *out_out,
        *head_out,
    )


def solution(mesh):
    n_dp, n_expert = mesh.shape["dp"], mesh.shape["expert"]
    shaped = mesh.devices.reshape(n_dp // QUAD, QUAD, n_expert // 2, 2)
    fine = Mesh(shaped, ALL)
    rows = P(ALL, None)
    dense = P(None, ALL, None)
    norms = P(None, ALL)
    experts = P(("x", "c"), ("g", "r"), None)
    placed = (rows,) * 6 + (dense,) * 4 + (rows,) * 4 + (norms,) * 4 + (experts,) * 8 + (rows,) * 4
    results = (
        (P(),) * 3 + (dense,) * 4 + (rows,) * 4 + (norms,) * 4 + (experts,) * 8 + (rows,) * 4
    )
    return jax.shard_map(body, mesh=fine, in_specs=placed, out_specs=results, check_vma=False)
```

```python
import functools
import math

import jax
import jax.numpy as jnp
from jax import lax
from jax.experimental import pallas as pl
from jax.experimental.pallas import tpu as pltpu
from jax.sharding import Mesh
from jax.sharding import PartitionSpec as P

HEADS = 12
TOP = 2
STEP_COUNT = 10
QUAD = 4

high_prec = lax.Precision.HIGHEST
eps_norm = 1e-06
aux_weight = 0.01
clip_limit = 1.0
base_rate = 0.05
norm_rate = 0.5
beta_first = 0.9
beta_second = 0.999
weight_decay = 0.1
polyak_decay = 0.7
adam_eps = 1e-08
mask_fill = -1e30

ALL = ("g", "r", "x", "c")
MEMBERS = ("x", "r")


def adam_update(weight, first_state, second_state, average_state, gradient, factor, step_rate):
    clipped = gradient * factor
    first_new = beta_first * first_state + (1.0 - beta_first) * clipped
    second_new = beta_second * second_state + (1.0 - beta_second) * clipped * clipped
    first_hat = first_new / (1.0 - beta_first**STEP_COUNT)
    second_hat = second_new / (1.0 - beta_second**STEP_COUNT)
    weight_new = weight - step_rate * (
        first_hat / (jnp.sqrt(second_hat) + adam_eps) + weight_decay * weight
    )
    average_new = polyak_decay * average_state + (1.0 - polyak_decay) * weight_new
    return (weight_new, first_new, second_new, average_new)


MESH_ID = pl.DeviceIdType.MESH
VMEM = pltpu.VMEM
ANY = pl.ANY
MIB = 1 << 20


def cost(microseconds):
    return pl.CostEstimate(flops=int(microseconds * 1.15e9), bytes_accessed=0, transcendentals=0)


def whole(space=None):
    return pl.BlockSpec(memory_space=space or VMEM)


def round_up(value, step):
    return (value + step - 1) // step * step


class Place:
    def __init__(self, sizes):
        self.G, self.X = sizes["g"], sizes["x"]
        self.Z, self.Y = QUAD, sizes["g"]
        self.chips = self.Z * self.Y * self.X
        spot = lax.axis_index("g") * QUAD + lax.axis_index("r")
        self.z, self.y = lax.div(spot, self.Y), lax.rem(spot, self.Y)
        self.x, self.c = lax.axis_index("x"), lax.axis_index("c")
        self.g, self.r = lax.axis_index("g"), lax.axis_index("r")
        self.chip = spot * self.X + self.x
        self.member = self.x * QUAD + self.r

    def at(self, z=None, y=None, x=None, c=None):
        spot = (self.z if z is None else z) * self.Y + (self.y if y is None else y)
        return {
            "g": lax.div(spot, QUAD),
            "r": lax.rem(spot, QUAD),
            "x": self.x if x is None else x,
            "c": self.c if c is None else c,
        }

    def of_chip(self, chip):
        spot = lax.div(chip, self.X)
        return {
            "g": lax.div(spot, QUAD),
            "r": lax.rem(spot, QUAD),
            "x": lax.rem(chip, self.X),
            "c": self.c,
        }

    def of_member(self, member):
        return {
            "g": self.g,
            "r": lax.rem(member, QUAD),
            "x": lax.div(member, QUAD),
            "c": self.c,
        }

    def sibling(self):
        return self.at(c=1 - self.c)


def greet(peers):
    barrier = pltpu.get_barrier_semaphore()
    for peer in peers:
        pl.semaphore_signal(barrier, inc=1, device_id=peer, device_id_type=MESH_ID)
    pl.semaphore_wait(barrier, len(peers))


def send(src, dst, send_sem, recv_sem, peer):
    return pltpu.make_async_remote_copy(
        src_ref=src,
        dst_ref=dst,
        send_sem=send_sem,
        recv_sem=recv_sem,
        device_id=peer,
        device_id_type=MESH_ID,
    )


def others(me, count):
    return [lax.rem(me + step, count) for step in range(1, count)]


def grid_peers(at):
    peers = [at.at(z=z) for z in others(at.z, at.Z)]
    peers += [at.at(y=y) for y in others(at.y, at.Y)]
    peers += [at.at(x=x) for x in others(at.x, at.X)]
    return peers + [at.sibling()]


def gather_dense(at, rows, mats, count, land, sems, started, beside, idle):
    Z, Y, X = at.Z, at.Y, at.X
    depth = land.shape[4]
    cut = depth // 2 // 16 * 16
    first, second = pl.ds(0, cut), pl.ds(cut, depth - cut)
    z_out, z_in, ya_out, ya_in, xb_out, xb_in, xa_out, xa_in, yb_out, yb_in, c_out, c_in = sems
    mine = land.at[at.c, at.z, at.x, at.y]

    def begin(copy):
        copy.start()
        started.append(copy)

    order = [at.z] + [lax.rem(at.z + k, Z) for k in (1, 3, 2)]
    for z in order[1:]:
        begin(send(mine, mine, z_out.at[z], z_in.at[at.z], at.at(z=z)))

    def one(z):
        part = land.at[at.c, z, at.x, at.y]
        for y in others(at.y, Y):
            begin(send(part.at[first], part.at[first], ya_out.at[z, y], ya_in.at[z, at.y], at.at(y=y)))
        for x in others(at.x, X):
            begin(send(part.at[second], part.at[second], xb_out.at[z, x], xb_in.at[z, at.x], at.at(x=x)))

    def two(z):
        for y in others(at.y, Y):
            part = land.at[at.c, z, at.x, y, first]
            send(part, part, ya_out.at[z, y], ya_in.at[z, y], at.at(y=y)).wait_recv()
        line = land.at[at.c, z, at.x, :, first]
        for x in others(at.x, X):
            begin(send(line, line, xa_out.at[z, x], xa_in.at[z, at.x], at.at(x=x)))
        for x in others(at.x, X):
            part = land.at[at.c, z, x, at.y, second]
            send(part, part, xb_out.at[z, x], xb_in.at[z, x], at.at(x=x)).wait_recv()
        line = land.at[at.c, z, :, at.y, second]
        for y in others(at.y, Y):
            begin(send(line, line, yb_out.at[z, y], yb_in.at[z, at.y], at.at(y=y)))

    def three(z):
        for x in others(at.x, X):
            line = land.at[at.c, z, x, :, first]
            send(line, line, xa_out.at[z, x], xa_in.at[z, x], at.at(x=x)).wait_recv()
        for y in others(at.y, Y):
            line = land.at[at.c, z, :, y, second]
            send(line, line, yb_out.at[z, y], yb_in.at[z, y], at.at(y=y)).wait_recv()
        plane = land.at[at.c, z]
        begin(send(plane, plane, c_out.at[z], c_in.at[z], at.sibling()))

    for step in range(Z + 2):
        if step < Z:
            if step > 0:
                z = order[step]
                part = land.at[at.c, z, at.x, at.y]
                send(part, part, z_out.at[z], z_in.at[z], at.at(z=z)).wait_recv()
            one(order[step])
        if step == 0:
            beside()
        if step == Z - 1:
            idle()
        if 0 <= step - 1 < Z:
            two(order[step - 1])
        if 0 <= step - 2 < Z:
            three(order[step - 2])
    for z in order:
        plane = land.at[1 - at.c, z]
        send(plane, plane, c_out.at[z], c_in.at[z], at.sibling()).wait_recv()


def assemble_dense(at, rows, mats, count, land, w_ref, gain_ref, router_ref):
    chips = [(z, y, x) for z in range(at.Z) for y in range(at.Y) for x in range(at.X)]
    cores = [(c, z, x, y) for z, y, x in chips for c in range(2)]
    group = 16 // math.gcd(16, rows)
    for start in range(0, len(cores), group):
        for mat in range(mats):
            w_ref[mat, start * rows : (start + group) * rows] = jnp.concatenate(
                [land[spot][mat * rows : (mat + 1) * rows] for spot in cores[start : start + group]], 0
            )
    base = mats * rows
    tails = [land[spot][base : base + count].astype(jnp.float32) for spot in cores]
    gain_ref[...] = jnp.concatenate([tail[:8, :rows] for tail in tails], 1)
    router_ref[...] = jnp.concatenate([tail[:, 128 : 128 + rows] for tail in tails], 1)


def total_square(value):
    return jnp.sum(jnp.sum(value * value, 0, keepdims=True), 1, keepdims=True)


def scatter_kernel(sizes, g_ref, out_ref, square_ref, hold, sib, got_xa, got_yb, got_ya, got_xb, got_z, *sems):
    at = Place(sizes)
    Z, Y, X = at.Z, at.Y, at.X
    depth = g_ref.shape[4]
    cut = depth // 2 // 16 * 16
    first, second = pl.ds(0, cut), pl.ds(cut, depth - cut)
    c_out, c_in, xa_out, xa_in, yb_out, yb_in, ya_out, ya_in, xb_out, xb_in, z_out, z_in = sems
    greet(grid_peers(at))
    started = []

    def begin(copy):
        copy.start()
        started.append(copy)

    wide = lambda value: value.astype(jnp.float32)
    order = [lax.rem(at.z + k, Z) for k in (2, 1, 3)] + [at.z]
    for z in order:
        begin(send(g_ref.at[1 - at.c, z], sib.at[z], c_out.at[z], c_in.at[z], at.sibling()))

    def one(z):
        send(sib.at[z], sib.at[z], c_out.at[z], c_in.at[z], at.sibling()).wait_recv()
        hold[z] = (wide(g_ref[at.c, z]) + wide(sib[z])).astype(jnp.bfloat16)
        for x in others(at.x, X):
            begin(send(hold.at[z, x, :, first], got_xa.at[z, at.x], xa_out.at[z, x], xa_in.at[z, at.x], at.at(x=x)))
        for y in others(at.y, Y):
            begin(send(hold.at[z, :, y, second], got_yb.at[z, at.y], yb_out.at[z, y], yb_in.at[z, at.y], at.at(y=y)))

    def two(z):
        total = wide(hold[z, at.x, :, first])
        for x in others(at.x, X):
            send(got_xa.at[z, x], got_xa.at[z, x], xa_out.at[z, x], xa_in.at[z, x], at.at(x=x)).wait_recv()
            total = total + wide(got_xa[z, x])
        hold[z, at.x, :, first] = total.astype(jnp.bfloat16)
        for y in others(at.y, Y):
            begin(send(hold.at[z, at.x, y, first], got_ya.at[z, at.y], ya_out.at[z, y], ya_in.at[z, at.y], at.at(y=y)))
        total = wide(hold[z, :, at.y, second])
        for y in others(at.y, Y):
            send(got_yb.at[z, y], got_yb.at[z, y], yb_out.at[z, y], yb_in.at[z, y], at.at(y=y)).wait_recv()
            total = total + wide(got_yb[z, y])
        hold[z, :, at.y, second] = total.astype(jnp.bfloat16)
        for x in others(at.x, X):
            begin(send(hold.at[z, x, at.y, second], got_xb.at[z, at.x], xb_out.at[z, x], xb_in.at[z, at.x], at.at(x=x)))

    def three(z, last):
        total = wide(hold[z, at.x, at.y, first])
        for y in others(at.y, Y):
            send(got_ya.at[z, y], got_ya.at[z, y], ya_out.at[z, y], ya_in.at[z, y], at.at(y=y)).wait_recv()
            total = total + wide(got_ya[z, y])
        rest = wide(hold[z, at.x, at.y, second])
        for x in others(at.x, X):
            send(got_xb.at[z, x], got_xb.at[z, x], xb_out.at[z, x], xb_in.at[z, x], at.at(x=x)).wait_recv()
            rest = rest + wide(got_xb[z, x])
        if last:
            out_ref[first] = total
            out_ref[second] = rest
            return
        mine = hold.at[z, at.x, at.y]
        mine[first] = total.astype(jnp.bfloat16)
        mine[second] = rest.astype(jnp.bfloat16)
        begin(send(mine, got_z.at[at.z], z_out.at[z], z_in.at[at.z], at.at(z=z)))

    for step in range(Z + 2):
        if step < Z:
            one(order[step])
        if 0 <= step - 1 < Z:
            two(order[step - 1])
        if 0 <= step - 2 < Z:
            three(order[step - 2], step - 2 == Z - 1)
    for z in order[:-1]:
        send(got_z.at[z], got_z.at[z], z_out.at[z], z_in.at[z], at.at(z=z)).wait_recv()
        out_ref[...] += wide(got_z[z])
    square_ref[...] = jnp.broadcast_to(total_square(out_ref[...]), square_ref.shape)
    for copy in started:
        copy.wait_send()


def scatter_dense(sizes, blocks):
    unused, Z, X, Y, depth, width = blocks.shape
    dma = pltpu.SemaphoreType.DMA
    by_y, by_x, by_z = dma((Z, Y)), dma((Z, X)), dma((Z,))
    cut = depth // 2 // 16 * 16
    half = jnp.bfloat16
    return pl.pallas_call(
        functools.partial(scatter_kernel, sizes),
        out_shape=(
            jax.ShapeDtypeStruct((depth, width), jnp.float32),
            jax.ShapeDtypeStruct((8, 128), jnp.float32),
        ),
        in_specs=[whole()],
        out_specs=(whole(), whole()),
        scratch_shapes=[
            VMEM((Z, X, Y, depth, width), half),
            VMEM((Z, X, Y, depth, width), half),
            VMEM((Z, X, Y, cut, width), half),
            VMEM((Z, Y, X, depth - cut, width), half),
            VMEM((Z, Y, cut, width), half),
            VMEM((Z, X, depth - cut, width), half),
            VMEM((Z, depth, width), half),
        ]
        + [by_z, by_z, by_x, by_x, by_y, by_y, by_y, by_y, by_x, by_x, by_z, by_z],
        compiler_params=pltpu.CompilerParams(
            collective_id=2, has_side_effects=True, vmem_limit_bytes=28 * MIB
        ),
        cost_estimate=cost(45),
        name="scatter_dense",
    )(blocks)


def finish_kernel(sizes, n_experts, head_ref, dense_ref, imp_ref, *refs):
    at = Place(sizes)
    many = len(refs) - 7
    parts = refs[:many]
    first_ref, second_ref, out_ref, land, own, out_sem, in_sem = refs[many:]
    count = 2 * at.chips
    me = at.chip * 2 + at.c
    ids = others(me, count)

    def peer(device):
        spot = at.of_chip(lax.div(device, 2))
        spot["c"] = lax.rem(device, 2)
        return spot

    greet([peer(device) for device in ids])
    place = lax.rem(at.g * QUAD + at.r, 2)
    square = dense_ref[0:1, 0:1] + head_ref[1:2, 0:1]
    for parity in range(2):
        expert = place if parity == 0 else 1 - place
        for index, ref in enumerate((first_ref, second_ref)):
            total = None
            for step in range(parity * many // 2, (parity + 1) * many // 2):
                found = parts[step][index].astype(jnp.float32)
                total = found if total is None else total + found
            ref[expert] = total
            square = square + total_square(total)
    line = lax.broadcasted_iota(jnp.int32, own.shape, 0)
    own[...] = jnp.where(line == 0, head_ref[0:1, 0:1], jnp.where(line == 1, square, 0.0))
    land[me] = own[...]
    copies = [send(own, land.at[me], out_sem.at[d], in_sem.at[me], peer(d)) for d in ids]
    for copy in copies:
        copy.start()
    importance = imp_ref[0:1, 0:128]
    head = lax.broadcasted_iota(jnp.int32, (1, 128), 1) < n_experts
    centre = jnp.sum(jnp.where(head, importance, 0.0), 1, keepdims=True) / n_experts
    away = jnp.where(head, importance - centre, 0.0)
    spread = jnp.sum(away * away, 1, keepdims=True) / n_experts
    balance = aux_weight * spread / (centre * centre)
    for d in ids:
        send(land.at[d], land.at[d], out_sem.at[d], in_sem.at[d], peer(d)).wait_recv()
    sums = jnp.sum(land[...], 0)
    norm = jnp.sqrt(sums[1:2, 0:1])
    factor = jnp.minimum(1.0, clip_limit / norm)
    loss = sums[0:1, 0:1] + balance
    out_ref[...] = jnp.where(line == 0, loss, jnp.where(line == 1, norm, factor))
    for copy in copies:
        copy.wait_send()


def finish(sizes, n_experts, parts, head_sums, dense_sums, importance):
    devices = sizes["g"] * QUAD * sizes["x"] * 2
    unused, rows, width = parts[0].shape
    dma = pltpu.SemaphoreType.DMA
    grads = jax.ShapeDtypeStruct((2, rows, width), jnp.float32)
    return pl.pallas_call(
        functools.partial(finish_kernel, sizes, n_experts),
        out_shape=(grads, grads, jax.ShapeDtypeStruct((8, 128), jnp.float32)),
        in_specs=[whole()] * (3 + len(parts)),
        out_specs=(whole(),) * 3,
        scratch_shapes=[
            VMEM((devices, 8, 128), jnp.float32),
            VMEM((8, 128), jnp.float32),
            dma((devices,)),
            dma((devices,)),
        ],
        compiler_params=pltpu.CompilerParams(
            collective_id=3, has_side_effects=True, vmem_limit_bytes=20 * MIB
        ),
        cost_estimate=cost(10),
        name="finish",
    )(head_sums, dense_sums, importance, *parts)


IMAGE_PAD = 16


def split_three(value):
    high = value.astype(jnp.bfloat16)
    rest = value - high.astype(jnp.float32)
    middle = rest.astype(jnp.bfloat16)
    return high, middle, (rest - middle.astype(jnp.float32)).astype(jnp.bfloat16)


def dot_f32(left, right, dims):
    return lax.dot_general(left, right, (dims, ((), ())), preferred_element_type=jnp.float32)


NN = ((1,), (0,))
NT = ((1,), (1,))
TN = ((0,), (0,))


def norm_parts(values):
    centre = values - jnp.mean(values, -1, keepdims=True)
    spread = jnp.mean(centre * centre, -1, keepdims=True)
    scale = lax.rsqrt(spread + eps_norm)
    return centre * scale, scale


def norm_back(d_out, scaled, scale, gain):
    pulled = d_out * gain
    return scale * (
        pulled
        - jnp.mean(pulled, -1, keepdims=True)
        - scaled * jnp.mean(pulled * scaled, -1, keepdims=True)
    )


def head_kernel(
    sizes, images, part_ref, own_ref, imp_ref, gain_ref, head_ref, label_ref,
    g_head_ref, d_pool_ref, own_d_ref, g_norm_ref, sums_ref, total_imp_ref,
    in_part, rows, d_rows, d_sib, d_sum, d_in, head_b, labels, d_logits, *sems
):
    at = Place(sizes)
    chips, members = at.chips, QUAD * at.X
    devices = 2 * chips
    p_out, p_in, r_out, r_in, s_out, s_in, d_out, d_in_sem, b_out, b_in = sems
    width = own_ref.shape[1]
    same_core = others(at.chip, chips)
    greet([at.of_chip(chip) for chip in same_core] + [at.sibling()])
    started = []

    def begin(copy):
        copy.start()
        started.append(copy)

    team = others(at.member, members)
    for member in team:
        begin(send(part_ref.at[member], in_part.at[at.member], p_out.at[member], p_in.at[at.member], at.of_member(member)))
    in_part[at.member] = part_ref[at.member]
    head_b[...] = head_ref[...].astype(jnp.bfloat16)
    wide = devices * IMAGE_PAD
    spot = lax.broadcasted_iota(jnp.int32, (label_ref.shape[1], wide), 1)
    given = lax.broadcasted_iota(jnp.int32, (label_ref.shape[1], wide), 0)
    image = lax.rem(spot, IMAGE_PAD)
    device = lax.rem(lax.div(spot, IMAGE_PAD), chips) * 2 + lax.div(spot, IMAGE_PAD * chips)
    chosen = ((device * images + image == given) & (image < images)).astype(jnp.bfloat16)
    labels[...] = dot_f32(label_ref[...].astype(jnp.float32).astype(jnp.bfloat16), chosen, NN).astype(jnp.bfloat16)
    for member in team:
        send(in_part.at[member], in_part.at[member], p_out.at[member], p_in.at[member], at.of_member(member)).wait_recv()
    pooled = own_ref[...] + jnp.sum(in_part[...], 0)
    scaled, scale = norm_parts(pooled)
    gain, shift = gain_ref[2:3], gain_ref[5:6]
    a_three = scaled * gain + shift
    row = lax.broadcasted_iota(jnp.int32, (IMAGE_PAD, width), 0)
    block = jnp.where(row < images, a_three, 0.0)
    pieces = split_three(imp_ref[0:1])
    for index, piece in enumerate(pieces):
        block = jnp.where(row == images + index, piece.astype(jnp.float32), block)
    rows[at.c, at.chip] = block.astype(jnp.bfloat16)
    mine = rows.at[at.c, at.chip]
    for chip in same_core:
        begin(send(mine, mine, r_out.at[chip], r_in.at[at.chip], at.of_chip(chip)))
    for chip in same_core:
        part = rows.at[at.c, chip]
        send(part, part, r_out.at[chip], r_in.at[chip], at.of_chip(chip)).wait_recv()
    begin(send(rows.at[at.c], rows.at[at.c], s_out.at[0], s_in.at[0], at.sibling()))
    send(rows.at[1 - at.c], rows.at[1 - at.c], s_out.at[0], s_in.at[0], at.sibling()).wait_recv()
    gathered = rows[...].reshape(wide, width)
    in_block = lax.rem(lax.broadcasted_iota(jnp.int32, (wide, width), 0), IMAGE_PAD)
    total = jnp.sum(jnp.where(in_block >= images, gathered.astype(jnp.float32), 0.0), 0, keepdims=True)
    total_imp_ref[...] = jnp.broadcast_to(total, total_imp_ref.shape)
    gathered = jnp.where(in_block < images, gathered.astype(jnp.float32), 0.0).astype(jnp.bfloat16)
    logits = dot_f32(head_b[...], gathered, NT)
    image = lax.rem(lax.broadcasted_iota(jnp.int32, logits.shape, 1), IMAGE_PAD)
    count = devices * images
    target = labels[...].astype(jnp.float32)
    power = jnp.exp(-jnp.abs(logits))
    loss = jnp.maximum(logits, 0.0) + jnp.log1p(power) - target * logits
    loss = jnp.sum(jnp.where(image < images, loss, 0.0), 1, keepdims=True)
    loss = jnp.sum(loss, 0, keepdims=True) / count
    chance = jnp.where(logits >= 0.0, 1.0, power) / (1.0 + power)
    d_logits[...] = jnp.where(image < images, (chance - target) / count, 0.0).astype(jnp.bfloat16)
    partial = dot_f32(d_logits[...], head_b[...], TN)
    d_rows[...] = partial.reshape(d_rows.shape).astype(jnp.bfloat16)
    begin(send(d_rows.at[1 - at.c], d_sib, s_out.at[1], s_in.at[1], at.sibling()))
    g_head = dot_f32(d_logits[...], gathered, NN)
    g_head_ref[...] = g_head
    line = lax.broadcasted_iota(jnp.int32, sums_ref.shape, 0)
    sums_ref[...] = jnp.where(line == 0, loss, jnp.where(line == 1, total_square(g_head), 0.0))
    send(d_sib, d_sib, s_out.at[1], s_in.at[1], at.sibling()).wait_recv()
    d_sum[...] = (d_rows[at.c].astype(jnp.float32) + d_sib[...].astype(jnp.float32)).astype(jnp.bfloat16)
    for chip in same_core:
        begin(send(d_sum.at[chip], d_in.at[at.chip], d_out.at[chip], d_in_sem.at[at.chip], at.of_chip(chip)))
    d_in[at.chip] = d_sum[at.chip]
    for chip in same_core:
        send(d_in.at[chip], d_in.at[chip], d_out.at[chip], d_in_sem.at[chip], at.of_chip(chip)).wait_recv()
    d_norm = jnp.sum(d_in[...].astype(jnp.float32), 0)
    d_norm = jnp.where(row < images, d_norm, 0.0)
    d_pooled = norm_back(d_norm, scaled, scale, gain)
    d_pooled = jnp.where(row < images, d_pooled, 0.0)
    d_gain = jnp.sum(d_norm * scaled, 0, keepdims=True)
    d_shift = jnp.sum(d_norm, 0, keepdims=True)
    line = lax.broadcasted_iota(jnp.int32, g_norm_ref.shape, 0)
    g_norm_ref[...] = jnp.where(line == 2, d_gain, jnp.where(line == 5, d_shift, 0.0))
    own_d_ref[...] = d_pooled
    d_pool_ref[at.member] = d_pooled
    mine = d_pool_ref.at[at.member]
    for member in team:
        begin(send(own_d_ref, mine, b_out.at[member], b_in.at[at.member], at.of_member(member)))
    for member in team:
        part = d_pool_ref.at[member]
        send(part, part, b_out.at[member], b_in.at[member], at.of_member(member)).wait_recv()
    for copy in started:
        copy.wait_send()


def head_step(sizes, images, part, own, imp, gains, head, label):
    members = QUAD * sizes["x"]
    chips = members * sizes["g"]
    classes, width = head.shape
    wide = 2 * chips * IMAGE_PAD
    dma = pltpu.SemaphoreType.DMA
    by_member, by_chip = dma((members,)), dma((chips,))
    f32, half = jnp.float32, jnp.bfloat16
    blocks = (chips, IMAGE_PAD, width)
    return pl.pallas_call(
        functools.partial(head_kernel, sizes, images),
        out_shape=(
            jax.ShapeDtypeStruct((classes, width), f32),
            jax.ShapeDtypeStruct((members, IMAGE_PAD, width), f32),
            jax.ShapeDtypeStruct((IMAGE_PAD, width), f32),
            jax.ShapeDtypeStruct((8, width), f32),
            jax.ShapeDtypeStruct((8, 128), f32),
            jax.ShapeDtypeStruct((8, width), f32),
        ),
        in_specs=[whole()] * 6,
        out_specs=(whole(),) * 6,
        scratch_shapes=[
            VMEM((members, IMAGE_PAD, width), f32),
            VMEM((2, *blocks), half),
            VMEM((2, *blocks), half),
            VMEM(blocks, half),
            VMEM(blocks, half),
            VMEM(blocks, half),
            VMEM((classes, width), half),
            VMEM((classes, wide), half),
            VMEM((classes, wide), half),
        ]
        + [by_member, by_member, by_chip, by_chip, dma((2,)), dma((2,)), by_chip, by_chip]
        + [by_member, by_member],
        compiler_params=pltpu.CompilerParams(
            collective_id=4, has_side_effects=True, vmem_limit_bytes=56 * MIB
        ),
        cost_estimate=cost(42),
        name="head_step",
    )(part, own, imp, gains, head, label)


def route_math(per_image, n_experts, capacity, padded, pick_ref, rank_ref, mask_ref, length_ref):
    rows_here, span = mask_ref.shape
    tokens = rows_here * span
    valid = mask_ref[...].astype(jnp.float32)
    lengths = length_ref[...]
    position = lax.broadcasted_iota(jnp.int32, (rows_here, span), 1)
    segment = jnp.zeros((rows_here, span), jnp.int32)
    bound = jnp.zeros((rows_here, 1), jnp.int32)
    for image in range(per_image):
        bound = bound + lengths[:, image : image + 1]
        segment = segment + jnp.where(position >= bound, 1, 0)
    pool = jnp.zeros_like(valid)
    for image in range(per_image):
        member = jnp.where(segment == image, valid, 0.0)
        pool = pool + member / jnp.maximum(jnp.sum(member, 1, keepdims=True), 1.0)
    line = lax.broadcasted_iota(jnp.int32, (rows_here, span), 0)
    image = (segment + per_image * line).astype(jnp.float32)

    def flat(value):
        return jnp.concatenate([value[i : i + 1] for i in range(rows_here)], 1)

    rank_row = rank_ref[...].astype(jnp.float32)
    picks = pick_ref[...].astype(jnp.float32)
    table = jnp.concatenate([flat(valid), flat(pool), flat(image), rank_row, picks], 0)
    table = jnp.concatenate([table, jnp.zeros((122, tokens), jnp.float32)], 0).T
    valid_col, pool_col, image_col, rank_col, pick_one, pick_two = (
        table[:, i : i + 1] for i in range(6)
    )
    lane = lax.broadcasted_iota(jnp.int32, (tokens, 128), 1)
    in_first, in_second = lane < n_experts, (lane >= n_experts) & (lane < 2 * n_experts)
    number = lane.astype(jnp.float32)
    hot = jnp.where(in_first & (pick_one == number), valid_col, 0.0)
    hot = hot + jnp.where(in_second & (pick_two == number - n_experts), valid_col, 0.0)
    shifted = jnp.where(in_second & (pick_one == number - n_experts), valid_col, 0.0)
    before = jnp.where(rank_row < rank_col, 1.0, 0.0).astype(jnp.bfloat16)
    ahead = dot_f32(before, hot.astype(jnp.bfloat16), NN) + jnp.sum(shifted, 0, keepdims=True)
    counted = hot * ahead
    pos_one = jnp.sum(jnp.where(in_first, counted, 0.0), 1, keepdims=True)
    pos_two = jnp.sum(jnp.where(in_second, counted, 0.0), 1, keepdims=True)

    def place(pick, pos):
        kept = (valid_col > 0.0) & (pos < capacity)
        return jnp.where(kept, pick * padded + pos, -1.0)

    columns = (
        place(pick_one, pos_one),
        place(pick_two, pos_two),
        valid_col,
        pool_col,
        image_col,
        pick_one,
        pick_two,
    )
    result = jnp.zeros((tokens, 128), jnp.float32)
    for index, column in enumerate(columns):
        result = jnp.where(lane == index, column, result)
    return result


def allowed_slots(lengths, row, images, valid_row, span):
    query = lax.broadcasted_iota(jnp.int32, (span, span), 0)
    key = lax.broadcasted_iota(jnp.int32, (span, span), 1)
    bound = 0
    query_seg, key_seg = jnp.zeros((span, span), jnp.int32), jnp.zeros((span, span), jnp.int32)
    for image in range(images):
        bound = bound + lengths[row, image]
        query_seg = query_seg + jnp.where(query >= bound, 1, 0)
        key_seg = key_seg + jnp.where(key >= bound, 1, 0)
    allowed = (query_seg == key_seg) & ((valid_row > 0) | (query == key))
    return jnp.where(allowed, 1.0, 0.0)


TILE = 32


def tiles(count, size=TILE):
    return [slice(start, min(start + size, count)) for start in range(0, count, size)]


def step_order(blocks):
    return [*range(0, 2 * blocks, 2), *range(1, 2 * blocks, 2)]


class Team:
    def __init__(self, at):
        self.at, self.span = at, 2 * at.G
        self.spot = at.g * QUAD + at.r

    def target(self, step):
        at = self.at
        chosen = lax.rem(self.spot + step_order(at.G)[step], self.span)
        block, index = lax.div(chosen, 2), lax.rem(chosen, 2)
        core = lax.div(self.spot, self.span)
        r = 2 * at.c + index
        own = (block == at.g) & (r == at.r) & (core == at.c)
        return {"g": block, "r": r, "x": at.x, "c": core}, index, own

    def peers(self):
        at = self.at
        count = 2 * at.G * QUAD
        me = self.spot * 2 + at.c
        line = []
        for device in others(me, count):
            spot = lax.div(device, 2)
            line.append(
                {"g": lax.div(spot, QUAD), "r": lax.rem(spot, QUAD), "x": at.x, "c": lax.rem(device, 2)}
            )
        for x in others(at.x, at.X):
            line += [{"g": at.g, "r": r, "x": x, "c": at.c} for r in range(QUAD)]
        return line


def image_hot(detail, padded):
    image = detail[2:3, :padded]
    line = lax.broadcasted_iota(jnp.int32, (IMAGE_PAD, padded), 0).astype(jnp.float32)
    return line == image


def forward_kernel(
    sizes, n_experts, images, padded,
    length_ref, lengths_ref, mask_ref, pick_ref, rank_ref, patch_ref, dense_ref, norm_ref, routing_ref, in_ref, out_ref,
    w_keep, gain_ref, router_ref, col_ref, x_zero_out, a_one_out, qkv_out, att_out, x_one_out, a_two_out, prob_ref, lse_ref, pool_ref, imp_ref,
    rows_out, detail_out, act_out, slope_out, y_out, part_ref, weight_out,
    land, w_ref, shard_ref, x_zero_buf, a_one_buf, qkv_buf, att_buf, x_one_buf, a_two_ref, weights, send_rows, send_detail, places,
    rows_in, detail_in, total, act_buf, slope_buf, dense_sem, keep_sem, own_sem,
    w_out, w_in, s_out, s_in, r_out, r_in, m_out, m_in, act_sem, slope_sem, cast_sem, *gather_sems
):
    at = Place(sizes)
    team = Team(at)
    half = weights.shape[1]
    early = half // 2
    rows_here, span = mask_ref.shape
    width = patch_ref.shape[1]
    tokens = rows_here * span
    mats, rows_own, unused = dense_ref.shape
    tall = router_ref.shape[0]
    capacity = (21 * tokens * TOP + 20 * n_experts - 1) // (20 * n_experts)

    part_rows = shard_ref.shape[2]
    casts = [
        pltpu.make_async_copy(ref.at[expert], total.at[pl.ds((index * 2 + expert) * part_rows, part_rows)], cast_sem.at[index, expert])
        for index, ref in enumerate((in_ref, out_ref))
        for expert in range(2)
    ]
    for copy in casts:
        copy.start()
    depth = land.shape[4]
    routing = routing_ref[...]
    routing = jnp.concatenate([routing, jnp.zeros((rows_own, 128 - n_experts), jnp.float32)], 1)
    routing = jnp.concatenate([routing, jnp.zeros((128 - rows_own, 128), jnp.float32)], 0).T
    norms = norm_ref[...]
    norms = jnp.concatenate([norms, jnp.zeros((norms.shape[0], 128 - rows_own), jnp.float32)], 1)
    norms = jnp.concatenate([norms, jnp.zeros((tall - norms.shape[0], 128), jnp.float32)], 0)
    tail = jnp.concatenate(
        [norms, routing[:tall], jnp.zeros((tall, width - 256), jnp.float32)], 1
    )
    block = jnp.concatenate([dense_ref[...].reshape(mats * rows_own, width), tail], 0)
    if block.shape[0] < depth:
        block = jnp.concatenate(
            [block, jnp.zeros((depth - block.shape[0], width), jnp.float32)], 0
        )
    land[at.c, at.z, at.x, at.y] = block.astype(jnp.bfloat16)
    greet(team.peers() + grid_peers(at))

    def spot_of(step, side=0):
        return step // early, side * early + step % early

    def swap_copy(step):
        return send(
            weights.at[spot_of(step)], weights.at[spot_of(step, 1)], s_out.at[step], s_in.at[step], at.sibling()
        )

    def shard_copy(step):
        device, index, own = team.target(step)
        return send(
            shard_ref.at[index], weights.at[spot_of(step)], w_out.at[step], w_in.at[step], device
        )

    def shard_own(step):
        device, index, own = team.target(step)
        return pltpu.make_async_copy(shard_ref.at[index], weights.at[spot_of(step)], w_in.at[step])

    def shard_starts(steps):
        for step in steps:
            own = team.target(step)[2]

            @pl.when(own)
            def _():
                shard_own(step).start()

            @pl.when(jnp.logical_not(own))
            def _():
                shard_copy(step).start()

    def shard_waits(steps):
        for step in steps:
            own = team.target(step)[2]

            @pl.when(own)
            def _():
                shard_own(step).wait()

            @pl.when(jnp.logical_not(own))
            def _():
                shard_copy(step).wait_recv()

            swap_copy(step).start()

    def beside_gather():
        col_ref[...] = route_math(
            images, n_experts, capacity, padded, pick_ref, rank_ref, mask_ref, lengths_ref
        )
        for copy in casts:
            copy.wait()
        for index in range(2):
            for expert in range(2):
                here = pl.ds((index * 2 + expert) * part_rows, part_rows)
                shard_ref[expert, index] = total[here].astype(jnp.bfloat16)

    gathers = []
    gather_dense(
        at, rows_own, mats, tall, land, gather_sems, gathers, beside_gather, lambda: shard_starts(range(early))
    )
    shard_starts(range(early, half))
    assemble_dense(at, rows_own, mats, tall, land, w_ref, gain_ref, router_ref)
    w_copy = pltpu.make_async_copy(w_ref, w_keep, keep_sem.at[5])
    w_copy.start()

    dense = (
        (x_zero_buf, x_zero_out), (a_one_buf, a_one_out), (qkv_buf, qkv_out), (att_buf, att_out), (x_one_buf, x_one_out),
    )

    def dense_copy(row, index):
        here = pl.ds(pl.multiple_of(row * span, 16), span)
        buf, out = dense[index]
        return pltpu.make_async_copy(buf, out.at[here], dense_sem.at[index])

    def keep_dense(row, index, value):
        @pl.when(row > 0)
        def _():
            dense_copy(row - 1, index).wait()

        dense[index][0][...] = value
        dense_copy(row, index).start()

    pool_ref[...] = jnp.zeros_like(pool_ref)
    imp_ref[...] = jnp.zeros_like(imp_ref)
    routers = router_ref[...].astype(jnp.bfloat16)
    if routers.shape[0] < 128:
        routers = jnp.concatenate(
            [routers, jnp.zeros((128 - routers.shape[0], width), jnp.bfloat16)], 0
        )
    lane = lax.broadcasted_iota(jnp.int32, (span, 128), 1)

    def dense_row(row, carry):
        here = pl.ds(pl.multiple_of(row * span, 16), span)
        x_zero = dot_f32(patch_ref[here], w_ref[0], NN)
        keep_dense(row, 0, x_zero)
        a_one = (norm_parts(x_zero)[0] * gain_ref[0:1] + gain_ref[3:4]).astype(jnp.bfloat16)
        keep_dense(row, 1, a_one)

        @pl.when(row > 0)
        def _():
            dense_copy(row - 1, 2).wait()

        for part in range(3):
            qkv_buf[:, part * width : (part + 1) * width] = dot_f32(
                a_one, w_ref[1 + part], NN
            ).astype(jnp.bfloat16)
        dense_copy(row, 2).start()
        open_to = allowed_slots(length_ref, row, images, mask_ref[pl.ds(row, 1)], span)
        logs = jnp.zeros((span, 128), jnp.float32)

        @pl.when(row > 0)
        def _():
            dense_copy(row - 1, 3).wait()

        for pair in range(width // 128):
            query, key, value = (
                qkv_buf[:, part * width + pair * 128 : part * width + (pair + 1) * 128]
                for part in range(3)
            )
            outs = []
            for side in range(2):
                held = jnp.where((lane < 64) == (side == 0), query, jnp.zeros_like(query))
                raw = dot_f32(held, key, NT)
                probs, sums = [], []
                for spot in tiles(span, 64):
                    scores = jnp.where(open_to[spot] > 0.0, raw[spot] * 64**-0.5, mask_fill)
                    top = jnp.max(scores, 1, keepdims=True)
                    powers = jnp.exp(scores - top)
                    whole_sum = jnp.sum(powers, 1, keepdims=True)
                    probs.append((powers * (1.0 / whole_sum)).astype(jnp.bfloat16))
                    sums.append(top + jnp.log(whole_sum))
                outs.append(dot_f32(jnp.concatenate(probs, 0), value, NN))
                logs = jnp.where(lane == 2 * pair + side, jnp.concatenate(sums, 0), logs)
            att_buf[:, pair * 128 : (pair + 1) * 128] = jnp.where(
                lane < 64, outs[0], outs[1]
            ).astype(jnp.bfloat16)
        lse_ref[here] = logs
        dense_copy(row, 3).start()
        x_one = x_zero + dot_f32(att_buf[...], w_ref[4], NN)
        keep_dense(row, 4, x_one)
        a_two = (norm_parts(x_one)[0] * gain_ref[1:2] + gain_ref[4:5]).astype(jnp.bfloat16)
        a_two_ref[here] = a_two
        logits = jnp.where(lane < n_experts, dot_f32(a_two, routers, NT), mask_fill)
        powers = jnp.exp(logits - jnp.max(logits, 1, keepdims=True))
        probs = powers / jnp.sum(powers, 1, keepdims=True)
        prob_ref[here] = probs
        columns = col_ref[here]
        valid, pool, image = columns[:, 2:3], columns[:, 3:4], columns[:, 4:5]
        imp_ref[0:1, 0:128] += jnp.sum(probs * valid, 0, keepdims=True)
        line = lax.broadcasted_iota(jnp.int32, pool_ref.shape, 0)
        for index in range(images):
            number = row * images + index
            weight = jnp.where(image == number.astype(jnp.float32), pool, 0.0)
            pooled = jnp.sum(x_one * weight, 0, keepdims=True)
            pool_ref[...] = jnp.where(line == number, pooled, pool_ref[...])
        return carry

    lax.fori_loop(0, rows_here, dense_row, 0)

    columns = col_ref[...]
    places[...] = columns.T[:8]
    def rows_of(member):
        slots = lax.broadcasted_iota(jnp.int32, (padded, tokens), 0) + member * padded
        slots = slots.astype(jnp.float32)
        match = (slots == places[0:1]) | (slots == places[1:2])
        match = jnp.where(match, 1.0, 0.0).astype(jnp.bfloat16)
        return dot_f32(match, a_two_ref[...], NN).astype(jnp.bfloat16)

    def row_copy(member, source):
        return send(
            send_rows.at[member], rows_in.at[source], r_out.at[member], r_in.at[source], at.of_member(member)
        )

    def detail_copy(member, source):
        return send(
            send_detail.at[member], detail_in.at[source], m_out.at[member], m_in.at[source], at.of_member(member)
        )

    def dispatch_step(index, carry):
        member = lax.rem(at.member + index, n_experts)
        send_rows[member] = rows_of(member)
        row_copy(member, at.member).start()
        return carry

    lax.fori_loop(1, n_experts, dispatch_step, 0)
    lane = lax.broadcasted_iota(jnp.int32, (tokens, 128), 1)
    kind, expert = lax.div(lane, n_experts), lax.rem(lane, n_experts).astype(jnp.float32)
    slot_lane = lax.broadcasted_iota(jnp.int32, (tokens, send_detail.shape[2]), 1).astype(jnp.float32)
    pool, image = columns[:, 3:4], columns[:, 4:5]
    details = None
    for choice in range(2):
        slot, pick = columns[:, choice : choice + 1], columns[:, 5 + choice : 6 + choice]
        hot = (expert == pick) & (slot >= 0.0)
        gate = jnp.sum(jnp.where(hot & (kind == 0), prob_ref[...], 0.0), 1, keepdims=True)
        values = jnp.zeros((tokens, 128), jnp.float32)
        pieces = [*split_three(gate), *split_three(pool), image]
        for index, piece in enumerate(pieces):
            values = jnp.where(kind == index, piece.astype(jnp.float32), values)
        values = jnp.where(hot, values, 0.0).astype(jnp.bfloat16)
        spot = jnp.where(slot >= 0.0, slot - pick * padded, -1.0)
        chosen = jnp.where(spot == slot_lane, 1.0, 0.0).astype(jnp.bfloat16)
        found = dot_f32(values, chosen, TN)
        details = found if details is None else details + found
    n = n_experts
    gates = details[0:n] + details[n : 2 * n] + details[2 * n : 3 * n]
    pools = details[3 * n : 4 * n] + details[4 * n : 5 * n] + details[5 * n : 6 * n]
    numbers = details[6 * n : 7 * n]
    for index in range(n):
        for spot, value in enumerate((gates, pools, numbers)):
            send_detail[index, spot : spot + 1] = value[index : index + 1]
        send_detail[index, 3:8] = jnp.zeros((5, send_detail.shape[2]), jnp.float32)

    for member in others(at.member, n_experts):
        detail_copy(member, at.member).start()
    rows_in[at.member] = rows_of(at.member)
    detail_in[at.member] = send_detail[at.member]
    a_two_copy = pltpu.make_async_copy(a_two_ref, a_two_out, keep_sem.at[0])
    a_two_copy.start()
    for index in range(len(dense)):
        dense_copy(rows_here - 1, index).wait()

    shard_waits(range(early))
    for step in range(early):
        swap_copy(step).wait_recv()

    many = act_buf.shape[1] // padded
    count = many * padded
    rounds = n_experts // many

    def hidden_copies(index, chunk):
        block, turn = block_of(index), lax.div(index, rounds)
        here = pl.ds(pl.multiple_of(block * count, 16), count)
        there = turn * half + chunk
        return (
            pltpu.make_async_copy(act_buf.at[chunk], act_out.at[there, here], act_sem.at[chunk]),
            pltpu.make_async_copy(slope_buf.at[chunk], slope_out.at[there, here], slope_sem.at[chunk]),
        )

    def block_of(index):
        return lax.rem(lax.div(at.member, many) + index, rounds)

    def expert_step(index, carry):
        turn = lax.div(index, rounds)
        block = block_of(index)

        @pl.when(turn == 0)
        def _():
            for spot in range(many):
                source = block * many + spot

                @pl.when(source != at.member)
                def _():
                    row_copy(source, source).wait_recv()
                    detail_copy(source, source).wait_recv()

        @pl.when(index == rounds)
        def _():
            shard_waits(range(early, half))

        rows = rows_in[pl.ds(block * many, many)].reshape(count, width)
        for chunk in range(half):
            if chunk == early:

                @pl.when(index == rounds)
                def _():
                    for step in range(early, half):
                        swap_copy(step).wait_recv()
                    keeps[2].start()

            hidden_all = dot_f32(rows, weights[turn, chunk, 0], NT)

            @pl.when(index > 0)
            def _():
                for copy in hidden_copies(index - 1, chunk):
                    copy.wait()

            for spot in tiles(count):
                hidden = hidden_all[spot]
                square = hidden * hidden
                curve = jnp.tanh(hidden * (0.7978845608 + 0.7978845608 * 0.044715 * square))
                upper = 0.5 + 0.5 * curve
                gelu = hidden * upper
                slope = upper + gelu * (1.0 - upper) * (
                    2.0 * 0.7978845608 + 6.0 * 0.7978845608 * 0.044715 * square
                )
                act_buf[chunk, spot] = gelu.astype(jnp.bfloat16)
                slope_buf[chunk, spot] = slope.astype(jnp.bfloat16)
            for copy in hidden_copies(index, chunk):
                copy.start()
        acts = jnp.concatenate([act_buf[chunk] for chunk in range(half)], 1)
        ends = jnp.concatenate([weights[turn, chunk, 1] for chunk in range(half)], 0)
        found = dot_f32(acts, ends, NN)
        here = pl.ds(pl.multiple_of(block * count, 16), count)

        @pl.when(turn == 0)
        def _():
            total[here] = found

        @pl.when(turn == 1)
        def _():
            result = (total[here] + found).astype(jnp.bfloat16)
            for spot in range(many):
                source = block * many + spot
                mine = result[spot * padded : (spot + 1) * padded]
                send_rows[source] = mine
                detail = detail_in[source]
                weight = detail[0:1, :padded] * detail[1:2, :padded]
                shares = jnp.where(image_hot(detail, padded), weight, 0.0)
                pieces = jnp.concatenate(split_three(shares), 0)
                sums = dot_f32(pieces, mine, NN)
                part_ref[source] = (
                    sums[:IMAGE_PAD] + sums[IMAGE_PAD : 2 * IMAGE_PAD] + sums[2 * IMAGE_PAD :]
                )

        @pl.when(index == rounds - 1)
        def _():
            for member in others(at.member, n_experts):
                row_copy(member, at.member).wait_send()
                detail_copy(member, at.member).wait_send()
            for copy in keeps[:2]:
                copy.start()

        return carry

    keeps = [
        pltpu.make_async_copy(rows_in, rows_out, keep_sem.at[1]),
        pltpu.make_async_copy(detail_in, detail_out, keep_sem.at[2]),
        pltpu.make_async_copy(weights, weight_out, keep_sem.at[4]),
        pltpu.make_async_copy(send_rows, y_out, keep_sem.at[3]),
    ]
    lax.fori_loop(0, 2 * rounds, expert_step, 0)
    keeps[3].start()
    for chunk in range(half):
        for copy in hidden_copies(2 * rounds - 1, chunk):
            copy.wait()
    for step in range(half):
        own = team.target(step)[2]
        swap_copy(step).wait_send()

        @pl.when(jnp.logical_not(own))
        def _():
            shard_copy(step).wait_send()

    a_two_copy.wait()
    w_copy.wait()
    for copy in keeps:
        copy.wait()
    for copy in gathers:
        copy.wait_send()


def forward(sizes, n_experts, padded, lengths, slot_mask, picks, ranks, patches, dense, norms, routers, expert_in, expert_out):
    rows_here, span = slot_mask.shape
    tokens, width = patches.shape
    part = expert_in.shape[1]
    mats, rows_own, unused = dense.shape
    tall = max(8, n_experts)
    depth = round_up(mats * rows_own + tall, 16)
    Z, Y, X = QUAD, sizes["g"], sizes["x"]
    half = 2 * sizes["g"]
    lanes = round_up(padded, 128)
    many = max(1, (144 if part % 128 else 576) // padded)
    count = n_experts * padded
    f32, kind = jnp.float32, jnp.bfloat16
    dma = pltpu.SemaphoreType.DMA
    each, parts, two = dma((n_experts,)), dma((half,)), dma((2,))
    by_y, by_x, by_z = dma((Z, Y)), dma((Z, X)), dma((Z,))

    def out(wide, dtype):
        return jax.ShapeDtypeStruct((tokens, wide), dtype)

    hidden = jax.ShapeDtypeStruct((2 * half, count, part), kind)
    rows = (n_experts, padded, width)
    return pl.pallas_call(
        functools.partial(forward_kernel, sizes, n_experts, lengths.shape[1], padded),
        out_shape=(
            jax.ShapeDtypeStruct((mats, width, width), kind), jax.ShapeDtypeStruct((8, width), f32),
            jax.ShapeDtypeStruct((tall, width), f32), out(128, f32),
            out(width, f32), out(width, kind), out(3 * width, kind), out(width, kind), out(width, f32),
            out(width, kind), out(128, f32), out(128, f32),
            jax.ShapeDtypeStruct((IMAGE_PAD, width), f32), jax.ShapeDtypeStruct((8, width), f32),
            jax.ShapeDtypeStruct(rows, kind), jax.ShapeDtypeStruct((n_experts, 8, lanes), f32),
            hidden, hidden, jax.ShapeDtypeStruct(rows, kind),
            jax.ShapeDtypeStruct((n_experts, IMAGE_PAD, width), f32),
            jax.ShapeDtypeStruct((2, half, 2, part, width), kind),
        ),
        in_specs=[whole(pltpu.SMEM)] + [whole()] * 8 + [whole(ANY)] * 2,
        out_specs=(whole(ANY), whole(), whole(), whole()) + (whole(ANY),) * 6 + (whole(),) * 4 + (whole(ANY),) * 5 + (whole(), whole(ANY)),
        scratch_shapes=[
            VMEM((2, Z, X, Y, depth, width), kind), VMEM((mats, width, width), kind), VMEM((2, 2, part, width), kind),
            VMEM((span, width), f32), VMEM((span, width), kind), VMEM((span, 3 * width), kind),
            VMEM((span, width), kind), VMEM((span, width), f32), VMEM((tokens, width), kind),
            VMEM((2, half, 2, part, width), kind), VMEM(rows, kind), VMEM((n_experts, 8, lanes), f32),
            VMEM((8, tokens), f32), VMEM(rows, kind), VMEM((n_experts, 8, lanes), f32),
            VMEM((count, width), f32), VMEM((half, many * padded, part), kind),
            VMEM((half, many * padded, part), kind), dma((5,)), dma((6,)), two,
            parts, parts, parts, parts, each, each, each, each, parts, parts, dma((2, 2)),
            by_z, by_z, by_y, by_y, by_x, by_x, by_x, by_x, by_y, by_y, by_z, by_z,
        ],
        compiler_params=pltpu.CompilerParams(
            collective_id=5, has_side_effects=True, vmem_limit_bytes=62 * MIB
        ),
        cost_estimate=cost(120),
        name="forward",
    )(lengths, lengths, slot_mask, picks.T, ranks, patches, dense, norms, routers, expert_in, expert_out)


def chunk_at(index, half):
    early = half // 2
    step = lax.rem(index, half)
    side = jnp.where(index < half, early, 0)
    return lax.div(step, early) * half + side + lax.rem(step, early)


def expert_backward_kernel(
    sizes, padded, rows_ref, detail_ref, pool_ref, y_ref, slope_ref, act_ref, weight_ref, *refs
):
    at = Place(sizes)
    sources, unused, width = rows_ref.shape
    chunks, unused, part = slope_ref.shape
    half = chunks // 2
    back_ref, gate_ref, *outs = refs[: 2 + half]
    d_hidden, d_rows, send_rows, send_gate, send_grad, got_grad = refs[2 + half : 8 + half]
    own_sem, r_out, r_in, m_out, m_in, g_out, g_in, g_keep = refs[8 + half :]
    many = y_ref.shape[0]
    rounds = sources // many
    step = pl.program_id(0)
    team = others(at.member, sources)

    def row_copy(member, source):
        return send(
            send_rows.at[member], back_ref.at[source], r_out.at[member], r_in.at[source], at.of_member(member)
        )

    def gate_copy(member, source):
        return send(
            send_gate.at[member], gate_ref.at[source], m_out.at[member], m_in.at[source], at.of_member(member)
        )

    def keep_copies():
        return (
            pltpu.make_async_copy(send_rows.at[at.member], back_ref.at[at.member], own_sem.at[0]),
            pltpu.make_async_copy(send_gate.at[at.member], gate_ref.at[at.member], own_sem.at[1]),
        )

    def grad_copy(index):
        return send(
            send_grad.at[index], got_grad.at[index], g_out.at[index], g_in.at[index], at.sibling()
        )

    def out_copy(index):
        return pltpu.make_async_copy(got_grad.at[index], outs[index], g_keep.at[index])

    @pl.when(step == 0)
    def _():
        greet([at.of_member(member) for member in team] + [at.sibling()])

    @pl.when(step < rounds)
    def _():
        block = lax.rem(lax.div(at.member, many) + 1 + step, rounds)
        d_out = []
        for index in range(many):
            source = block * many + index
            detail = detail_ref[source]
            hot = image_hot(detail, padded)
            hots = jnp.where(hot, 1.0, 0.0).astype(jnp.bfloat16)
            pools = jnp.concatenate(split_three(pool_ref[source]), 0)
            wide = dot_f32(jnp.concatenate([hots] * 3, 0), pools, TN)
            lanes = detail.shape[1]
            upright = jnp.concatenate([detail, jnp.zeros((120, lanes), jnp.float32)], 0).T
            gate, pool = upright[:padded, 0:1], upright[:padded, 1:2]
            d_out.append((gate * (pool * wide)).astype(jnp.bfloat16))
            along = dot_f32(pools, y_ref[index], NT)
            along = along[:IMAGE_PAD] + along[IMAGE_PAD : 2 * IMAGE_PAD] + along[2 * IMAGE_PAD :]
            d_gate = jnp.sum(jnp.where(hot, along, 0.0), 0, keepdims=True) * detail[1:2, :padded]
            send_gate[source] = jnp.zeros(detail.shape, jnp.float32)
            send_gate[source, 0:1, :padded] = d_gate
        d_out = jnp.concatenate(d_out, 0)
        count = many * padded
        span = pl.ds(pl.multiple_of(block * count, 16), count)
        d_rows[span] = d_out

        def weight(index, which):
            return weight_ref[index // half, index % half, which]

        for index in range(chunks):
            d_act = dot_f32(d_out, weight(index, 1), NT)
            for spot in tiles(count):
                rows_now = pl.ds(pl.multiple_of(block * count + spot.start, 16), spot.stop - spot.start)
                d_hidden[index, rows_now] = (
                    d_act[spot] * slope_ref[index, spot].astype(jnp.float32)
                ).astype(jnp.bfloat16)
        d_hids = jnp.concatenate([d_hidden[index, span] for index in range(chunks)], 1)
        starts = jnp.concatenate([weight(index, 0) for index in range(chunks)], 0)
        total = dot_f32(d_hids, starts, NN)
        total = total.astype(jnp.bfloat16)
        for index in range(many):
            source = block * many + index
            send_rows[source] = total[index * padded : (index + 1) * padded]

            @pl.when(source != at.member)
            def _():
                row_copy(source, at.member).start()
                gate_copy(source, at.member).start()

            @pl.when(source == at.member)
            def _():
                for copy in keep_copies():
                    copy.start()

    @pl.when(step >= rounds)
    def _():
        index = step - rounds
        chunk = chunk_at(index, half)
        rows = rows_ref[...].reshape(sources * padded, width)
        g_one = dot_f32(d_hidden[chunk], rows, TN)
        g_two = dot_f32(act_ref[0], d_rows[...], TN)

        @pl.when(index < half)
        def _():
            send_grad[index, 0] = g_one.astype(jnp.bfloat16)
            send_grad[index, 1] = g_two.astype(jnp.bfloat16)
            grad_copy(index).start()

        @pl.when(index >= half)
        def _():
            spot = index - half
            grad_copy(spot).wait_recv()
            got_grad[spot, 0] = (got_grad[spot, 0].astype(jnp.float32) + g_one).astype(jnp.bfloat16)
            got_grad[spot, 1] = (got_grad[spot, 1].astype(jnp.float32) + g_two).astype(jnp.bfloat16)

        for spot in range(half):

            @pl.when(index == spot + half)
            def _():
                out_copy(spot).start()

    @pl.when(step == rounds + chunks - 1)
    def _():
        for member in team:
            row_copy(member, member).wait_recv()
            gate_copy(member, member).wait_recv()
        for member in team:
            row_copy(member, at.member).wait_send()
            gate_copy(member, at.member).wait_send()
        for copy in keep_copies():
            copy.wait()
        for spot in range(half):
            grad_copy(spot).wait_send()
            out_copy(spot).wait()


def expert_backward(sizes, rows, details, pools, results, slopes, acts, weights):
    sources, padded, width = rows.shape
    chunks, count, part = acts.shape
    many = max(1, (288 if part % 128 else 576) // padded)
    rounds, half = sources // many, chunks // 2
    lanes = details.shape[2]
    kind = jnp.bfloat16
    dma = pltpu.SemaphoreType.DMA
    each, parts = dma((sources,)), dma((half,))

    def block_of(step):
        member = lax.axis_index("x") * QUAD + lax.axis_index("r")
        return lax.rem(lax.div(member, many) + 1 + jnp.minimum(step, rounds - 1), rounds)

    def chunk_of(step):
        return chunk_at(jnp.maximum(step - rounds, 0), half)

    return pl.pallas_call(
        functools.partial(expert_backward_kernel, sizes, padded),
        grid=(rounds + chunks,),
        out_shape=(
            jax.ShapeDtypeStruct((sources, padded, width), kind),
            jax.ShapeDtypeStruct((sources, 8, lanes), jnp.float32),
        )
        + (jax.ShapeDtypeStruct((2, part, width), kind),) * half,
        in_specs=[
            whole(), whole(), whole(),
            pl.BlockSpec((many, padded, width), lambda i: (block_of(i), 0, 0)),
            pl.BlockSpec((chunks, many * padded, part), lambda i: (0, block_of(i), 0)),
            pl.BlockSpec((1, count, part), lambda i: (chunk_of(i), 0, 0)),
        ]
        + [whole()],
        out_specs=(whole(ANY),) * (2 + half),
        scratch_shapes=[
            VMEM((chunks, count, part), kind),
            VMEM((count, width), kind),
            VMEM((sources, padded, width), kind),
            VMEM((sources, 8, lanes), jnp.float32),
            VMEM((half, 2, part, width), kind),
            VMEM((half, 2, part, width), kind),
            dma((2,)), each, each, each, each, parts, parts, parts,
        ],
        compiler_params=pltpu.CompilerParams(
            collective_id=6, has_side_effects=True, vmem_limit_bytes=62 * MIB
        ),
        cost_estimate=cost(65),
        name="expert_backward",
    )(rows, details, pools, results, slopes, acts, weights)


def dense_backward_kernel(
    sizes, n_experts, images, padded, length_ref, mask_ref, patch_ref, x_zero_ref, a_one_ref, qkv_ref, att_ref,
    x_one_ref, a_two_ref, prob_ref, lse_ref, col_ref, w_ref, gain_ref, router_ref, back_ref, gate_ref,
    pool_ref, imp_ref, third_ref, out_ref, grads, g_norm, d_qkv, d_atts, d_zeros, d_routers
):
    row = pl.program_id(0)
    span, width = x_zero_ref.shape
    mats, rows = grads.shape[0], width // (8 * sizes["g"] * sizes["x"])

    here = pl.ds(pl.multiple_of(row * span, 16), span)

    @pl.when(row == 0)
    def _():
        g_norm[...] = third_ref[...]

    columns = col_ref[...]
    slot_one, slot_two = columns[:, 0:1], columns[:, 1:2]
    count = n_experts * padded
    slot = lax.broadcasted_iota(jnp.int32, (span, count), 1).astype(jnp.float32)
    match = jnp.where((slot == slot_one) | (slot == slot_two), 1.0, 0.0).astype(jnp.bfloat16)
    d_a_two = dot_f32(match, back_ref[...].reshape(count, width), NN)
    lanes = gate_ref.shape[2]
    spot = lax.broadcasted_iota(jnp.int32, (span, lanes), 1)
    inside = spot < padded
    spot = spot.astype(jnp.float32)
    found_one, found_two = jnp.zeros((span, lanes), jnp.float32), jnp.zeros((span, lanes), jnp.float32)
    for expert in range(n_experts):
        line = jnp.broadcast_to(gate_ref[expert, 0:1], (span, lanes))
        found_one = jnp.where(inside & (spot == slot_one - expert * padded), line, found_one)
        found_two = jnp.where(inside & (spot == slot_two - expert * padded), line, found_two)
    d_gate_one = jnp.sum(found_one, 1, keepdims=True)
    d_gate_two = jnp.sum(found_two, 1, keepdims=True)
    lane = lax.broadcasted_iota(jnp.int32, (span, 128), 1)
    number = lane.astype(jnp.float32)
    valid, pool, image = columns[:, 2:3], columns[:, 3:4], columns[:, 4:5]
    head = lax.broadcasted_iota(jnp.int32, (1, 128), 1) < n_experts
    importance = imp_ref[0:1, 0:128]
    centre = jnp.sum(jnp.where(head, importance, 0.0), 1, keepdims=True) / n_experts
    away = jnp.where(head, importance - centre, 0.0)
    spread = jnp.sum(away * away, 1, keepdims=True) / n_experts
    d_imp = aux_weight * (
        2.0 * away / (n_experts * centre * centre)
        - 2.0 * spread / (n_experts * centre * centre * centre)
    )
    d_probs = valid * d_imp
    d_probs = d_probs + jnp.where(number == columns[:, 5:6], d_gate_one, 0.0)
    d_probs = d_probs + jnp.where(number == columns[:, 6:7], d_gate_two, 0.0)
    probs = prob_ref[...]
    d_router = (probs * (d_probs - jnp.sum(probs * d_probs, 1, keepdims=True))).astype(jnp.bfloat16)
    d_routers[here] = d_router
    routers = router_ref[...].astype(jnp.bfloat16)
    if routers.shape[0] < 128:
        routers = jnp.concatenate(
            [routers, jnp.zeros((128 - routers.shape[0], width), jnp.bfloat16)], 0
        )
    d_a_two = d_a_two + dot_f32(d_router, routers, NN)
    scaled, scale = norm_parts(x_one_ref[...])
    g_norm[1:2] += jnp.sum(d_a_two * scaled, 0, keepdims=True)
    g_norm[4:5] += jnp.sum(d_a_two, 0, keepdims=True)
    d_x_one = norm_back(d_a_two, scaled, scale, gain_ref[1:2])
    for index in range(images):
        place = row * images + index
        weight = jnp.where(image == place.astype(jnp.float32), pool, 0.0)
        d_x_one = d_x_one + weight * pool_ref[pl.ds(place, 1)]
    d_att = d_x_one.astype(jnp.bfloat16)
    d_atts[here] = d_att
    d_out = dot_f32(d_att, w_ref[4], NT).astype(jnp.bfloat16)
    open_to = allowed_slots(length_ref, row, images, mask_ref[0], span)
    logs = lse_ref[...]
    for pair in range(width // 128):
        query, key, value = (
            qkv_ref[:, part * width + pair * 128 : part * width + (pair + 1) * 128]
            for part in range(3)
        )
        d_pair = d_out[:, pair * 128 : (pair + 1) * 128]
        found = []
        for side in range(2):
            left = (lane < 64) == (side == 0)
            held = jnp.where(left, query, jnp.zeros_like(query))
            raw = dot_f32(held, key, NT)
            d_held = jnp.where(left, d_pair, jnp.zeros_like(d_pair))
            d_raw = dot_f32(d_held, value, NT)
            chances, d_scores = [], []
            for spot in tiles(span, 64):
                scores = jnp.where(open_to[spot] > 0.0, raw[spot] * 64**-0.5, mask_fill)
                chance = jnp.exp(scores - logs[spot, 2 * pair + side : 2 * pair + side + 1])
                chances.append(chance.astype(jnp.bfloat16))
                d_chance = d_raw[spot]
                d_score = chance * (d_chance - jnp.sum(chance * d_chance, 1, keepdims=True))
                d_scores.append(d_score.astype(jnp.bfloat16))
            d_value = dot_f32(jnp.concatenate(chances, 0), d_pair, TN)
            d_scores = jnp.concatenate(d_scores, 0)
            d_query = dot_f32(d_scores, key, NN) * 64**-0.5
            d_key = dot_f32(d_scores, query, TN) * 64**-0.5
            found.append((d_query, d_key, d_value))
        for part in range(3):
            d_qkv[here, part * width + pair * 128 : part * width + (pair + 1) * 128] = jnp.where(
                lane < 64, found[0][part], found[1][part]
            ).astype(jnp.bfloat16)
    d_a_one = None
    for part in range(3):
        piece = d_qkv[here, part * width : (part + 1) * width]
        found = dot_f32(piece, w_ref[1 + part], NT)
        d_a_one = found if d_a_one is None else d_a_one + found
    scaled, scale = norm_parts(x_zero_ref[...])
    g_norm[0:1] += jnp.sum(d_a_one * scaled, 0, keepdims=True)
    g_norm[3:4] += jnp.sum(d_a_one, 0, keepdims=True)
    d_x_zero = norm_back(d_a_one, scaled, scale, gain_ref[0:1]) + d_x_one
    d_zeros[here] = d_x_zero.astype(jnp.bfloat16)

    @pl.when(row == pl.num_programs(0) - 1)
    def _():
        grads[0] = dot_f32(patch_ref[...], d_zeros[...], TN)
        for part in range(3):
            piece = d_qkv[:, part * width : (part + 1) * width]
            grads[1 + part] = dot_f32(a_one_ref[...], piece, TN)
        grads[4] = dot_f32(att_ref[...], d_atts[...], TN)
        g_router = dot_f32(d_routers[...], a_two_ref[...], TN)
        Z, Y, X = QUAD, sizes["g"], sizes["x"]
        tall = max(8, n_experts)
        norms = g_norm[...]
        if tall > 8:
            norms = jnp.concatenate([norms, jnp.zeros((tall - 8, width), jnp.float32)], 0)
        router_grads = g_router[:tall]
        depth = out_ref.shape[4]
        device = 0
        for z in range(Z):
            for y in range(Y):
                for x in range(X):
                    for c in range(2):
                        spot = slice(device * rows, (device + 1) * rows)
                        blank = jnp.zeros((tall, 128 - rows), jnp.float32)
                        tail = [norms[:, spot], blank, router_grads[:, spot], blank]
                        tail.append(jnp.zeros((tall, width - 256), jnp.float32))
                        pieces = [grads[mat, spot] for mat in range(mats)]
                        pieces.append(jnp.concatenate(tail, 1))
                        left = depth - mats * rows - tall
                        if left:
                            pieces.append(jnp.zeros((left, width), jnp.float32))
                        out_ref[c, z, x, y] = jnp.concatenate(pieces, 0).astype(jnp.bfloat16)
                        device += 1


def dense_backward(
    sizes, n_experts, padded, rows_own, lengths, slot_mask, patches, kept, columns, weights, gains, routers, back,
    gates, pooled, importance, third
):
    rows_here, span = slot_mask.shape
    tokens, width = patches.shape
    mats = weights.shape[0]
    depth = round_up(mats * rows_own + max(8, n_experts), 16)
    x_zero, a_one, qkv, att, x_one, a_two, probs, logs = kept

    def block(wide):
        return pl.BlockSpec((span, wide), lambda i: (i, 0))

    return pl.pallas_call(
        functools.partial(dense_backward_kernel, sizes, n_experts, lengths.shape[1], padded),
        grid=(rows_here,),
        out_shape=jax.ShapeDtypeStruct(
            (2, QUAD, sizes["x"], sizes["g"], depth, width), jnp.bfloat16
        ),
        in_specs=[
            whole(pltpu.SMEM), pl.BlockSpec((1, 1, span), lambda i: (i, 0, 0)), whole(),
            block(width), whole(), block(3 * width), whole(), block(width), whole(),
            block(128), block(128), block(128),
        ]
        + [whole()] * 8,
        out_specs=whole(),
        scratch_shapes=[
            VMEM((mats, width, width), jnp.float32),
            VMEM((8, width), jnp.float32),
            VMEM((tokens, 3 * width), jnp.bfloat16),
            VMEM((tokens, width), jnp.bfloat16),
            VMEM((tokens, width), jnp.bfloat16),
            VMEM((tokens, 128), jnp.bfloat16),
        ],
        compiler_params=pltpu.CompilerParams(vmem_limit_bytes=60 * MIB),
        cost_estimate=cost(50),
        name="dense_backward",
    )(
        lengths, slot_mask[:, None, :], patches, x_zero, a_one, qkv, att, x_one, a_two, probs, logs, columns,
        weights, gains, routers, back, gates, pooled, importance, third,
    )


def shard_moves(n_blocks):
    span = 2 * n_blocks
    moves = []
    for step in step_order(n_blocks):
        pairs = []
        for place in range(QUAD * n_blocks):
            for core in range(2):
                target = (place + step) % span
                src = place * 2 + core
                dst = (target // 2 * QUAD + 2 * core + target % 2) * 2 + place // span
                pairs.append((src, dst))
        moves.append(pairs)
    return moves


def return_experts(parts, n_blocks):
    return [
        lax.ppermute(part, ("g", "r", "c"), [(dst, src) for src, dst in pairs])
        for part, pairs in zip(parts, shard_moves(n_blocks))
    ]


def body(
    patches,
    lengths,
    slot_mask,
    expert_picks,
    priority_rank,
    class_labels,
    dense_weights,
    dense_first,
    dense_second,
    dense_average,
    router_weights,
    router_first,
    router_second,
    router_average,
    norm_params,
    norm_first,
    norm_second,
    norm_average,
    expert_in,
    in_first,
    in_second,
    in_average,
    expert_out,
    out_first,
    out_second,
    out_average,
    head_weights,
    head_first,
    head_second,
    head_average,
):
    n_blocks = lax.axis_size("g")
    sizes = {name: lax.axis_size(name) for name in ALL}
    rows_own, n_experts = router_weights.shape
    rows_here, n_slots_row = slot_mask.shape
    tokens, model_width = patches.shape
    n_images = lengths.shape[0] * lengths.shape[1]
    capacity = (21 * tokens * TOP + 20 * n_experts - 1) // (20 * n_experts)
    padded = round_up(capacity, 16)
    (
        layer_b, gain_rows, router_t, columns,
        x_zero, a_one, qkv, att_out, x_one, a_two, router_probs, logs, pooled, part_importance,
        arrived, details, activated, slope, result, part_pooled, expert_weights
    ) = forward(
        sizes, n_experts, padded, lengths, slot_mask, expert_picks, priority_rank, patches, dense_weights, norm_params,
        router_weights, expert_in, expert_out
    )
    g_head, d_pooled_all, d_pooled, g_norm_three, head_sums, total_importance = head_step(
        sizes,
        n_images,
        part_pooled,
        pooled,
        part_importance,
        gain_rows,
        head_weights,
        class_labels,
    )
    d_back, back_gate, *grads = expert_backward(
        sizes, arrived, details, d_pooled_all, result, slope, activated, expert_weights
    )
    parts = return_experts(grads, n_blocks)
    blocks = dense_backward(
        sizes,
        n_experts,
        padded,
        rows_own,
        lengths,
        slot_mask,
        patches,
        (x_zero, a_one, qkv, att_out, x_one, a_two, router_probs, logs),
        columns,
        layer_b,
        gain_rows,
        router_t,
        d_back,
        back_gate,
        d_pooled,
        total_importance,
        g_norm_three,
    )
    reduced, dense_sums = scatter_dense(sizes, blocks)
    g_one, g_two, totals = finish(
        sizes, n_experts, parts, head_sums, dense_sums, total_importance
    )
    n_dense = dense_weights.shape[0] * rows_own
    g_layers = reduced[:n_dense].reshape(-1, rows_own, model_width)
    g_norms = reduced[n_dense : n_dense + 6, :rows_own]
    g_router = reduced[n_dense : n_dense + n_experts, 128 : 128 + rows_own].T
    importance = total_importance[0, :n_experts]
    loss_value, grad_norm, factor = totals[0, 0], totals[1, 0], totals[2, 0]
    dense_out = adam_update(
        dense_weights, dense_first, dense_second, dense_average, g_layers, factor, base_rate
    )
    router_out = adam_update(
        router_weights, router_first, router_second, router_average, g_router, factor, base_rate
    )
    norm_out = adam_update(
        norm_params, norm_first, norm_second, norm_average, g_norms, factor, norm_rate
    )
    in_out = adam_update(expert_in, in_first, in_second, in_average, g_one, factor, base_rate)
    out_out = adam_update(expert_out, out_first, out_second, out_average, g_two, factor, base_rate)
    head_out = adam_update(
        head_weights, head_first, head_second, head_average, g_head, factor, base_rate
    )
    return (
        loss_value,
        importance,
        grad_norm,
        *dense_out,
        *router_out,
        *norm_out,
        *in_out,
        *out_out,
        *head_out,
    )


def solution(mesh):
    n_dp, n_expert = mesh.shape["dp"], mesh.shape["expert"]
    shaped = mesh.devices.reshape(n_dp // QUAD, QUAD, n_expert // 2, 2)
    fine = Mesh(shaped, ALL)
    rows = P(ALL, None)
    dense = P(None, ALL, None)
    norms = P(None, ALL)
    experts = P(("x", "c"), ("g", "r"), None)
    placed = (rows,) * 6 + (dense,) * 4 + (rows,) * 4 + (norms,) * 4 + (experts,) * 8 + (rows,) * 4
    results = (
        (P(),) * 3 + (dense,) * 4 + (rows,) * 4 + (norms,) * 4 + (experts,) * 8 + (rows,) * 4
    )
    return jax.shard_map(body, mesh=fine, in_specs=placed, out_specs=results, check_vma=False)
```

```python
import functools
import math

import jax
import jax.numpy as jnp
from jax import lax
from jax.experimental import pallas as pl
from jax.experimental.pallas import tpu as pltpu
from jax.sharding import Mesh
from jax.sharding import PartitionSpec as P

HEADS = 12
TOP = 2
STEP_COUNT = 10
QUAD = 4

high_prec = lax.Precision.HIGHEST
eps_norm = 1e-06
aux_weight = 0.01
clip_limit = 1.0
base_rate = 0.05
norm_rate = 0.5
beta_first = 0.9
beta_second = 0.999
weight_decay = 0.1
polyak_decay = 0.7
adam_eps = 1e-08
mask_fill = -1e30

ALL = ("g", "r", "x", "c")
MEMBERS = ("x", "r")


def adam_update(weight, first_state, second_state, average_state, gradient, factor, step_rate):
    clipped = gradient * factor
    first_new = beta_first * first_state + (1.0 - beta_first) * clipped
    second_new = beta_second * second_state + (1.0 - beta_second) * clipped * clipped
    first_hat = first_new / (1.0 - beta_first**STEP_COUNT)
    second_hat = second_new / (1.0 - beta_second**STEP_COUNT)
    weight_new = weight - step_rate * (
        first_hat / (jnp.sqrt(second_hat) + adam_eps) + weight_decay * weight
    )
    average_new = polyak_decay * average_state + (1.0 - polyak_decay) * weight_new
    return (weight_new, first_new, second_new, average_new)


MESH_ID = pl.DeviceIdType.MESH
VMEM = pltpu.VMEM
ANY = pl.ANY
MIB = 1 << 20


def cost(microseconds):
    return pl.CostEstimate(flops=int(microseconds * 1.15e9), bytes_accessed=0, transcendentals=0)


def whole(space=None):
    return pl.BlockSpec(memory_space=space or VMEM)


def round_up(value, step):
    return (value + step - 1) // step * step


class Place:
    def __init__(self, sizes):
        self.G, self.X = sizes["g"], sizes["x"]
        self.Z, self.Y = QUAD, sizes["g"]
        self.chips = self.Z * self.Y * self.X
        spot = lax.axis_index("g") * QUAD + lax.axis_index("r")
        self.z, self.y = lax.div(spot, self.Y), lax.rem(spot, self.Y)
        self.x, self.c = lax.axis_index("x"), lax.axis_index("c")
        self.g, self.r = lax.axis_index("g"), lax.axis_index("r")
        self.chip = spot * self.X + self.x
        self.member = self.x * QUAD + self.r

    def at(self, z=None, y=None, x=None, c=None):
        spot = (self.z if z is None else z) * self.Y + (self.y if y is None else y)
        return {
            "g": lax.div(spot, QUAD),
            "r": lax.rem(spot, QUAD),
            "x": self.x if x is None else x,
            "c": self.c if c is None else c,
        }

    def of_chip(self, chip):
        spot = lax.div(chip, self.X)
        return {
            "g": lax.div(spot, QUAD),
            "r": lax.rem(spot, QUAD),
            "x": lax.rem(chip, self.X),
            "c": self.c,
        }

    def of_member(self, member):
        return {
            "g": self.g,
            "r": lax.rem(member, QUAD),
            "x": lax.div(member, QUAD),
            "c": self.c,
        }

    def sibling(self):
        return self.at(c=1 - self.c)


def greet(peers):
    barrier = pltpu.get_barrier_semaphore()
    for peer in peers:
        pl.semaphore_signal(barrier, inc=1, device_id=peer, device_id_type=MESH_ID)
    pl.semaphore_wait(barrier, len(peers))


def send(src, dst, send_sem, recv_sem, peer):
    return pltpu.make_async_remote_copy(
        src_ref=src,
        dst_ref=dst,
        send_sem=send_sem,
        recv_sem=recv_sem,
        device_id=peer,
        device_id_type=MESH_ID,
    )


def others(me, count):
    return [lax.rem(me + step, count) for step in range(1, count)]


def grid_peers(at):
    peers = [at.at(z=z) for z in others(at.z, at.Z)]
    peers += [at.at(y=y) for y in others(at.y, at.Y)]
    peers += [at.at(x=x) for x in others(at.x, at.X)]
    return peers + [at.sibling()]


def gather_dense(at, rows, mats, land, w_ref, sems, started, beside, idle):
    Z, Y, X = at.Z, at.Y, at.X
    depth = land.shape[4]
    cut = depth // 2 // 16 * 16
    first, second = pl.ds(0, cut), pl.ds(cut, depth - cut)
    z_out, z_in, ya_out, ya_in, xb_out, xb_in, xa_out, xa_in, yb_out, yb_in, c_out, c_in = sems
    mine = land.at[at.c, at.z, at.x, at.y]

    def begin(copy):
        copy.start()
        started.append(copy)

    order = [at.z] + [lax.rem(at.z + k, Z) for k in (1, 3, 2)]
    for z in order[1:]:
        begin(send(mine, mine, z_out.at[z], z_in.at[at.z], at.at(z=z)))

    def one(z):
        part = land.at[at.c, z, at.x, at.y]
        for y in others(at.y, Y):
            begin(send(part.at[first], part.at[first], ya_out.at[z, y], ya_in.at[z, at.y], at.at(y=y)))
        for x in others(at.x, X):
            begin(send(part.at[second], part.at[second], xb_out.at[z, x], xb_in.at[z, at.x], at.at(x=x)))

    def two(z):
        for y in others(at.y, Y):
            part = land.at[at.c, z, at.x, y, first]
            send(part, part, ya_out.at[z, y], ya_in.at[z, y], at.at(y=y)).wait_recv()
        line = land.at[at.c, z, at.x, :, first]
        for x in others(at.x, X):
            begin(send(line, line, xa_out.at[z, x], xa_in.at[z, at.x], at.at(x=x)))
        for x in others(at.x, X):
            part = land.at[at.c, z, x, at.y, second]
            send(part, part, xb_out.at[z, x], xb_in.at[z, x], at.at(x=x)).wait_recv()
        line = land.at[at.c, z, :, at.y, second]
        for y in others(at.y, Y):
            begin(send(line, line, yb_out.at[z, y], yb_in.at[z, at.y], at.at(y=y)))

    def three(z):
        for x in others(at.x, X):
            line = land.at[at.c, z, x, :, first]
            send(line, line, xa_out.at[z, x], xa_in.at[z, x], at.at(x=x)).wait_recv()
        for y in others(at.y, Y):
            line = land.at[at.c, z, :, y, second]
            send(line, line, yb_out.at[z, y], yb_in.at[z, y], at.at(y=y)).wait_recv()
        plane = land.at[at.c, z]
        begin(send(plane, plane, c_out.at[z], c_in.at[z], at.sibling()))

    def place(z):
        plane = land.at[1 - at.c, z]
        send(plane, plane, c_out.at[z], c_in.at[z], at.sibling()).wait_recv()
        group = 16 // math.gcd(16, rows)
        cores = [(c, x, y) for y in range(Y) for x in range(X) for c in range(2)]
        for start in range(0, len(cores), group):
            spot = pl.multiple_of((z * len(cores) + start) * rows, 16)
            for mat in range(mats):
                w_ref[mat, pl.ds(spot, group * rows)] = jnp.concatenate(
                    [
                        land[c, z, x, y, mat * rows : (mat + 1) * rows]
                        for c, x, y in cores[start : start + group]
                    ],
                    0,
                )

    for step in range(Z + 2):
        if step < Z:
            if step > 0:
                z = order[step]
                part = land.at[at.c, z, at.x, at.y]
                send(part, part, z_out.at[z], z_in.at[z], at.at(z=z)).wait_recv()
            one(order[step])
        if step == 0:
            beside()
        if step == Z - 1:
            idle()
        if 0 <= step - 1 < Z:
            two(order[step - 1])
        if 0 <= step - 2 < Z:
            three(order[step - 2])
        if 0 <= step - 3 < Z:
            place(order[step - 3])
    place(order[Z - 1])


def gather_small(at, rows, mats, count, land, gain_ref, router_ref):
    chips = [(z, y, x) for z in range(at.Z) for y in range(at.Y) for x in range(at.X)]
    cores = [(c, z, x, y) for z, y, x in chips for c in range(2)]
    base = mats * rows
    tails = [land[spot][base : base + count].astype(jnp.float32) for spot in cores]
    gain_ref[...] = jnp.concatenate([tail[:8, :rows] for tail in tails], 1)
    router_ref[...] = jnp.concatenate([tail[:, 128 : 128 + rows] for tail in tails], 1)


def total_square(value):
    return jnp.sum(jnp.sum(value * value, 0, keepdims=True), 1, keepdims=True)


def scatter_kernel(sizes, g_ref, out_ref, square_ref, hold, sib, got_xa, got_yb, got_ya, got_xb, got_z, *sems):
    at = Place(sizes)
    Z, Y, X = at.Z, at.Y, at.X
    depth = g_ref.shape[4]
    cut = depth // 2 // 16 * 16
    first, second = pl.ds(0, cut), pl.ds(cut, depth - cut)
    c_out, c_in, xa_out, xa_in, yb_out, yb_in, ya_out, ya_in, xb_out, xb_in, z_out, z_in = sems
    greet(grid_peers(at))
    started = []

    def begin(copy):
        copy.start()
        started.append(copy)

    wide = lambda value: value.astype(jnp.float32)
    order = [lax.rem(at.z + k, Z) for k in (2, 1, 3)] + [at.z]
    for z in order:
        begin(send(g_ref.at[1 - at.c, z], sib.at[z], c_out.at[z], c_in.at[z], at.sibling()))

    def one(z):
        send(sib.at[z], sib.at[z], c_out.at[z], c_in.at[z], at.sibling()).wait_recv()
        hold[z] = (wide(g_ref[at.c, z]) + wide(sib[z])).astype(jnp.bfloat16)
        for x in others(at.x, X):
            begin(send(hold.at[z, x, :, first], got_xa.at[z, at.x], xa_out.at[z, x], xa_in.at[z, at.x], at.at(x=x)))
        for y in others(at.y, Y):
            begin(send(hold.at[z, :, y, second], got_yb.at[z, at.y], yb_out.at[z, y], yb_in.at[z, at.y], at.at(y=y)))

    def two(z):
        total = wide(hold[z, at.x, :, first])
        for x in others(at.x, X):
            send(got_xa.at[z, x], got_xa.at[z, x], xa_out.at[z, x], xa_in.at[z, x], at.at(x=x)).wait_recv()
            total = total + wide(got_xa[z, x])
        hold[z, at.x, :, first] = total.astype(jnp.bfloat16)
        for y in others(at.y, Y):
            begin(send(hold.at[z, at.x, y, first], got_ya.at[z, at.y], ya_out.at[z, y], ya_in.at[z, at.y], at.at(y=y)))
        total = wide(hold[z, :, at.y, second])
        for y in others(at.y, Y):
            send(got_yb.at[z, y], got_yb.at[z, y], yb_out.at[z, y], yb_in.at[z, y], at.at(y=y)).wait_recv()
            total = total + wide(got_yb[z, y])
        hold[z, :, at.y, second] = total.astype(jnp.bfloat16)
        for x in others(at.x, X):
            begin(send(hold.at[z, x, at.y, second], got_xb.at[z, at.x], xb_out.at[z, x], xb_in.at[z, at.x], at.at(x=x)))

    def three(z, last):
        total = wide(hold[z, at.x, at.y, first])
        for y in others(at.y, Y):
            send(got_ya.at[z, y], got_ya.at[z, y], ya_out.at[z, y], ya_in.at[z, y], at.at(y=y)).wait_recv()
            total = total + wide(got_ya[z, y])
        rest = wide(hold[z, at.x, at.y, second])
        for x in others(at.x, X):
            send(got_xb.at[z, x], got_xb.at[z, x], xb_out.at[z, x], xb_in.at[z, x], at.at(x=x)).wait_recv()
            rest = rest + wide(got_xb[z, x])
        if last:
            out_ref[first] = total
            out_ref[second] = rest
            return
        mine = hold.at[z, at.x, at.y]
        mine[first] = total.astype(jnp.bfloat16)
        mine[second] = rest.astype(jnp.bfloat16)
        begin(send(mine, got_z.at[at.z], z_out.at[z], z_in.at[at.z], at.at(z=z)))

    for step in range(Z + 2):
        if step < Z:
            one(order[step])
        if 0 <= step - 1 < Z:
            two(order[step - 1])
        if 0 <= step - 2 < Z:
            three(order[step - 2], step - 2 == Z - 1)
    for z in order[:-1]:
        send(got_z.at[z], got_z.at[z], z_out.at[z], z_in.at[z], at.at(z=z)).wait_recv()
        out_ref[...] += wide(got_z[z])
    square_ref[...] = jnp.broadcast_to(total_square(out_ref[...]), square_ref.shape)
    for copy in started:
        copy.wait_send()


def scatter_dense(sizes, blocks):
    unused, Z, X, Y, depth, width = blocks.shape
    dma = pltpu.SemaphoreType.DMA
    by_y, by_x, by_z = dma((Z, Y)), dma((Z, X)), dma((Z,))
    cut = depth // 2 // 16 * 16
    half = jnp.bfloat16
    return pl.pallas_call(
        functools.partial(scatter_kernel, sizes),
        out_shape=(
            jax.ShapeDtypeStruct((depth, width), jnp.float32),
            jax.ShapeDtypeStruct((8, 128), jnp.float32),
        ),
        in_specs=[whole()],
        out_specs=(whole(), whole()),
        scratch_shapes=[
            VMEM((Z, X, Y, depth, width), half),
            VMEM((Z, X, Y, depth, width), half),
            VMEM((Z, X, Y, cut, width), half),
            VMEM((Z, Y, X, depth - cut, width), half),
            VMEM((Z, Y, cut, width), half),
            VMEM((Z, X, depth - cut, width), half),
            VMEM((Z, depth, width), half),
        ]
        + [by_z, by_z, by_x, by_x, by_y, by_y, by_y, by_y, by_x, by_x, by_z, by_z],
        compiler_params=pltpu.CompilerParams(
            collective_id=2, has_side_effects=True, vmem_limit_bytes=28 * MIB
        ),
        cost_estimate=cost(45),
        name="scatter_dense",
    )(blocks)


def finish_kernel(sizes, n_experts, head_ref, dense_ref, imp_ref, *refs):
    at = Place(sizes)
    many = len(refs) - 7
    parts = refs[:many]
    first_ref, second_ref, out_ref, land, own, out_sem, in_sem = refs[many:]
    count = 2 * at.chips
    me = at.chip * 2 + at.c
    ids = others(me, count)

    def peer(device):
        spot = at.of_chip(lax.div(device, 2))
        spot["c"] = lax.rem(device, 2)
        return spot

    greet([peer(device) for device in ids])
    place = lax.rem(at.g * QUAD + at.r, 2)
    square = dense_ref[0:1, 0:1] + head_ref[1:2, 0:1]
    for parity in range(2):
        expert = place if parity == 0 else 1 - place
        for index, ref in enumerate((first_ref, second_ref)):
            total = None
            for step in range(parity * many // 2, (parity + 1) * many // 2):
                found = parts[step][index].astype(jnp.float32)
                total = found if total is None else total + found
            ref[expert] = total
            square = square + total_square(total)
    line = lax.broadcasted_iota(jnp.int32, own.shape, 0)
    own[...] = jnp.where(line == 0, head_ref[0:1, 0:1], jnp.where(line == 1, square, 0.0))
    land[me] = own[...]
    copies = [send(own, land.at[me], out_sem.at[d], in_sem.at[me], peer(d)) for d in ids]
    for copy in copies:
        copy.start()
    importance = imp_ref[0:1, 0:128]
    head = lax.broadcasted_iota(jnp.int32, (1, 128), 1) < n_experts
    centre = jnp.sum(jnp.where(head, importance, 0.0), 1, keepdims=True) / n_experts
    away = jnp.where(head, importance - centre, 0.0)
    spread = jnp.sum(away * away, 1, keepdims=True) / n_experts
    balance = aux_weight * spread / (centre * centre)
    for d in ids:
        send(land.at[d], land.at[d], out_sem.at[d], in_sem.at[d], peer(d)).wait_recv()
    sums = jnp.sum(land[...], 0)
    norm = jnp.sqrt(sums[1:2, 0:1])
    factor = jnp.minimum(1.0, clip_limit / norm)
    loss = sums[0:1, 0:1] + balance
    out_ref[...] = jnp.where(line == 0, loss, jnp.where(line == 1, norm, factor))
    for copy in copies:
        copy.wait_send()


def finish(sizes, n_experts, parts, head_sums, dense_sums, importance):
    devices = sizes["g"] * QUAD * sizes["x"] * 2
    unused, rows, width = parts[0].shape
    dma = pltpu.SemaphoreType.DMA
    grads = jax.ShapeDtypeStruct((2, rows, width), jnp.float32)
    return pl.pallas_call(
        functools.partial(finish_kernel, sizes, n_experts),
        out_shape=(grads, grads, jax.ShapeDtypeStruct((8, 128), jnp.float32)),
        in_specs=[whole()] * (3 + len(parts)),
        out_specs=(whole(),) * 3,
        scratch_shapes=[
            VMEM((devices, 8, 128), jnp.float32),
            VMEM((8, 128), jnp.float32),
            dma((devices,)),
            dma((devices,)),
        ],
        compiler_params=pltpu.CompilerParams(
            collective_id=3, has_side_effects=True, vmem_limit_bytes=20 * MIB
        ),
        cost_estimate=cost(10),
        name="finish",
    )(head_sums, dense_sums, importance, *parts)


IMAGE_PAD = 16


def split_three(value):
    high = value.astype(jnp.bfloat16)
    rest = value - high.astype(jnp.float32)
    middle = rest.astype(jnp.bfloat16)
    return high, middle, (rest - middle.astype(jnp.float32)).astype(jnp.bfloat16)


def dot_f32(left, right, dims):
    return lax.dot_general(left, right, (dims, ((), ())), preferred_element_type=jnp.float32)


NN = ((1,), (0,))
NT = ((1,), (1,))
TN = ((0,), (0,))


def norm_parts(values):
    centre = values - jnp.mean(values, -1, keepdims=True)
    spread = jnp.mean(centre * centre, -1, keepdims=True)
    scale = lax.rsqrt(spread + eps_norm)
    return centre * scale, scale


def norm_back(d_out, scaled, scale, gain):
    pulled = d_out * gain
    return scale * (
        pulled
        - jnp.mean(pulled, -1, keepdims=True)
        - scaled * jnp.mean(pulled * scaled, -1, keepdims=True)
    )


def head_kernel(
    sizes, images, part_ref, own_ref, imp_ref, gain_ref, head_ref, label_ref,
    g_head_ref, d_pool_ref, own_d_ref, g_norm_ref, sums_ref, total_imp_ref,
    in_part, rows, d_rows, d_sib, d_sum, d_in, head_b, labels, d_logits, *sems
):
    at = Place(sizes)
    chips, members = at.chips, QUAD * at.X
    devices = 2 * chips
    p_out, p_in, r_out, r_in, s_out, s_in, d_out, d_in_sem, b_out, b_in = sems
    width = own_ref.shape[1]
    same_core = others(at.chip, chips)
    greet([at.of_chip(chip) for chip in same_core] + [at.sibling()])
    started = []

    def begin(copy):
        copy.start()
        started.append(copy)

    team = others(at.member, members)
    for member in team:
        begin(send(part_ref.at[member], in_part.at[at.member], p_out.at[member], p_in.at[at.member], at.of_member(member)))
    in_part[at.member] = part_ref[at.member]
    head_b[...] = head_ref[...].astype(jnp.bfloat16)
    wide = devices * IMAGE_PAD
    spot = lax.broadcasted_iota(jnp.int32, (label_ref.shape[1], wide), 1)
    given = lax.broadcasted_iota(jnp.int32, (label_ref.shape[1], wide), 0)
    image = lax.rem(spot, IMAGE_PAD)
    device = lax.rem(lax.div(spot, IMAGE_PAD), chips) * 2 + lax.div(spot, IMAGE_PAD * chips)
    chosen = ((device * images + image == given) & (image < images)).astype(jnp.bfloat16)
    labels[...] = dot_f32(label_ref[...].astype(jnp.float32).astype(jnp.bfloat16), chosen, NN).astype(jnp.bfloat16)
    for member in team:
        send(in_part.at[member], in_part.at[member], p_out.at[member], p_in.at[member], at.of_member(member)).wait_recv()
    pooled = own_ref[...] + jnp.sum(in_part[...], 0)
    scaled, scale = norm_parts(pooled)
    gain, shift = gain_ref[2:3], gain_ref[5:6]
    a_three = scaled * gain + shift
    row = lax.broadcasted_iota(jnp.int32, (IMAGE_PAD, width), 0)
    block = jnp.where(row < images, a_three, 0.0)
    pieces = split_three(imp_ref[0:1])
    for index, piece in enumerate(pieces):
        block = jnp.where(row == images + index, piece.astype(jnp.float32), block)
    rows[at.c, at.chip] = block.astype(jnp.bfloat16)
    mine = rows.at[at.c, at.chip]
    for chip in same_core:
        begin(send(mine, mine, r_out.at[chip], r_in.at[at.chip], at.of_chip(chip)))
    for chip in same_core:
        part = rows.at[at.c, chip]
        send(part, part, r_out.at[chip], r_in.at[chip], at.of_chip(chip)).wait_recv()
    begin(send(rows.at[at.c], rows.at[at.c], s_out.at[0], s_in.at[0], at.sibling()))
    send(rows.at[1 - at.c], rows.at[1 - at.c], s_out.at[0], s_in.at[0], at.sibling()).wait_recv()
    gathered = rows[...].reshape(wide, width)
    in_block = lax.rem(lax.broadcasted_iota(jnp.int32, (wide, width), 0), IMAGE_PAD)
    total = jnp.sum(jnp.where(in_block >= images, gathered.astype(jnp.float32), 0.0), 0, keepdims=True)
    total_imp_ref[...] = jnp.broadcast_to(total, total_imp_ref.shape)
    gathered = jnp.where(in_block < images, gathered.astype(jnp.float32), 0.0).astype(jnp.bfloat16)
    logits = dot_f32(head_b[...], gathered, NT)
    image = lax.rem(lax.broadcasted_iota(jnp.int32, logits.shape, 1), IMAGE_PAD)
    count = devices * images
    target = labels[...].astype(jnp.float32)
    power = jnp.exp(-jnp.abs(logits))
    loss = jnp.maximum(logits, 0.0) + jnp.log1p(power) - target * logits
    loss = jnp.sum(jnp.where(image < images, loss, 0.0), 1, keepdims=True)
    loss = jnp.sum(loss, 0, keepdims=True) / count
    chance = jnp.where(logits >= 0.0, 1.0, power) / (1.0 + power)
    d_logits[...] = jnp.where(image < images, (chance - target) / count, 0.0).astype(jnp.bfloat16)
    partial = dot_f32(d_logits[...], head_b[...], TN)
    d_rows[...] = partial.reshape(d_rows.shape).astype(jnp.bfloat16)
    begin(send(d_rows.at[1 - at.c], d_sib, s_out.at[1], s_in.at[1], at.sibling()))
    g_head = dot_f32(d_logits[...], gathered, NN)
    g_head_ref[...] = g_head
    line = lax.broadcasted_iota(jnp.int32, sums_ref.shape, 0)
    sums_ref[...] = jnp.where(line == 0, loss, jnp.where(line == 1, total_square(g_head), 0.0))
    send(d_sib, d_sib, s_out.at[1], s_in.at[1], at.sibling()).wait_recv()
    d_sum[...] = (d_rows[at.c].astype(jnp.float32) + d_sib[...].astype(jnp.float32)).astype(jnp.bfloat16)
    for chip in same_core:
        begin(send(d_sum.at[chip], d_in.at[at.chip], d_out.at[chip], d_in_sem.at[at.chip], at.of_chip(chip)))
    d_in[at.chip] = d_sum[at.chip]
    for chip in same_core:
        send(d_in.at[chip], d_in.at[chip], d_out.at[chip], d_in_sem.at[chip], at.of_chip(chip)).wait_recv()
    d_norm = jnp.sum(d_in[...].astype(jnp.float32), 0)
    d_norm = jnp.where(row < images, d_norm, 0.0)
    d_pooled = norm_back(d_norm, scaled, scale, gain)
    d_pooled = jnp.where(row < images, d_pooled, 0.0)
    d_gain = jnp.sum(d_norm * scaled, 0, keepdims=True)
    d_shift = jnp.sum(d_norm, 0, keepdims=True)
    line = lax.broadcasted_iota(jnp.int32, g_norm_ref.shape, 0)
    g_norm_ref[...] = jnp.where(line == 2, d_gain, jnp.where(line == 5, d_shift, 0.0))
    own_d_ref[...] = d_pooled
    d_pool_ref[at.member] = d_pooled
    mine = d_pool_ref.at[at.member]
    for member in team:
        begin(send(own_d_ref, mine, b_out.at[member], b_in.at[at.member], at.of_member(member)))
    for member in team:
        part = d_pool_ref.at[member]
        send(part, part, b_out.at[member], b_in.at[member], at.of_member(member)).wait_recv()
    for copy in started:
        copy.wait_send()


def head_step(sizes, images, part, own, imp, gains, head, label):
    members = QUAD * sizes["x"]
    chips = members * sizes["g"]
    classes, width = head.shape
    wide = 2 * chips * IMAGE_PAD
    dma = pltpu.SemaphoreType.DMA
    by_member, by_chip = dma((members,)), dma((chips,))
    f32, half = jnp.float32, jnp.bfloat16
    blocks = (chips, IMAGE_PAD, width)
    return pl.pallas_call(
        functools.partial(head_kernel, sizes, images),
        out_shape=(
            jax.ShapeDtypeStruct((classes, width), f32),
            jax.ShapeDtypeStruct((members, IMAGE_PAD, width), f32),
            jax.ShapeDtypeStruct((IMAGE_PAD, width), f32),
            jax.ShapeDtypeStruct((8, width), f32),
            jax.ShapeDtypeStruct((8, 128), f32),
            jax.ShapeDtypeStruct((8, width), f32),
        ),
        in_specs=[whole()] * 6,
        out_specs=(whole(),) * 6,
        scratch_shapes=[
            VMEM((members, IMAGE_PAD, width), f32),
            VMEM((2, *blocks), half),
            VMEM((2, *blocks), half),
            VMEM(blocks, half),
            VMEM(blocks, half),
            VMEM(blocks, half),
            VMEM((classes, width), half),
            VMEM((classes, wide), half),
            VMEM((classes, wide), half),
        ]
        + [by_member, by_member, by_chip, by_chip, dma((2,)), dma((2,)), by_chip, by_chip]
        + [by_member, by_member],
        compiler_params=pltpu.CompilerParams(
            collective_id=4, has_side_effects=True, vmem_limit_bytes=(56 if wide > 1024 else 28) * MIB
        ),
        cost_estimate=cost(42),
        name="head_step",
    )(part, own, imp, gains, head, label)


def route_math(per_image, n_experts, capacity, padded, pick_ref, rank_ref, mask_ref, length_ref):
    rows_here, span = mask_ref.shape
    tokens = rows_here * span
    valid = mask_ref[...].astype(jnp.float32)
    lengths = length_ref[...]
    position = lax.broadcasted_iota(jnp.int32, (rows_here, span), 1)
    segment = jnp.zeros((rows_here, span), jnp.int32)
    bound = jnp.zeros((rows_here, 1), jnp.int32)
    for image in range(per_image):
        bound = bound + lengths[:, image : image + 1]
        segment = segment + jnp.where(position >= bound, 1, 0)
    pool = jnp.zeros_like(valid)
    for image in range(per_image):
        member = jnp.where(segment == image, valid, 0.0)
        pool = pool + member / jnp.maximum(jnp.sum(member, 1, keepdims=True), 1.0)
    line = lax.broadcasted_iota(jnp.int32, (rows_here, span), 0)
    image = (segment + per_image * line).astype(jnp.float32)

    def flat(value):
        return jnp.concatenate([value[i : i + 1] for i in range(rows_here)], 1)

    rank_row = rank_ref[...].astype(jnp.float32)
    picks = pick_ref[...].astype(jnp.float32)
    table = jnp.concatenate([flat(valid), flat(pool), flat(image), rank_row, picks], 0)
    table = jnp.concatenate([table, jnp.zeros((122, tokens), jnp.float32)], 0).T
    valid_col, pool_col, image_col, rank_col, pick_one, pick_two = (
        table[:, i : i + 1] for i in range(6)
    )
    lane = lax.broadcasted_iota(jnp.int32, (tokens, 128), 1)
    in_first, in_second = lane < n_experts, (lane >= n_experts) & (lane < 2 * n_experts)
    number = lane.astype(jnp.float32)
    hot = jnp.where(in_first & (pick_one == number), valid_col, 0.0)
    hot = hot + jnp.where(in_second & (pick_two == number - n_experts), valid_col, 0.0)
    shifted = jnp.where(in_second & (pick_one == number - n_experts), valid_col, 0.0)
    before = jnp.where(rank_row < rank_col, 1.0, 0.0).astype(jnp.bfloat16)
    ahead = dot_f32(before, hot.astype(jnp.bfloat16), NN) + jnp.sum(shifted, 0, keepdims=True)
    counted = hot * ahead
    pos_one = jnp.sum(jnp.where(in_first, counted, 0.0), 1, keepdims=True)
    pos_two = jnp.sum(jnp.where(in_second, counted, 0.0), 1, keepdims=True)

    def place(pick, pos):
        kept = (valid_col > 0.0) & (pos < capacity)
        return jnp.where(kept, pick * padded + pos, -1.0)

    columns = (
        place(pick_one, pos_one),
        place(pick_two, pos_two),
        valid_col,
        pool_col,
        image_col,
        pick_one,
        pick_two,
    )
    result = jnp.zeros((tokens, 128), jnp.float32)
    for index, column in enumerate(columns):
        result = jnp.where(lane == index, column, result)
    return result


def allowed_slots(lengths, row, images, valid_row, span):
    query = lax.broadcasted_iota(jnp.int32, (span, span), 0)
    key = lax.broadcasted_iota(jnp.int32, (span, span), 1)
    bound = 0
    query_seg, key_seg = jnp.zeros((span, span), jnp.int32), jnp.zeros((span, span), jnp.int32)
    for image in range(images):
        bound = bound + lengths[row, image]
        query_seg = query_seg + jnp.where(query >= bound, 1, 0)
        key_seg = key_seg + jnp.where(key >= bound, 1, 0)
    allowed = (query_seg == key_seg) & ((valid_row > 0) | (query == key))
    return jnp.where(allowed, 1.0, 0.0)


TILE = 32


def tiles(count, size=TILE):
    return [slice(start, min(start + size, count)) for start in range(0, count, size)]


def step_order(blocks):
    return [*range(0, 2 * blocks, 2), *range(1, 2 * blocks, 2)]


class Team:
    def __init__(self, at):
        self.at, self.span = at, 2 * at.G
        self.spot = at.g * QUAD + at.r

    def target(self, step):
        at = self.at
        chosen = lax.rem(self.spot + step_order(at.G)[step], self.span)
        block, index = lax.div(chosen, 2), lax.rem(chosen, 2)
        core = lax.div(self.spot, self.span)
        r = 2 * at.c + index
        own = (block == at.g) & (r == at.r) & (core == at.c)
        return {"g": block, "r": r, "x": at.x, "c": core}, index, own

    def peers(self):
        at = self.at
        count = 2 * at.G * QUAD
        me = self.spot * 2 + at.c
        line = []
        for device in others(me, count):
            spot = lax.div(device, 2)
            line.append(
                {"g": lax.div(spot, QUAD), "r": lax.rem(spot, QUAD), "x": at.x, "c": lax.rem(device, 2)}
            )
        for x in others(at.x, at.X):
            line += [{"g": at.g, "r": r, "x": x, "c": at.c} for r in range(QUAD)]
        return line


def image_hot(detail, padded):
    image = detail[2:3, :padded]
    line = lax.broadcasted_iota(jnp.int32, (IMAGE_PAD, padded), 0).astype(jnp.float32)
    return line == image


def forward_kernel(
    sizes, n_experts, images, padded,
    length_ref, lengths_ref, mask_ref, pick_ref, rank_ref, patch_ref, dense_ref, norm_ref, routing_ref, in_ref, out_ref,
    w_keep, gain_ref, router_ref, col_ref, x_zero_out, a_one_out, qkv_out, att_out, x_one_out, a_two_out, prob_ref, lse_ref, pool_ref, imp_ref,
    rows_out, detail_out, act_out, slope_out, y_out, part_ref, weight_out,
    land, w_ref, shard_ref, x_zero_buf, a_one_buf, qkv_buf, att_buf, x_one_buf, a_two_ref, weights, send_rows, send_detail, places,
    rows_in, detail_in, total, act_buf, slope_buf, dense_sem, keep_sem, own_sem,
    w_out, w_in, s_out, s_in, r_out, r_in, m_out, m_in, act_sem, slope_sem, cast_sem, *gather_sems
):
    at = Place(sizes)
    team = Team(at)
    half = weights.shape[1]
    early = half // 2
    rows_here, span = mask_ref.shape
    width = patch_ref.shape[1]
    tokens = rows_here * span
    mats, rows_own, unused = dense_ref.shape
    tall = router_ref.shape[0]
    capacity = (21 * tokens * TOP + 20 * n_experts - 1) // (20 * n_experts)

    part_rows = shard_ref.shape[2]
    casts = [
        pltpu.make_async_copy(ref.at[expert], total.at[pl.ds((index * 2 + expert) * part_rows, part_rows)], cast_sem.at[index, expert])
        for index, ref in enumerate((in_ref, out_ref))
        for expert in range(2)
    ]
    for copy in casts:
        copy.start()
    depth = land.shape[4]
    routing = routing_ref[...]
    routing = jnp.concatenate([routing, jnp.zeros((n_experts, 128 - rows_own), jnp.float32)], 1)
    if n_experts < tall:
        routing = jnp.concatenate([routing, jnp.zeros((tall - n_experts, 128), jnp.float32)], 0)
    norms = norm_ref[...]
    norms = jnp.concatenate([norms, jnp.zeros((norms.shape[0], 128 - rows_own), jnp.float32)], 1)
    norms = jnp.concatenate([norms, jnp.zeros((tall - norms.shape[0], 128), jnp.float32)], 0)
    tail = jnp.concatenate(
        [norms, routing, jnp.zeros((tall, width - 256), jnp.float32)], 1
    )
    block = jnp.concatenate([dense_ref[...].reshape(mats * rows_own, width), tail], 0)
    if block.shape[0] < depth:
        block = jnp.concatenate(
            [block, jnp.zeros((depth - block.shape[0], width), jnp.float32)], 0
        )
    land[at.c, at.z, at.x, at.y] = block.astype(jnp.bfloat16)
    greet(team.peers() + grid_peers(at))

    def spot_of(step, side=0):
        return step // early, side * early + step % early

    def swap_copy(step):
        return send(
            weights.at[spot_of(step)], weights.at[spot_of(step, 1)], s_out.at[step], s_in.at[step], at.sibling()
        )

    def shard_copy(step):
        device, index, own = team.target(step)
        return send(
            shard_ref.at[index], weights.at[spot_of(step)], w_out.at[step], w_in.at[step], device
        )

    def shard_own(step):
        device, index, own = team.target(step)
        return pltpu.make_async_copy(shard_ref.at[index], weights.at[spot_of(step)], w_in.at[step])

    def shard_starts(steps):
        for step in steps:
            own = team.target(step)[2]

            @pl.when(own)
            def _():
                shard_own(step).start()

            @pl.when(jnp.logical_not(own))
            def _():
                shard_copy(step).start()

    def shard_waits(steps):
        for step in steps:
            own = team.target(step)[2]

            @pl.when(own)
            def _():
                shard_own(step).wait()

            @pl.when(jnp.logical_not(own))
            def _():
                shard_copy(step).wait_recv()

            swap_copy(step).start()

    def beside_gather():
        col_ref[...] = route_math(
            images, n_experts, capacity, padded, pick_ref, rank_ref, mask_ref, lengths_ref
        )
        for copy in casts:
            copy.wait()
        for index in range(2):
            for expert in range(2):
                here = pl.ds((index * 2 + expert) * part_rows, part_rows)
                shard_ref[expert, index] = total[here].astype(jnp.bfloat16)

    gathers = []
    gather_dense(
        at, rows_own, mats, land, w_ref, gather_sems, gathers, beside_gather, lambda: shard_starts(range(early))
    )
    shard_starts(range(early, half))
    gather_small(at, rows_own, mats, tall, land, gain_ref, router_ref)
    w_copy = pltpu.make_async_copy(w_ref, w_keep, keep_sem.at[5])
    w_copy.start()

    dense = (
        (x_zero_buf, x_zero_out), (a_one_buf, a_one_out), (qkv_buf, qkv_out), (att_buf, att_out), (x_one_buf, x_one_out),
    )

    def dense_copy(row, index):
        here = pl.ds(pl.multiple_of(row * span, 16), span)
        buf, out = dense[index]
        return pltpu.make_async_copy(buf, out.at[here], dense_sem.at[index])

    def keep_dense(row, index, value):
        @pl.when(row > 0)
        def _():
            dense_copy(row - 1, index).wait()

        dense[index][0][...] = value
        dense_copy(row, index).start()

    pool_ref[...] = jnp.zeros_like(pool_ref)
    imp_ref[...] = jnp.zeros_like(imp_ref)
    routers = router_ref[...].astype(jnp.bfloat16)
    if routers.shape[0] < 128:
        routers = jnp.concatenate(
            [routers, jnp.zeros((128 - routers.shape[0], width), jnp.bfloat16)], 0
        )
    lane = lax.broadcasted_iota(jnp.int32, (span, 128), 1)

    def dense_row(row, carry):
        here = pl.ds(pl.multiple_of(row * span, 16), span)
        x_zero = dot_f32(patch_ref[here], w_ref[0], NN)
        keep_dense(row, 0, x_zero)
        a_one = (norm_parts(x_zero)[0] * gain_ref[0:1] + gain_ref[3:4]).astype(jnp.bfloat16)
        keep_dense(row, 1, a_one)

        @pl.when(row > 0)
        def _():
            dense_copy(row - 1, 2).wait()

        for part in range(3):
            qkv_buf[:, part * width : (part + 1) * width] = dot_f32(
                a_one, w_ref[1 + part], NN
            ).astype(jnp.bfloat16)
        dense_copy(row, 2).start()
        open_to = allowed_slots(length_ref, row, images, mask_ref[pl.ds(row, 1)], span)
        logs = jnp.zeros((span, 128), jnp.float32)

        @pl.when(row > 0)
        def _():
            dense_copy(row - 1, 3).wait()

        for pair in range(width // 128):
            query, key, value = (
                qkv_buf[:, part * width + pair * 128 : part * width + (pair + 1) * 128]
                for part in range(3)
            )
            outs = []
            for side in range(2):
                held = jnp.where((lane < 64) == (side == 0), query, jnp.zeros_like(query))
                raw = dot_f32(held, key, NT)
                probs, sums = [], []
                for spot in tiles(span, 64):
                    scores = jnp.where(open_to[spot] > 0.0, raw[spot] * 64**-0.5, mask_fill)
                    top = jnp.max(scores, 1, keepdims=True)
                    powers = jnp.exp(scores - top)
                    whole_sum = jnp.sum(powers, 1, keepdims=True)
                    probs.append((powers * (1.0 / whole_sum)).astype(jnp.bfloat16))
                    sums.append(top + jnp.log(whole_sum))
                outs.append(dot_f32(jnp.concatenate(probs, 0), value, NN))
                logs = jnp.where(lane == 2 * pair + side, jnp.concatenate(sums, 0), logs)
            att_buf[:, pair * 128 : (pair + 1) * 128] = jnp.where(
                lane < 64, outs[0], outs[1]
            ).astype(jnp.bfloat16)
        lse_ref[here] = logs
        dense_copy(row, 3).start()
        x_one = x_zero + dot_f32(att_buf[...], w_ref[4], NN)
        keep_dense(row, 4, x_one)
        a_two = (norm_parts(x_one)[0] * gain_ref[1:2] + gain_ref[4:5]).astype(jnp.bfloat16)
        a_two_ref[here] = a_two
        logits = jnp.where(lane < n_experts, dot_f32(a_two, routers, NT), mask_fill)
        powers = jnp.exp(logits - jnp.max(logits, 1, keepdims=True))
        probs = powers / jnp.sum(powers, 1, keepdims=True)
        prob_ref[here] = probs
        columns = col_ref[here]
        valid, pool, image = columns[:, 2:3], columns[:, 3:4], columns[:, 4:5]
        imp_ref[0:1, 0:128] += jnp.sum(probs * valid, 0, keepdims=True)
        line = lax.broadcasted_iota(jnp.int32, pool_ref.shape, 0)
        for index in range(images):
            number = row * images + index
            weight = jnp.where(image == number.astype(jnp.float32), pool, 0.0)
            pooled = jnp.sum(x_one * weight, 0, keepdims=True)
            pool_ref[...] = jnp.where(line == number, pooled, pool_ref[...])
        return carry

    lax.fori_loop(0, rows_here, dense_row, 0)

    columns = col_ref[...]
    places[...] = columns.T[:8]
    def rows_of(member):
        slots = lax.broadcasted_iota(jnp.int32, (padded, tokens), 0) + member * padded
        slots = slots.astype(jnp.float32)
        match = (slots == places[0:1]) | (slots == places[1:2])
        match = jnp.where(match, 1.0, 0.0).astype(jnp.bfloat16)
        return dot_f32(match, a_two_ref[...], NN).astype(jnp.bfloat16)

    def row_copy(member, source):
        return send(
            send_rows.at[member], rows_in.at[source], r_out.at[member], r_in.at[source], at.of_member(member)
        )

    def detail_copy(member, source):
        return send(
            send_detail.at[member], detail_in.at[source], m_out.at[member], m_in.at[source], at.of_member(member)
        )

    def dispatch_step(index, carry):
        member = lax.rem(at.member + index, n_experts)
        send_rows[member] = rows_of(member)
        row_copy(member, at.member).start()
        return carry

    lax.fori_loop(1, n_experts, dispatch_step, 0)
    lane = lax.broadcasted_iota(jnp.int32, (tokens, 128), 1)
    kind, expert = lax.div(lane, n_experts), lax.rem(lane, n_experts).astype(jnp.float32)
    slot_lane = lax.broadcasted_iota(jnp.int32, (tokens, send_detail.shape[2]), 1).astype(jnp.float32)
    pool, image = columns[:, 3:4], columns[:, 4:5]
    details = None
    for choice in range(2):
        slot, pick = columns[:, choice : choice + 1], columns[:, 5 + choice : 6 + choice]
        hot = (expert == pick) & (slot >= 0.0)
        gate = jnp.sum(jnp.where(hot & (kind == 0), prob_ref[...], 0.0), 1, keepdims=True)
        values = jnp.zeros((tokens, 128), jnp.float32)
        pieces = [*split_three(gate), *split_three(pool), image]
        for index, piece in enumerate(pieces):
            values = jnp.where(kind == index, piece.astype(jnp.float32), values)
        values = jnp.where(hot, values, 0.0).astype(jnp.bfloat16)
        spot = jnp.where(slot >= 0.0, slot - pick * padded, -1.0)
        chosen = jnp.where(spot == slot_lane, 1.0, 0.0).astype(jnp.bfloat16)
        found = dot_f32(values, chosen, TN)
        details = found if details is None else details + found
    n = n_experts
    gates = details[0:n] + details[n : 2 * n] + details[2 * n : 3 * n]
    pools = details[3 * n : 4 * n] + details[4 * n : 5 * n] + details[5 * n : 6 * n]
    numbers = details[6 * n : 7 * n]
    for index in range(n):
        for spot, value in enumerate((gates, pools, numbers)):
            send_detail[index, spot : spot + 1] = value[index : index + 1]
        send_detail[index, 3:8] = jnp.zeros((5, send_detail.shape[2]), jnp.float32)

    for member in others(at.member, n_experts):
        detail_copy(member, at.member).start()
    rows_in[at.member] = rows_of(at.member)
    detail_in[at.member] = send_detail[at.member]
    a_two_copy = pltpu.make_async_copy(a_two_ref, a_two_out, keep_sem.at[0])
    a_two_copy.start()
    for index in range(len(dense)):
        dense_copy(rows_here - 1, index).wait()

    shard_waits(range(early))
    for step in range(early):
        swap_copy(step).wait_recv()

    many = act_buf.shape[1] // padded
    count = many * padded
    rounds = n_experts // many

    def hidden_copies(index, chunk):
        block, turn = block_of(index), lax.div(index, rounds)
        here = pl.ds(pl.multiple_of(block * count, 16), count)
        there = turn * half + chunk
        return (
            pltpu.make_async_copy(act_buf.at[chunk], act_out.at[there, here], act_sem.at[chunk]),
            pltpu.make_async_copy(slope_buf.at[chunk], slope_out.at[there, here], slope_sem.at[chunk]),
        )

    def block_of(index):
        return lax.rem(lax.div(at.member, many) + index, rounds)

    def expert_step(index, carry):
        turn = lax.div(index, rounds)
        block = block_of(index)

        @pl.when(turn == 0)
        def _():
            for spot in range(many):
                source = block * many + spot

                @pl.when(source != at.member)
                def _():
                    row_copy(source, source).wait_recv()
                    detail_copy(source, source).wait_recv()

        @pl.when(index == rounds)
        def _():
            shard_waits(range(early, half))

        rows = rows_in[pl.ds(block * many, many)].reshape(count, width)
        for chunk in range(half):
            if chunk == early:

                @pl.when(index == rounds)
                def _():
                    for step in range(early, half):
                        swap_copy(step).wait_recv()
                    keeps[2].start()

            hidden_all = dot_f32(rows, weights[turn, chunk, 0], NT)

            @pl.when(index > 0)
            def _():
                for copy in hidden_copies(index - 1, chunk):
                    copy.wait()

            for spot in tiles(count):
                hidden = hidden_all[spot]
                square = hidden * hidden
                curve = jnp.tanh(hidden * (0.7978845608 + 0.7978845608 * 0.044715 * square))
                upper = 0.5 + 0.5 * curve
                gelu = hidden * upper
                slope = upper + gelu * (1.0 - upper) * (
                    2.0 * 0.7978845608 + 6.0 * 0.7978845608 * 0.044715 * square
                )
                act_buf[chunk, spot] = gelu.astype(jnp.bfloat16)
                slope_buf[chunk, spot] = slope.astype(jnp.bfloat16)
            for copy in hidden_copies(index, chunk):
                copy.start()
        acts = jnp.concatenate([act_buf[chunk] for chunk in range(half)], 1)
        ends = jnp.concatenate([weights[turn, chunk, 1] for chunk in range(half)], 0)
        found = dot_f32(acts, ends, NN)
        here = pl.ds(pl.multiple_of(block * count, 16), count)

        @pl.when(turn == 0)
        def _():
            total[here] = found

        @pl.when(turn == 1)
        def _():
            result = (total[here] + found).astype(jnp.bfloat16)
            for spot in range(many):
                source = block * many + spot
                mine = result[spot * padded : (spot + 1) * padded]
                send_rows[source] = mine
                detail = detail_in[source]
                weight = detail[0:1, :padded] * detail[1:2, :padded]
                shares = jnp.where(image_hot(detail, padded), weight, 0.0)
                pieces = jnp.concatenate(split_three(shares), 0)
                sums = dot_f32(pieces, mine, NN)
                part_ref[source] = (
                    sums[:IMAGE_PAD] + sums[IMAGE_PAD : 2 * IMAGE_PAD] + sums[2 * IMAGE_PAD :]
                )

        @pl.when(index == rounds - 1)
        def _():
            for member in others(at.member, n_experts):
                row_copy(member, at.member).wait_send()
                detail_copy(member, at.member).wait_send()
            for copy in keeps[:2]:
                copy.start()

        return carry

    keeps = [
        pltpu.make_async_copy(rows_in, rows_out, keep_sem.at[1]),
        pltpu.make_async_copy(detail_in, detail_out, keep_sem.at[2]),
        pltpu.make_async_copy(weights, weight_out, keep_sem.at[4]),
        pltpu.make_async_copy(send_rows, y_out, keep_sem.at[3]),
    ]
    lax.fori_loop(0, 2 * rounds, expert_step, 0)
    keeps[3].start()
    for chunk in range(half):
        for copy in hidden_copies(2 * rounds - 1, chunk):
            copy.wait()
    for step in range(half):
        own = team.target(step)[2]
        swap_copy(step).wait_send()

        @pl.when(jnp.logical_not(own))
        def _():
            shard_copy(step).wait_send()

    a_two_copy.wait()
    w_copy.wait()
    for copy in keeps:
        copy.wait()
    for copy in gathers:
        copy.wait_send()


def forward(sizes, n_experts, padded, lengths, slot_mask, picks, ranks, patches, dense, norms, routers, expert_in, expert_out):
    rows_here, span = slot_mask.shape
    tokens, width = patches.shape
    part = expert_in.shape[1]
    mats, rows_own, unused = dense.shape
    tall = max(8, n_experts)
    depth = round_up(mats * rows_own + tall, 16)
    Z, Y, X = QUAD, sizes["g"], sizes["x"]
    half = 2 * sizes["g"]
    lanes = round_up(padded, 128)
    many = max(1, (144 if part % 128 else 576) // padded)
    count = n_experts * padded
    f32, kind = jnp.float32, jnp.bfloat16
    dma = pltpu.SemaphoreType.DMA
    each, parts, two = dma((n_experts,)), dma((half,)), dma((2,))
    by_y, by_x, by_z = dma((Z, Y)), dma((Z, X)), dma((Z,))

    def out(wide, dtype):
        return jax.ShapeDtypeStruct((tokens, wide), dtype)

    hidden = jax.ShapeDtypeStruct((2 * half, count, part), kind)
    rows = (n_experts, padded, width)
    return pl.pallas_call(
        functools.partial(forward_kernel, sizes, n_experts, lengths.shape[1], padded),
        out_shape=(
            jax.ShapeDtypeStruct((mats, width, width), kind), jax.ShapeDtypeStruct((8, width), f32),
            jax.ShapeDtypeStruct((tall, width), f32), out(128, f32),
            out(width, f32), out(width, kind), out(3 * width, kind), out(width, kind), out(width, f32),
            out(width, kind), out(128, f32), out(128, f32),
            jax.ShapeDtypeStruct((IMAGE_PAD, width), f32), jax.ShapeDtypeStruct((8, width), f32),
            jax.ShapeDtypeStruct(rows, kind), jax.ShapeDtypeStruct((n_experts, 8, lanes), f32),
            hidden, hidden, jax.ShapeDtypeStruct(rows, kind),
            jax.ShapeDtypeStruct((n_experts, IMAGE_PAD, width), f32),
            jax.ShapeDtypeStruct((2, half, 2, part, width), kind),
        ),
        in_specs=[whole(pltpu.SMEM)] + [whole()] * 8 + [whole(ANY)] * 2,
        out_specs=(whole(ANY), whole(), whole(), whole()) + (whole(ANY),) * 6 + (whole(),) * 4 + (whole(ANY),) * 5 + (whole(), whole(ANY)),
        scratch_shapes=[
            VMEM((2, Z, X, Y, depth, width), kind), VMEM((mats, width, width), kind), VMEM((2, 2, part, width), kind),
            VMEM((span, width), f32), VMEM((span, width), kind), VMEM((span, 3 * width), kind),
            VMEM((span, width), kind), VMEM((span, width), f32), VMEM((tokens, width), kind),
            VMEM((2, half, 2, part, width), kind), VMEM(rows, kind), VMEM((n_experts, 8, lanes), f32),
            VMEM((8, tokens), f32), VMEM(rows, kind), VMEM((n_experts, 8, lanes), f32),
            VMEM((count, width), f32), VMEM((half, many * padded, part), kind),
            VMEM((half, many * padded, part), kind), dma((5,)), dma((6,)), two,
            parts, parts, parts, parts, each, each, each, each, parts, parts, dma((2, 2)),
            by_z, by_z, by_y, by_y, by_x, by_x, by_x, by_x, by_y, by_y, by_z, by_z,
        ],
        compiler_params=pltpu.CompilerParams(
            collective_id=5, has_side_effects=True, vmem_limit_bytes=62 * MIB
        ),
        cost_estimate=cost(120),
        name="forward",
    )(lengths, lengths, slot_mask, picks.T, ranks, patches, dense, norms, routers.T, expert_in, expert_out)


def chunk_at(index, half):
    early = half // 2
    step = lax.rem(index, half)
    side = jnp.where(index < half, early, 0)
    return lax.div(step, early) * half + side + lax.rem(step, early)


def expert_backward_kernel(
    sizes, padded, rows_ref, detail_ref, pool_ref, y_ref, slope_ref, act_ref, weight_ref, *refs
):
    at = Place(sizes)
    sources, unused, width = rows_ref.shape
    chunks, unused, part = slope_ref.shape
    half = chunks // 2
    back_ref, gate_ref, *outs = refs[: 2 + half]
    d_hidden, d_rows, send_rows, send_gate, send_grad, got_grad = refs[2 + half : 8 + half]
    own_sem, r_out, r_in, m_out, m_in, g_out, g_in, g_keep = refs[8 + half :]
    many = y_ref.shape[0]
    rounds = sources // many
    step = pl.program_id(0)
    team = others(at.member, sources)

    def row_copy(member, source):
        return send(
            send_rows.at[member], back_ref.at[source], r_out.at[member], r_in.at[source], at.of_member(member)
        )

    def gate_copy(member, source):
        return send(
            send_gate.at[member], gate_ref.at[source], m_out.at[member], m_in.at[source], at.of_member(member)
        )

    def keep_copies():
        return (
            pltpu.make_async_copy(send_rows.at[at.member], back_ref.at[at.member], own_sem.at[0]),
            pltpu.make_async_copy(send_gate.at[at.member], gate_ref.at[at.member], own_sem.at[1]),
        )

    def grad_copy(index):
        return send(
            send_grad.at[index], got_grad.at[index], g_out.at[index], g_in.at[index], at.sibling()
        )

    def out_copy(index):
        return pltpu.make_async_copy(got_grad.at[index], outs[index], g_keep.at[index])

    @pl.when(step == 0)
    def _():
        greet([at.of_member(member) for member in team] + [at.sibling()])

    @pl.when(step < rounds)
    def _():
        block = lax.rem(lax.div(at.member, many) + 1 + step, rounds)
        d_out = []
        for index in range(many):
            source = block * many + index
            detail = detail_ref[source]
            hot = image_hot(detail, padded)
            hots = jnp.where(hot, 1.0, 0.0).astype(jnp.bfloat16)
            pools = jnp.concatenate(split_three(pool_ref[source]), 0)
            wide = dot_f32(jnp.concatenate([hots] * 3, 0), pools, TN)
            lanes = detail.shape[1]
            upright = jnp.concatenate([detail, jnp.zeros((120, lanes), jnp.float32)], 0).T
            gate, pool = upright[:padded, 0:1], upright[:padded, 1:2]
            d_out.append((gate * (pool * wide)).astype(jnp.bfloat16))
            along = dot_f32(pools, y_ref[index], NT)
            along = along[:IMAGE_PAD] + along[IMAGE_PAD : 2 * IMAGE_PAD] + along[2 * IMAGE_PAD :]
            d_gate = jnp.sum(jnp.where(hot, along, 0.0), 0, keepdims=True) * detail[1:2, :padded]
            send_gate[source] = jnp.zeros(detail.shape, jnp.float32)
            send_gate[source, 0:1, :padded] = d_gate
        d_out = jnp.concatenate(d_out, 0)
        count = many * padded
        span = pl.ds(pl.multiple_of(block * count, 16), count)
        d_rows[span] = d_out

        def weight(index, which):
            return weight_ref[index // half, index % half, which]

        for index in range(chunks):
            d_act = dot_f32(d_out, weight(index, 1), NT)
            for spot in tiles(count):
                rows_now = pl.ds(pl.multiple_of(block * count + spot.start, 16), spot.stop - spot.start)
                d_hidden[index, rows_now] = (
                    d_act[spot] * slope_ref[index, spot].astype(jnp.float32)
                ).astype(jnp.bfloat16)
        d_hids = jnp.concatenate([d_hidden[index, span] for index in range(chunks)], 1)
        starts = jnp.concatenate([weight(index, 0) for index in range(chunks)], 0)
        total = dot_f32(d_hids, starts, NN)
        total = total.astype(jnp.bfloat16)
        for index in range(many):
            source = block * many + index
            send_rows[source] = total[index * padded : (index + 1) * padded]

            @pl.when(source != at.member)
            def _():
                row_copy(source, at.member).start()
                gate_copy(source, at.member).start()

            @pl.when(source == at.member)
            def _():
                for copy in keep_copies():
                    copy.start()

    @pl.when(step >= rounds)
    def _():
        index = step - rounds
        chunk = chunk_at(index, half)
        rows = rows_ref[...].reshape(sources * padded, width)
        g_one = dot_f32(d_hidden[chunk], rows, TN)
        g_two = dot_f32(act_ref[0], d_rows[...], TN)

        @pl.when(index < half)
        def _():
            send_grad[index, 0] = g_one.astype(jnp.bfloat16)
            send_grad[index, 1] = g_two.astype(jnp.bfloat16)
            grad_copy(index).start()

        @pl.when(index >= half)
        def _():
            spot = index - half
            grad_copy(spot).wait_recv()
            got_grad[spot, 0] = (got_grad[spot, 0].astype(jnp.float32) + g_one).astype(jnp.bfloat16)
            got_grad[spot, 1] = (got_grad[spot, 1].astype(jnp.float32) + g_two).astype(jnp.bfloat16)

        for spot in range(half):

            @pl.when(index == spot + half)
            def _():
                out_copy(spot).start()

    @pl.when(step == rounds + chunks - 1)
    def _():
        for member in team:
            row_copy(member, member).wait_recv()
            gate_copy(member, member).wait_recv()
        for member in team:
            row_copy(member, at.member).wait_send()
            gate_copy(member, at.member).wait_send()
        for copy in keep_copies():
            copy.wait()
        for spot in range(half):
            grad_copy(spot).wait_send()
            out_copy(spot).wait()


def expert_backward(sizes, rows, details, pools, results, slopes, acts, weights):
    sources, padded, width = rows.shape
    chunks, count, part = acts.shape
    many = max(1, (288 if part % 128 else 576) // padded)
    rounds, half = sources // many, chunks // 2
    lanes = details.shape[2]
    kind = jnp.bfloat16
    dma = pltpu.SemaphoreType.DMA
    each, parts = dma((sources,)), dma((half,))

    def block_of(step):
        member = lax.axis_index("x") * QUAD + lax.axis_index("r")
        return lax.rem(lax.div(member, many) + 1 + jnp.minimum(step, rounds - 1), rounds)

    def chunk_of(step):
        return chunk_at(jnp.maximum(step - rounds, 0), half)

    return pl.pallas_call(
        functools.partial(expert_backward_kernel, sizes, padded),
        grid=(rounds + chunks,),
        out_shape=(
            jax.ShapeDtypeStruct((sources, padded, width), kind),
            jax.ShapeDtypeStruct((sources, 8, lanes), jnp.float32),
        )
        + (jax.ShapeDtypeStruct((2, part, width), kind),) * half,
        in_specs=[
            whole(), whole(), whole(),
            pl.BlockSpec((many, padded, width), lambda i: (block_of(i), 0, 0)),
            pl.BlockSpec((chunks, many * padded, part), lambda i: (0, block_of(i), 0)),
            pl.BlockSpec((1, count, part), lambda i: (chunk_of(i), 0, 0)),
        ]
        + [whole()],
        out_specs=(whole(ANY),) * (2 + half),
        scratch_shapes=[
            VMEM((chunks, count, part), kind),
            VMEM((count, width), kind),
            VMEM((sources, padded, width), kind),
            VMEM((sources, 8, lanes), jnp.float32),
            VMEM((half, 2, part, width), kind),
            VMEM((half, 2, part, width), kind),
            dma((2,)), each, each, each, each, parts, parts, parts,
        ],
        compiler_params=pltpu.CompilerParams(
            collective_id=6, has_side_effects=True, vmem_limit_bytes=62 * MIB
        ),
        cost_estimate=cost(65),
        name="expert_backward",
    )(rows, details, pools, results, slopes, acts, weights)


def dense_backward_kernel(
    sizes, n_experts, images, padded, length_ref, mask_ref, patch_ref, x_zero_ref, a_one_ref, qkv_ref, att_ref,
    x_one_ref, a_two_ref, prob_ref, lse_ref, col_ref, w_ref, gain_ref, router_ref, back_ref, gate_ref,
    pool_ref, imp_ref, third_ref, out_ref, grads, g_router, g_norm, d_qkv
):
    row = pl.program_id(0)
    span, width = x_zero_ref.shape
    mats, rows = grads.shape[0], width // (8 * sizes["g"] * sizes["x"])

    @pl.when(row == 0)
    def _():
        grads[...] = jnp.zeros_like(grads)
        g_router[...] = jnp.zeros_like(g_router)
        g_norm[...] = third_ref[...]

    columns = col_ref[...]
    slot_one, slot_two = columns[:, 0:1], columns[:, 1:2]
    count = n_experts * padded
    slot = lax.broadcasted_iota(jnp.int32, (span, count), 1).astype(jnp.float32)
    match = jnp.where((slot == slot_one) | (slot == slot_two), 1.0, 0.0).astype(jnp.bfloat16)
    d_a_two = dot_f32(match, back_ref[...].reshape(count, width), NN)
    lanes = gate_ref.shape[2]
    spot = lax.broadcasted_iota(jnp.int32, (span, lanes), 1)
    inside = spot < padded
    spot = spot.astype(jnp.float32)
    found_one, found_two = jnp.zeros((span, lanes), jnp.float32), jnp.zeros((span, lanes), jnp.float32)
    for expert in range(n_experts):
        line = jnp.broadcast_to(gate_ref[expert, 0:1], (span, lanes))
        found_one = jnp.where(inside & (spot == slot_one - expert * padded), line, found_one)
        found_two = jnp.where(inside & (spot == slot_two - expert * padded), line, found_two)
    d_gate_one = jnp.sum(found_one, 1, keepdims=True)
    d_gate_two = jnp.sum(found_two, 1, keepdims=True)
    lane = lax.broadcasted_iota(jnp.int32, (span, 128), 1)
    number = lane.astype(jnp.float32)
    valid, pool, image = columns[:, 2:3], columns[:, 3:4], columns[:, 4:5]
    head = lax.broadcasted_iota(jnp.int32, (1, 128), 1) < n_experts
    importance = imp_ref[0:1, 0:128]
    centre = jnp.sum(jnp.where(head, importance, 0.0), 1, keepdims=True) / n_experts
    away = jnp.where(head, importance - centre, 0.0)
    spread = jnp.sum(away * away, 1, keepdims=True) / n_experts
    d_imp = aux_weight * (
        2.0 * away / (n_experts * centre * centre)
        - 2.0 * spread / (n_experts * centre * centre * centre)
    )
    d_probs = valid * d_imp
    d_probs = d_probs + jnp.where(number == columns[:, 5:6], d_gate_one, 0.0)
    d_probs = d_probs + jnp.where(number == columns[:, 6:7], d_gate_two, 0.0)
    probs = prob_ref[...]
    d_router = (probs * (d_probs - jnp.sum(probs * d_probs, 1, keepdims=True))).astype(jnp.bfloat16)
    g_router[...] += dot_f32(d_router, a_two_ref[...], TN)
    routers = router_ref[...].astype(jnp.bfloat16)
    if routers.shape[0] < 128:
        routers = jnp.concatenate(
            [routers, jnp.zeros((128 - routers.shape[0], width), jnp.bfloat16)], 0
        )
    d_a_two = d_a_two + dot_f32(d_router, routers, NN)
    scaled, scale = norm_parts(x_one_ref[...])
    g_norm[1:2] += jnp.sum(d_a_two * scaled, 0, keepdims=True)
    g_norm[4:5] += jnp.sum(d_a_two, 0, keepdims=True)
    d_x_one = norm_back(d_a_two, scaled, scale, gain_ref[1:2])
    for index in range(images):
        place = row * images + index
        weight = jnp.where(image == place.astype(jnp.float32), pool, 0.0)
        d_x_one = d_x_one + weight * pool_ref[pl.ds(place, 1)]
    d_att = d_x_one.astype(jnp.bfloat16)
    grads[4] += dot_f32(att_ref[...], d_att, TN)
    d_out = dot_f32(d_att, w_ref[4], NT).astype(jnp.bfloat16)
    open_to = allowed_slots(length_ref, row, images, mask_ref[pl.ds(row, 1)], span)
    logs = lse_ref[...]
    for pair in range(width // 128):
        query, key, value = (
            qkv_ref[:, part * width + pair * 128 : part * width + (pair + 1) * 128]
            for part in range(3)
        )
        d_pair = d_out[:, pair * 128 : (pair + 1) * 128]
        found = []
        for side in range(2):
            left = (lane < 64) == (side == 0)
            held = jnp.where(left, query, jnp.zeros_like(query))
            raw = dot_f32(held, key, NT)
            d_held = jnp.where(left, d_pair, jnp.zeros_like(d_pair))
            d_raw = dot_f32(d_held, value, NT)
            chances, d_scores = [], []
            for spot in tiles(span, 64):
                scores = jnp.where(open_to[spot] > 0.0, raw[spot] * 64**-0.5, mask_fill)
                chance = jnp.exp(scores - logs[spot, 2 * pair + side : 2 * pair + side + 1])
                chances.append(chance.astype(jnp.bfloat16))
                d_chance = d_raw[spot]
                d_score = chance * (d_chance - jnp.sum(chance * d_chance, 1, keepdims=True))
                d_scores.append(d_score.astype(jnp.bfloat16))
            d_value = dot_f32(jnp.concatenate(chances, 0), d_pair, TN)
            d_scores = jnp.concatenate(d_scores, 0)
            d_query = dot_f32(d_scores, key, NN) * 64**-0.5
            d_key = dot_f32(d_scores, query, TN) * 64**-0.5
            found.append((d_query, d_key, d_value))
        for part in range(3):
            d_qkv[:, part * width + pair * 128 : part * width + (pair + 1) * 128] = jnp.where(
                lane < 64, found[0][part], found[1][part]
            ).astype(jnp.bfloat16)
    d_a_one = None
    for part in range(3):
        piece = d_qkv[:, part * width : (part + 1) * width]
        grads[1 + part] += dot_f32(a_one_ref[...], piece, TN)
        found = dot_f32(piece, w_ref[1 + part], NT)
        d_a_one = found if d_a_one is None else d_a_one + found
    scaled, scale = norm_parts(x_zero_ref[...])
    g_norm[0:1] += jnp.sum(d_a_one * scaled, 0, keepdims=True)
    g_norm[3:4] += jnp.sum(d_a_one, 0, keepdims=True)
    d_x_zero = norm_back(d_a_one, scaled, scale, gain_ref[0:1]) + d_x_one
    grads[0] += dot_f32(patch_ref[...], d_x_zero.astype(jnp.bfloat16), TN)

    @pl.when(row == pl.num_programs(0) - 1)
    def _():
        Z, Y, X = QUAD, sizes["g"], sizes["x"]
        tall = max(8, n_experts)
        norms = g_norm[...]
        if tall > 8:
            norms = jnp.concatenate([norms, jnp.zeros((tall - 8, width), jnp.float32)], 0)
        router_grads = g_router[:tall]
        depth = out_ref.shape[4]
        device = 0
        for z in range(Z):
            for y in range(Y):
                for x in range(X):
                    for c in range(2):
                        spot = slice(device * rows, (device + 1) * rows)
                        blank = jnp.zeros((tall, 128 - rows), jnp.float32)
                        tail = [norms[:, spot], blank, router_grads[:, spot], blank]
                        tail.append(jnp.zeros((tall, width - 256), jnp.float32))
                        pieces = [grads[mat, spot] for mat in range(mats)]
                        pieces.append(jnp.concatenate(tail, 1))
                        left = depth - mats * rows - tall
                        if left:
                            pieces.append(jnp.zeros((left, width), jnp.float32))
                        out_ref[c, z, x, y] = jnp.concatenate(pieces, 0).astype(jnp.bfloat16)
                        device += 1


def dense_backward(
    sizes, n_experts, padded, rows_own, lengths, slot_mask, patches, kept, columns, weights, gains, routers, back,
    gates, pooled, importance, third
):
    rows_here, span = slot_mask.shape
    tokens, width = patches.shape
    mats = weights.shape[0]
    depth = round_up(mats * rows_own + max(8, n_experts), 16)
    x_zero, a_one, qkv, att, x_one, a_two, probs, logs = kept

    def block(wide):
        return pl.BlockSpec((span, wide), lambda i: (i, 0))

    return pl.pallas_call(
        functools.partial(dense_backward_kernel, sizes, n_experts, lengths.shape[1], padded),
        grid=(rows_here,),
        out_shape=jax.ShapeDtypeStruct(
            (2, QUAD, sizes["x"], sizes["g"], depth, width), jnp.bfloat16
        ),
        in_specs=[
            whole(pltpu.SMEM), whole(), block(width),
            block(width), block(width), block(3 * width), block(width), block(width), block(width),
            block(128), block(128), block(128),
        ]
        + [whole()] * 8,
        out_specs=whole(),
        scratch_shapes=[
            VMEM((mats, width, width), jnp.float32),
            VMEM((128, width), jnp.float32),
            VMEM((8, width), jnp.float32),
            VMEM((span, 3 * width), jnp.bfloat16),
        ],
        compiler_params=pltpu.CompilerParams(vmem_limit_bytes=60 * MIB),
        cost_estimate=cost(50),
        name="dense_backward",
    )(
        lengths, slot_mask, patches, x_zero, a_one, qkv, att, x_one, a_two, probs, logs, columns,
        weights, gains, routers, back, gates, pooled, importance, third,
    )


def shard_moves(n_blocks):
    span = 2 * n_blocks
    moves = []
    for step in step_order(n_blocks):
        pairs = []
        for place in range(QUAD * n_blocks):
            for core in range(2):
                target = (place + step) % span
                src = place * 2 + core
                dst = (target // 2 * QUAD + 2 * core + target % 2) * 2 + place // span
                pairs.append((src, dst))
        moves.append(pairs)
    return moves


def return_experts(parts, n_blocks):
    return [
        lax.ppermute(part, ("g", "r", "c"), [(dst, src) for src, dst in pairs])
        for part, pairs in zip(parts, shard_moves(n_blocks))
    ]


def body(
    patches,
    lengths,
    slot_mask,
    expert_picks,
    priority_rank,
    class_labels,
    dense_weights,
    dense_first,
    dense_second,
    dense_average,
    router_weights,
    router_first,
    router_second,
    router_average,
    norm_params,
    norm_first,
    norm_second,
    norm_average,
    expert_in,
    in_first,
    in_second,
    in_average,
    expert_out,
    out_first,
    out_second,
    out_average,
    head_weights,
    head_first,
    head_second,
    head_average,
):
    n_blocks = lax.axis_size("g")
    sizes = {name: lax.axis_size(name) for name in ALL}
    rows_own, n_experts = router_weights.shape
    rows_here, n_slots_row = slot_mask.shape
    tokens, model_width = patches.shape
    n_images = lengths.shape[0] * lengths.shape[1]
    capacity = (21 * tokens * TOP + 20 * n_experts - 1) // (20 * n_experts)
    padded = round_up(capacity, 16)
    (
        layer_b, gain_rows, router_t, columns,
        x_zero, a_one, qkv, att_out, x_one, a_two, router_probs, logs, pooled, part_importance,
        arrived, details, activated, slope, result, part_pooled, expert_weights
    ) = forward(
        sizes, n_experts, padded, lengths, slot_mask, expert_picks, priority_rank, patches, dense_weights, norm_params,
        router_weights, expert_in, expert_out
    )
    g_head, d_pooled_all, d_pooled, g_norm_three, head_sums, total_importance = head_step(
        sizes,
        n_images,
        part_pooled,
        pooled,
        part_importance,
        gain_rows,
        head_weights,
        class_labels,
    )
    d_back, back_gate, *grads = expert_backward(
        sizes, arrived, details, d_pooled_all, result, slope, activated, expert_weights
    )
    parts = return_experts(grads, n_blocks)
    blocks = dense_backward(
        sizes,
        n_experts,
        padded,
        rows_own,
        lengths,
        slot_mask,
        patches,
        (x_zero, a_one, qkv, att_out, x_one, a_two, router_probs, logs),
        columns,
        layer_b,
        gain_rows,
        router_t,
        d_back,
        back_gate,
        d_pooled,
        total_importance,
        g_norm_three,
    )
    reduced, dense_sums = scatter_dense(sizes, blocks)
    g_one, g_two, totals = finish(
        sizes, n_experts, parts, head_sums, dense_sums, total_importance
    )
    n_dense = dense_weights.shape[0] * rows_own
    g_layers = reduced[:n_dense].reshape(-1, rows_own, model_width)
    g_norms = reduced[n_dense : n_dense + 6, :rows_own]
    g_router = reduced[n_dense : n_dense + n_experts, 128 : 128 + rows_own].T
    importance = total_importance[0, :n_experts]
    loss_value, grad_norm, factor = totals[0, 0], totals[1, 0], totals[2, 0]
    dense_out = adam_update(
        dense_weights, dense_first, dense_second, dense_average, g_layers, factor, base_rate
    )
    router_out = adam_update(
        router_weights, router_first, router_second, router_average, g_router, factor, base_rate
    )
    norm_out = adam_update(
        norm_params, norm_first, norm_second, norm_average, g_norms, factor, norm_rate
    )
    in_out = adam_update(expert_in, in_first, in_second, in_average, g_one, factor, base_rate)
    out_out = adam_update(expert_out, out_first, out_second, out_average, g_two, factor, base_rate)
    head_out = adam_update(
        head_weights, head_first, head_second, head_average, g_head, factor, base_rate
    )
    return (
        loss_value,
        importance,
        grad_norm,
        *dense_out,
        *router_out,
        *norm_out,
        *in_out,
        *out_out,
        *head_out,
    )


def solution(mesh):
    n_dp, n_expert = mesh.shape["dp"], mesh.shape["expert"]
    shaped = mesh.devices.reshape(n_dp // QUAD, QUAD, n_expert // 2, 2)
    fine = Mesh(shaped, ALL)
    rows = P(ALL, None)
    dense = P(None, ALL, None)
    norms = P(None, ALL)
    experts = P(("x", "c"), ("g", "r"), None)
    placed = (rows,) * 6 + (dense,) * 4 + (rows,) * 4 + (norms,) * 4 + (experts,) * 8 + (rows,) * 4
    results = (
        (P(),) * 3 + (dense,) * 4 + (rows,) * 4 + (norms,) * 4 + (experts,) * 8 + (rows,) * 4
    )
    return jax.shard_map(body, mesh=fine, in_specs=placed, out_specs=results, check_vma=False)
```

```python
import functools
import math

import jax
import jax.numpy as jnp
from jax import lax
from jax.experimental import pallas as pl
from jax.experimental.pallas import tpu as pltpu
from jax.sharding import Mesh
from jax.sharding import PartitionSpec as P

HEADS = 12
TOP = 2
STEP_COUNT = 10
QUAD = 4

high_prec = lax.Precision.HIGHEST
eps_norm = 1e-06
aux_weight = 0.01
clip_limit = 1.0
base_rate = 0.05
norm_rate = 0.5
beta_first = 0.9
beta_second = 0.999
weight_decay = 0.1
polyak_decay = 0.7
adam_eps = 1e-08
mask_fill = -1e30

ALL = ("g", "r", "x", "c")
MEMBERS = ("x", "r")


def adam_update(weight, first_state, second_state, average_state, gradient, factor, step_rate):
    clipped = gradient * factor
    first_new = beta_first * first_state + (1.0 - beta_first) * clipped
    second_new = beta_second * second_state + (1.0 - beta_second) * clipped * clipped
    first_hat = first_new / (1.0 - beta_first**STEP_COUNT)
    second_hat = second_new / (1.0 - beta_second**STEP_COUNT)
    weight_new = weight - step_rate * (
        first_hat / (jnp.sqrt(second_hat) + adam_eps) + weight_decay * weight
    )
    average_new = polyak_decay * average_state + (1.0 - polyak_decay) * weight_new
    return (weight_new, first_new, second_new, average_new)


MESH_ID = pl.DeviceIdType.MESH
VMEM = pltpu.VMEM
ANY = pl.ANY
MIB = 1 << 20


def cost(microseconds):
    return pl.CostEstimate(flops=int(microseconds * 1.15e9), bytes_accessed=0, transcendentals=0)


def whole(space=None):
    return pl.BlockSpec(memory_space=space or VMEM)


def round_up(value, step):
    return (value + step - 1) // step * step


class Place:
    def __init__(self, sizes):
        self.G, self.X = sizes["g"], sizes["x"]
        self.Z, self.Y = QUAD, sizes["g"]
        self.chips = self.Z * self.Y * self.X
        spot = lax.axis_index("g") * QUAD + lax.axis_index("r")
        self.z, self.y = lax.div(spot, self.Y), lax.rem(spot, self.Y)
        self.x, self.c = lax.axis_index("x"), lax.axis_index("c")
        self.g, self.r = lax.axis_index("g"), lax.axis_index("r")
        self.chip = spot * self.X + self.x
        self.member = self.x * QUAD + self.r

    def at(self, z=None, y=None, x=None, c=None):
        spot = (self.z if z is None else z) * self.Y + (self.y if y is None else y)
        return {
            "g": lax.div(spot, QUAD),
            "r": lax.rem(spot, QUAD),
            "x": self.x if x is None else x,
            "c": self.c if c is None else c,
        }

    def of_chip(self, chip):
        spot = lax.div(chip, self.X)
        return {
            "g": lax.div(spot, QUAD),
            "r": lax.rem(spot, QUAD),
            "x": lax.rem(chip, self.X),
            "c": self.c,
        }

    def of_member(self, member):
        return {
            "g": self.g,
            "r": lax.rem(member, QUAD),
            "x": lax.div(member, QUAD),
            "c": self.c,
        }

    def sibling(self):
        return self.at(c=1 - self.c)


def greet(peers):
    barrier = pltpu.get_barrier_semaphore()
    for peer in peers:
        pl.semaphore_signal(barrier, inc=1, device_id=peer, device_id_type=MESH_ID)
    pl.semaphore_wait(barrier, len(peers))


def send(src, dst, send_sem, recv_sem, peer):
    return pltpu.make_async_remote_copy(
        src_ref=src,
        dst_ref=dst,
        send_sem=send_sem,
        recv_sem=recv_sem,
        device_id=peer,
        device_id_type=MESH_ID,
    )


def others(me, count):
    return [lax.rem(me + step, count) for step in range(1, count)]


def grid_peers(at):
    peers = [at.at(z=z) for z in others(at.z, at.Z)]
    peers += [at.at(y=y) for y in others(at.y, at.Y)]
    peers += [at.at(x=x) for x in others(at.x, at.X)]
    return peers + [at.sibling()]


def gather_dense(at, rows, mats, land, w_ref, sems, started, beside, idle):
    Z, Y, X = at.Z, at.Y, at.X
    depth = land.shape[4]
    cut = depth // 2 // 16 * 16
    first, second = pl.ds(0, cut), pl.ds(cut, depth - cut)
    z_out, z_in, ya_out, ya_in, xb_out, xb_in, xa_out, xa_in, yb_out, yb_in, c_out, c_in = sems
    mine = land.at[at.c, at.z, at.x, at.y]

    def begin(copy):
        copy.start()
        started.append(copy)

    order = [at.z] + [lax.rem(at.z + k, Z) for k in (1, 3, 2)]
    for z in order[1:]:
        begin(send(mine, mine, z_out.at[z], z_in.at[at.z], at.at(z=z)))

    def one(z):
        part = land.at[at.c, z, at.x, at.y]
        for y in others(at.y, Y):
            begin(send(part.at[first], part.at[first], ya_out.at[z, y], ya_in.at[z, at.y], at.at(y=y)))
        for x in others(at.x, X):
            begin(send(part.at[second], part.at[second], xb_out.at[z, x], xb_in.at[z, at.x], at.at(x=x)))

    def two(z):
        for y in others(at.y, Y):
            part = land.at[at.c, z, at.x, y, first]
            send(part, part, ya_out.at[z, y], ya_in.at[z, y], at.at(y=y)).wait_recv()
        line = land.at[at.c, z, at.x, :, first]
        for x in others(at.x, X):
            begin(send(line, line, xa_out.at[z, x], xa_in.at[z, at.x], at.at(x=x)))
        for x in others(at.x, X):
            part = land.at[at.c, z, x, at.y, second]
            send(part, part, xb_out.at[z, x], xb_in.at[z, x], at.at(x=x)).wait_recv()
        line = land.at[at.c, z, :, at.y, second]
        for y in others(at.y, Y):
            begin(send(line, line, yb_out.at[z, y], yb_in.at[z, at.y], at.at(y=y)))

    def three(z):
        for x in others(at.x, X):
            line = land.at[at.c, z, x, :, first]
            send(line, line, xa_out.at[z, x], xa_in.at[z, x], at.at(x=x)).wait_recv()
        for y in others(at.y, Y):
            line = land.at[at.c, z, :, y, second]
            send(line, line, yb_out.at[z, y], yb_in.at[z, y], at.at(y=y)).wait_recv()
        plane = land.at[at.c, z]
        begin(send(plane, plane, c_out.at[z], c_in.at[z], at.sibling()))

    def place(z):
        plane = land.at[1 - at.c, z]
        send(plane, plane, c_out.at[z], c_in.at[z], at.sibling()).wait_recv()
        group = 16 // math.gcd(16, rows)
        cores = [(c, x, y) for y in range(Y) for x in range(X) for c in range(2)]
        for start in range(0, len(cores), group):
            spot = pl.multiple_of((z * len(cores) + start) * rows, 16)
            for mat in range(mats):
                w_ref[mat, pl.ds(spot, group * rows)] = jnp.concatenate(
                    [
                        land[c, z, x, y, mat * rows : (mat + 1) * rows]
                        for c, x, y in cores[start : start + group]
                    ],
                    0,
                )

    for step in range(Z + 2):
        if step < Z:
            if step > 0:
                z = order[step]
                part = land.at[at.c, z, at.x, at.y]
                send(part, part, z_out.at[z], z_in.at[z], at.at(z=z)).wait_recv()
            one(order[step])
        if step == 0:
            beside()
        if step == Z - 1:
            idle()
        if 0 <= step - 1 < Z:
            two(order[step - 1])
        if 0 <= step - 2 < Z:
            three(order[step - 2])
        if 0 <= step - 3 < Z:
            place(order[step - 3])
    place(order[Z - 1])


def gather_small(at, rows, mats, count, land, gain_ref, router_ref):
    chips = [(z, y, x) for z in range(at.Z) for y in range(at.Y) for x in range(at.X)]
    cores = [(c, z, x, y) for z, y, x in chips for c in range(2)]
    base = mats * rows
    tails = [land[spot][base : base + count].astype(jnp.float32) for spot in cores]
    gain_ref[...] = jnp.concatenate([tail[:8, :rows] for tail in tails], 1)
    router_ref[...] = jnp.concatenate([tail[:, 128 : 128 + rows] for tail in tails], 1)


def total_square(value):
    return jnp.sum(jnp.sum(value * value, 0, keepdims=True), 1, keepdims=True)


def scatter_kernel(sizes, g_ref, out_ref, square_ref, hold, sib, got_xa, got_yb, got_ya, got_xb, got_z, *sems):
    at = Place(sizes)
    Z, Y, X = at.Z, at.Y, at.X
    depth = g_ref.shape[4]
    cut = depth // 2 // 16 * 16
    first, second = pl.ds(0, cut), pl.ds(cut, depth - cut)
    c_out, c_in, xa_out, xa_in, yb_out, yb_in, ya_out, ya_in, xb_out, xb_in, z_out, z_in = sems
    greet(grid_peers(at))
    started = []

    def begin(copy):
        copy.start()
        started.append(copy)

    wide = lambda value: value.astype(jnp.float32)
    order = [lax.rem(at.z + k, Z) for k in (2, 1, 3)] + [at.z]
    for z in order:
        begin(send(g_ref.at[1 - at.c, z], sib.at[z], c_out.at[z], c_in.at[z], at.sibling()))

    def one(z):
        send(sib.at[z], sib.at[z], c_out.at[z], c_in.at[z], at.sibling()).wait_recv()
        hold[z] = (wide(g_ref[at.c, z]) + wide(sib[z])).astype(jnp.bfloat16)
        for x in others(at.x, X):
            begin(send(hold.at[z, x, :, first], got_xa.at[z, at.x], xa_out.at[z, x], xa_in.at[z, at.x], at.at(x=x)))
        for y in others(at.y, Y):
            begin(send(hold.at[z, :, y, second], got_yb.at[z, at.y], yb_out.at[z, y], yb_in.at[z, at.y], at.at(y=y)))

    def two(z):
        total = wide(hold[z, at.x, :, first])
        for x in others(at.x, X):
            send(got_xa.at[z, x], got_xa.at[z, x], xa_out.at[z, x], xa_in.at[z, x], at.at(x=x)).wait_recv()
            total = total + wide(got_xa[z, x])
        hold[z, at.x, :, first] = total.astype(jnp.bfloat16)
        for y in others(at.y, Y):
            begin(send(hold.at[z, at.x, y, first], got_ya.at[z, at.y], ya_out.at[z, y], ya_in.at[z, at.y], at.at(y=y)))
        total = wide(hold[z, :, at.y, second])
        for y in others(at.y, Y):
            send(got_yb.at[z, y], got_yb.at[z, y], yb_out.at[z, y], yb_in.at[z, y], at.at(y=y)).wait_recv()
            total = total + wide(got_yb[z, y])
        hold[z, :, at.y, second] = total.astype(jnp.bfloat16)
        for x in others(at.x, X):
            begin(send(hold.at[z, x, at.y, second], got_xb.at[z, at.x], xb_out.at[z, x], xb_in.at[z, at.x], at.at(x=x)))

    def three(z, last):
        total = wide(hold[z, at.x, at.y, first])
        for y in others(at.y, Y):
            send(got_ya.at[z, y], got_ya.at[z, y], ya_out.at[z, y], ya_in.at[z, y], at.at(y=y)).wait_recv()
            total = total + wide(got_ya[z, y])
        rest = wide(hold[z, at.x, at.y, second])
        for x in others(at.x, X):
            send(got_xb.at[z, x], got_xb.at[z, x], xb_out.at[z, x], xb_in.at[z, x], at.at(x=x)).wait_recv()
            rest = rest + wide(got_xb[z, x])
        if last:
            out_ref[first] = total
            out_ref[second] = rest
            return
        mine = hold.at[z, at.x, at.y]
        mine[first] = total.astype(jnp.bfloat16)
        mine[second] = rest.astype(jnp.bfloat16)
        begin(send(mine, got_z.at[at.z], z_out.at[z], z_in.at[at.z], at.at(z=z)))

    for step in range(Z + 2):
        if step < Z:
            one(order[step])
        if 0 <= step - 1 < Z:
            two(order[step - 1])
        if 0 <= step - 2 < Z:
            three(order[step - 2], step - 2 == Z - 1)
    for z in order[:-1]:
        send(got_z.at[z], got_z.at[z], z_out.at[z], z_in.at[z], at.at(z=z)).wait_recv()
        out_ref[...] += wide(got_z[z])
    square_ref[...] = jnp.broadcast_to(total_square(out_ref[...]), square_ref.shape)
    for copy in started:
        copy.wait_send()


def scatter_dense(sizes, blocks):
    unused, Z, X, Y, depth, width = blocks.shape
    dma = pltpu.SemaphoreType.DMA
    by_y, by_x, by_z = dma((Z, Y)), dma((Z, X)), dma((Z,))
    cut = depth // 2 // 16 * 16
    half = jnp.bfloat16
    return pl.pallas_call(
        functools.partial(scatter_kernel, sizes),
        out_shape=(
            jax.ShapeDtypeStruct((depth, width), jnp.float32),
            jax.ShapeDtypeStruct((8, 128), jnp.float32),
        ),
        in_specs=[whole()],
        out_specs=(whole(), whole()),
        scratch_shapes=[
            VMEM((Z, X, Y, depth, width), half),
            VMEM((Z, X, Y, depth, width), half),
            VMEM((Z, X, Y, cut, width), half),
            VMEM((Z, Y, X, depth - cut, width), half),
            VMEM((Z, Y, cut, width), half),
            VMEM((Z, X, depth - cut, width), half),
            VMEM((Z, depth, width), half),
        ]
        + [by_z, by_z, by_x, by_x, by_y, by_y, by_y, by_y, by_x, by_x, by_z, by_z],
        compiler_params=pltpu.CompilerParams(
            collective_id=2, has_side_effects=True, vmem_limit_bytes=28 * MIB
        ),
        cost_estimate=cost(45),
        name="scatter_dense",
    )(blocks)


def finish_kernel(sizes, n_experts, head_ref, dense_ref, imp_ref, *refs):
    at = Place(sizes)
    many = len(refs) - 7
    parts = refs[:many]
    first_ref, second_ref, out_ref, land, own, out_sem, in_sem = refs[many:]
    count = 2 * at.chips
    me = at.chip * 2 + at.c
    ids = others(me, count)

    def peer(device):
        spot = at.of_chip(lax.div(device, 2))
        spot["c"] = lax.rem(device, 2)
        return spot

    greet([peer(device) for device in ids])
    place = lax.rem(at.g * QUAD + at.r, 2)
    square = dense_ref[0:1, 0:1] + head_ref[1:2, 0:1]
    for parity in range(2):
        expert = place if parity == 0 else 1 - place
        for index, ref in enumerate((first_ref, second_ref)):
            total = None
            for step in range(parity * many // 2, (parity + 1) * many // 2):
                found = parts[step][index].astype(jnp.float32)
                total = found if total is None else total + found
            ref[expert] = total
            square = square + total_square(total)
    line = lax.broadcasted_iota(jnp.int32, own.shape, 0)
    own[...] = jnp.where(line == 0, head_ref[0:1, 0:1], jnp.where(line == 1, square, 0.0))
    land[me] = own[...]
    copies = [send(own, land.at[me], out_sem.at[d], in_sem.at[me], peer(d)) for d in ids]
    for copy in copies:
        copy.start()
    importance = imp_ref[0:1, 0:128]
    head = lax.broadcasted_iota(jnp.int32, (1, 128), 1) < n_experts
    centre = jnp.sum(jnp.where(head, importance, 0.0), 1, keepdims=True) / n_experts
    away = jnp.where(head, importance - centre, 0.0)
    spread = jnp.sum(away * away, 1, keepdims=True) / n_experts
    balance = aux_weight * spread / (centre * centre)
    for d in ids:
        send(land.at[d], land.at[d], out_sem.at[d], in_sem.at[d], peer(d)).wait_recv()
    sums = jnp.sum(land[...], 0)
    norm = jnp.sqrt(sums[1:2, 0:1])
    factor = jnp.minimum(1.0, clip_limit / norm)
    loss = sums[0:1, 0:1] + balance
    out_ref[...] = jnp.where(line == 0, loss, jnp.where(line == 1, norm, factor))
    for copy in copies:
        copy.wait_send()


def finish(sizes, n_experts, parts, head_sums, dense_sums, importance):
    devices = sizes["g"] * QUAD * sizes["x"] * 2
    unused, rows, width = parts[0].shape
    dma = pltpu.SemaphoreType.DMA
    grads = jax.ShapeDtypeStruct((2, rows, width), jnp.float32)
    return pl.pallas_call(
        functools.partial(finish_kernel, sizes, n_experts),
        out_shape=(grads, grads, jax.ShapeDtypeStruct((8, 128), jnp.float32)),
        in_specs=[whole()] * (3 + len(parts)),
        out_specs=(whole(),) * 3,
        scratch_shapes=[
            VMEM((devices, 8, 128), jnp.float32),
            VMEM((8, 128), jnp.float32),
            dma((devices,)),
            dma((devices,)),
        ],
        compiler_params=pltpu.CompilerParams(
            collective_id=3, has_side_effects=True, vmem_limit_bytes=20 * MIB
        ),
        cost_estimate=cost(10),
        name="finish",
    )(head_sums, dense_sums, importance, *parts)


IMAGE_PAD = 16


def split_three(value):
    high = value.astype(jnp.bfloat16)
    rest = value - high.astype(jnp.float32)
    middle = rest.astype(jnp.bfloat16)
    return high, middle, (rest - middle.astype(jnp.float32)).astype(jnp.bfloat16)


def dot_f32(left, right, dims):
    return lax.dot_general(left, right, (dims, ((), ())), preferred_element_type=jnp.float32)


NN = ((1,), (0,))
NT = ((1,), (1,))
TN = ((0,), (0,))


def norm_parts(values):
    centre = values - jnp.mean(values, -1, keepdims=True)
    spread = jnp.mean(centre * centre, -1, keepdims=True)
    scale = lax.rsqrt(spread + eps_norm)
    return centre * scale, scale


def norm_back(d_out, scaled, scale, gain):
    pulled = d_out * gain
    return scale * (
        pulled
        - jnp.mean(pulled, -1, keepdims=True)
        - scaled * jnp.mean(pulled * scaled, -1, keepdims=True)
    )


def head_kernel(
    sizes, images, part_ref, own_ref, imp_ref, gain_ref, head_ref, label_ref,
    g_head_ref, d_pool_ref, own_d_ref, g_norm_ref, sums_ref, total_imp_ref,
    in_part, rows, d_rows, d_sib, d_sum, d_in, head_b, labels, d_logits, *sems
):
    at = Place(sizes)
    chips, members = at.chips, QUAD * at.X
    devices = 2 * chips
    p_out, p_in, r_out, r_in, s_out, s_in, d_out, d_in_sem, b_out, b_in = sems
    width = own_ref.shape[1]
    same_core = others(at.chip, chips)
    greet([at.of_chip(chip) for chip in same_core] + [at.sibling()])
    started = []

    def begin(copy):
        copy.start()
        started.append(copy)

    team = others(at.member, members)
    for member in team:
        begin(send(part_ref.at[member], in_part.at[at.member], p_out.at[member], p_in.at[at.member], at.of_member(member)))
    in_part[at.member] = part_ref[at.member]
    head_b[...] = head_ref[...].astype(jnp.bfloat16)
    wide = devices * IMAGE_PAD
    spot = lax.broadcasted_iota(jnp.int32, (label_ref.shape[1], wide), 1)
    given = lax.broadcasted_iota(jnp.int32, (label_ref.shape[1], wide), 0)
    image = lax.rem(spot, IMAGE_PAD)
    device = lax.rem(lax.div(spot, IMAGE_PAD), chips) * 2 + lax.div(spot, IMAGE_PAD * chips)
    chosen = ((device * images + image == given) & (image < images)).astype(jnp.bfloat16)
    labels[...] = dot_f32(label_ref[...].astype(jnp.float32).astype(jnp.bfloat16), chosen, NN).astype(jnp.bfloat16)
    for member in team:
        send(in_part.at[member], in_part.at[member], p_out.at[member], p_in.at[member], at.of_member(member)).wait_recv()
    pooled = own_ref[...] + jnp.sum(in_part[...], 0)
    scaled, scale = norm_parts(pooled)
    gain, shift = gain_ref[2:3], gain_ref[5:6]
    a_three = scaled * gain + shift
    row = lax.broadcasted_iota(jnp.int32, (IMAGE_PAD, width), 0)
    block = jnp.where(row < images, a_three, 0.0)
    pieces = split_three(imp_ref[0:1])
    for index, piece in enumerate(pieces):
        block = jnp.where(row == images + index, piece.astype(jnp.float32), block)
    rows[at.c, at.chip] = block.astype(jnp.bfloat16)
    mine = rows.at[at.c, at.chip]
    for chip in same_core:
        begin(send(mine, mine, r_out.at[chip], r_in.at[at.chip], at.of_chip(chip)))
    for chip in same_core:
        part = rows.at[at.c, chip]
        send(part, part, r_out.at[chip], r_in.at[chip], at.of_chip(chip)).wait_recv()
    begin(send(rows.at[at.c], rows.at[at.c], s_out.at[0], s_in.at[0], at.sibling()))
    send(rows.at[1 - at.c], rows.at[1 - at.c], s_out.at[0], s_in.at[0], at.sibling()).wait_recv()
    gathered = rows[...].reshape(wide, width)
    in_block = lax.rem(lax.broadcasted_iota(jnp.int32, (wide, width), 0), IMAGE_PAD)
    total = jnp.sum(jnp.where(in_block >= images, gathered.astype(jnp.float32), 0.0), 0, keepdims=True)
    total_imp_ref[...] = jnp.broadcast_to(total, total_imp_ref.shape)
    gathered = jnp.where(in_block < images, gathered.astype(jnp.float32), 0.0).astype(jnp.bfloat16)
    logits = dot_f32(head_b[...], gathered, NT)
    image = lax.rem(lax.broadcasted_iota(jnp.int32, logits.shape, 1), IMAGE_PAD)
    count = devices * images
    target = labels[...].astype(jnp.float32)
    power = jnp.exp(-jnp.abs(logits))
    loss = jnp.maximum(logits, 0.0) + jnp.log1p(power) - target * logits
    loss = jnp.sum(jnp.where(image < images, loss, 0.0), 1, keepdims=True)
    loss = jnp.sum(loss, 0, keepdims=True) / count
    chance = jnp.where(logits >= 0.0, 1.0, power) / (1.0 + power)
    d_logits[...] = jnp.where(image < images, (chance - target) / count, 0.0).astype(jnp.bfloat16)
    partial = dot_f32(d_logits[...], head_b[...], TN)
    d_rows[...] = partial.reshape(d_rows.shape).astype(jnp.bfloat16)
    begin(send(d_rows.at[1 - at.c], d_sib, s_out.at[1], s_in.at[1], at.sibling()))
    g_head = dot_f32(d_logits[...], gathered, NN)
    g_head_ref[...] = g_head
    line = lax.broadcasted_iota(jnp.int32, sums_ref.shape, 0)
    sums_ref[...] = jnp.where(line == 0, loss, jnp.where(line == 1, total_square(g_head), 0.0))
    send(d_sib, d_sib, s_out.at[1], s_in.at[1], at.sibling()).wait_recv()
    d_sum[...] = (d_rows[at.c].astype(jnp.float32) + d_sib[...].astype(jnp.float32)).astype(jnp.bfloat16)
    for chip in same_core:
        begin(send(d_sum.at[chip], d_in.at[at.chip], d_out.at[chip], d_in_sem.at[at.chip], at.of_chip(chip)))
    d_in[at.chip] = d_sum[at.chip]
    for chip in same_core:
        send(d_in.at[chip], d_in.at[chip], d_out.at[chip], d_in_sem.at[chip], at.of_chip(chip)).wait_recv()
    d_norm = jnp.sum(d_in[...].astype(jnp.float32), 0)
    d_norm = jnp.where(row < images, d_norm, 0.0)
    d_pooled = norm_back(d_norm, scaled, scale, gain)
    d_pooled = jnp.where(row < images, d_pooled, 0.0)
    d_gain = jnp.sum(d_norm * scaled, 0, keepdims=True)
    d_shift = jnp.sum(d_norm, 0, keepdims=True)
    line = lax.broadcasted_iota(jnp.int32, g_norm_ref.shape, 0)
    g_norm_ref[...] = jnp.where(line == 2, d_gain, jnp.where(line == 5, d_shift, 0.0))
    own_d_ref[...] = d_pooled
    d_pool_ref[at.member] = d_pooled
    mine = d_pool_ref.at[at.member]
    for member in team:
        begin(send(own_d_ref, mine, b_out.at[member], b_in.at[at.member], at.of_member(member)))
    for member in team:
        part = d_pool_ref.at[member]
        send(part, part, b_out.at[member], b_in.at[member], at.of_member(member)).wait_recv()
    for copy in started:
        copy.wait_send()


def head_step(sizes, images, part, own, imp, gains, head, label):
    members = QUAD * sizes["x"]
    chips = members * sizes["g"]
    classes, width = head.shape
    wide = 2 * chips * IMAGE_PAD
    dma = pltpu.SemaphoreType.DMA
    by_member, by_chip = dma((members,)), dma((chips,))
    f32, half = jnp.float32, jnp.bfloat16
    blocks = (chips, IMAGE_PAD, width)
    return pl.pallas_call(
        functools.partial(head_kernel, sizes, images),
        out_shape=(
            jax.ShapeDtypeStruct((classes, width), f32),
            jax.ShapeDtypeStruct((members, IMAGE_PAD, width), f32),
            jax.ShapeDtypeStruct((IMAGE_PAD, width), f32),
            jax.ShapeDtypeStruct((8, width), f32),
            jax.ShapeDtypeStruct((8, 128), f32),
            jax.ShapeDtypeStruct((8, width), f32),
        ),
        in_specs=[whole()] * 6,
        out_specs=(whole(),) * 6,
        scratch_shapes=[
            VMEM((members, IMAGE_PAD, width), f32),
            VMEM((2, *blocks), half),
            VMEM((2, *blocks), half),
            VMEM(blocks, half),
            VMEM(blocks, half),
            VMEM(blocks, half),
            VMEM((classes, width), half),
            VMEM((classes, wide), half),
            VMEM((classes, wide), half),
        ]
        + [by_member, by_member, by_chip, by_chip, dma((2,)), dma((2,)), by_chip, by_chip]
        + [by_member, by_member],
        compiler_params=pltpu.CompilerParams(
            collective_id=4, has_side_effects=True, vmem_limit_bytes=56 * MIB
        ),
        cost_estimate=cost(42),
        name="head_step",
    )(part, own, imp, gains, head, label)


def route_math(per_image, n_experts, capacity, padded, pick_ref, rank_ref, mask_ref, length_ref):
    rows_here, span = mask_ref.shape
    tokens = rows_here * span
    valid = mask_ref[...].astype(jnp.float32)
    lengths = length_ref[...]
    position = lax.broadcasted_iota(jnp.int32, (rows_here, span), 1)
    segment = jnp.zeros((rows_here, span), jnp.int32)
    bound = jnp.zeros((rows_here, 1), jnp.int32)
    for image in range(per_image):
        bound = bound + lengths[:, image : image + 1]
        segment = segment + jnp.where(position >= bound, 1, 0)
    pool = jnp.zeros_like(valid)
    for image in range(per_image):
        member = jnp.where(segment == image, valid, 0.0)
        pool = pool + member / jnp.maximum(jnp.sum(member, 1, keepdims=True), 1.0)
    line = lax.broadcasted_iota(jnp.int32, (rows_here, span), 0)
    image = (segment + per_image * line).astype(jnp.float32)

    def flat(value):
        return jnp.concatenate([value[i : i + 1] for i in range(rows_here)], 1)

    rank_row = rank_ref[...].astype(jnp.float32)
    picks = pick_ref[...].astype(jnp.float32)
    table = jnp.concatenate([flat(valid), flat(pool), flat(image), rank_row, picks], 0)
    table = jnp.concatenate([table, jnp.zeros((122, tokens), jnp.float32)], 0).T
    valid_col, pool_col, image_col, rank_col, pick_one, pick_two = (
        table[:, i : i + 1] for i in range(6)
    )
    lane = lax.broadcasted_iota(jnp.int32, (tokens, 128), 1)
    in_first, in_second = lane < n_experts, (lane >= n_experts) & (lane < 2 * n_experts)
    number = lane.astype(jnp.float32)
    hot = jnp.where(in_first & (pick_one == number), valid_col, 0.0)
    hot = hot + jnp.where(in_second & (pick_two == number - n_experts), valid_col, 0.0)
    shifted = jnp.where(in_second & (pick_one == number - n_experts), valid_col, 0.0)
    before = jnp.where(rank_row < rank_col, 1.0, 0.0).astype(jnp.bfloat16)
    ahead = dot_f32(before, hot.astype(jnp.bfloat16), NN) + jnp.sum(shifted, 0, keepdims=True)
    counted = hot * ahead
    pos_one = jnp.sum(jnp.where(in_first, counted, 0.0), 1, keepdims=True)
    pos_two = jnp.sum(jnp.where(in_second, counted, 0.0), 1, keepdims=True)

    def place(pick, pos):
        kept = (valid_col > 0.0) & (pos < capacity)
        return jnp.where(kept, pick * padded + pos, -1.0)

    columns = (
        place(pick_one, pos_one),
        place(pick_two, pos_two),
        valid_col,
        pool_col,
        image_col,
        pick_one,
        pick_two,
    )
    result = jnp.zeros((tokens, 128), jnp.float32)
    for index, column in enumerate(columns):
        result = jnp.where(lane == index, column, result)
    return result


def allowed_slots(lengths, row, images, valid_row, span):
    query = lax.broadcasted_iota(jnp.int32, (span, span), 0)
    key = lax.broadcasted_iota(jnp.int32, (span, span), 1)
    bound = 0
    query_seg, key_seg = jnp.zeros((span, span), jnp.int32), jnp.zeros((span, span), jnp.int32)
    for image in range(images):
        bound = bound + lengths[row, image]
        query_seg = query_seg + jnp.where(query >= bound, 1, 0)
        key_seg = key_seg + jnp.where(key >= bound, 1, 0)
    allowed = (query_seg == key_seg) & ((valid_row > 0) | (query == key))
    return jnp.where(allowed, 1.0, 0.0)


TILE = 32


def tiles(count, size=TILE):
    return [slice(start, min(start + size, count)) for start in range(0, count, size)]


def step_order(blocks):
    return [*range(0, 2 * blocks, 2), *range(1, 2 * blocks, 2)]


class Team:
    def __init__(self, at):
        self.at, self.span = at, 2 * at.G
        self.spot = at.g * QUAD + at.r

    def target(self, step):
        at = self.at
        chosen = lax.rem(self.spot + step_order(at.G)[step], self.span)
        block, index = lax.div(chosen, 2), lax.rem(chosen, 2)
        core = lax.div(self.spot, self.span)
        r = 2 * at.c + index
        own = (block == at.g) & (r == at.r) & (core == at.c)
        return {"g": block, "r": r, "x": at.x, "c": core}, index, own

    def peers(self):
        at = self.at
        count = 2 * at.G * QUAD
        me = self.spot * 2 + at.c
        line = []
        for device in others(me, count):
            spot = lax.div(device, 2)
            line.append(
                {"g": lax.div(spot, QUAD), "r": lax.rem(spot, QUAD), "x": at.x, "c": lax.rem(device, 2)}
            )
        for x in others(at.x, at.X):
            line += [{"g": at.g, "r": r, "x": x, "c": at.c} for r in range(QUAD)]
        return line


def image_hot(detail, padded):
    image = detail[2:3, :padded]
    line = lax.broadcasted_iota(jnp.int32, (IMAGE_PAD, padded), 0).astype(jnp.float32)
    return line == image


def forward_kernel(
    sizes, n_experts, images, padded,
    length_ref, lengths_ref, mask_ref, pick_ref, rank_ref, patch_ref, dense_ref, norm_ref, routing_ref, in_ref, out_ref,
    w_keep, gain_ref, router_ref, col_ref, x_zero_out, a_one_out, qkv_out, att_out, x_one_out, a_two_out, prob_ref, lse_ref, pool_ref, imp_ref,
    rows_out, detail_out, act_out, slope_out, y_out, part_ref, weight_out,
    land, w_ref, shard_ref, x_zero_buf, a_one_buf, qkv_buf, att_buf, x_one_buf, a_two_ref, weights, send_rows, send_detail, places,
    rows_in, detail_in, total, act_buf, slope_buf, dense_sem, keep_sem, own_sem,
    w_out, w_in, s_out, s_in, r_out, r_in, m_out, m_in, act_sem, slope_sem, cast_sem, *gather_sems
):
    at = Place(sizes)
    team = Team(at)
    half = weights.shape[1]
    early, middle = half // 2, half * 3 // 4
    rows_here, span = mask_ref.shape
    width = patch_ref.shape[1]
    tokens = rows_here * span
    mats, rows_own, unused = dense_ref.shape
    tall = router_ref.shape[0]
    capacity = (21 * tokens * TOP + 20 * n_experts - 1) // (20 * n_experts)

    part_rows = shard_ref.shape[2]
    casts = [
        pltpu.make_async_copy(ref.at[expert], total.at[pl.ds((index * 2 + expert) * part_rows, part_rows)], cast_sem.at[index, expert])
        for index, ref in enumerate((in_ref, out_ref))
        for expert in range(2)
    ]
    for copy in casts:
        copy.start()
    depth = land.shape[4]
    routing = routing_ref[...]
    routing = jnp.concatenate([routing, jnp.zeros((n_experts, 128 - rows_own), jnp.float32)], 1)
    if n_experts < tall:
        routing = jnp.concatenate([routing, jnp.zeros((tall - n_experts, 128), jnp.float32)], 0)
    norms = norm_ref[...]
    norms = jnp.concatenate([norms, jnp.zeros((norms.shape[0], 128 - rows_own), jnp.float32)], 1)
    norms = jnp.concatenate([norms, jnp.zeros((tall - norms.shape[0], 128), jnp.float32)], 0)
    tail = jnp.concatenate(
        [norms, routing, jnp.zeros((tall, width - 256), jnp.float32)], 1
    )
    block = jnp.concatenate([dense_ref[...].reshape(mats * rows_own, width), tail], 0)
    if block.shape[0] < depth:
        block = jnp.concatenate(
            [block, jnp.zeros((depth - block.shape[0], width), jnp.float32)], 0
        )
    land[at.c, at.z, at.x, at.y] = block.astype(jnp.bfloat16)
    greet(team.peers() + grid_peers(at))

    def spot_of(step, side=0):
        return step // early, side * early + step % early

    def swap_copy(step):
        return send(
            weights.at[spot_of(step)], weights.at[spot_of(step, 1)], s_out.at[step], s_in.at[step], at.sibling()
        )

    def shard_copy(step):
        device, index, own = team.target(step)
        return send(
            shard_ref.at[index], weights.at[spot_of(step)], w_out.at[step], w_in.at[step], device
        )

    def shard_own(step):
        device, index, own = team.target(step)
        return pltpu.make_async_copy(shard_ref.at[index], weights.at[spot_of(step)], w_in.at[step])

    def shard_starts(steps):
        for step in steps:
            own = team.target(step)[2]

            @pl.when(own)
            def _():
                shard_own(step).start()

            @pl.when(jnp.logical_not(own))
            def _():
                shard_copy(step).start()

    def shard_waits(steps):
        for step in steps:
            own = team.target(step)[2]

            @pl.when(own)
            def _():
                shard_own(step).wait()

            @pl.when(jnp.logical_not(own))
            def _():
                shard_copy(step).wait_recv()

            swap_copy(step).start()

    def beside_gather():
        col_ref[...] = route_math(
            images, n_experts, capacity, padded, pick_ref, rank_ref, mask_ref, lengths_ref
        )
        for copy in casts:
            copy.wait()
        for index in range(2):
            for expert in range(2):
                here = pl.ds((index * 2 + expert) * part_rows, part_rows)
                shard_ref[expert, index] = total[here].astype(jnp.bfloat16)

    gathers = []
    gather_dense(
        at, rows_own, mats, land, w_ref, gather_sems, gathers, beside_gather, lambda: shard_starts(range(early))
    )
    shard_starts(range(early, middle))
    gather_small(at, rows_own, mats, tall, land, gain_ref, router_ref)
    w_copy = pltpu.make_async_copy(w_ref, w_keep, keep_sem.at[5])
    w_copy.start()

    dense = (
        (x_zero_buf, x_zero_out), (a_one_buf, a_one_out), (qkv_buf, qkv_out), (att_buf, att_out), (x_one_buf, x_one_out),
    )

    def dense_copy(row, index):
        here = pl.ds(pl.multiple_of(row * span, 16), span)
        buf, out = dense[index]
        return pltpu.make_async_copy(buf, out.at[here], dense_sem.at[index])

    def keep_dense(row, index, value):
        @pl.when(row > 0)
        def _():
            dense_copy(row - 1, index).wait()

        dense[index][0][...] = value
        dense_copy(row, index).start()

    pool_ref[...] = jnp.zeros_like(pool_ref)
    imp_ref[...] = jnp.zeros_like(imp_ref)
    routers = router_ref[...].astype(jnp.bfloat16)
    if routers.shape[0] < 128:
        routers = jnp.concatenate(
            [routers, jnp.zeros((128 - routers.shape[0], width), jnp.bfloat16)], 0
        )
    lane = lax.broadcasted_iota(jnp.int32, (span, 128), 1)

    def dense_row(row, carry):
        here = pl.ds(pl.multiple_of(row * span, 16), span)
        x_zero = dot_f32(patch_ref[here], w_ref[0], NN)
        keep_dense(row, 0, x_zero)
        a_one = (norm_parts(x_zero)[0] * gain_ref[0:1] + gain_ref[3:4]).astype(jnp.bfloat16)
        keep_dense(row, 1, a_one)

        @pl.when(row > 0)
        def _():
            dense_copy(row - 1, 2).wait()

        for part in range(3):
            qkv_buf[:, part * width : (part + 1) * width] = dot_f32(
                a_one, w_ref[1 + part], NN
            ).astype(jnp.bfloat16)
        dense_copy(row, 2).start()
        open_to = allowed_slots(length_ref, row, images, mask_ref[pl.ds(row, 1)], span)
        logs = jnp.zeros((span, 128), jnp.float32)

        @pl.when(row > 0)
        def _():
            dense_copy(row - 1, 3).wait()

        for pair in range(width // 128):
            query, key, value = (
                qkv_buf[:, part * width + pair * 128 : part * width + (pair + 1) * 128]
                for part in range(3)
            )
            outs = []
            for side in range(2):
                held = jnp.where((lane < 64) == (side == 0), query, jnp.zeros_like(query))
                raw = dot_f32(held, key, NT)
                probs, sums = [], []
                for spot in tiles(span, 64):
                    scores = jnp.where(open_to[spot] > 0.0, raw[spot] * 64**-0.5, mask_fill)
                    top = jnp.max(scores, 1, keepdims=True)
                    powers = jnp.exp(scores - top)
                    whole_sum = jnp.sum(powers, 1, keepdims=True)
                    probs.append((powers * (1.0 / whole_sum)).astype(jnp.bfloat16))
                    sums.append(top + jnp.log(whole_sum))
                outs.append(dot_f32(jnp.concatenate(probs, 0), value, NN))
                logs = jnp.where(lane == 2 * pair + side, jnp.concatenate(sums, 0), logs)
            att_buf[:, pair * 128 : (pair + 1) * 128] = jnp.where(
                lane < 64, outs[0], outs[1]
            ).astype(jnp.bfloat16)
        lse_ref[here] = logs
        dense_copy(row, 3).start()
        x_one = x_zero + dot_f32(att_buf[...], w_ref[4], NN)
        keep_dense(row, 4, x_one)
        a_two = (norm_parts(x_one)[0] * gain_ref[1:2] + gain_ref[4:5]).astype(jnp.bfloat16)
        a_two_ref[here] = a_two
        logits = jnp.where(lane < n_experts, dot_f32(a_two, routers, NT), mask_fill)
        powers = jnp.exp(logits - jnp.max(logits, 1, keepdims=True))
        probs = powers / jnp.sum(powers, 1, keepdims=True)
        prob_ref[here] = probs
        columns = col_ref[here]
        valid, pool, image = columns[:, 2:3], columns[:, 3:4], columns[:, 4:5]
        imp_ref[0:1, 0:128] += jnp.sum(probs * valid, 0, keepdims=True)
        line = lax.broadcasted_iota(jnp.int32, pool_ref.shape, 0)
        for index in range(images):
            number = row * images + index
            weight = jnp.where(image == number.astype(jnp.float32), pool, 0.0)
            pooled = jnp.sum(x_one * weight, 0, keepdims=True)
            pool_ref[...] = jnp.where(line == number, pooled, pool_ref[...])
        return carry

    lax.fori_loop(0, rows_here, dense_row, 0)

    columns = col_ref[...]
    places[...] = columns.T[:8]
    def rows_of(member):
        slots = lax.broadcasted_iota(jnp.int32, (padded, tokens), 0) + member * padded
        slots = slots.astype(jnp.float32)
        match = (slots == places[0:1]) | (slots == places[1:2])
        match = jnp.where(match, 1.0, 0.0).astype(jnp.bfloat16)
        return dot_f32(match, a_two_ref[...], NN).astype(jnp.bfloat16)

    def row_copy(member, source):
        return send(
            send_rows.at[member], rows_in.at[source], r_out.at[member], r_in.at[source], at.of_member(member)
        )

    def detail_copy(member, source):
        return send(
            send_detail.at[member], detail_in.at[source], m_out.at[member], m_in.at[source], at.of_member(member)
        )

    def dispatch_step(index, carry):
        member = lax.rem(at.member + index, n_experts)
        send_rows[member] = rows_of(member)
        row_copy(member, at.member).start()
        return carry

    lax.fori_loop(1, n_experts, dispatch_step, 0)
    lane = lax.broadcasted_iota(jnp.int32, (tokens, 128), 1)
    kind, expert = lax.div(lane, n_experts), lax.rem(lane, n_experts).astype(jnp.float32)
    slot_lane = lax.broadcasted_iota(jnp.int32, (tokens, send_detail.shape[2]), 1).astype(jnp.float32)
    pool, image = columns[:, 3:4], columns[:, 4:5]
    details = None
    for choice in range(2):
        slot, pick = columns[:, choice : choice + 1], columns[:, 5 + choice : 6 + choice]
        hot = (expert == pick) & (slot >= 0.0)
        gate = jnp.sum(jnp.where(hot & (kind == 0), prob_ref[...], 0.0), 1, keepdims=True)
        values = jnp.zeros((tokens, 128), jnp.float32)
        pieces = [*split_three(gate), *split_three(pool), image]
        for index, piece in enumerate(pieces):
            values = jnp.where(kind == index, piece.astype(jnp.float32), values)
        values = jnp.where(hot, values, 0.0).astype(jnp.bfloat16)
        spot = jnp.where(slot >= 0.0, slot - pick * padded, -1.0)
        chosen = jnp.where(spot == slot_lane, 1.0, 0.0).astype(jnp.bfloat16)
        found = dot_f32(values, chosen, TN)
        details = found if details is None else details + found
    n = n_experts
    gates = details[0:n] + details[n : 2 * n] + details[2 * n : 3 * n]
    pools = details[3 * n : 4 * n] + details[4 * n : 5 * n] + details[5 * n : 6 * n]
    numbers = details[6 * n : 7 * n]
    for index in range(n):
        for spot, value in enumerate((gates, pools, numbers)):
            send_detail[index, spot : spot + 1] = value[index : index + 1]
        send_detail[index, 3:8] = jnp.zeros((5, send_detail.shape[2]), jnp.float32)

    for member in others(at.member, n_experts):
        detail_copy(member, at.member).start()
    rows_in[at.member] = rows_of(at.member)
    detail_in[at.member] = send_detail[at.member]
    a_two_copy = pltpu.make_async_copy(a_two_ref, a_two_out, keep_sem.at[0])
    a_two_copy.start()
    for index in range(len(dense)):
        dense_copy(rows_here - 1, index).wait()

    shard_waits(range(early))
    for step in range(early):
        swap_copy(step).wait_recv()

    many = act_buf.shape[1] // padded
    count = many * padded
    rounds = n_experts // many

    def hidden_copies(index, chunk):
        block, turn = block_of(index), lax.div(index, rounds)
        here = pl.ds(pl.multiple_of(block * count, 16), count)
        there = turn * half + chunk
        return (
            pltpu.make_async_copy(act_buf.at[chunk], act_out.at[there, here], act_sem.at[chunk]),
            pltpu.make_async_copy(slope_buf.at[chunk], slope_out.at[there, here], slope_sem.at[chunk]),
        )

    def block_of(index):
        return lax.rem(lax.div(at.member, many) + index, rounds)

    def expert_step(index, carry):
        turn = lax.div(index, rounds)
        block = block_of(index)

        @pl.when(turn == 0)
        def _():
            for spot in range(many):
                source = block * many + spot

                @pl.when(source != at.member)
                def _():
                    row_copy(source, source).wait_recv()
                    detail_copy(source, source).wait_recv()

        @pl.when(index == 0)
        def _():
            shard_starts(range(middle, half))

        @pl.when(index == rounds)
        def _():
            shard_waits(range(early, half))

        rows = rows_in[pl.ds(block * many, many)].reshape(count, width)
        for chunk in range(half):
            if chunk == early:

                @pl.when(index == rounds)
                def _():
                    for step in range(early, half):
                        swap_copy(step).wait_recv()
                    keeps[2].start()

            hidden_all = dot_f32(rows, weights[turn, chunk, 0], NT)

            @pl.when(index > 0)
            def _():
                for copy in hidden_copies(index - 1, chunk):
                    copy.wait()

            for spot in tiles(count):
                hidden = hidden_all[spot]
                square = hidden * hidden
                curve = jnp.tanh(hidden * (0.7978845608 + 0.7978845608 * 0.044715 * square))
                upper = 0.5 + 0.5 * curve
                gelu = hidden * upper
                slope = upper + gelu * (1.0 - upper) * (
                    2.0 * 0.7978845608 + 6.0 * 0.7978845608 * 0.044715 * square
                )
                act_buf[chunk, spot] = gelu.astype(jnp.bfloat16)
                slope_buf[chunk, spot] = slope.astype(jnp.bfloat16)
            for copy in hidden_copies(index, chunk):
                copy.start()
        acts = jnp.concatenate([act_buf[chunk] for chunk in range(half)], 1)
        ends = jnp.concatenate([weights[turn, chunk, 1] for chunk in range(half)], 0)
        found = dot_f32(acts, ends, NN)
        here = pl.ds(pl.multiple_of(block * count, 16), count)

        @pl.when(turn == 0)
        def _():
            total[here] = found

        @pl.when(turn == 1)
        def _():
            result = (total[here] + found).astype(jnp.bfloat16)
            for spot in range(many):
                source = block * many + spot
                mine = result[spot * padded : (spot + 1) * padded]
                send_rows[source] = mine
                detail = detail_in[source]
                weight = detail[0:1, :padded] * detail[1:2, :padded]
                shares = jnp.where(image_hot(detail, padded), weight, 0.0)
                pieces = jnp.concatenate(split_three(shares), 0)
                sums = dot_f32(pieces, mine, NN)
                part_ref[source] = (
                    sums[:IMAGE_PAD] + sums[IMAGE_PAD : 2 * IMAGE_PAD] + sums[2 * IMAGE_PAD :]
                )

        @pl.when(index == rounds - 1)
        def _():
            for member in others(at.member, n_experts):
                row_copy(member, at.member).wait_send()
                detail_copy(member, at.member).wait_send()
            for copy in keeps[:2]:
                copy.start()

        return carry

    keeps = [
        pltpu.make_async_copy(rows_in, rows_out, keep_sem.at[1]),
        pltpu.make_async_copy(detail_in, detail_out, keep_sem.at[2]),
        pltpu.make_async_copy(weights, weight_out, keep_sem.at[4]),
        pltpu.make_async_copy(send_rows, y_out, keep_sem.at[3]),
    ]
    lax.fori_loop(0, 2 * rounds, expert_step, 0)
    keeps[3].start()
    for chunk in range(half):
        for copy in hidden_copies(2 * rounds - 1, chunk):
            copy.wait()
    for step in range(half):
        own = team.target(step)[2]
        swap_copy(step).wait_send()

        @pl.when(jnp.logical_not(own))
        def _():
            shard_copy(step).wait_send()

    a_two_copy.wait()
    w_copy.wait()
    for copy in keeps:
        copy.wait()
    for copy in gathers:
        copy.wait_send()


def forward(sizes, n_experts, padded, lengths, slot_mask, picks, ranks, patches, dense, norms, routers, expert_in, expert_out):
    rows_here, span = slot_mask.shape
    tokens, width = patches.shape
    part = expert_in.shape[1]
    mats, rows_own, unused = dense.shape
    tall = max(8, n_experts)
    depth = round_up(mats * rows_own + tall, 16)
    Z, Y, X = QUAD, sizes["g"], sizes["x"]
    half = 2 * sizes["g"]
    lanes = round_up(padded, 128)
    many = max(1, (144 if part % 128 else 576) // padded)
    count = n_experts * padded
    f32, kind = jnp.float32, jnp.bfloat16
    dma = pltpu.SemaphoreType.DMA
    each, parts, two = dma((n_experts,)), dma((half,)), dma((2,))
    by_y, by_x, by_z = dma((Z, Y)), dma((Z, X)), dma((Z,))

    def out(wide, dtype):
        return jax.ShapeDtypeStruct((tokens, wide), dtype)

    hidden = jax.ShapeDtypeStruct((2 * half, count, part), kind)
    rows = (n_experts, padded, width)
    return pl.pallas_call(
        functools.partial(forward_kernel, sizes, n_experts, lengths.shape[1], padded),
        out_shape=(
            jax.ShapeDtypeStruct((mats, width, width), kind), jax.ShapeDtypeStruct((8, width), f32),
            jax.ShapeDtypeStruct((tall, width), f32), out(128, f32),
            out(width, f32), out(width, kind), out(3 * width, kind), out(width, kind), out(width, f32),
            out(width, kind), out(128, f32), out(128, f32),
            jax.ShapeDtypeStruct((IMAGE_PAD, width), f32), jax.ShapeDtypeStruct((8, width), f32),
            jax.ShapeDtypeStruct(rows, kind), jax.ShapeDtypeStruct((n_experts, 8, lanes), f32),
            hidden, hidden, jax.ShapeDtypeStruct(rows, kind),
            jax.ShapeDtypeStruct((n_experts, IMAGE_PAD, width), f32),
            jax.ShapeDtypeStruct((2, half, 2, part, width), kind),
        ),
        in_specs=[whole(pltpu.SMEM)] + [whole()] * 8 + [whole(ANY)] * 2,
        out_specs=(whole(ANY), whole(), whole(), whole()) + (whole(ANY),) * 6 + (whole(),) * 4 + (whole(ANY),) * 5 + (whole(), whole(ANY)),
        scratch_shapes=[
            VMEM((2, Z, X, Y, depth, width), kind), VMEM((mats, width, width), kind), VMEM((2, 2, part, width), kind),
            VMEM((span, width), f32), VMEM((span, width), kind), VMEM((span, 3 * width), kind),
            VMEM((span, width), kind), VMEM((span, width), f32), VMEM((tokens, width), kind),
            VMEM((2, half, 2, part, width), kind), VMEM(rows, kind), VMEM((n_experts, 8, lanes), f32),
            VMEM((8, tokens), f32), VMEM(rows, kind), VMEM((n_experts, 8, lanes), f32),
            VMEM((count, width), f32), VMEM((half, many * padded, part), kind),
            VMEM((half, many * padded, part), kind), dma((5,)), dma((6,)), two,
            parts, parts, parts, parts, each, each, each, each, parts, parts, dma((2, 2)),
            by_z, by_z, by_y, by_y, by_x, by_x, by_x, by_x, by_y, by_y, by_z, by_z,
        ],
        compiler_params=pltpu.CompilerParams(
            collective_id=5, has_side_effects=True, vmem_limit_bytes=62 * MIB
        ),
        cost_estimate=cost(120),
        name="forward",
    )(lengths, lengths, slot_mask, picks.T, ranks, patches, dense, norms, routers.T, expert_in, expert_out)


def chunk_at(index, half):
    early = half // 2
    step = lax.rem(index, half)
    side = jnp.where(index < half, early, 0)
    return lax.div(step, early) * half + side + lax.rem(step, early)


def expert_backward_kernel(
    sizes, padded, rows_ref, detail_ref, pool_ref, y_ref, slope_ref, act_ref, weight_ref, *refs
):
    at = Place(sizes)
    sources, unused, width = rows_ref.shape
    chunks, unused, part = slope_ref.shape
    half = chunks // 2
    back_ref, gate_ref, *outs = refs[: 2 + half]
    d_hidden, d_rows, send_rows, send_gate, send_grad, got_grad = refs[2 + half : 8 + half]
    own_sem, r_out, r_in, m_out, m_in, g_out, g_in, g_keep = refs[8 + half :]
    many = y_ref.shape[0]
    rounds = sources // many
    step = pl.program_id(0)
    team = others(at.member, sources)

    def row_copy(member, source):
        return send(
            send_rows.at[member], back_ref.at[source], r_out.at[member], r_in.at[source], at.of_member(member)
        )

    def gate_copy(member, source):
        return send(
            send_gate.at[member], gate_ref.at[source], m_out.at[member], m_in.at[source], at.of_member(member)
        )

    def keep_copies():
        return (
            pltpu.make_async_copy(send_rows.at[at.member], back_ref.at[at.member], own_sem.at[0]),
            pltpu.make_async_copy(send_gate.at[at.member], gate_ref.at[at.member], own_sem.at[1]),
        )

    def grad_copy(index):
        return send(
            send_grad.at[index], got_grad.at[index], g_out.at[index], g_in.at[index], at.sibling()
        )

    def out_copy(index):
        return pltpu.make_async_copy(got_grad.at[index], outs[index], g_keep.at[index])

    @pl.when(step == 0)
    def _():
        greet([at.of_member(member) for member in team] + [at.sibling()])

    @pl.when(step < rounds)
    def _():
        block = lax.rem(lax.div(at.member, many) + 1 + step, rounds)
        d_out = []
        for index in range(many):
            source = block * many + index
            detail = detail_ref[source]
            hot = image_hot(detail, padded)
            hots = jnp.where(hot, 1.0, 0.0).astype(jnp.bfloat16)
            pools = jnp.concatenate(split_three(pool_ref[source]), 0)
            wide = dot_f32(jnp.concatenate([hots] * 3, 0), pools, TN)
            lanes = detail.shape[1]
            upright = jnp.concatenate([detail, jnp.zeros((120, lanes), jnp.float32)], 0).T
            gate, pool = upright[:padded, 0:1], upright[:padded, 1:2]
            d_out.append((gate * (pool * wide)).astype(jnp.bfloat16))
            along = dot_f32(pools, y_ref[index], NT)
            along = along[:IMAGE_PAD] + along[IMAGE_PAD : 2 * IMAGE_PAD] + along[2 * IMAGE_PAD :]
            d_gate = jnp.sum(jnp.where(hot, along, 0.0), 0, keepdims=True) * detail[1:2, :padded]
            send_gate[source] = jnp.zeros(detail.shape, jnp.float32)
            send_gate[source, 0:1, :padded] = d_gate
        d_out = jnp.concatenate(d_out, 0)
        count = many * padded
        span = pl.ds(pl.multiple_of(block * count, 16), count)
        d_rows[span] = d_out

        def weight(index, which):
            return weight_ref[index // half, index % half, which]

        for index in range(chunks):
            d_act = dot_f32(d_out, weight(index, 1), NT)
            for spot in tiles(count):
                rows_now = pl.ds(pl.multiple_of(block * count + spot.start, 16), spot.stop - spot.start)
                d_hidden[index, rows_now] = (
                    d_act[spot] * slope_ref[index, spot].astype(jnp.float32)
                ).astype(jnp.bfloat16)
        d_hids = jnp.concatenate([d_hidden[index, span] for index in range(chunks)], 1)
        starts = jnp.concatenate([weight(index, 0) for index in range(chunks)], 0)
        total = dot_f32(d_hids, starts, NN)
        total = total.astype(jnp.bfloat16)
        for index in range(many):
            source = block * many + index
            send_rows[source] = total[index * padded : (index + 1) * padded]

            @pl.when(source != at.member)
            def _():
                row_copy(source, at.member).start()
                gate_copy(source, at.member).start()

            @pl.when(source == at.member)
            def _():
                for copy in keep_copies():
                    copy.start()

    @pl.when(step >= rounds)
    def _():
        index = step - rounds
        chunk = chunk_at(index, half)
        rows = rows_ref[...].reshape(sources * padded, width)
        g_one = dot_f32(d_hidden[chunk], rows, TN)
        g_two = dot_f32(act_ref[0], d_rows[...], TN)

        @pl.when(index < half)
        def _():
            send_grad[index, 0] = g_one.astype(jnp.bfloat16)
            send_grad[index, 1] = g_two.astype(jnp.bfloat16)
            grad_copy(index).start()

        @pl.when(index >= half)
        def _():
            spot = index - half
            grad_copy(spot).wait_recv()
            got_grad[spot, 0] = (got_grad[spot, 0].astype(jnp.float32) + g_one).astype(jnp.bfloat16)
            got_grad[spot, 1] = (got_grad[spot, 1].astype(jnp.float32) + g_two).astype(jnp.bfloat16)

        for spot in range(half):

            @pl.when(index == spot + half)
            def _():
                out_copy(spot).start()

    @pl.when(step == rounds + chunks - 1)
    def _():
        for member in team:
            row_copy(member, member).wait_recv()
            gate_copy(member, member).wait_recv()
        for member in team:
            row_copy(member, at.member).wait_send()
            gate_copy(member, at.member).wait_send()
        for copy in keep_copies():
            copy.wait()
        for spot in range(half):
            grad_copy(spot).wait_send()
            out_copy(spot).wait()


def expert_backward(sizes, rows, details, pools, results, slopes, acts, weights):
    sources, padded, width = rows.shape
    chunks, count, part = acts.shape
    many = max(1, (288 if part % 128 else 576) // padded)
    rounds, half = sources // many, chunks // 2
    lanes = details.shape[2]
    kind = jnp.bfloat16
    dma = pltpu.SemaphoreType.DMA
    each, parts = dma((sources,)), dma((half,))

    def block_of(step):
        member = lax.axis_index("x") * QUAD + lax.axis_index("r")
        return lax.rem(lax.div(member, many) + 1 + jnp.minimum(step, rounds - 1), rounds)

    def chunk_of(step):
        return chunk_at(jnp.maximum(step - rounds, 0), half)

    return pl.pallas_call(
        functools.partial(expert_backward_kernel, sizes, padded),
        grid=(rounds + chunks,),
        out_shape=(
            jax.ShapeDtypeStruct((sources, padded, width), kind),
            jax.ShapeDtypeStruct((sources, 8, lanes), jnp.float32),
        )
        + (jax.ShapeDtypeStruct((2, part, width), kind),) * half,
        in_specs=[
            whole(), whole(), whole(),
            pl.BlockSpec((many, padded, width), lambda i: (block_of(i), 0, 0)),
            pl.BlockSpec((chunks, many * padded, part), lambda i: (0, block_of(i), 0)),
            pl.BlockSpec((1, count, part), lambda i: (chunk_of(i), 0, 0)),
        ]
        + [whole()],
        out_specs=(whole(ANY),) * (2 + half),
        scratch_shapes=[
            VMEM((chunks, count, part), kind),
            VMEM((count, width), kind),
            VMEM((sources, padded, width), kind),
            VMEM((sources, 8, lanes), jnp.float32),
            VMEM((half, 2, part, width), kind),
            VMEM((half, 2, part, width), kind),
            dma((2,)), each, each, each, each, parts, parts, parts,
        ],
        compiler_params=pltpu.CompilerParams(
            collective_id=6, has_side_effects=True, vmem_limit_bytes=62 * MIB
        ),
        cost_estimate=cost(65),
        name="expert_backward",
    )(rows, details, pools, results, slopes, acts, weights)


def dense_backward_kernel(
    sizes, n_experts, images, padded, length_ref, mask_ref, patch_ref, x_zero_ref, a_one_ref, qkv_ref, att_ref,
    x_one_ref, a_two_ref, prob_ref, lse_ref, col_ref, w_ref, gain_ref, router_ref, back_ref, gate_ref,
    pool_ref, imp_ref, third_ref, out_ref, grads, g_router, g_norm, d_qkv
):
    row = pl.program_id(0)
    span, width = x_zero_ref.shape
    mats, rows = grads.shape[0], width // (8 * sizes["g"] * sizes["x"])

    @pl.when(row == 0)
    def _():
        grads[...] = jnp.zeros_like(grads)
        g_router[...] = jnp.zeros_like(g_router)
        g_norm[...] = third_ref[...]

    columns = col_ref[...]
    slot_one, slot_two = columns[:, 0:1], columns[:, 1:2]
    count = n_experts * padded
    slot = lax.broadcasted_iota(jnp.int32, (span, count), 1).astype(jnp.float32)
    match = jnp.where((slot == slot_one) | (slot == slot_two), 1.0, 0.0).astype(jnp.bfloat16)
    d_a_two = dot_f32(match, back_ref[...].reshape(count, width), NN)
    lanes = gate_ref.shape[2]
    spot = lax.broadcasted_iota(jnp.int32, (span, lanes), 1)
    inside = spot < padded
    spot = spot.astype(jnp.float32)
    found_one, found_two = jnp.zeros((span, lanes), jnp.float32), jnp.zeros((span, lanes), jnp.float32)
    for expert in range(n_experts):
        line = jnp.broadcast_to(gate_ref[expert, 0:1], (span, lanes))
        found_one = jnp.where(inside & (spot == slot_one - expert * padded), line, found_one)
        found_two = jnp.where(inside & (spot == slot_two - expert * padded), line, found_two)
    d_gate_one = jnp.sum(found_one, 1, keepdims=True)
    d_gate_two = jnp.sum(found_two, 1, keepdims=True)
    lane = lax.broadcasted_iota(jnp.int32, (span, 128), 1)
    number = lane.astype(jnp.float32)
    valid, pool, image = columns[:, 2:3], columns[:, 3:4], columns[:, 4:5]
    head = lax.broadcasted_iota(jnp.int32, (1, 128), 1) < n_experts
    importance = imp_ref[0:1, 0:128]
    centre = jnp.sum(jnp.where(head, importance, 0.0), 1, keepdims=True) / n_experts
    away = jnp.where(head, importance - centre, 0.0)
    spread = jnp.sum(away * away, 1, keepdims=True) / n_experts
    d_imp = aux_weight * (
        2.0 * away / (n_experts * centre * centre)
        - 2.0 * spread / (n_experts * centre * centre * centre)
    )
    d_probs = valid * d_imp
    d_probs = d_probs + jnp.where(number == columns[:, 5:6], d_gate_one, 0.0)
    d_probs = d_probs + jnp.where(number == columns[:, 6:7], d_gate_two, 0.0)
    probs = prob_ref[...]
    d_router = (probs * (d_probs - jnp.sum(probs * d_probs, 1, keepdims=True))).astype(jnp.bfloat16)
    g_router[...] += dot_f32(d_router, a_two_ref[...], TN)
    routers = router_ref[...].astype(jnp.bfloat16)
    if routers.shape[0] < 128:
        routers = jnp.concatenate(
            [routers, jnp.zeros((128 - routers.shape[0], width), jnp.bfloat16)], 0
        )
    d_a_two = d_a_two + dot_f32(d_router, routers, NN)
    scaled, scale = norm_parts(x_one_ref[...])
    g_norm[1:2] += jnp.sum(d_a_two * scaled, 0, keepdims=True)
    g_norm[4:5] += jnp.sum(d_a_two, 0, keepdims=True)
    d_x_one = norm_back(d_a_two, scaled, scale, gain_ref[1:2])
    for index in range(images):
        place = row * images + index
        weight = jnp.where(image == place.astype(jnp.float32), pool, 0.0)
        d_x_one = d_x_one + weight * pool_ref[pl.ds(place, 1)]
    d_att = d_x_one.astype(jnp.bfloat16)
    grads[4] += dot_f32(att_ref[...], d_att, TN)
    d_out = dot_f32(d_att, w_ref[4], NT).astype(jnp.bfloat16)
    open_to = allowed_slots(length_ref, row, images, mask_ref[pl.ds(row, 1)], span)
    logs = lse_ref[...]
    for pair in range(width // 128):
        query, key, value = (
            qkv_ref[:, part * width + pair * 128 : part * width + (pair + 1) * 128]
            for part in range(3)
        )
        d_pair = d_out[:, pair * 128 : (pair + 1) * 128]
        found = []
        for side in range(2):
            left = (lane < 64) == (side == 0)
            held = jnp.where(left, query, jnp.zeros_like(query))
            raw = dot_f32(held, key, NT)
            d_held = jnp.where(left, d_pair, jnp.zeros_like(d_pair))
            d_raw = dot_f32(d_held, value, NT)
            chances, d_scores = [], []
            for spot in tiles(span, 64):
                scores = jnp.where(open_to[spot] > 0.0, raw[spot] * 64**-0.5, mask_fill)
                chance = jnp.exp(scores - logs[spot, 2 * pair + side : 2 * pair + side + 1])
                chances.append(chance.astype(jnp.bfloat16))
                d_chance = d_raw[spot]
                d_score = chance * (d_chance - jnp.sum(chance * d_chance, 1, keepdims=True))
                d_scores.append(d_score.astype(jnp.bfloat16))
            d_value = dot_f32(jnp.concatenate(chances, 0), d_pair, TN)
            d_scores = jnp.concatenate(d_scores, 0)
            d_query = dot_f32(d_scores, key, NN) * 64**-0.5
            d_key = dot_f32(d_scores, query, TN) * 64**-0.5
            found.append((d_query, d_key, d_value))
        for part in range(3):
            d_qkv[:, part * width + pair * 128 : part * width + (pair + 1) * 128] = jnp.where(
                lane < 64, found[0][part], found[1][part]
            ).astype(jnp.bfloat16)
    d_a_one = None
    for part in range(3):
        piece = d_qkv[:, part * width : (part + 1) * width]
        grads[1 + part] += dot_f32(a_one_ref[...], piece, TN)
        found = dot_f32(piece, w_ref[1 + part], NT)
        d_a_one = found if d_a_one is None else d_a_one + found
    scaled, scale = norm_parts(x_zero_ref[...])
    g_norm[0:1] += jnp.sum(d_a_one * scaled, 0, keepdims=True)
    g_norm[3:4] += jnp.sum(d_a_one, 0, keepdims=True)
    d_x_zero = norm_back(d_a_one, scaled, scale, gain_ref[0:1]) + d_x_one
    grads[0] += dot_f32(patch_ref[...], d_x_zero.astype(jnp.bfloat16), TN)

    @pl.when(row == pl.num_programs(0) - 1)
    def _():
        Z, Y, X = QUAD, sizes["g"], sizes["x"]
        tall = max(8, n_experts)
        norms = g_norm[...]
        if tall > 8:
            norms = jnp.concatenate([norms, jnp.zeros((tall - 8, width), jnp.float32)], 0)
        router_grads = g_router[:tall]
        depth = out_ref.shape[4]
        device = 0
        for z in range(Z):
            for y in range(Y):
                for x in range(X):
                    for c in range(2):
                        spot = slice(device * rows, (device + 1) * rows)
                        blank = jnp.zeros((tall, 128 - rows), jnp.float32)
                        tail = [norms[:, spot], blank, router_grads[:, spot], blank]
                        tail.append(jnp.zeros((tall, width - 256), jnp.float32))
                        pieces = [grads[mat, spot] for mat in range(mats)]
                        pieces.append(jnp.concatenate(tail, 1))
                        left = depth - mats * rows - tall
                        if left:
                            pieces.append(jnp.zeros((left, width), jnp.float32))
                        out_ref[c, z, x, y] = jnp.concatenate(pieces, 0).astype(jnp.bfloat16)
                        device += 1


def dense_backward(
    sizes, n_experts, padded, rows_own, lengths, slot_mask, patches, kept, columns, weights, gains, routers, back,
    gates, pooled, importance, third
):
    rows_here, span = slot_mask.shape
    tokens, width = patches.shape
    mats = weights.shape[0]
    depth = round_up(mats * rows_own + max(8, n_experts), 16)
    x_zero, a_one, qkv, att, x_one, a_two, probs, logs = kept

    def block(wide):
        return pl.BlockSpec((span, wide), lambda i: (i, 0))

    return pl.pallas_call(
        functools.partial(dense_backward_kernel, sizes, n_experts, lengths.shape[1], padded),
        grid=(rows_here,),
        out_shape=jax.ShapeDtypeStruct(
            (2, QUAD, sizes["x"], sizes["g"], depth, width), jnp.bfloat16
        ),
        in_specs=[
            whole(pltpu.SMEM), whole(), block(width),
            block(width), block(width), block(3 * width), block(width), block(width), block(width),
            block(128), block(128), block(128),
        ]
        + [whole()] * 8,
        out_specs=whole(),
        scratch_shapes=[
            VMEM((mats, width, width), jnp.float32),
            VMEM((128, width), jnp.float32),
            VMEM((8, width), jnp.float32),
            VMEM((span, 3 * width), jnp.bfloat16),
        ],
        compiler_params=pltpu.CompilerParams(vmem_limit_bytes=60 * MIB),
        cost_estimate=cost(50),
        name="dense_backward",
    )(
        lengths, slot_mask, patches, x_zero, a_one, qkv, att, x_one, a_two, probs, logs, columns,
        weights, gains, routers, back, gates, pooled, importance, third,
    )


def shard_moves(n_blocks):
    span = 2 * n_blocks
    moves = []
    for step in step_order(n_blocks):
        pairs = []
        for place in range(QUAD * n_blocks):
            for core in range(2):
                target = (place + step) % span
                src = place * 2 + core
                dst = (target // 2 * QUAD + 2 * core + target % 2) * 2 + place // span
                pairs.append((src, dst))
        moves.append(pairs)
    return moves


def return_experts(parts, n_blocks):
    return [
        lax.ppermute(part, ("g", "r", "c"), [(dst, src) for src, dst in pairs])
        for part, pairs in zip(parts, shard_moves(n_blocks))
    ]


def body(
    patches,
    lengths,
    slot_mask,
    expert_picks,
    priority_rank,
    class_labels,
    dense_weights,
    dense_first,
    dense_second,
    dense_average,
    router_weights,
    router_first,
    router_second,
    router_average,
    norm_params,
    norm_first,
    norm_second,
    norm_average,
    expert_in,
    in_first,
    in_second,
    in_average,
    expert_out,
    out_first,
    out_second,
    out_average,
    head_weights,
    head_first,
    head_second,
    head_average,
):
    n_blocks = lax.axis_size("g")
    sizes = {name: lax.axis_size(name) for name in ALL}
    rows_own, n_experts = router_weights.shape
    rows_here, n_slots_row = slot_mask.shape
    tokens, model_width = patches.shape
    n_images = lengths.shape[0] * lengths.shape[1]
    capacity = (21 * tokens * TOP + 20 * n_experts - 1) // (20 * n_experts)
    padded = round_up(capacity, 16)
    (
        layer_b, gain_rows, router_t, columns,
        x_zero, a_one, qkv, att_out, x_one, a_two, router_probs, logs, pooled, part_importance,
        arrived, details, activated, slope, result, part_pooled, expert_weights
    ) = forward(
        sizes, n_experts, padded, lengths, slot_mask, expert_picks, priority_rank, patches, dense_weights, norm_params,
        router_weights, expert_in, expert_out
    )
    g_head, d_pooled_all, d_pooled, g_norm_three, head_sums, total_importance = head_step(
        sizes,
        n_images,
        part_pooled,
        pooled,
        part_importance,
        gain_rows,
        head_weights,
        class_labels,
    )
    d_back, back_gate, *grads = expert_backward(
        sizes, arrived, details, d_pooled_all, result, slope, activated, expert_weights
    )
    parts = return_experts(grads, n_blocks)
    blocks = dense_backward(
        sizes,
        n_experts,
        padded,
        rows_own,
        lengths,
        slot_mask,
        patches,
        (x_zero, a_one, qkv, att_out, x_one, a_two, router_probs, logs),
        columns,
        layer_b,
        gain_rows,
        router_t,
        d_back,
        back_gate,
        d_pooled,
        total_importance,
        g_norm_three,
    )
    reduced, dense_sums = scatter_dense(sizes, blocks)
    g_one, g_two, totals = finish(
        sizes, n_experts, parts, head_sums, dense_sums, total_importance
    )
    n_dense = dense_weights.shape[0] * rows_own
    g_layers = reduced[:n_dense].reshape(-1, rows_own, model_width)
    g_norms = reduced[n_dense : n_dense + 6, :rows_own]
    g_router = reduced[n_dense : n_dense + n_experts, 128 : 128 + rows_own].T
    importance = total_importance[0, :n_experts]
    loss_value, grad_norm, factor = totals[0, 0], totals[1, 0], totals[2, 0]
    dense_out = adam_update(
        dense_weights, dense_first, dense_second, dense_average, g_layers, factor, base_rate
    )
    router_out = adam_update(
        router_weights, router_first, router_second, router_average, g_router, factor, base_rate
    )
    norm_out = adam_update(
        norm_params, norm_first, norm_second, norm_average, g_norms, factor, norm_rate
    )
    in_out = adam_update(expert_in, in_first, in_second, in_average, g_one, factor, base_rate)
    out_out = adam_update(expert_out, out_first, out_second, out_average, g_two, factor, base_rate)
    head_out = adam_update(
        head_weights, head_first, head_second, head_average, g_head, factor, base_rate
    )
    return (
        loss_value,
        importance,
        grad_norm,
        *dense_out,
        *router_out,
        *norm_out,
        *in_out,
        *out_out,
        *head_out,
    )


def solution(mesh):
    n_dp, n_expert = mesh.shape["dp"], mesh.shape["expert"]
    shaped = mesh.devices.reshape(n_dp // QUAD, QUAD, n_expert // 2, 2)
    fine = Mesh(shaped, ALL)
    rows = P(ALL, None)
    dense = P(None, ALL, None)
    norms = P(None, ALL)
    experts = P(("x", "c"), ("g", "r"), None)
    placed = (rows,) * 6 + (dense,) * 4 + (rows,) * 4 + (norms,) * 4 + (experts,) * 8 + (rows,) * 4
    results = (
        (P(),) * 3 + (dense,) * 4 + (rows,) * 4 + (norms,) * 4 + (experts,) * 8 + (rows,) * 4
    )
    return jax.shard_map(body, mesh=fine, in_specs=placed, out_specs=results, check_vma=False)
```
